32 devices in a mesh: bulk: 8 (over z, y), rep: 4 (over x, core).
Axes of the slice: x: 2, y: 2, z: 4, core: 2. Of those that a mesh axis runs over, the one named last changes fastest.
Arguments:
- orbitals: float32 [1024, 2048], P('rep', 'bulk'), may hold values from -6 to 6
- triangles: float32 [1024, 1024], P('rep', 'bulk'), may hold values from -0.09375 to 0.09375
- coupling: float32 [1024, 1024], P('rep', 'bulk'), may hold values from -0.09375 to 0.09375
- diagonals: float32 [2, 1024], P(None, 'bulk'), may hold values from 1 to 2
Outputs:
- solved: float32 [1024, 2048], P(('rep', 'bulk'))
The draws below stay inside these ranges and needn't reach their ends.
All inputs are finite; a program needn't handle non-finite values.
Results may differ from the reference program's by a relative error of at most 0.000084.
Values sent between devices are 32-bit elements; how exact they have to be, the bound alone decides.
No kernel may reach another device: no remote copies, remote signals or barrier semaphores. Data moves between devices by JAX's collectives and lax.ppermute only.
A program may use at most 64 MiB of HBM per device.

```python
import jax
import jax.numpy as jnp
from jax import lax

PW = 1024
NB = 2048
COEF = 1024


def shard_levels(rng, dims, pieces, low, largest):
    factor_of = 1.0
    for axis_at, shards_of in pieces:
        heights = jax.random.uniform(jax.random.fold_in(jax.random.fold_in(rng, 6), axis_at), (shards_of,), jnp.float32, low / len(pieces), largest / len(pieces))
        factor_of = factor_of * jnp.repeat(jnp.exp(heights), dims[axis_at] // shards_of).reshape((-1,) + (1,) * (len(dims) - 1 - axis_at))
    return factor_of


def centred(own_key, extent, spread, bound, shards=(), held_as=jnp.bfloat16):
    level = shard_levels(own_key, extent, shards, -0.22, 0.18) if shards else 1.0
    values = jax.random.normal(own_key, extent, jnp.float32) * spread * level
    return jnp.minimum(jnp.maximum(values, -bound), bound).astype(held_as)


def setup_inputs(seed: int = 0) -> dict:
    arg_keys = jax.random.split(jax.random.key(seed), 5)
    orbitals = centred(arg_keys[0], (COEF, NB), 1.0, 6.0, ((0, 4), (1, 8)), jnp.float32)
    triangles = centred(arg_keys[1], (PW, PW), (4 * PW) ** -0.5, 0.09375, ((0, 4), (1, 8)), jnp.float32)
    coupling = centred(arg_keys[2], (PW, PW), (4 * PW) ** -0.5, 0.09375, ((0, 4), (1, 8)), jnp.float32)
    diagonals = jnp.clip(1.0 + 1.0 * jax.random.uniform(arg_keys[3], (2, PW), jnp.float32) ** shard_levels(arg_keys[3], (2, PW), ((1, 8),), -0.2, 0.2), 1.0, 2.0)
    return dict(orbitals=orbitals, triangles=triangles, coupling=coupling, diagonals=diagonals)


def unpack(triangles, diagonals):
    first_block = jnp.tril(triangles, -1) + jnp.diag(diagonals[0])
    second_block = jnp.tril(triangles.T, -1) + jnp.diag(diagonals[1])
    return (first_block, second_block)

def reference(orbitals, triangles, coupling, diagonals):
    first_block, second_block = unpack(triangles, diagonals)
    left_part = orbitals[:, :PW]
    right_part = orbitals[:, PW:]
    solved_one = jax.scipy.linalg.solve_triangular(first_block, left_part.T, lower=True).T
    update = jnp.dot(solved_one.astype(jnp.float32), coupling.T.astype(jnp.float32), precision=lax.Precision.HIGHEST, preferred_element_type=jnp.float32)
    solved_two = jax.scipy.linalg.solve_triangular(second_block, (right_part - update).T, lower=True).T
    return jnp.concatenate([solved_one, solved_two], axis=1)
```

```python
import jax
import jax.numpy as jnp
from jax import lax
from jax.experimental import pallas as pl
from jax.experimental.pallas import tpu as pltpu
from jax.sharding import PartitionSpec as P

F32 = jnp.float32
BF16 = jnp.bfloat16
NN = (((1,), (0,)), ((), ()))
NT = (((1,), (1,)), ((), ()))


def unpack(triangles, diagonals):
    first_block = jnp.tril(triangles, -1) + jnp.diag(diagonals[0])
    second_block = jnp.tril(triangles.T, -1) + jnp.diag(diagonals[1])
    return (first_block, second_block)


def per_device_any(orbitals, triangles, coupling, diagonals):
    tri_rows, couple_rows = (
        lax.all_gather(triangles, "rep", axis=0, tiled=True),
        lax.all_gather(coupling, "rep", axis=0, tiled=True),
    )
    tri_whole, couple_whole, diag_whole = (
        lax.all_gather(tri_rows, "bulk", axis=1, tiled=True),
        lax.all_gather(couple_rows, "bulk", axis=1, tiled=True),
        lax.all_gather(diagonals, "bulk", axis=1, tiled=True),
    )
    first_block, second_block = unpack(tri_whole, diag_whole)
    panel = first_block.shape[0]
    groups = lax.axis_size("bulk")
    local_rows = orbitals.shape[0] // groups
    blocks = orbitals.reshape(groups, local_rows, orbitals.shape[1])
    received = lax.all_to_all(blocks, "bulk", split_axis=0, concat_axis=2, tiled=True)
    rows_now = received.reshape(local_rows, received.shape[2])
    left_part = rows_now[:, :panel]
    right_part = rows_now[:, panel:]
    solved_one = jax.scipy.linalg.solve_triangular(first_block, left_part.T, lower=True).T
    update = jnp.dot(
        solved_one,
        couple_whole.T,
        precision=lax.Precision.HIGHEST,
        preferred_element_type=jnp.float32,
    )
    solved_two = jax.scipy.linalg.solve_triangular(
        second_block, (right_part - update).T, lower=True
    ).T
    return jnp.concatenate([solved_one, solved_two], axis=1)


def dot(a, b, dims=NN):
    return lax.dot_general(a, b, dims, preferred_element_type=F32)


def dot_exact(a, b):
    return lax.dot_general(a, b, NN, precision=lax.Precision.HIGHEST, preferred_element_type=F32)


def split(x):
    high = x.astype(BF16)
    return high, (x - high.astype(F32)).astype(BF16)


def mul(x, b, dims=NN):
    xh, xl = split(x)
    bh, bl = b
    m = x.shape[0]
    both = dot(jnp.concatenate([xh, xl], axis=0), bh, dims)
    return (both[:m] + both[m:]) + dot(xh, bl, dims)


def mul3(a, b):
    (ah, al), (bh, bl) = split(a), split(b)
    return dot(ah, bh) + (dot(al, bh) + dot(ah, bl))


def iotas(n):
    return lax.broadcasted_iota(jnp.int32, (n, n), 0), lax.broadcasted_iota(jnp.int32, (n, n), 1)


def invert_kernel(place_ref, tri_ref, diag_ref, out_ref):
    rep, bulk = place_ref[0], place_ref[1]
    n = tri_ref.shape[1]
    rows = tri_ref.shape[0]
    out_ref[0:rows, :] = tri_ref[...]
    inv = 1.0 / diag_ref[...]
    out_ref[rows : rows + 8, :] = jnp.concatenate([inv, jnp.zeros((6, n), F32)], axis=0)

    @pl.when(rep == bulk // 2)
    def _():
        start = pl.multiple_of((bulk % 2) * n, n)
        block = tri_ref[pl.ds(start, n), :]
        i, j = iotas(n)
        eye = i == j
        ans = []
        for which in range(2):
            row, col = (i, j) if which == 0 else (j, i)
            along = inv[which : which + 1, :]
            d = jnp.where(eye, along, 0.0)
            down = jnp.sum(d, axis=1, keepdims=True)
            part = (row >> 1 == col >> 1) & (row > col)
            ans.append(d - jnp.where(part, block * along * down, 0.0))
        level = 1
        while (1 << level) < n:
            for which in range(2):
                row, col = (i, j) if which == 0 else (j, i)
                part = (row >> (level + 1) == col >> (level + 1)) & (row >> level > col >> level)
                t = ans[which]
                ans[which] = t - dot_exact(dot_exact(t, jnp.where(part, block, 0.0)), t)
            level += 1
        out_ref[pl.ds(start, n), :] = jnp.where(i >= j, ans[0], ans[1])


def place_block(place_ref, dx, dy, dc, m):
    return place_ref[0] ^ (2 * dx + dc), place_ref[1] ^ (2 * m + dy)


STACKS = [(dx, dy, dc) for dc in range(2) for dy in range(2) for dx in range(2)]


def first_kernel(place_ref, b_ref, *refs):
    stacks, (x_ref, uh_ref, ul_ref, tri, diag, res, sem, sem2) = refs[:8], refs[8:]
    copies = []
    for s, (dx, dy, dc) in enumerate(STACKS):
        for m in range(4):
            rep, bulk = place_block(place_ref, dx, dy, dc, m)
            copies.append(
                pltpu.make_async_copy(
                    stacks[s].at[m, pl.ds(0, 256), :],
                    tri.at[pl.ds(pl.multiple_of(rep * 256, 256), 256), pl.ds(pl.multiple_of(bulk * 128, 128), 128)],
                    sem.at[s, m],
                )
            )
            if dx == 0 and dc == 0:
                copies.append(
                    pltpu.make_async_copy(
                        stacks[s].at[m, pl.ds(256, 8), :], diag.at[bulk], sem2.at[dy, m]
                    )
                )
    for copy in copies:
        copy.start()
    for copy in copies:
        copy.wait()

    n = 128
    i, j = iotas(n)
    lower, upper, eye = i > j, i < j, i == j

    def low_block(k):
        block = tri[k * n : (k + 1) * n, k * n : (k + 1) * n]
        return jnp.where(lower, block, 0.0) + jnp.where(eye, diag[k, 0:1, :], 0.0)

    def up_block(k):
        block = tri[k * n : (k + 1) * n, k * n : (k + 1) * n]
        return jnp.where(upper, block, 0.0) + jnp.where(eye, diag[k, 1:2, :], 0.0)

    zero = jnp.zeros((n, n), F32)
    lows = []
    for k in range(4):
        ta, tb = low_block(2 * k), low_block(2 * k + 1)
        lba = tri[k * 256 + 128 : k * 256 + 256, k * 256 : k * 256 + 128]
        off = -mul3(mul3(tb, lba), ta)
        lows.append(
            jnp.concatenate(
                [jnp.concatenate([ta, zero], axis=1), jnp.concatenate([off, tb], axis=1)], axis=0
            )
        )
    ups = []
    for k in range(4):
        ta, tb = up_block(2 * k), up_block(2 * k + 1)
        uab = tri[k * 256 : k * 256 + 128, k * 256 + 128 : k * 256 + 256]
        off = -mul3(mul3(ta, uab), tb)
        ups.append(
            jnp.concatenate(
                [jnp.concatenate([ta, off], axis=1), jnp.concatenate([zero, tb], axis=1)], axis=0
            )
        )

    for k in range(4):
        res[:, k * 256 : (k + 1) * 256] = b_ref[k]
    for k in range(4):
        x = mul(res[:, k * 256 : (k + 1) * 256], split(lows[k]), NT)
        x_ref[:, k * 256 : (k + 1) * 256] = x
        if k < 3:
            later = tri[(k + 1) * 256 :, k * 256 : (k + 1) * 256]
            res[:, (k + 1) * 256 :] -= mul(x, split(later), NT)

    def put(r, c, value):
        h, l = split(value)
        uh_ref[r * 256 : r * 256 + value.shape[0], c * 256 : c * 256 + value.shape[1]] = h
        ul_ref[r * 256 : r * 256 + value.shape[0], c * 256 : c * 256 + value.shape[1]] = l

    for k in range(2):
        ta, tb = ups[2 * k], ups[2 * k + 1]
        uab = tri[k * 512 : k * 512 + 256, k * 512 + 256 : k * 512 + 512]
        put(2 * k, 2 * k, ta)
        put(2 * k + 1, 2 * k + 1, tb)
        put(2 * k, 2 * k + 1, -mul3(mul3(ta, uab), tb))
        put(2 * k + 1, 2 * k, jnp.zeros((256, 256), F32))
    put(0, 2, tri[0:512, 512:1024])


def second_kernel(place_ref, b_ref, x_ref, uh_ref, ul_ref, *refs):
    stacks, (out_ref, coup, sem) = refs[:8], refs[8:]
    copies = []
    for s, (dx, dy, dc) in enumerate(STACKS):
        for m in range(4):
            rep, bulk = place_block(place_ref, dx, dy, dc, m)
            copies.append(
                pltpu.make_async_copy(
                    stacks[s].at[m],
                    coup.at[pl.ds(pl.multiple_of(rep * 256, 256), 256), pl.ds(pl.multiple_of(bulk * 128, 128), 128)],
                    sem.at[s, m],
                )
            )
    for copy in copies:
        copy.start()
    x = x_ref[...]
    out_ref[:, 0:1024] = x
    for copy in copies:
        copy.wait()
    parts = []
    for k in range(4):
        upd = mul(x, split(coup[k * 256 : (k + 1) * 256, :]), NT)
        parts.append(b_ref[4 + k] - upd)
    ra = jnp.concatenate(parts[:2], axis=1)
    rb = jnp.concatenate(parts[2:], axis=1)

    def u(r, c):
        rows, cols = slice(r * 512, r * 512 + 512), slice(c * 512, c * 512 + 512)
        return uh_ref[rows, cols], ul_ref[rows, cols]

    xa = mul(ra, u(0, 0))
    xb = mul(rb - mul(xa, u(0, 1)), u(1, 1))
    out_ref[:, 1024:1536] = xa
    out_ref[:, 1536:2048] = xb


def swap(x, axis, bit):
    size = lax.axis_size(axis)
    return lax.ppermute(x, axis, [(k, k ^ bit) for k in range(size)])


def gather_stacks(piece, order):
    along_z = [piece] + [swap(piece, "bulk", 2 * m) for m in range(1, 4)]
    stack = jnp.stack(along_z, axis=0)
    held = {(0, 0): stack}
    for axis in order:
        for key in list(held):
            if axis == "x":
                held[(1, key[1])] = swap(held[key], "rep", 2)
            else:
                held[(key[0], 1)] = swap(held[key], "bulk", 1)
    out = {(dx, dy, 0): s for (dx, dy), s in held.items()}
    for (dx, dy), s in held.items():
        out[(dx, dy, 1)] = swap(s, "rep", 1)
    return [out[key] for key in STACKS]


ANY = pl.BlockSpec(memory_space=pl.ANY)
VMEM = pl.BlockSpec(memory_space=pltpu.VMEM)
SMEM = pl.BlockSpec(memory_space=pltpu.SMEM)


def per_device(orbitals, triangles, coupling, diagonals):
    place = jnp.stack([lax.axis_index("rep"), lax.axis_index("bulk")]).astype(jnp.int32)
    blocks = orbitals.reshape(8, 32, 256)
    mine = lax.all_to_all(blocks, "bulk", split_axis=0, concat_axis=0, tiled=True)

    piece = pl.pallas_call(
        invert_kernel,
        out_shape=jax.ShapeDtypeStruct((264, 128), F32),
        in_specs=[SMEM, VMEM, VMEM],
        out_specs=VMEM,
        compiler_params=pltpu.CompilerParams(vmem_limit_bytes=8 << 20),
        name="invert",
    )(place, triangles, diagonals)

    tri_stacks = gather_stacks(piece, "xy")
    coup_stacks = gather_stacks(coupling, "yx")

    x, uh, ul = pl.pallas_call(
        first_kernel,
        out_shape=[
            jax.ShapeDtypeStruct((32, 1024), F32),
            jax.ShapeDtypeStruct((1024, 1024), BF16),
            jax.ShapeDtypeStruct((1024, 1024), BF16),
        ],
        in_specs=[SMEM, VMEM] + [ANY] * 8,
        out_specs=[VMEM] * 3,
        scratch_shapes=[
            pltpu.VMEM((1024, 1024), F32),
            pltpu.VMEM((8, 8, 128), F32),
            pltpu.VMEM((32, 1024), F32),
            pltpu.SemaphoreType.DMA((8, 4)),
            pltpu.SemaphoreType.DMA((2, 4)),
        ],
        compiler_params=pltpu.CompilerParams(vmem_limit_bytes=32 << 20),
        cost_estimate=pl.CostEstimate(flops=600_000_000, bytes_accessed=8 << 20, transcendentals=0),
        name="first_panel",
    )(place, mine, *tri_stacks)

    return pl.pallas_call(
        second_kernel,
        out_shape=jax.ShapeDtypeStruct((32, 2048), F32),
        in_specs=[SMEM, VMEM, VMEM, VMEM, VMEM] + [ANY] * 8,
        out_specs=VMEM,
        scratch_shapes=[
            pltpu.VMEM((1024, 1024), F32),
            pltpu.SemaphoreType.DMA((8, 4)),
        ],
        compiler_params=pltpu.CompilerParams(vmem_limit_bytes=32 << 20),
        cost_estimate=pl.CostEstimate(flops=600_000_000, bytes_accessed=8 << 20, transcendentals=0),
        name="second_panel",
    )(place, mine, x, uh, ul, *coup_stacks)


def solution(mesh):
    special = mesh.shape["bulk"] == 8 and mesh.shape["rep"] == 4

    def run(orbitals, triangles, coupling, diagonals):
        fits = orbitals.shape == (1024, 2048) and triangles.shape == (1024, 1024)
        body = per_device if special and fits else per_device_any
        return jax.shard_map(
            body,
            mesh=mesh,
            in_specs=(P("rep", "bulk"), P("rep", "bulk"), P("rep", "bulk"), P(None, "bulk")),
            out_specs=P(("rep", "bulk"), None),
            check_vma=False,
        )(orbitals, triangles, coupling, diagonals)

    return run
```

```python
import jax
import jax.numpy as jnp
from jax import lax
from jax.experimental import pallas as pl
from jax.experimental.pallas import tpu as pltpu
from jax.sharding import PartitionSpec as P

F32 = jnp.float32
BF16 = jnp.bfloat16
NN = (((1,), (0,)), ((), ()))
NT = (((1,), (1,)), ((), ()))


def unpack(triangles, diagonals):
    first_block = jnp.tril(triangles, -1) + jnp.diag(diagonals[0])
    second_block = jnp.tril(triangles.T, -1) + jnp.diag(diagonals[1])
    return (first_block, second_block)


def per_device_any(orbitals, triangles, coupling, diagonals):
    tri_rows, couple_rows = (
        lax.all_gather(triangles, "rep", axis=0, tiled=True),
        lax.all_gather(coupling, "rep", axis=0, tiled=True),
    )
    tri_whole, couple_whole, diag_whole = (
        lax.all_gather(tri_rows, "bulk", axis=1, tiled=True),
        lax.all_gather(couple_rows, "bulk", axis=1, tiled=True),
        lax.all_gather(diagonals, "bulk", axis=1, tiled=True),
    )
    first_block, second_block = unpack(tri_whole, diag_whole)
    panel = first_block.shape[0]
    groups = lax.axis_size("bulk")
    local_rows = orbitals.shape[0] // groups
    blocks = orbitals.reshape(groups, local_rows, orbitals.shape[1])
    received = lax.all_to_all(blocks, "bulk", split_axis=0, concat_axis=2, tiled=True)
    rows_now = received.reshape(local_rows, received.shape[2])
    left_part = rows_now[:, :panel]
    right_part = rows_now[:, panel:]
    solved_one = jax.scipy.linalg.solve_triangular(first_block, left_part.T, lower=True).T
    update = jnp.dot(
        solved_one,
        couple_whole.T,
        precision=lax.Precision.HIGHEST,
        preferred_element_type=jnp.float32,
    )
    solved_two = jax.scipy.linalg.solve_triangular(
        second_block, (right_part - update).T, lower=True
    ).T
    return jnp.concatenate([solved_one, solved_two], axis=1)


def dot(a, b, dims=NN):
    return lax.dot_general(a, b, dims, preferred_element_type=F32)


def dot_exact(a, b):
    return lax.dot_general(a, b, NN, precision=lax.Precision.HIGHEST, preferred_element_type=F32)


def split(x):
    high = x.astype(BF16)
    return high, (x - high.astype(F32)).astype(BF16)


def mul(x, b, dims=NN):
    xh, xl = split(x)
    bh, bl = b
    m = x.shape[0]
    both = dot(jnp.concatenate([xh, xl], axis=0), bh, dims)
    return (both[:m] + both[m:]) + dot(xh, bl, dims)


def mul3(a, b):
    (ah, al), (bh, bl) = split(a), split(b)
    return dot(ah, bh) + (dot(al, bh) + dot(ah, bl))


def iotas(n):
    return lax.broadcasted_iota(jnp.int32, (n, n), 0), lax.broadcasted_iota(jnp.int32, (n, n), 1)


def invert_kernel(place_ref, tri_hbm, diag_hbm, orb_hbm, out_ref, b1_ref, b2_ref, b3_ref, tri_ref, diag_ref, sem):
    z = place_ref[1] >> 1
    copies = [
        pltpu.make_async_copy(tri_hbm, tri_ref, sem.at[0]),
        pltpu.make_async_copy(diag_hbm, diag_ref, sem.at[1]),
    ]
    parts = [
        pltpu.make_async_copy(orb_hbm.at[z ^ m], ref, sem.at[1 + m])
        for m, ref in ((1, b1_ref), (2, b2_ref), (3, b3_ref))
    ]
    for copy in copies + parts:
        copy.start()
    for copy in copies:
        copy.wait()
    rep, bulk = place_ref[0], place_ref[1]
    n = tri_ref.shape[1]
    rows = tri_ref.shape[0]
    out_ref[0:rows, :] = tri_ref[...]
    inv = 1.0 / diag_ref[...]
    out_ref[rows : rows + 8, :] = jnp.concatenate([inv, jnp.zeros((6, n), F32)], axis=0)

    @pl.when(rep == bulk // 2)
    def _():
        start = pl.multiple_of((bulk % 2) * n, n)
        block = tri_ref[pl.ds(start, n), :]
        i, j = iotas(n)
        eye = i == j
        ans = []
        for which in range(2):
            row, col = (i, j) if which == 0 else (j, i)
            along = inv[which : which + 1, :]
            d = jnp.where(eye, along, 0.0)
            down = jnp.sum(d, axis=1, keepdims=True)
            part = (row >> 1 == col >> 1) & (row > col)
            ans.append(d - jnp.where(part, block * along * down, 0.0))
        level = 1
        while (1 << level) < n:
            for which in range(2):
                row, col = (i, j) if which == 0 else (j, i)
                part = (row >> (level + 1) == col >> (level + 1)) & (row >> level > col >> level)
                t = ans[which]
                ans[which] = t - mul3(mul3(t, jnp.where(part, block, 0.0)), t)
            level += 1
        out_ref[pl.ds(start, n), :] = jnp.where(i >= j, ans[0], ans[1])

    for copy in parts:
        copy.wait()


def leave_kernel(place_ref, b0_ref, b1_ref, b2_ref, b3_ref, out_ref):
    y = place_ref[1] & 1
    for m, ref in enumerate((b0_ref, b1_ref, b2_ref, b3_ref)):
        out_ref[m] = ref[1 - y]


GROUPS = ((0,), (1,), (2, 3))


def origin(place_ref, crossed, first, second, m):
    rep, bulk = place_ref[0], place_ref[1]
    core = (rep & 1) ^ crossed
    dx = jnp.where(core == 0, first, second)
    dy = jnp.where(core == 0, second, first)
    return rep ^ (2 * dx + crossed), bulk ^ (2 * m + dy)


def pieces(crossed):
    found = []
    for g, group in enumerate(GROUPS):
        for second in range(2):
            for first in range(2):
                for at, m in enumerate(group):
                    found.append((2 * g + second, first * len(group) + at, (crossed, first, second, m)))
    return found


def offset(index, size):
    return pl.ds(pl.multiple_of(index * size, size), size)


def orbital_block(place_ref, refs, k):
    z, y = place_ref[1] >> 1, place_ref[1] & 1
    m, dy = (k >> 1) ^ z, (k & 1) ^ y
    stayed = [ref[y] for ref in refs[:4]]
    near = jnp.where(m == 0, stayed[0], jnp.where(m == 1, stayed[1], jnp.where(m == 2, stayed[2], stayed[3])))
    return jnp.where(dy == 0, near, refs[4][m])


def first_kernel(place_ref, *refs):
    orb, bufs, (x_ref, uh_ref, ul_ref, tri, diag, res, sem, sem2) = refs[:5], refs[5:17], refs[17:]
    copies = []
    for crossed in range(2):
        for buf, entry, args in pieces(crossed):
            rep, bulk = origin(place_ref, *args)
            src = bufs[6 * crossed + buf]
            copies.append(
                pltpu.make_async_copy(
                    src.at[entry, pl.ds(0, 256), :],
                    tri.at[offset(rep, 256), offset(bulk, 128)],
                    sem.at[crossed, buf, entry],
                )
            )
            copies.append(
                pltpu.make_async_copy(
                    src.at[entry, pl.ds(256, 8), :], diag.at[rep, bulk], sem2.at[crossed, buf, entry]
                )
            )
    for copy in copies:
        copy.start()
    for k in range(4):
        res[:, k * 256 : (k + 1) * 256] = orbital_block(place_ref, orb, k)
    for copy in copies:
        copy.wait()

    n = 128
    i, j = iotas(n)
    lower, upper, eye = i > j, i < j, i == j

    def low_block(k):
        block = tri[k * n : (k + 1) * n, k * n : (k + 1) * n]
        return jnp.where(lower, block, 0.0) + jnp.where(eye, diag[k // 2, k, 0:1, :], 0.0)

    def up_block(k):
        block = tri[k * n : (k + 1) * n, k * n : (k + 1) * n]
        return jnp.where(upper, block, 0.0) + jnp.where(eye, diag[k // 2, k, 1:2, :], 0.0)

    zero = jnp.zeros((n, n), F32)
    lows = []
    for k in range(4):
        ta, tb = low_block(2 * k), low_block(2 * k + 1)
        lba = tri[k * 256 + 128 : k * 256 + 256, k * 256 : k * 256 + 128]
        off = -mul3(mul3(tb, lba), ta)
        lows.append(
            jnp.concatenate(
                [jnp.concatenate([ta, zero], axis=1), jnp.concatenate([off, tb], axis=1)], axis=0
            )
        )
    ups = []
    for k in range(4):
        ta, tb = up_block(2 * k), up_block(2 * k + 1)
        uab = tri[k * 256 : k * 256 + 128, k * 256 + 128 : k * 256 + 256]
        off = -mul3(mul3(ta, uab), tb)
        ups.append(
            jnp.concatenate(
                [jnp.concatenate([ta, off], axis=1), jnp.concatenate([zero, tb], axis=1)], axis=0
            )
        )

    for k in range(4):
        x = mul(res[:, k * 256 : (k + 1) * 256], split(lows[k]), NT)
        x_ref[:, k * 256 : (k + 1) * 256] = x
        if k < 3:
            later = tri[(k + 1) * 256 :, k * 256 : (k + 1) * 256]
            res[:, (k + 1) * 256 :] -= mul(x, split(later), NT)

    def put(r, c, value):
        h, l = split(value)
        uh_ref[r * 256 : r * 256 + value.shape[0], c * 256 : c * 256 + value.shape[1]] = h
        ul_ref[r * 256 : r * 256 + value.shape[0], c * 256 : c * 256 + value.shape[1]] = l

    for k in range(2):
        ta, tb = ups[2 * k], ups[2 * k + 1]
        uab = tri[k * 512 : k * 512 + 256, k * 512 + 256 : k * 512 + 512]
        put(2 * k, 2 * k, ta)
        put(2 * k + 1, 2 * k + 1, tb)
        put(2 * k, 2 * k + 1, -mul3(mul3(ta, uab), tb))
        put(2 * k + 1, 2 * k, jnp.zeros((256, 256), F32))
    put(0, 2, tri[0:512, 512:1024])


def update_kernel(place_ref, x_ref, other_ref, *refs):
    bufs, (mine_ref, theirs_ref, coup, sem) = refs[:6], refs[6:]
    copies = []
    for buf, entry, args in pieces(0):
        rep, bulk = origin(place_ref, *args)
        copies.append(
            pltpu.make_async_copy(
                bufs[buf].at[entry],
                coup.at[offset(rep >> 1, 256), offset(bulk, 128)],
                sem.at[buf, entry],
            )
        )
    for copy in copies:
        copy.start()
    x = jnp.concatenate([x_ref[...], other_ref[...]], axis=0)
    for copy in copies:
        copy.wait()
    for k in range(2):
        upd = mul(x, split(coup[k * 256 : (k + 1) * 256, :]), NT)
        mine_ref[k] = upd[:32]
        theirs_ref[k] = upd[32:]


def second_kernel(place_ref, *refs):
    orb, (x_ref, uh_ref, ul_ref, mine_ref, theirs_ref, out_ref) = refs[:5], refs[5:]
    out_ref[:, 0:1024] = x_ref[...]
    core = place_ref[0] & 1
    parts = []
    for k in range(4):
        upd = jnp.where(core == k % 2, mine_ref[k // 2], theirs_ref[k // 2])
        parts.append(orbital_block(place_ref, orb, 4 + k) - upd)
    ra = jnp.concatenate(parts[:2], axis=1)
    rb = jnp.concatenate(parts[2:], axis=1)

    def u(r, c):
        rows, cols = slice(r * 512, r * 512 + 512), slice(c * 512, c * 512 + 512)
        return uh_ref[rows, cols], ul_ref[rows, cols]

    xa = mul(ra, u(0, 0))
    xb = mul(rb - mul(xa, u(0, 1)), u(1, 1))
    out_ref[:, 1024:1536] = xa
    out_ref[:, 1536:2048] = xb


BOTH = ("bulk", "rep")


def swap_z(x, m):
    return lax.ppermute(x, "bulk", [(k, k ^ (2 * m)) for k in range(8)])


def swap_y(x):
    return lax.ppermute(x, "bulk", [(k, k ^ 1) for k in range(8)])


def swap_core(x):
    return lax.ppermute(x, "rep", [(k, k ^ 1) for k in range(4)])


def cross(x, stage):
    pairs = []
    for rep in range(4):
        for bulk in range(8):
            to = (rep ^ 2, bulk) if (rep & 1) == stage else (rep, bulk ^ 1)
            pairs.append((bulk * 4 + rep, to[1] * 4 + to[0]))
    return lax.ppermute(x, BOTH, pairs)


def after(x, *deps):
    return lax.optimization_barrier((x,) + deps)[0]


ANY = pl.BlockSpec(memory_space=pl.ANY)
VMEM = pl.BlockSpec(memory_space=pltpu.VMEM)
SMEM = pl.BlockSpec(memory_space=pltpu.SMEM)


def call(kernel, out, specs, outs, scratch, flops, size, name):
    return pl.pallas_call(
        kernel,
        out_shape=out,
        in_specs=specs,
        out_specs=outs,
        scratch_shapes=scratch,
        compiler_params=pltpu.CompilerParams(vmem_limit_bytes=size << 20),
        cost_estimate=pl.CostEstimate(flops=flops, bytes_accessed=2 << 20, transcendentals=0),
        name=name,
    )


def shape(*dims, dtype=F32):
    return jax.ShapeDtypeStruct(dims, dtype)


def per_device(orbitals, triangles, coupling, diagonals):
    rep, bulk = lax.axis_index("rep"), lax.axis_index("bulk")
    place = jnp.stack([rep, bulk]).astype(jnp.int32)
    blocks = orbitals.reshape(4, 2, 32, 256)
    own = coupling[None]

    tri, b1, b2, b3 = call(
        invert_kernel,
        [shape(264, 128)] + [shape(2, 32, 256)] * 3,
        [SMEM, ANY, ANY, ANY],
        [VMEM] * 4,
        [pltpu.VMEM((256, 128), F32), pltpu.VMEM((2, 128), F32), pltpu.SemaphoreType.DMA((5,))],
        3_500_000_000,
        40,
        "invert",
    )(place, triangles, diagonals, blocks)
    tri = tri[None]

    tz = [swap_z(tri, m) for m in range(1, 4)]
    ta0 = cross(tri, 0)
    tq0 = jnp.concatenate([tri, ta0], axis=0)
    tb0 = cross(tq0, 1)
    ca0 = cross(after(own, ta0), 0)
    ta1 = cross(after(tz[0], ta0), 0)
    cq0 = jnp.concatenate([own, ca0], axis=0)
    cb0 = cross(after(cq0, tb0), 1)
    tq1 = jnp.concatenate([tz[0], ta1], axis=0)
    tb1 = cross(after(tq1, ca0), 1)
    bufs = [swap_core(after(tq0, ta1)), swap_core(after(tb0, ta1))]

    tfar = jnp.concatenate([tz[1], tz[2]], axis=0)
    ta2 = cross(after(tfar, cb0), 0)
    b_own = lax.dynamic_index_in_dim(blocks, bulk >> 1, 0, keepdims=False)
    b_z = [b_own] + [swap_z(after(b, tfar), m + 1) for m, b in enumerate((b1, b2, b3))]
    cz = [swap_z(after(own, tfar), m) for m in range(1, 4)]
    bufs += [swap_core(after(tq1, tb1)), swap_core(tb1)]
    tq2 = jnp.concatenate([tfar, ta2], axis=0)
    tb2 = cross(after(tq2, tb1, bufs[0], bufs[1]), 1)
    leave = call(
        leave_kernel, shape(4, 32, 256), [SMEM] + [VMEM] * 4, VMEM, [], 500_000_000, 4, "leave"
    )(place, *b_z)
    orb = b_z + [swap_y(after(leave, ta2))]
    ca1 = cross(after(cz[0], ta2, bufs[2], bufs[3]), 0)
    cq1 = jnp.concatenate([cz[0], ca1], axis=0)
    bufs += [swap_core(after(tq2, ca1)), swap_core(after(tb2, ca1))]
    cb1 = cross(after(cq1, tb2), 1)
    order = (0, 1, 2, 3, 4, 5)
    held = [tq0, tb0, tq1, tb1, tq2, tb2]
    bufs = held + [bufs[k] for k in order]

    x, uh, ul = call(
        first_kernel,
        [shape(32, 1024), shape(1024, 1024, dtype=BF16), shape(1024, 1024, dtype=BF16)],
        [SMEM] + [VMEM] * 5 + [ANY] * 12,
        [VMEM] * 3,
        [
            pltpu.VMEM((1024, 1024), F32),
            pltpu.VMEM((4, 8, 8, 128), F32),
            pltpu.VMEM((32, 1024), F32),
            pltpu.SemaphoreType.DMA((2, 6, 4)),
            pltpu.SemaphoreType.DMA((2, 6, 4)),
        ],
        5_000_000_000,
        32,
        "first_panel",
    )(place, *orb, *bufs)

    cfar = jnp.concatenate([cz[1], cz[2]], axis=0)
    ca2 = cross(after(cfar, ca1, x), 0)
    x_other = swap_core(x)
    cq2 = jnp.concatenate([cfar, ca2], axis=0)
    cb2 = cross(after(cq2, cb1, x_other), 1)

    upd, theirs = call(
        update_kernel,
        [shape(2, 32, 256)] * 2,
        [SMEM, VMEM, VMEM] + [ANY] * 6,
        [VMEM] * 2,
        [pltpu.VMEM((512, 1024), F32), pltpu.SemaphoreType.DMA((6, 4))],
        2_000_000_000,
        32,
        "update",
    )(place, x, x_other, cq0, cb0, cq1, cb1, cq2, cb2)

    return call(
        second_kernel,
        shape(32, 2048),
        [SMEM] + [VMEM] * 10,
        VMEM,
        [],
        2_500_000_000,
        32,
        "second_panel",
    )(place, *orb, x, uh, ul, upd, swap_core(theirs))


def solution(mesh):
    special = mesh.shape["bulk"] == 8 and mesh.shape["rep"] == 4

    def run(orbitals, triangles, coupling, diagonals):
        fits = orbitals.shape == (1024, 2048) and triangles.shape == (1024, 1024)
        body = per_device if special and fits else per_device_any
        return jax.shard_map(
            body,
            mesh=mesh,
            in_specs=(P("rep", "bulk"), P("rep", "bulk"), P("rep", "bulk"), P(None, "bulk")),
            out_specs=P(("rep", "bulk"), None),
            check_vma=False,
        )(orbitals, triangles, coupling, diagonals)

    return run
```

```python
import jax
import jax.numpy as jnp
from jax import lax
from jax.experimental import pallas as pl
from jax.experimental.pallas import tpu as pltpu
from jax.sharding import PartitionSpec as P

F32 = jnp.float32
BF16 = jnp.bfloat16
NN = (((1,), (0,)), ((), ()))
NT = (((1,), (1,)), ((), ()))


def unpack(triangles, diagonals):
    first_block = jnp.tril(triangles, -1) + jnp.diag(diagonals[0])
    second_block = jnp.tril(triangles.T, -1) + jnp.diag(diagonals[1])
    return (first_block, second_block)


def per_device_any(orbitals, triangles, coupling, diagonals):
    tri_rows, couple_rows = (
        lax.all_gather(triangles, "rep", axis=0, tiled=True),
        lax.all_gather(coupling, "rep", axis=0, tiled=True),
    )
    tri_whole, couple_whole, diag_whole = (
        lax.all_gather(tri_rows, "bulk", axis=1, tiled=True),
        lax.all_gather(couple_rows, "bulk", axis=1, tiled=True),
        lax.all_gather(diagonals, "bulk", axis=1, tiled=True),
    )
    first_block, second_block = unpack(tri_whole, diag_whole)
    panel = first_block.shape[0]
    groups = lax.axis_size("bulk")
    local_rows = orbitals.shape[0] // groups
    blocks = orbitals.reshape(groups, local_rows, orbitals.shape[1])
    received = lax.all_to_all(blocks, "bulk", split_axis=0, concat_axis=2, tiled=True)
    rows_now = received.reshape(local_rows, received.shape[2])
    left_part = rows_now[:, :panel]
    right_part = rows_now[:, panel:]
    solved_one = jax.scipy.linalg.solve_triangular(first_block, left_part.T, lower=True).T
    update = jnp.dot(
        solved_one,
        couple_whole.T,
        precision=lax.Precision.HIGHEST,
        preferred_element_type=jnp.float32,
    )
    solved_two = jax.scipy.linalg.solve_triangular(
        second_block, (right_part - update).T, lower=True
    ).T
    return jnp.concatenate([solved_one, solved_two], axis=1)


def dot(a, b, dims=NN):
    return lax.dot_general(a, b, dims, preferred_element_type=F32)


def dot_exact(a, b):
    return lax.dot_general(a, b, NN, precision=lax.Precision.HIGHEST, preferred_element_type=F32)


def split(x):
    high = x.astype(BF16)
    return high, (x - high.astype(F32)).astype(BF16)


def mul(x, b, dims=NN):
    xh, xl = split(x)
    bh, bl = b
    m = x.shape[0]
    both = dot(jnp.concatenate([xh, xl], axis=0), bh, dims)
    return (both[:m] + both[m:]) + dot(xh, bl, dims)


def mul3(a, b):
    (ah, al), (bh, bl) = split(a), split(b)
    return dot(ah, bh) + (dot(al, bh) + dot(ah, bl))


def iotas(n):
    return lax.broadcasted_iota(jnp.int32, (n, n), 0), lax.broadcasted_iota(jnp.int32, (n, n), 1)


TRI, DIAG, COUP, OWN = 256, 264, 264, 520


def invert_kernel(place_ref, tri_hbm, diag_hbm, coup_hbm, orb_hbm, own_ref, t_ref, c1_ref, c2_ref, c3_ref, diag_ref, sem):
    rep, bulk = place_ref[0], place_ref[1]
    z = bulk >> 1
    copies = [
        pltpu.make_async_copy(tri_hbm, t_ref.at[pl.ds(0, TRI)], sem.at[0]),
        pltpu.make_async_copy(diag_hbm, diag_ref, sem.at[1]),
        pltpu.make_async_copy(coup_hbm, own_ref.at[pl.ds(COUP, 256)], sem.at[2]),
    ]
    parts = []
    for m, ref in ((1, c1_ref), (2, c2_ref), (3, c3_ref)):
        parts.append(pltpu.make_async_copy(coup_hbm, ref.at[pl.ds(0, 256)], sem.at[3 + m]))
        for y in range(2):
            for h in range(2):
                parts.append(
                    pltpu.make_async_copy(
                        orb_hbm.at[z ^ m, y, :, pl.ds(128 * h, 128)],
                        ref.at[pl.ds(256 + 64 * y + 32 * h, 32)],
                        sem.at[7 + 4 * (m - 1) + 2 * y + h],
                    )
                )
    for copy in copies + parts:
        copy.start()
    for copy in copies[:2]:
        copy.wait()
    n = t_ref.shape[1]
    inv = 1.0 / diag_ref[...]
    t_ref[TRI:DIAG, :] = jnp.concatenate([inv, jnp.zeros((6, n), F32)], axis=0)

    @pl.when(rep == bulk // 2)
    def _():
        start = pl.multiple_of((bulk % 2) * n, n)
        block = t_ref[pl.ds(start, n), :]
        i, j = iotas(n)
        eye = i == j
        ans = []
        for which in range(2):
            row, col = (i, j) if which == 0 else (j, i)
            along = inv[which : which + 1, :]
            d = jnp.where(eye, along, 0.0)
            down = jnp.sum(d, axis=1, keepdims=True)
            part = (row >> 1 == col >> 1) & (row > col)
            ans.append(d - jnp.where(part, block * along * down, 0.0))
        level = 1
        while (1 << level) < n:
            for which in range(2):
                row, col = (i, j) if which == 0 else (j, i)
                part = (row >> (level + 1) == col >> (level + 1)) & (row >> level > col >> level)
                t = ans[which]
                ans[which] = t - mul3(mul3(t, jnp.where(part, block, 0.0)), t)
            level += 1
        t_ref[pl.ds(start, n), :] = jnp.where(i >= j, ans[0], ans[1])

    own_ref[0:DIAG, :] = t_ref[...]
    for copy in copies[2:] + parts:
        copy.wait()


def leave_kernel(place_ref, orb_ref, c1_ref, c2_ref, c3_ref, out_ref):
    z, y = place_ref[1] >> 1, place_ref[1] & 1
    out_ref[0] = orb_ref[z, 1 - y]
    for m, ref in ((1, c1_ref), (2, c2_ref), (3, c3_ref)):
        for h in range(2):
            rows = pl.ds(pl.multiple_of(256 + 64 * (1 - y) + 32 * h, 32), 32)
            out_ref[m, :, 128 * h : 128 * (h + 1)] = ref[rows, :]


def origin(place_ref, crossed, first, second, m):
    rep, bulk = place_ref[0], place_ref[1]
    core = (rep & 1) ^ crossed
    dx = jnp.where(core == 0, first, second)
    dy = jnp.where(core == 0, second, first)
    return rep ^ (2 * dx + crossed), bulk ^ (2 * m + dy)


def pieces(crossed):
    found = []
    for second in range(2):
        for first in range(2):
            found.append((second, first, (crossed, first, second, 0)))
            for m in range(1, 4):
                found.append((2 + second, 3 * first + m - 1, (crossed, first, second, m)))
    return found


def offset(index, size):
    return pl.ds(pl.multiple_of(index * size, size), size)


def first_kernel(place_ref, orb, c1, c2, c3, came, *refs):
    bufs, (x_ref, rest_ref, uh_ref, ul_ref, tri, diag, res, sem, sem2, sem3) = refs[:8], refs[8:]
    z, y = place_ref[1] >> 1, place_ref[1] & 1
    copies = []
    for crossed in range(2):
        for buf, entry, args in pieces(crossed):
            rep, bulk = origin(place_ref, *args)
            src = bufs[4 * crossed + buf]
            copies.append(
                pltpu.make_async_copy(
                    src.at[entry, pl.ds(0, TRI), :],
                    tri.at[offset(rep, 256), offset(bulk, 128)],
                    sem.at[crossed, buf, entry],
                )
            )
            copies.append(
                pltpu.make_async_copy(
                    src.at[entry, pl.ds(TRI, 8), :], diag.at[rep, bulk], sem2.at[crossed, buf, entry]
                )
            )
    copies.append(pltpu.make_async_copy(orb.at[z, y], res.at[2 * z + y], sem3.at[0, 0]))
    for m, ref in ((1, c1), (2, c2), (3, c3)):
        for h in range(2):
            copies.append(
                pltpu.make_async_copy(
                    ref.at[pl.ds(pl.multiple_of(256 + 64 * y + 32 * h, 32), 32)],
                    res.at[2 * (z ^ m) + y, :, pl.ds(128 * h, 128)],
                    sem3.at[m, h],
                )
            )
    for m in range(4):
        copies.append(pltpu.make_async_copy(came.at[m], res.at[2 * (z ^ m) + 1 - y], sem3.at[4, m]))
    for copy in copies:
        copy.start()
    for copy in copies:
        copy.wait()

    n = 128
    i, j = iotas(n)
    lower, upper, eye = i > j, i < j, i == j

    def low_block(k):
        block = tri[k * n : (k + 1) * n, k * n : (k + 1) * n]
        return jnp.where(lower, block, 0.0) + jnp.where(eye, diag[k // 2, k, 0:1, :], 0.0)

    def up_block(k):
        block = tri[k * n : (k + 1) * n, k * n : (k + 1) * n]
        return jnp.where(upper, block, 0.0) + jnp.where(eye, diag[k // 2, k, 1:2, :], 0.0)

    zero = jnp.zeros((n, n), F32)
    lows = []
    for k in range(4):
        ta, tb = low_block(2 * k), low_block(2 * k + 1)
        lba = tri[k * 256 + 128 : k * 256 + 256, k * 256 : k * 256 + 128]
        off = -mul3(mul3(tb, lba), ta)
        lows.append(
            jnp.concatenate(
                [jnp.concatenate([ta, zero], axis=1), jnp.concatenate([off, tb], axis=1)], axis=0
            )
        )
    ups = []
    for k in range(4):
        ta, tb = up_block(2 * k), up_block(2 * k + 1)
        uab = tri[k * 256 : k * 256 + 128, k * 256 + 128 : k * 256 + 256]
        off = -mul3(mul3(ta, uab), tb)
        ups.append(
            jnp.concatenate(
                [jnp.concatenate([ta, off], axis=1), jnp.concatenate([zero, tb], axis=1)], axis=0
            )
        )

    rest = jnp.concatenate([res[k] for k in range(4)], axis=1)
    for k in range(4):
        x = mul(rest[:, :256], split(lows[k]), NT)
        x_ref[:, k * 256 : (k + 1) * 256] = x
        rest_ref[:, k * 256 : (k + 1) * 256] = res[4 + k]
        if k < 3:
            later = tri[(k + 1) * 256 :, k * 256 : (k + 1) * 256]
            rest = rest[:, 256:] - mul(x, split(later), NT)

    def put(r, c, value):
        h, l = split(value)
        uh_ref[r * 256 : r * 256 + value.shape[0], c * 256 : c * 256 + value.shape[1]] = h
        ul_ref[r * 256 : r * 256 + value.shape[0], c * 256 : c * 256 + value.shape[1]] = l

    for k in range(2):
        ta, tb = ups[2 * k], ups[2 * k + 1]
        uab = tri[k * 512 : k * 512 + 256, k * 512 + 256 : k * 512 + 512]
        put(2 * k, 2 * k, ta)
        put(2 * k + 1, 2 * k + 1, tb)
        put(2 * k, 2 * k + 1, -mul3(mul3(ta, uab), tb))
        put(2 * k + 1, 2 * k, jnp.zeros((256, 256), F32))
    put(0, 2, tri[0:512, 512:1024])


def update_kernel(place_ref, x_ref, other_ref, *refs):
    bufs, (mine_ref, theirs_ref, coup, sem) = refs[:4], refs[4:]
    copies = []
    for buf, entry, args in pieces(0):
        rep, bulk = origin(place_ref, *args)
        src = bufs[buf].at[entry, pl.ds(COUP, 256)] if buf < 2 else bufs[buf].at[entry]
        copies.append(
            pltpu.make_async_copy(src, coup.at[offset(rep >> 1, 256), offset(bulk, 128)], sem.at[buf, entry])
        )
    for copy in copies:
        copy.start()
    x = jnp.concatenate([x_ref[...], other_ref[...]], axis=0)
    for copy in copies:
        copy.wait()
    for k in range(2):
        upd = mul(x, split(coup[k * 256 : (k + 1) * 256, :]), NT)
        mine_ref[k] = upd[:32]
        theirs_ref[k] = upd[32:]


def second_kernel(place_ref, x_ref, rest_ref, uh_ref, ul_ref, mine_ref, theirs_ref, out_ref):
    out_ref[:, 0:1024] = x_ref[...]
    core = place_ref[0] & 1
    parts = []
    for k in range(4):
        upd = jnp.where(core == k % 2, mine_ref[k // 2], theirs_ref[k // 2])
        parts.append(rest_ref[:, k * 256 : (k + 1) * 256] - upd)
    ra = jnp.concatenate(parts[:2], axis=1)
    rb = jnp.concatenate(parts[2:], axis=1)

    def u(r, c):
        rows, cols = slice(r * 512, r * 512 + 512), slice(c * 512, c * 512 + 512)
        return uh_ref[rows, cols], ul_ref[rows, cols]

    xa = mul(ra, u(0, 0))
    xb = mul(rb - mul(xa, u(0, 1)), u(1, 1))
    out_ref[:, 1024:1536] = xa
    out_ref[:, 1536:2048] = xb


BOTH = ("bulk", "rep")


def swap_z(x, m):
    return lax.ppermute(x, "bulk", [(k, k ^ (2 * m)) for k in range(8)])


def swap_y(x):
    return lax.ppermute(x, "bulk", [(k, k ^ 1) for k in range(8)])


def swap_core(x):
    return lax.ppermute(x, "rep", [(k, k ^ 1) for k in range(4)])


def cross(x, stage):
    pairs = []
    for rep in range(4):
        for bulk in range(8):
            to = (rep ^ 2, bulk) if (rep & 1) == stage else (rep, bulk ^ 1)
            pairs.append((bulk * 4 + rep, to[1] * 4 + to[0]))
    return lax.ppermute(x, BOTH, pairs)


def after(x, *deps):
    return lax.optimization_barrier((x,) + deps)[0]


ANY = pl.BlockSpec(memory_space=pl.ANY)
VMEM = pl.BlockSpec(memory_space=pltpu.VMEM)
SMEM = pl.BlockSpec(memory_space=pltpu.SMEM)


def call(kernel, out, specs, outs, scratch, flops, size, name):
    return pl.pallas_call(
        kernel,
        out_shape=out,
        in_specs=specs,
        out_specs=outs,
        scratch_shapes=scratch,
        compiler_params=pltpu.CompilerParams(vmem_limit_bytes=size << 20),
        cost_estimate=pl.CostEstimate(flops=flops, bytes_accessed=2 << 20, transcendentals=0),
        name=name,
    )


def shape(*dims, dtype=F32):
    return jax.ShapeDtypeStruct(dims, dtype)


def per_device(orbitals, triangles, coupling, diagonals):
    rep, bulk = lax.axis_index("rep"), lax.axis_index("bulk")
    place = jnp.stack([rep, bulk]).astype(jnp.int32)
    blocks = orbitals.reshape(4, 2, 32, 256)

    own, t, *c_out = call(
        invert_kernel,
        [shape(OWN, 128), shape(DIAG, 128)] + [shape(384, 128)] * 3,
        [SMEM, ANY, ANY, ANY, ANY],
        [VMEM] * 5,
        [pltpu.VMEM((2, 128), F32), pltpu.SemaphoreType.DMA((19,))],
        3_500_000_000,
        8,
        "invert",
    )(place, triangles, diagonals, coupling, blocks)

    tz = [swap_z(t, m) for m in range(1, 4)]
    near = jnp.stack([own, cross(own, 0)])
    near_got = cross(near, 1)
    near_swap = [swap_core(near), swap_core(near_got)]
    tfar = jnp.stack(tz)
    cz = [swap_z(after(c, tfar), m + 1) for m, c in enumerate(c_out)]
    far = jnp.concatenate([tfar, cross(after(tfar, near_got), 0)], axis=0)
    far_got = cross(after(far, cz[0], cz[1], *near_swap), 1)
    bufs = [near, near_got, far, far_got] + near_swap + [swap_core(far), swap_core(far_got)]
    leave = call(
        leave_kernel, shape(4, 32, 256), [SMEM] + [VMEM] * 4, VMEM, [], 500_000_000, 4, "leave"
    )(place, blocks, *cz)
    came = swap_y(leave)
    cfar = jnp.stack([c[:256] for c in cz])
    chalf = jnp.concatenate([cfar, cross(after(cfar, bufs[6]), 0)], axis=0)
    cgot = cross(chalf, 1)

    x, rest, uh, ul = call(
        first_kernel,
        [shape(32, 1024)] * 2 + [shape(1024, 1024, dtype=BF16)] * 2,
        [SMEM] + [ANY] * 13,
        [VMEM] * 4,
        [
            pltpu.VMEM((1024, 1024), F32),
            pltpu.VMEM((4, 8, 8, 128), F32),
            pltpu.VMEM((8, 32, 256), F32),
            pltpu.SemaphoreType.DMA((2, 4, 6)),
            pltpu.SemaphoreType.DMA((2, 4, 6)),
            pltpu.SemaphoreType.DMA((5, 4)),
        ],
        5_000_000_000,
        32,
        "first_panel",
    )(place, blocks, *cz, came, *bufs)
    x_other = swap_core(x)

    upd, theirs = call(
        update_kernel,
        [shape(2, 32, 256)] * 2,
        [SMEM, VMEM, VMEM] + [ANY] * 4,
        [VMEM] * 2,
        [pltpu.VMEM((512, 1024), F32), pltpu.SemaphoreType.DMA((4, 6))],
        2_000_000_000,
        32,
        "update",
    )(place, x, x_other, near, near_got, chalf, cgot)

    return call(
        second_kernel,
        shape(32, 2048),
        [SMEM] + [VMEM] * 6,
        VMEM,
        [],
        2_500_000_000,
        32,
        "second_panel",
    )(place, x, rest, uh, ul, upd, swap_core(theirs))


def solution(mesh):
    special = mesh.shape["bulk"] == 8 and mesh.shape["rep"] == 4

    def run(orbitals, triangles, coupling, diagonals):
        fits = orbitals.shape == (1024, 2048) and triangles.shape == (1024, 1024)
        body = per_device if special and fits else per_device_any
        return jax.shard_map(
            body,
            mesh=mesh,
            in_specs=(P("rep", "bulk"), P("rep", "bulk"), P("rep", "bulk"), P(None, "bulk")),
            out_specs=P(("rep", "bulk"), None),
            check_vma=False,
        )(orbitals, triangles, coupling, diagonals)

    return run
```

```python
import jax
import jax.numpy as jnp
from jax import lax
from jax.experimental import pallas as pl
from jax.experimental.pallas import tpu as pltpu
from jax.sharding import PartitionSpec as P

F32 = jnp.float32
BF16 = jnp.bfloat16
NN = (((1,), (0,)), ((), ()))
NT = (((1,), (1,)), ((), ()))


def unpack(triangles, diagonals):
    first_block = jnp.tril(triangles, -1) + jnp.diag(diagonals[0])
    second_block = jnp.tril(triangles.T, -1) + jnp.diag(diagonals[1])
    return (first_block, second_block)


def per_device_any(orbitals, triangles, coupling, diagonals):
    tri_rows, couple_rows = (
        lax.all_gather(triangles, "rep", axis=0, tiled=True),
        lax.all_gather(coupling, "rep", axis=0, tiled=True),
    )
    tri_whole, couple_whole, diag_whole = (
        lax.all_gather(tri_rows, "bulk", axis=1, tiled=True),
        lax.all_gather(couple_rows, "bulk", axis=1, tiled=True),
        lax.all_gather(diagonals, "bulk", axis=1, tiled=True),
    )
    first_block, second_block = unpack(tri_whole, diag_whole)
    panel = first_block.shape[0]
    groups = lax.axis_size("bulk")
    local_rows = orbitals.shape[0] // groups
    blocks = orbitals.reshape(groups, local_rows, orbitals.shape[1])
    received = lax.all_to_all(blocks, "bulk", split_axis=0, concat_axis=2, tiled=True)
    rows_now = received.reshape(local_rows, received.shape[2])
    left_part = rows_now[:, :panel]
    right_part = rows_now[:, panel:]
    solved_one = jax.scipy.linalg.solve_triangular(first_block, left_part.T, lower=True).T
    update = jnp.dot(
        solved_one,
        couple_whole.T,
        precision=lax.Precision.HIGHEST,
        preferred_element_type=jnp.float32,
    )
    solved_two = jax.scipy.linalg.solve_triangular(
        second_block, (right_part - update).T, lower=True
    ).T
    return jnp.concatenate([solved_one, solved_two], axis=1)


def dot(a, b, dims=NN):
    return lax.dot_general(a, b, dims, preferred_element_type=F32)


def dot_exact(a, b):
    return lax.dot_general(a, b, NN, precision=lax.Precision.HIGHEST, preferred_element_type=F32)


def split(x):
    high = x.astype(BF16)
    return high, (x - high.astype(F32)).astype(BF16)


def mul(x, b, dims=NN):
    xh, xl = split(x)
    bh, bl = b
    m = x.shape[0]
    both = dot(jnp.concatenate([xh, xl], axis=0), bh, dims)
    return (both[:m] + both[m:]) + dot(xh, bl, dims)


def mul3(a, b):
    (ah, al), (bh, bl) = split(a), split(b)
    return dot(ah, bh) + (dot(al, bh) + dot(ah, bl))


def iotas(n):
    return lax.broadcasted_iota(jnp.int32, (n, n), 0), lax.broadcasted_iota(jnp.int32, (n, n), 1)


def invert_kernel(place_ref, tri_hbm, diag_hbm, t_ref, diag_ref, sem):
    rep, bulk = place_ref[0], place_ref[1]
    rows, n = tri_hbm.shape
    copies = [
        pltpu.make_async_copy(tri_hbm, t_ref.at[pl.ds(0, rows)], sem.at[0]),
        pltpu.make_async_copy(diag_hbm, diag_ref, sem.at[1]),
    ]
    for copy in copies:
        copy.start()
    for copy in copies:
        copy.wait()
    inv = 1.0 / diag_ref[...]
    t_ref[rows : rows + 8, :] = jnp.concatenate([inv, jnp.zeros((6, n), F32)], axis=0)

    @pl.when(rep == bulk // 2)
    def _():
        start = pl.multiple_of((bulk % 2) * n, n)
        block = t_ref[pl.ds(start, n), :]
        i, j = iotas(n)
        eye = i == j
        ans = []
        for which in range(2):
            row, col = (i, j) if which == 0 else (j, i)
            along = inv[which : which + 1, :]
            d = jnp.where(eye, along, 0.0)
            down = jnp.sum(d, axis=1, keepdims=True)
            part = (row >> 1 == col >> 1) & (row > col)
            ans.append(d - jnp.where(part, block * along * down, 0.0))
        level = 1
        while (1 << level) < n:
            for which in range(2):
                row, col = (i, j) if which == 0 else (j, i)
                part = (row >> (level + 1) == col >> (level + 1)) & (row >> level > col >> level)
                t = ans[which]
                ans[which] = t - mul3(mul3(t, jnp.where(part, block, 0.0)), t)
            level += 1
        t_ref[pl.ds(start, n), :] = jnp.where(i >= j, ans[0], ans[1])


def spread_kernel(place_ref, orb, b1, b2, b3, sem):
    z = place_ref[1] >> 1
    copies = [
        pltpu.make_async_copy(orb.at[z ^ m], ref, sem.at[m])
        for m, ref in ((1, b1), (2, b2), (3, b3))
    ]
    for copy in copies:
        copy.start()
    for copy in copies:
        copy.wait()


def leave_kernel(place_ref, orb, b1, b2, b3, out, sem):
    z, y = place_ref[1] >> 1, place_ref[1] & 1
    copies = [pltpu.make_async_copy(orb.at[z, 1 - y], out.at[0], sem.at[0])]
    for m, ref in ((1, b1), (2, b2), (3, b3)):
        copies.append(pltpu.make_async_copy(ref.at[1 - y], out.at[m], sem.at[m]))
    for copy in copies:
        copy.start()
    for copy in copies:
        copy.wait()


def rows_kernel(place_ref, orb, b1, b2, b3, came, left, right, res, sem):
    z, y = place_ref[1] >> 1, place_ref[1] & 1
    copies = [pltpu.make_async_copy(orb.at[z, y], res.at[2 * z + y], sem.at[0, 0])]
    for m, ref in ((1, b1), (2, b2), (3, b3)):
        copies.append(pltpu.make_async_copy(ref.at[y], res.at[2 * (z ^ m) + y], sem.at[0, m]))
    for m in range(4):
        copies.append(pltpu.make_async_copy(came.at[m], res.at[2 * (z ^ m) + 1 - y], sem.at[1, m]))
    for copy in copies:
        copy.start()
    for copy in copies:
        copy.wait()
    for k in range(4):
        left[:, k * 256 : (k + 1) * 256] = res[k]
        right[:, k * 256 : (k + 1) * 256] = res[4 + k]


def origin(place_ref, crossed, first, second, m):
    rep, bulk = place_ref[0], place_ref[1]
    core = (rep & 1) ^ crossed
    dx = jnp.where(core == 0, first, second)
    dy = jnp.where(core == 0, second, first)
    return rep ^ (2 * dx + crossed), bulk ^ (2 * m + dy), dx


def pieces(crossed):
    found = []
    for group in range(2):
        for second in range(2):
            for first in range(2):
                for at in range(2):
                    found.append((2 * group + second, 2 * first + at, (crossed, first, second, 2 * group + at)))
    return found


def offset(index, size):
    return pl.ds(pl.multiple_of(index * size, size), size)


def first_kernel(place_ref, own, others, *refs):
    bufs, (x_ref, uh_ref, ul_ref, tri, diag, sem, sem2) = refs[:8], refs[8:]
    copies = []
    for crossed in range(2):
        for buf, entry, args in pieces(crossed):
            rep, bulk, dx = origin(place_ref, *args)
            src = bufs[4 * crossed + buf]
            copies.append(
                pltpu.make_async_copy(
                    src.at[entry, pl.ds(0, 256), :],
                    tri.at[offset(rep, 256), offset(bulk, 128)],
                    sem.at[crossed, buf, entry],
                )
            )
            if not crossed:
                copies.append(
                    pltpu.make_async_copy(src.at[entry, pl.ds(256, 8), :], diag.at[dx, bulk], sem2.at[buf, entry])
                )
    for copy in copies:
        copy.start()
    for copy in copies:
        copy.wait()

    n = 128
    i, j = iotas(n)
    lower, upper, eye = i > j, i < j, i == j

    def low_block(k):
        block = tri[k * n : (k + 1) * n, k * n : (k + 1) * n]
        return jnp.where(lower, block, 0.0) + jnp.where(eye, diag[0, k, 0:1, :], 0.0)

    def up_block(k):
        block = tri[k * n : (k + 1) * n, k * n : (k + 1) * n]
        return jnp.where(upper, block, 0.0) + jnp.where(eye, diag[0, k, 1:2, :], 0.0)

    zero = jnp.zeros((n, n), F32)
    lows = []
    for k in range(4):
        ta, tb = low_block(2 * k), low_block(2 * k + 1)
        lba = tri[k * 256 + 128 : k * 256 + 256, k * 256 : k * 256 + 128]
        off = -mul3(mul3(tb, lba), ta)
        lows.append(
            jnp.concatenate(
                [jnp.concatenate([ta, zero], axis=1), jnp.concatenate([off, tb], axis=1)], axis=0
            )
        )
    ups = []
    for k in range(4):
        ta, tb = up_block(2 * k), up_block(2 * k + 1)
        uab = tri[k * 256 : k * 256 + 128, k * 256 + 128 : k * 256 + 256]
        off = -mul3(mul3(ta, uab), tb)
        ups.append(
            jnp.concatenate(
                [jnp.concatenate([ta, off], axis=1), jnp.concatenate([zero, tb], axis=1)], axis=0
            )
        )

    rest = jnp.concatenate([own[...]] + [others[k] for k in range(3)], axis=0)
    for k in range(4):
        x = mul(rest[:, :256], split(lows[k]), NT)
        x_ref[:, k * 256 : (k + 1) * 256] = x
        if k < 3:
            later = tri[(k + 1) * 256 :, k * 256 : (k + 1) * 256]
            rest = rest[:, 256:] - mul(x, split(later), NT)

    def put(r, c, value):
        h, l = split(value)
        uh_ref[r * 256 : r * 256 + value.shape[0], c * 256 : c * 256 + value.shape[1]] = h
        ul_ref[r * 256 : r * 256 + value.shape[0], c * 256 : c * 256 + value.shape[1]] = l

    for k in range(2):
        ta, tb = ups[2 * k], ups[2 * k + 1]
        uab = tri[k * 512 : k * 512 + 256, k * 512 + 256 : k * 512 + 512]
        put(2 * k, 2 * k, ta)
        put(2 * k + 1, 2 * k + 1, tb)
        put(2 * k, 2 * k + 1, -mul3(mul3(ta, uab), tb))
        put(2 * k + 1, 2 * k, jnp.zeros((256, 256), F32))
    put(0, 2, tri[0:512, 512:1024])


def update_kernel(place_ref, x_ref, own, c1, c2, c3, got0, got1, *refs):
    outs, (coup, sem) = refs[:4], refs[4:]
    bulk = place_ref[1]
    copies = []
    for m, ref in enumerate((own, c1, c2, c3)):
        copies.append(pltpu.make_async_copy(ref, coup.at[:, offset(bulk ^ (2 * m), 128)], sem.at[0, m]))
        src = (got0, got1)[m // 2].at[m % 2]
        copies.append(pltpu.make_async_copy(src, coup.at[:, offset(bulk ^ (2 * m + 1), 128)], sem.at[1, m]))
    for copy in copies:
        copy.start()
    x = x_ref[...]
    for copy in copies:
        copy.wait()
    upd = mul(x, split(coup[...]), NT)
    for k, out in enumerate(outs):
        out[...] = upd[32 * k : 32 * (k + 1)]


def second_kernel(place_ref, x_ref, rest_ref, uh_ref, ul_ref, mine, from_x, from_core, from_both, out_ref):
    x = x_ref[0:32, :]
    out_ref[:, 0:1024] = x
    parts = []
    for k in range(4):
        way = place_ref[0] ^ k
        upd = jnp.where(
            way == 0,
            mine[...],
            jnp.where(way == 2, from_x[...], jnp.where(way == 1, from_core[...], from_both[...])),
        )
        parts.append(rest_ref[:, k * 256 : (k + 1) * 256] - upd)
    ra = jnp.concatenate(parts[:2], axis=1)
    rb = jnp.concatenate(parts[2:], axis=1)

    def u(r, c):
        rows, cols = slice(r * 512, r * 512 + 512), slice(c * 512, c * 512 + 512)
        return uh_ref[rows, cols], ul_ref[rows, cols]

    xa = mul(ra, u(0, 0))
    xb = mul(rb - mul(xa, u(0, 1)), u(1, 1))
    out_ref[:, 1024:1536] = xa
    out_ref[:, 1536:2048] = xb


BOTH = ("bulk", "rep")


def swap_z(x, m):
    return lax.ppermute(x, "bulk", [(k, k ^ (2 * m)) for k in range(8)])


def swap_y(x):
    return lax.ppermute(x, "bulk", [(k, k ^ 1) for k in range(8)])


def swap_rep(x, bits):
    return lax.ppermute(x, "rep", [(k, k ^ bits) for k in range(4)])


def cross(x, stage):
    pairs = []
    for rep in range(4):
        for bulk in range(8):
            to = (rep ^ 2, bulk) if (rep & 1) == stage else (rep, bulk ^ 1)
            pairs.append((bulk * 4 + rep, to[1] * 4 + to[0]))
    return lax.ppermute(x, BOTH, pairs)


def after(x, *deps):
    return lax.optimization_barrier((x,) + deps)[0]


ANY = pl.BlockSpec(memory_space=pl.ANY)
VMEM = pl.BlockSpec(memory_space=pltpu.VMEM)
SMEM = pl.BlockSpec(memory_space=pltpu.SMEM)


def call(kernel, out, specs, outs, scratch, flops, size, name):
    return pl.pallas_call(
        kernel,
        out_shape=out,
        in_specs=specs,
        out_specs=outs,
        scratch_shapes=scratch,
        compiler_params=pltpu.CompilerParams(vmem_limit_bytes=size << 20),
        cost_estimate=pl.CostEstimate(flops=flops, bytes_accessed=2 << 20, transcendentals=0),
        name=name,
    )


def shape(*dims, dtype=F32):
    return jax.ShapeDtypeStruct(dims, dtype)


def dmas(*dims):
    return pltpu.SemaphoreType.DMA(dims)


def per_device(orbitals, triangles, coupling, diagonals):
    rep, bulk = lax.axis_index("rep"), lax.axis_index("bulk")
    place = jnp.stack([rep, bulk]).astype(jnp.int32)
    blocks = orbitals.reshape(4, 2, 32, 256)

    t = call(
        invert_kernel,
        shape(264, 128),
        [SMEM, ANY, ANY],
        VMEM,
        [pltpu.VMEM((2, 128), F32), dmas(2)],
        3_500_000_000,
        8,
        "invert",
    )(place, triangles, diagonals)

    tz = [swap_z(t, m) for m in range(1, 4)]
    pair = jnp.stack([t, tz[0]])
    near = jnp.concatenate([pair, cross(pair, 0)], axis=0)
    near_got = cross(near, 1)
    tfar = jnp.stack(tz[1:])
    far = jnp.concatenate([tfar, cross(after(tfar, near), 0)], axis=0)

    b_out = call(
        spread_kernel, [shape(2, 32, 256)] * 3, [SMEM, ANY], [VMEM] * 3, [dmas(4)], 500_000_000, 4, "spread"
    )(place, blocks)
    b_z = [swap_z(after(b, tfar), m + 1) for m, b in enumerate(b_out)]
    cz = [swap_z(after(coupling, tfar), m) for m in range(1, 4)]
    far_got = cross(after(far, near_got, cz[0], cz[1], *b_z), 1)
    swaps = [swap_rep(b, 1) for b in (near, near_got, far, far_got)]

    leave = call(
        leave_kernel, shape(4, 32, 256), [SMEM] + [ANY] * 4, VMEM, [dmas(4)], 500_000_000, 4, "leave"
    )(place, blocks, *b_z)
    came = swap_y(leave)
    left, right = call(
        rows_kernel,
        [shape(32, 1024)] * 2,
        [SMEM] + [ANY] * 5,
        [VMEM] * 2,
        [pltpu.VMEM((8, 32, 256), F32), dmas(2, 4)],
        500_000_000,
        4,
        "rows",
    )(place, blocks, *b_z, came)
    others = [swap_rep(left, bits) for bits in (2, 1, 3)]

    cgot0 = swap_y(jnp.stack([coupling, cz[0]]))
    cgot1 = swap_y(jnp.stack(cz[1:]))

    x, uh, ul = call(
        first_kernel,
        [shape(128, 1024)] + [shape(1024, 1024, dtype=BF16)] * 2,
        [SMEM, VMEM, VMEM] + [ANY] * 8,
        [VMEM] * 3,
        [pltpu.VMEM((1024, 1024), F32), pltpu.VMEM((2, 8, 8, 128), F32), dmas(2, 4, 4), dmas(4, 4)],
        5_000_000_000,
        32,
        "first_panel",
    )(place, left, jnp.stack(others), near, near_got, far, far_got, *swaps)

    mine, to_x, to_core, to_both = call(
        update_kernel,
        [shape(32, 256)] * 4,
        [SMEM, VMEM] + [ANY] * 6,
        [VMEM] * 4,
        [pltpu.VMEM((256, 1024), F32), dmas(2, 4)],
        2_000_000_000,
        32,
        "update",
    )(place, x, coupling, *cz, cgot0, cgot1)
    back = [swap_rep(to_x, 2), swap_rep(to_core, 1), swap_rep(to_both, 3)]

    return call(
        second_kernel,
        shape(32, 2048),
        [SMEM] + [VMEM] * 8,
        VMEM,
        [],
        2_500_000_000,
        32,
        "second_panel",
    )(place, x, right, uh, ul, mine, *back)


def solution(mesh):
    special = mesh.shape["bulk"] == 8 and mesh.shape["rep"] == 4

    def run(orbitals, triangles, coupling, diagonals):
        fits = orbitals.shape == (1024, 2048) and triangles.shape == (1024, 1024)
        body = per_device if special and fits else per_device_any
        return jax.shard_map(
            body,
            mesh=mesh,
            in_specs=(P("rep", "bulk"), P("rep", "bulk"), P("rep", "bulk"), P(None, "bulk")),
            out_specs=P(("rep", "bulk"), None),
            check_vma=False,
        )(orbitals, triangles, coupling, diagonals)

    return run
```

```python
import jax
import jax.numpy as jnp
from jax import lax
from jax.experimental import pallas as pl
from jax.experimental.pallas import tpu as pltpu
from jax.sharding import PartitionSpec as P

F32 = jnp.float32
BF16 = jnp.bfloat16
NN = (((1,), (0,)), ((), ()))
NT = (((1,), (1,)), ((), ()))


def unpack(triangles, diagonals):
    first_block = jnp.tril(triangles, -1) + jnp.diag(diagonals[0])
    second_block = jnp.tril(triangles.T, -1) + jnp.diag(diagonals[1])
    return (first_block, second_block)


def per_device_any(orbitals, triangles, coupling, diagonals):
    tri_rows, couple_rows = (
        lax.all_gather(triangles, "rep", axis=0, tiled=True),
        lax.all_gather(coupling, "rep", axis=0, tiled=True),
    )
    tri_whole, couple_whole, diag_whole = (
        lax.all_gather(tri_rows, "bulk", axis=1, tiled=True),
        lax.all_gather(couple_rows, "bulk", axis=1, tiled=True),
        lax.all_gather(diagonals, "bulk", axis=1, tiled=True),
    )
    first_block, second_block = unpack(tri_whole, diag_whole)
    panel = first_block.shape[0]
    groups = lax.axis_size("bulk")
    local_rows = orbitals.shape[0] // groups
    blocks = orbitals.reshape(groups, local_rows, orbitals.shape[1])
    received = lax.all_to_all(blocks, "bulk", split_axis=0, concat_axis=2, tiled=True)
    rows_now = received.reshape(local_rows, received.shape[2])
    left_part = rows_now[:, :panel]
    right_part = rows_now[:, panel:]
    solved_one = jax.scipy.linalg.solve_triangular(first_block, left_part.T, lower=True).T
    update = jnp.dot(
        solved_one,
        couple_whole.T,
        precision=lax.Precision.HIGHEST,
        preferred_element_type=jnp.float32,
    )
    solved_two = jax.scipy.linalg.solve_triangular(
        second_block, (right_part - update).T, lower=True
    ).T
    return jnp.concatenate([solved_one, solved_two], axis=1)


def dot(a, b, dims=NN):
    return lax.dot_general(a, b, dims, preferred_element_type=F32)


def dot_exact(a, b):
    return lax.dot_general(a, b, NN, precision=lax.Precision.HIGHEST, preferred_element_type=F32)


def split(x):
    high = x.astype(BF16)
    return high, (x - high.astype(F32)).astype(BF16)


def mul(x, b, dims=NN):
    xh, xl = split(x)
    bh, bl = b
    m = x.shape[0]
    both = dot(jnp.concatenate([xh, xl], axis=0), bh, dims)
    return (both[:m] + both[m:]) + dot(xh, bl, dims)


def mul3(a, b):
    (ah, al), (bh, bl) = split(a), split(b)
    return dot(ah, bh) + (dot(al, bh) + dot(ah, bl))


def iotas(n):
    return lax.broadcasted_iota(jnp.int32, (n, n), 0), lax.broadcasted_iota(jnp.int32, (n, n), 1)


def invert_kernel(place_ref, tri_hbm, diag_hbm, t_ref, diag_ref, sem):
    rep, bulk = place_ref[0], place_ref[1]
    rows, n = tri_hbm.shape
    copies = [
        pltpu.make_async_copy(tri_hbm, t_ref.at[pl.ds(0, rows)], sem.at[0]),
        pltpu.make_async_copy(diag_hbm, diag_ref, sem.at[1]),
    ]
    for copy in copies:
        copy.start()
    for copy in copies:
        copy.wait()
    inv = 1.0 / diag_ref[...]
    t_ref[rows : rows + 8, :] = jnp.concatenate([inv, jnp.zeros((6, n), F32)], axis=0)

    @pl.when(rep == bulk // 2)
    def _():
        start = pl.multiple_of((bulk % 2) * n, n)
        block = t_ref[pl.ds(start, n), :]
        i, j = iotas(n)
        eye = i == j
        ans = []
        for which in range(2):
            row, col = (i, j) if which == 0 else (j, i)
            along = inv[which : which + 1, :]
            d = jnp.where(eye, along, 0.0)
            down = jnp.sum(d, axis=1, keepdims=True)
            part = (row >> 1 == col >> 1) & (row > col)
            ans.append(d - jnp.where(part, block * along * down, 0.0))
        level = 1
        while (1 << level) < n:
            for which in range(2):
                row, col = (i, j) if which == 0 else (j, i)
                part = (row >> (level + 1) == col >> (level + 1)) & (row >> level > col >> level)
                t = ans[which]
                ans[which] = t - mul3(mul3(t, jnp.where(part, block, 0.0)), t)
            level += 1
        t_ref[pl.ds(start, n), :] = jnp.where(i >= j, ans[0], ans[1])


def spread_kernel(place_ref, orb, came, b1, b2, b3, sem):
    z, y = place_ref[1] >> 1, place_ref[1] & 1
    copies = []
    for m, ref in ((1, b1), (2, b2), (3, b3)):
        copies.append(pltpu.make_async_copy(orb.at[z ^ m, y], ref.at[0], sem.at[0, m]))
        copies.append(pltpu.make_async_copy(came.at[z ^ m], ref.at[1], sem.at[1, m]))
    for copy in copies:
        copy.start()
    for copy in copies:
        copy.wait()


def rows_kernel(place_ref, orb, came, b1, b2, b3, left, right, res, sem):
    z, y = place_ref[1] >> 1, place_ref[1] & 1
    copies = [
        pltpu.make_async_copy(orb.at[z, y], res.at[2 * z + y], sem.at[0, 0]),
        pltpu.make_async_copy(came.at[z], res.at[2 * z + 1 - y], sem.at[1, 0]),
    ]
    for m, ref in ((1, b1), (2, b2), (3, b3)):
        copies.append(pltpu.make_async_copy(ref.at[0], res.at[2 * (z ^ m) + y], sem.at[0, m]))
        copies.append(pltpu.make_async_copy(ref.at[1], res.at[2 * (z ^ m) + 1 - y], sem.at[1, m]))
    for copy in copies:
        copy.start()
    for copy in copies:
        copy.wait()
    for k in range(4):
        left[:, k * 256 : (k + 1) * 256] = res[k]
        right[:, k * 256 : (k + 1) * 256] = res[4 + k]


def origin(place_ref, crossed, first, second, m):
    rep, bulk = place_ref[0], place_ref[1]
    core = (rep & 1) ^ crossed
    dx = jnp.where(core == 0, first, second)
    dy = jnp.where(core == 0, second, first)
    return rep ^ (2 * dx + crossed), bulk ^ (2 * m + dy), dx


GROUPS = ((0, 1, 2), (3,))


def pieces(crossed):
    found = []
    for g, group in enumerate(GROUPS):
        for second in range(2):
            for first in range(2):
                for at, m in enumerate(group):
                    found.append((4 * g + 2 * second + first, at, (crossed, first, second, m)))
    return found


def offset(index, size):
    return pl.ds(pl.multiple_of(index * size, size), size)


def first_kernel(place_ref, own, others, *refs):
    bufs, (x_ref, uh_ref, ul_ref, tri, diag, sem, sem2) = refs[:16], refs[16:]
    copies = []
    for crossed in range(2):
        for buf, entry, args in pieces(crossed):
            rep, bulk, dx = origin(place_ref, *args)
            src = bufs[8 * crossed + buf]
            copies.append(
                pltpu.make_async_copy(
                    src.at[entry, pl.ds(0, 256), :],
                    tri.at[offset(rep, 256), offset(bulk, 128)],
                    sem.at[crossed, buf, entry],
                )
            )
            if not crossed:
                copies.append(
                    pltpu.make_async_copy(src.at[entry, pl.ds(256, 8), :], diag.at[dx, bulk], sem2.at[buf, entry])
                )
    for copy in copies:
        copy.start()
    for copy in copies:
        copy.wait()

    n = 128
    i, j = iotas(n)
    lower, upper, eye = i > j, i < j, i == j

    def low_block(k):
        block = tri[k * n : (k + 1) * n, k * n : (k + 1) * n]
        return jnp.where(lower, block, 0.0) + jnp.where(eye, diag[0, k, 0:1, :], 0.0)

    def up_block(k):
        block = tri[k * n : (k + 1) * n, k * n : (k + 1) * n]
        return jnp.where(upper, block, 0.0) + jnp.where(eye, diag[0, k, 1:2, :], 0.0)

    zero = jnp.zeros((n, n), F32)
    lows = []
    for k in range(4):
        ta, tb = low_block(2 * k), low_block(2 * k + 1)
        lba = tri[k * 256 + 128 : k * 256 + 256, k * 256 : k * 256 + 128]
        off = -mul3(mul3(tb, lba), ta)
        lows.append(
            jnp.concatenate(
                [jnp.concatenate([ta, zero], axis=1), jnp.concatenate([off, tb], axis=1)], axis=0
            )
        )
    ups = []
    for k in range(4):
        ta, tb = up_block(2 * k), up_block(2 * k + 1)
        uab = tri[k * 256 : k * 256 + 128, k * 256 + 128 : k * 256 + 256]
        off = -mul3(mul3(ta, uab), tb)
        ups.append(
            jnp.concatenate(
                [jnp.concatenate([ta, off], axis=1), jnp.concatenate([zero, tb], axis=1)], axis=0
            )
        )

    rest = jnp.concatenate([own[...]] + [others[k] for k in range(3)], axis=0)
    for k in range(4):
        x = mul(rest[:, :256], split(lows[k]), NT)
        x_ref[:, k * 256 : (k + 1) * 256] = x
        if k < 3:
            later = tri[(k + 1) * 256 :, k * 256 : (k + 1) * 256]
            rest = rest[:, 256:] - mul(x, split(later), NT)

    def put(r, c, value):
        h, l = split(value)
        uh_ref[r * 256 : r * 256 + value.shape[0], c * 256 : c * 256 + value.shape[1]] = h
        ul_ref[r * 256 : r * 256 + value.shape[0], c * 256 : c * 256 + value.shape[1]] = l

    for k in range(2):
        ta, tb = ups[2 * k], ups[2 * k + 1]
        uab = tri[k * 512 : k * 512 + 256, k * 512 + 256 : k * 512 + 512]
        put(2 * k, 2 * k, ta)
        put(2 * k + 1, 2 * k + 1, tb)
        put(2 * k, 2 * k + 1, -mul3(mul3(ta, uab), tb))
        put(2 * k + 1, 2 * k, jnp.zeros((256, 256), F32))
    put(0, 2, tri[0:512, 512:1024])


def update_kernel(place_ref, x_ref, coup, *outs):
    x = x_ref[...]
    parts = [split(coup[k]) for k in range(8)]
    both = [jnp.concatenate([part[h] for part in parts], axis=1) for h in range(2)]
    upd = mul(x, both, NT)
    for k, out in enumerate(outs):
        out[...] = upd[32 * k : 32 * (k + 1)]


def second_kernel(place_ref, x_ref, rest_ref, uh_ref, ul_ref, mine, from_x, from_core, from_both, out_ref):
    x = x_ref[0:32, :]
    out_ref[:, 0:1024] = x
    parts = []
    for k in range(4):
        way = place_ref[0] ^ k
        upd = jnp.where(
            way == 0,
            mine[...],
            jnp.where(way == 2, from_x[...], jnp.where(way == 1, from_core[...], from_both[...])),
        )
        parts.append(rest_ref[:, k * 256 : (k + 1) * 256] - upd)
    ra = jnp.concatenate(parts[:2], axis=1)
    rb = jnp.concatenate(parts[2:], axis=1)

    def u(r, c):
        rows, cols = slice(r * 512, r * 512 + 512), slice(c * 512, c * 512 + 512)
        return uh_ref[rows, cols], ul_ref[rows, cols]

    xa = mul(ra, u(0, 0))
    xb = mul(rb - mul(xa, u(0, 1)), u(1, 1))
    out_ref[:, 1024:1536] = xa
    out_ref[:, 1536:2048] = xb


BOTH = ("bulk", "rep")


def swap_z(x, m):
    return lax.ppermute(x, "bulk", [(k, k ^ (2 * m)) for k in range(8)])


def swap_y(x):
    return lax.ppermute(x, "bulk", [(k, k ^ 1) for k in range(8)])


def swap_rep(x, bits):
    return lax.ppermute(x, "rep", [(k, k ^ bits) for k in range(4)])


def cross(x, stage):
    pairs = []
    for rep in range(4):
        for bulk in range(8):
            to = (rep ^ 2, bulk) if (rep & 1) == stage else (rep, bulk ^ 1)
            pairs.append((bulk * 4 + rep, to[1] * 4 + to[0]))
    return lax.ppermute(x, BOTH, pairs)


def after(x, *deps):
    return lax.optimization_barrier((x,) + deps)[0]


ANY = pl.BlockSpec(memory_space=pl.ANY)
VMEM = pl.BlockSpec(memory_space=pltpu.VMEM)
SMEM = pl.BlockSpec(memory_space=pltpu.SMEM)


def call(kernel, out, specs, outs, scratch, flops, size, name):
    return pl.pallas_call(
        kernel,
        out_shape=out,
        in_specs=specs,
        out_specs=outs,
        scratch_shapes=scratch,
        compiler_params=pltpu.CompilerParams(vmem_limit_bytes=size << 20),
        cost_estimate=pl.CostEstimate(flops=flops, bytes_accessed=2 << 20, transcendentals=0),
        name=name,
    )


def shape(*dims, dtype=F32):
    return jax.ShapeDtypeStruct(dims, dtype)


def dmas(*dims):
    return pltpu.SemaphoreType.DMA(dims)


def per_device(orbitals, triangles, coupling, diagonals):
    rep, bulk = lax.axis_index("rep"), lax.axis_index("bulk")
    place = jnp.stack([rep, bulk]).astype(jnp.int32)
    blocks = orbitals.reshape(4, 2, 32, 256)

    coup = lax.all_gather(coupling, "bulk", axis=0, tiled=False)

    t = call(
        invert_kernel,
        shape(264, 128),
        [SMEM, ANY, ANY],
        VMEM,
        [pltpu.VMEM((2, 128), F32), dmas(2)],
        3_500_000_000,
        8,
        "invert",
    )(place, triangles, diagonals)

    tz = [swap_z(t, m) for m in range(1, 4)]
    came = swap_y(lax.dynamic_index_in_dim(blocks, 1 - (bulk & 1), 1, keepdims=False))

    near = jnp.stack([t, tz[0], tz[1]])
    near0 = cross(after(near, came), 0)
    near1 = cross(near, 1)
    near01 = cross(after(near0, tz[2]), 1)
    far = after(tz[2], near0, near1)[None]
    far0 = cross(far, 0)
    far1 = cross(far, 1)

    b_out = call(
        spread_kernel, [shape(2, 32, 256)] * 3, [SMEM, ANY, ANY], [VMEM] * 3, [dmas(2, 4)], 500_000_000, 4, "spread"
    )(place, blocks, after(came, near))
    b_z = [swap_z(b, m + 1) for m, b in enumerate(b_out)]
    far01 = cross(after(far0, *b_z), 1)
    left, right = call(
        rows_kernel,
        [shape(32, 1024)] * 2,
        [SMEM] + [ANY] * 5,
        [VMEM] * 2,
        [pltpu.VMEM((8, 32, 256), F32), dmas(2, 4)],
        500_000_000,
        4,
        "rows",
    )(place, blocks, came, *b_z)
    others = [swap_rep(left, bits) for bits in (2, 1, 3)]

    held = [near, near0, near1, near01, far, far0, far1, far01]
    swaps = [swap_rep(b, 1) for b in held]

    x, uh, ul = call(
        first_kernel,
        [shape(128, 1024)] + [shape(1024, 1024, dtype=BF16)] * 2,
        [SMEM, VMEM, VMEM] + [ANY] * 16,
        [VMEM] * 3,
        [pltpu.VMEM((1024, 1024), F32), pltpu.VMEM((2, 8, 8, 128), F32), dmas(2, 8, 3), dmas(8, 3)],
        5_000_000_000,
        32,
        "first_panel",
    )(place, after(left, coup), jnp.stack(others), *held, *swaps)

    mine, to_x, to_core, to_both = call(
        update_kernel,
        [shape(32, 256)] * 4,
        [SMEM, VMEM, VMEM],
        [VMEM] * 4,
        [],
        2_000_000_000,
        32,
        "update",
    )(place, x, coup)
    back = [swap_rep(to_x, 2), swap_rep(to_core, 1), swap_rep(to_both, 3)]

    return call(
        second_kernel,
        shape(32, 2048),
        [SMEM] + [VMEM] * 8,
        VMEM,
        [],
        2_500_000_000,
        32,
        "second_panel",
    )(place, x, right, uh, ul, mine, *back)


def solution(mesh):
    special = mesh.shape["bulk"] == 8 and mesh.shape["rep"] == 4

    def run(orbitals, triangles, coupling, diagonals):
        fits = orbitals.shape == (1024, 2048) and triangles.shape == (1024, 1024)
        body = per_device if special and fits else per_device_any
        return jax.shard_map(
            body,
            mesh=mesh,
            in_specs=(P("rep", "bulk"), P("rep", "bulk"), P("rep", "bulk"), P(None, "bulk")),
            out_specs=P(("rep", "bulk"), None),
            check_vma=False,
        )(orbitals, triangles, coupling, diagonals)

    return run
```

```python
import jax
import jax.numpy as jnp
from jax import lax
from jax.experimental import pallas as pl
from jax.experimental.pallas import tpu as pltpu
from jax.sharding import PartitionSpec as P

F32 = jnp.float32
BF16 = jnp.bfloat16
NN = (((1,), (0,)), ((), ()))
NT = (((1,), (1,)), ((), ()))


def unpack(triangles, diagonals):
    first_block = jnp.tril(triangles, -1) + jnp.diag(diagonals[0])
    second_block = jnp.tril(triangles.T, -1) + jnp.diag(diagonals[1])
    return (first_block, second_block)


def per_device_any(orbitals, triangles, coupling, diagonals):
    tri_rows, couple_rows = (
        lax.all_gather(triangles, "rep", axis=0, tiled=True),
        lax.all_gather(coupling, "rep", axis=0, tiled=True),
    )
    tri_whole, couple_whole, diag_whole = (
        lax.all_gather(tri_rows, "bulk", axis=1, tiled=True),
        lax.all_gather(couple_rows, "bulk", axis=1, tiled=True),
        lax.all_gather(diagonals, "bulk", axis=1, tiled=True),
    )
    first_block, second_block = unpack(tri_whole, diag_whole)
    panel = first_block.shape[0]
    groups = lax.axis_size("bulk")
    local_rows = orbitals.shape[0] // groups
    blocks = orbitals.reshape(groups, local_rows, orbitals.shape[1])
    received = lax.all_to_all(blocks, "bulk", split_axis=0, concat_axis=2, tiled=True)
    rows_now = received.reshape(local_rows, received.shape[2])
    left_part = rows_now[:, :panel]
    right_part = rows_now[:, panel:]
    solved_one = jax.scipy.linalg.solve_triangular(first_block, left_part.T, lower=True).T
    update = jnp.dot(
        solved_one,
        couple_whole.T,
        precision=lax.Precision.HIGHEST,
        preferred_element_type=jnp.float32,
    )
    solved_two = jax.scipy.linalg.solve_triangular(
        second_block, (right_part - update).T, lower=True
    ).T
    return jnp.concatenate([solved_one, solved_two], axis=1)


def dot(a, b, dims=NN):
    return lax.dot_general(a, b, dims, preferred_element_type=F32)


def dot_exact(a, b):
    return lax.dot_general(a, b, NN, precision=lax.Precision.HIGHEST, preferred_element_type=F32)


def split(x):
    high = x.astype(BF16)
    return high, (x - high.astype(F32)).astype(BF16)


def mul(x, b, dims=NN):
    xh, xl = split(x)
    bh, bl = b
    m = x.shape[0]
    both = dot(jnp.concatenate([xh, xl], axis=0), bh, dims)
    return (both[:m] + both[m:]) + dot(xh, bl, dims)


def mul3(a, b):
    (ah, al), (bh, bl) = split(a), split(b)
    return dot(ah, bh) + (dot(al, bh) + dot(ah, bl))


def iotas(n):
    return lax.broadcasted_iota(jnp.int32, (n, n), 0), lax.broadcasted_iota(jnp.int32, (n, n), 1)


def invert_kernel(place_ref, tri_hbm, diag_hbm, t_ref, diag_ref, sem):
    rep, bulk = place_ref[0], place_ref[1]
    rows, n = tri_hbm.shape
    copies = [
        pltpu.make_async_copy(tri_hbm, t_ref.at[pl.ds(0, rows)], sem.at[0]),
        pltpu.make_async_copy(diag_hbm, diag_ref, sem.at[1]),
    ]
    for copy in copies:
        copy.start()
    for copy in copies:
        copy.wait()
    inv = 1.0 / diag_ref[...]
    t_ref[rows : rows + 8, :] = jnp.concatenate([inv, jnp.zeros((6, n), F32)], axis=0)

    @pl.when(rep == bulk // 2)
    def _():
        start = pl.multiple_of((bulk % 2) * n, n)
        block = t_ref[pl.ds(start, n), :]
        i, j = iotas(n)
        eye = i == j
        ans = []
        for which in range(2):
            row, col = (i, j) if which == 0 else (j, i)
            along = inv[which : which + 1, :]
            d = jnp.where(eye, along, 0.0)
            down = jnp.sum(d, axis=1, keepdims=True)
            part = (row >> 1 == col >> 1) & (row > col)
            ans.append(d - jnp.where(part, block * along * down, 0.0))
        level = 1
        while (1 << level) < n:
            for which in range(2):
                row, col = (i, j) if which == 0 else (j, i)
                part = (row >> (level + 1) == col >> (level + 1)) & (row >> level > col >> level)
                t = ans[which]
                ans[which] = t - mul3(mul3(t, jnp.where(part, block, 0.0)), t)
            level += 1
        t_ref[pl.ds(start, n), :] = jnp.where(i >= j, ans[0], ans[1])


def spread_kernel(place_ref, orb, b1, b2, b3, sem):
    z = place_ref[1] >> 1
    copies = [
        pltpu.make_async_copy(orb.at[z ^ m], ref, sem.at[m])
        for m, ref in ((1, b1), (2, b2), (3, b3))
    ]
    for copy in copies:
        copy.start()
    for copy in copies:
        copy.wait()


def leave_kernel(place_ref, orb, b1, b2, b3, out, sem):
    z, y = place_ref[1] >> 1, place_ref[1] & 1
    copies = [pltpu.make_async_copy(orb.at[z, 1 - y], out.at[0], sem.at[0])]
    for m, ref in ((1, b1), (2, b2), (3, b3)):
        copies.append(pltpu.make_async_copy(ref.at[1 - y], out.at[m], sem.at[m]))
    for copy in copies:
        copy.start()
    for copy in copies:
        copy.wait()


def rows_kernel(place_ref, orb, b1, b2, b3, came, left, right, res, sem):
    z, y = place_ref[1] >> 1, place_ref[1] & 1
    copies = [pltpu.make_async_copy(orb.at[z, y], res.at[2 * z + y], sem.at[0, 0])]
    for m, ref in ((1, b1), (2, b2), (3, b3)):
        copies.append(pltpu.make_async_copy(ref.at[y], res.at[2 * (z ^ m) + y], sem.at[0, m]))
    for m in range(4):
        copies.append(pltpu.make_async_copy(came.at[m], res.at[2 * (z ^ m) + 1 - y], sem.at[1, m]))
    for copy in copies:
        copy.start()
    for copy in copies:
        copy.wait()
    for k in range(4):
        left[:, k * 256 : (k + 1) * 256] = res[k]
        right[:, k * 256 : (k + 1) * 256] = res[4 + k]


def origin(place_ref, crossed, first, second, m):
    rep, bulk = place_ref[0], place_ref[1]
    core = (rep & 1) ^ crossed
    dx = jnp.where(core == 0, first, second)
    dy = jnp.where(core == 0, second, first)
    return rep ^ (2 * dx + crossed), bulk ^ (2 * m + dy), dx


def pieces(crossed):
    found = []
    for second in range(2):
        for first in range(2):
            found.append((0, 2 * second + first, (crossed, first, second, 0)))
            for m in range(1, 4):
                found.append((1 + 2 * second + first, m - 1, (crossed, first, second, m)))
    return found


def offset(index, size):
    return pl.ds(pl.multiple_of(index * size, size), size)


def first_kernel(place_ref, own, others, *refs):
    bufs, (x_ref, uh_ref, ul_ref, tri, diag, sem, sem2) = refs[:10], refs[10:]
    copies = []
    for crossed in range(2):
        for buf, entry, args in pieces(crossed):
            rep, bulk, dx = origin(place_ref, *args)
            src = bufs[5 * crossed + buf]
            copies.append(
                pltpu.make_async_copy(
                    src.at[entry, pl.ds(0, 256), :],
                    tri.at[offset(rep, 256), offset(bulk, 128)],
                    sem.at[crossed, buf, entry],
                )
            )
            if not crossed:
                copies.append(
                    pltpu.make_async_copy(src.at[entry, pl.ds(256, 8), :], diag.at[dx, bulk], sem2.at[buf, entry])
                )
    for copy in copies:
        copy.start()
    for copy in copies:
        copy.wait()

    n = 128
    i, j = iotas(n)
    lower, upper, eye = i > j, i < j, i == j

    def low_block(k):
        block = tri[k * n : (k + 1) * n, k * n : (k + 1) * n]
        return jnp.where(lower, block, 0.0) + jnp.where(eye, diag[0, k, 0:1, :], 0.0)

    def up_block(k):
        block = tri[k * n : (k + 1) * n, k * n : (k + 1) * n]
        return jnp.where(upper, block, 0.0) + jnp.where(eye, diag[0, k, 1:2, :], 0.0)

    zero = jnp.zeros((n, n), F32)
    lows = []
    for k in range(4):
        ta, tb = low_block(2 * k), low_block(2 * k + 1)
        lba = tri[k * 256 + 128 : k * 256 + 256, k * 256 : k * 256 + 128]
        off = -mul3(mul3(tb, lba), ta)
        lows.append(
            jnp.concatenate(
                [jnp.concatenate([ta, zero], axis=1), jnp.concatenate([off, tb], axis=1)], axis=0
            )
        )
    ups = []
    for k in range(4):
        ta, tb = up_block(2 * k), up_block(2 * k + 1)
        uab = tri[k * 256 : k * 256 + 128, k * 256 + 128 : k * 256 + 256]
        off = -mul3(mul3(ta, uab), tb)
        ups.append(
            jnp.concatenate(
                [jnp.concatenate([ta, off], axis=1), jnp.concatenate([zero, tb], axis=1)], axis=0
            )
        )

    rest = jnp.concatenate([own[...]] + [others[k] for k in range(3)], axis=0)
    for k in range(4):
        x = mul(rest[:, :256], split(lows[k]), NT)
        x_ref[:, k * 256 : (k + 1) * 256] = x
        if k < 3:
            later = tri[(k + 1) * 256 :, k * 256 : (k + 1) * 256]
            rest = rest[:, 256:] - mul(x, split(later), NT)

    def put(r, c, value):
        h, l = split(value)
        uh_ref[r * 256 : r * 256 + value.shape[0], c * 256 : c * 256 + value.shape[1]] = h
        ul_ref[r * 256 : r * 256 + value.shape[0], c * 256 : c * 256 + value.shape[1]] = l

    for k in range(2):
        ta, tb = ups[2 * k], ups[2 * k + 1]
        uab = tri[k * 512 : k * 512 + 256, k * 512 + 256 : k * 512 + 512]
        put(2 * k, 2 * k, ta)
        put(2 * k + 1, 2 * k + 1, tb)
        put(2 * k, 2 * k + 1, -mul3(mul3(ta, uab), tb))
        put(2 * k + 1, 2 * k, jnp.zeros((256, 256), F32))
    put(0, 2, tri[0:512, 512:1024])


def stack_kernel(c1, c2, c3, out, sem):
    copies = [pltpu.make_async_copy(ref, out.at[k], sem.at[k]) for k, ref in enumerate((c1, c2, c3))]
    for copy in copies:
        copy.start()
    for copy in copies:
        copy.wait()


def update_kernel(place_ref, x_ref, own, own_got, held, got, *refs):
    outs, (coup, sem) = refs[:4], refs[4:]
    bulk = place_ref[1]
    copies = []
    for m in range(4):
        for dy in range(2):
            src = (own, own_got)[dy] if m == 0 else (held, got)[dy].at[m - 1]
            copies.append(
                pltpu.make_async_copy(src, coup.at[:, offset(bulk ^ (2 * m + dy), 128)], sem.at[dy, m])
            )
    for copy in copies:
        copy.start()
    x = x_ref[...]
    for copy in copies:
        copy.wait()
    upd = mul(x, split(coup[...]), NT)
    for k, out in enumerate(outs):
        out[...] = upd[32 * k : 32 * (k + 1)]


def second_kernel(place_ref, x_ref, rest_ref, uh_ref, ul_ref, mine, from_x, from_core, from_both, out_ref):
    x = x_ref[0:32, :]
    out_ref[:, 0:1024] = x
    parts = []
    for k in range(4):
        way = place_ref[0] ^ k
        upd = jnp.where(
            way == 0,
            mine[...],
            jnp.where(way == 2, from_x[...], jnp.where(way == 1, from_core[...], from_both[...])),
        )
        parts.append(rest_ref[:, k * 256 : (k + 1) * 256] - upd)
    ra = jnp.concatenate(parts[:2], axis=1)
    rb = jnp.concatenate(parts[2:], axis=1)

    def u(r, c):
        rows, cols = slice(r * 512, r * 512 + 512), slice(c * 512, c * 512 + 512)
        return uh_ref[rows, cols], ul_ref[rows, cols]

    xa = mul(ra, u(0, 0))
    xb = mul(rb - mul(xa, u(0, 1)), u(1, 1))
    out_ref[:, 1024:1536] = xa
    out_ref[:, 1536:2048] = xb


BOTH = ("bulk", "rep")

SPREAD, INVERT, LEAVE, ROWS, STACK = 1_000_000_000, 3_500_000_000, 500_000_000, 1_000_000_000, 20_000_000_000


def swap_z(x, m):
    return lax.ppermute(x, "bulk", [(k, k ^ (2 * m)) for k in range(8)])


def swap_y(x):
    return lax.ppermute(x, "bulk", [(k, k ^ 1) for k in range(8)])


def swap_rep(x, bits):
    return lax.ppermute(x, "rep", [(k, k ^ bits) for k in range(4)])


def cross(x, stage):
    pairs = []
    for rep in range(4):
        for bulk in range(8):
            to = (rep ^ 2, bulk) if (rep & 1) == stage else (rep, bulk ^ 1)
            pairs.append((bulk * 4 + rep, to[1] * 4 + to[0]))
    return lax.ppermute(x, BOTH, pairs)


def after(x, *deps):
    return lax.optimization_barrier((x,) + deps)[0]


ANY = pl.BlockSpec(memory_space=pl.ANY)
VMEM = pl.BlockSpec(memory_space=pltpu.VMEM)
SMEM = pl.BlockSpec(memory_space=pltpu.SMEM)


def call(kernel, out, specs, outs, scratch, flops, size, name):
    return pl.pallas_call(
        kernel,
        out_shape=out,
        in_specs=specs,
        out_specs=outs,
        scratch_shapes=scratch,
        compiler_params=pltpu.CompilerParams(vmem_limit_bytes=size << 20),
        cost_estimate=pl.CostEstimate(flops=flops, bytes_accessed=2 << 20, transcendentals=0),
        name=name,
    )


def shape(*dims, dtype=F32):
    return jax.ShapeDtypeStruct(dims, dtype)


def dmas(*dims):
    return pltpu.SemaphoreType.DMA(dims)


def per_device(orbitals, triangles, coupling, diagonals):
    rep, bulk = lax.axis_index("rep"), lax.axis_index("bulk")
    place = jnp.stack([rep, bulk]).astype(jnp.int32)
    blocks = orbitals.reshape(4, 2, 32, 256)

    b_out = call(
        spread_kernel, [shape(2, 32, 256)] * 3, [SMEM, ANY], [VMEM] * 3, [dmas(4)], SPREAD, 4, "spread"
    )(place, blocks)
    b_z = [swap_z(b, m + 1) for m, b in enumerate(b_out)]

    t = call(
        invert_kernel,
        shape(264, 128),
        [SMEM, ANY, ANY],
        VMEM,
        [pltpu.VMEM((2, 128), F32), dmas(2)],
        INVERT,
        8,
        "invert",
    )(place, triangles, diagonals)

    t = after(t, *b_z)
    tz = [swap_z(t, m) for m in range(1, 4)]
    own0 = cross(t, 0)
    own1 = cross(t, 1)
    own01 = cross(own0, 1)
    own = jnp.stack([t, own0, own1, own01])
    own_swap = swap_rep(own, 1)

    leave = call(
        leave_kernel, shape(4, 32, 256), [SMEM] + [ANY] * 4, VMEM, [dmas(4)], LEAVE, 4, "leave"
    )(place, blocks, *b_z)
    came = swap_y(leave)
    left, right = call(
        rows_kernel,
        [shape(32, 1024)] * 2,
        [SMEM] + [ANY] * 5,
        [VMEM] * 2,
        [pltpu.VMEM((8, 32, 256), F32), dmas(2, 4)],
        ROWS,
        4,
        "rows",
    )(place, blocks, *b_z, came)
    others = [swap_rep(left, bits) for bits in (2, 1, 3)]

    far = jnp.stack(tz)
    cz = [swap_z(after(coupling, far), m) for m in range(1, 4)]
    far_now = after(far, own0, came)
    far0 = cross(far_now, 0)
    far1 = cross(far_now, 1)
    far01 = cross(after(far0, own1, own01, cz[0], left), 1)
    held = [far, far0, far1, far01]
    swaps = [swap_rep(b, 1) for b in held]
    cfar = call(stack_kernel, shape(3, 256, 128), [ANY] * 3, VMEM, [dmas(3)], STACK, 4, "stack")(*cz)
    cown = swap_y(coupling)
    cgot = swap_y(cfar)

    x, uh, ul = call(
        first_kernel,
        [shape(128, 1024)] + [shape(1024, 1024, dtype=BF16)] * 2,
        [SMEM, VMEM, VMEM] + [ANY] * 10,
        [VMEM] * 3,
        [pltpu.VMEM((1024, 1024), F32), pltpu.VMEM((2, 8, 8, 128), F32), dmas(2, 5, 4), dmas(5, 4)],
        5_000_000_000,
        32,
        "first_panel",
    )(place, after(left, cown), jnp.stack(others), own, *held, own_swap, *swaps)

    mine, to_x, to_core, to_both = call(
        update_kernel,
        [shape(32, 256)] * 4,
        [SMEM, VMEM] + [ANY] * 4,
        [VMEM] * 4,
        [pltpu.VMEM((256, 1024), F32), dmas(2, 4)],
        2_000_000_000,
        32,
        "update",
    )(place, x, coupling, cown, cfar, cgot)
    back = [swap_rep(to_x, 2), swap_rep(to_core, 1), swap_rep(to_both, 3)]

    return call(
        second_kernel,
        shape(32, 2048),
        [SMEM] + [VMEM] * 8,
        VMEM,
        [],
        2_500_000_000,
        32,
        "second_panel",
    )(place, x, right, uh, ul, mine, *back)


def solution(mesh):
    special = mesh.shape["bulk"] == 8 and mesh.shape["rep"] == 4

    def run(orbitals, triangles, coupling, diagonals):
        fits = orbitals.shape == (1024, 2048) and triangles.shape == (1024, 1024)
        body = per_device if special and fits else per_device_any
        return jax.shard_map(
            body,
            mesh=mesh,
            in_specs=(P("rep", "bulk"), P("rep", "bulk"), P("rep", "bulk"), P(None, "bulk")),
            out_specs=P(("rep", "bulk"), None),
            check_vma=False,
        )(orbitals, triangles, coupling, diagonals)

    return run
```

```python
import jax
import jax.numpy as jnp
from jax import lax
from jax.experimental import pallas as pl
from jax.experimental.pallas import tpu as pltpu
from jax.sharding import PartitionSpec as P

F32 = jnp.float32
BF16 = jnp.bfloat16
NN = (((1,), (0,)), ((), ()))
NT = (((1,), (1,)), ((), ()))


def unpack(triangles, diagonals):
    first_block = jnp.tril(triangles, -1) + jnp.diag(diagonals[0])
    second_block = jnp.tril(triangles.T, -1) + jnp.diag(diagonals[1])
    return (first_block, second_block)


def per_device_any(orbitals, triangles, coupling, diagonals):
    tri_rows, couple_rows = (
        lax.all_gather(triangles, "rep", axis=0, tiled=True),
        lax.all_gather(coupling, "rep", axis=0, tiled=True),
    )
    tri_whole, couple_whole, diag_whole = (
        lax.all_gather(tri_rows, "bulk", axis=1, tiled=True),
        lax.all_gather(couple_rows, "bulk", axis=1, tiled=True),
        lax.all_gather(diagonals, "bulk", axis=1, tiled=True),
    )
    first_block, second_block = unpack(tri_whole, diag_whole)
    panel = first_block.shape[0]
    groups = lax.axis_size("bulk")
    local_rows = orbitals.shape[0] // groups
    blocks = orbitals.reshape(groups, local_rows, orbitals.shape[1])
    received = lax.all_to_all(blocks, "bulk", split_axis=0, concat_axis=2, tiled=True)
    rows_now = received.reshape(local_rows, received.shape[2])
    left_part = rows_now[:, :panel]
    right_part = rows_now[:, panel:]
    solved_one = jax.scipy.linalg.solve_triangular(first_block, left_part.T, lower=True).T
    update = jnp.dot(
        solved_one,
        couple_whole.T,
        precision=lax.Precision.HIGHEST,
        preferred_element_type=jnp.float32,
    )
    solved_two = jax.scipy.linalg.solve_triangular(
        second_block, (right_part - update).T, lower=True
    ).T
    return jnp.concatenate([solved_one, solved_two], axis=1)


def dot(a, b, dims=NN):
    return lax.dot_general(a, b, dims, preferred_element_type=F32)


def dot_exact(a, b):
    return lax.dot_general(a, b, NN, precision=lax.Precision.HIGHEST, preferred_element_type=F32)


def split(x):
    high = x.astype(BF16)
    return high, (x - high.astype(F32)).astype(BF16)


def mul(x, b, dims=NN):
    xh, xl = split(x)
    bh, bl = b
    m = x.shape[0]
    both = dot(jnp.concatenate([xh, xl], axis=0), bh, dims)
    return (both[:m] + both[m:]) + dot(xh, bl, dims)


def mul3(a, b):
    (ah, al), (bh, bl) = split(a), split(b)
    return dot(ah, bh) + (dot(al, bh) + dot(ah, bl))


def iotas(n):
    return lax.broadcasted_iota(jnp.int32, (n, n), 0), lax.broadcasted_iota(jnp.int32, (n, n), 1)


def invert_kernel(place_ref, tri_hbm, diag_hbm, t_ref, diag_ref, sem):
    rep, bulk = place_ref[0], place_ref[1]
    rows, n = tri_hbm.shape
    copies = [
        pltpu.make_async_copy(tri_hbm, t_ref.at[pl.ds(0, rows)], sem.at[0]),
        pltpu.make_async_copy(diag_hbm, diag_ref, sem.at[1]),
    ]
    for copy in copies:
        copy.start()
    for copy in copies:
        copy.wait()
    inv = 1.0 / diag_ref[...]
    t_ref[rows : rows + 8, :] = jnp.concatenate([inv, jnp.zeros((6, n), F32)], axis=0)

    @pl.when(rep == bulk // 2)
    def _():
        start = pl.multiple_of((bulk % 2) * n, n)
        block = t_ref[pl.ds(start, n), :]
        i, j = iotas(n)
        eye = i == j
        ans = []
        for which in range(2):
            row, col = (i, j) if which == 0 else (j, i)
            along = inv[which : which + 1, :]
            d = jnp.where(eye, along, 0.0)
            down = jnp.sum(d, axis=1, keepdims=True)
            part = (row >> 1 == col >> 1) & (row > col)
            ans.append(d - jnp.where(part, block * along * down, 0.0))
        level = 1
        while (1 << level) < n:
            for which in range(2):
                row, col = (i, j) if which == 0 else (j, i)
                part = (row >> (level + 1) == col >> (level + 1)) & (row >> level > col >> level)
                t = ans[which]
                ans[which] = t - mul3(mul3(t, jnp.where(part, block, 0.0)), t)
            level += 1
        t_ref[pl.ds(start, n), :] = jnp.where(i >= j, ans[0], ans[1])


COUP, PAYLOAD = 256, 384


def part(y, h):
    return pl.ds(pl.multiple_of(COUP + 64 * y + 32 * h, 32), 32)


def pack_kernel(place_ref, coup, orb, *refs):
    outs, sem = refs[:4], refs[4]
    z = place_ref[1] >> 1
    copies = []
    for m, out in enumerate(outs):
        copies.append(pltpu.make_async_copy(coup, out.at[pl.ds(0, COUP)], sem.at[m, 4]))
        for y in range(2):
            for h in range(2):
                src = orb.at[z ^ m, y, :, pl.ds(128 * h, 128)]
                copies.append(pltpu.make_async_copy(src, out.at[part(y, h)], sem.at[m, 2 * y + h]))
    for copy in copies:
        copy.start()
    for copy in copies:
        copy.wait()


def rows_kernel(place_ref, *refs):
    payloads, (left, right, res, sem) = refs[:8], refs[8:]
    z, y = place_ref[1] >> 1, place_ref[1] & 1
    copies = []
    for dy in range(2):
        for m in range(4):
            for h in range(2):
                dst = res.at[2 * (z ^ m) + (y ^ dy), :, pl.ds(128 * h, 128)]
                copies.append(pltpu.make_async_copy(payloads[4 * dy + m].at[part(y, h)], dst, sem.at[dy, m, h]))
    for copy in copies:
        copy.start()
    for copy in copies:
        copy.wait()
    for k in range(4):
        left[:, k * 256 : (k + 1) * 256] = res[k]
        right[:, k * 256 : (k + 1) * 256] = res[4 + k]


def origin(place_ref, crossed, first, second, m):
    rep, bulk = place_ref[0], place_ref[1]
    core = (rep & 1) ^ crossed
    dx = jnp.where(core == 0, first, second)
    dy = jnp.where(core == 0, second, first)
    return rep ^ (2 * dx + crossed), bulk ^ (2 * m + dy), dx


GROUPS = ((0, 1, 2), (3,))


def pieces(crossed):
    found = []
    for g, group in enumerate(GROUPS):
        for second in range(2):
            for first in range(2):
                for at, m in enumerate(group):
                    found.append((4 * g + 2 * second + first, at, (crossed, first, second, m)))
    return found


def offset(index, size):
    return pl.ds(pl.multiple_of(index * size, size), size)


def first_kernel(place_ref, own, others, *refs):
    bufs, (x_ref, uh_ref, ul_ref, tri, diag, sem, sem2) = refs[:16], refs[16:]
    copies = []
    for crossed in range(2):
        for buf, entry, args in pieces(crossed):
            rep, bulk, dx = origin(place_ref, *args)
            src = bufs[8 * crossed + buf]
            copies.append(
                pltpu.make_async_copy(
                    src.at[entry, pl.ds(0, 256), :],
                    tri.at[offset(rep, 256), offset(bulk, 128)],
                    sem.at[crossed, buf, entry],
                )
            )
            if not crossed:
                copies.append(
                    pltpu.make_async_copy(src.at[entry, pl.ds(256, 8), :], diag.at[dx, bulk], sem2.at[buf, entry])
                )
    for copy in copies:
        copy.start()
    for copy in copies:
        copy.wait()

    n = 128
    i, j = iotas(n)
    lower, upper, eye = i > j, i < j, i == j

    def low_block(k):
        block = tri[k * n : (k + 1) * n, k * n : (k + 1) * n]
        return jnp.where(lower, block, 0.0) + jnp.where(eye, diag[0, k, 0:1, :], 0.0)

    def up_block(k):
        block = tri[k * n : (k + 1) * n, k * n : (k + 1) * n]
        return jnp.where(upper, block, 0.0) + jnp.where(eye, diag[0, k, 1:2, :], 0.0)

    zero = jnp.zeros((n, n), F32)
    lows = []
    for k in range(4):
        ta, tb = low_block(2 * k), low_block(2 * k + 1)
        lba = tri[k * 256 + 128 : k * 256 + 256, k * 256 : k * 256 + 128]
        off = -mul3(mul3(tb, lba), ta)
        lows.append(
            jnp.concatenate(
                [jnp.concatenate([ta, zero], axis=1), jnp.concatenate([off, tb], axis=1)], axis=0
            )
        )
    ups = []
    for k in range(4):
        ta, tb = up_block(2 * k), up_block(2 * k + 1)
        uab = tri[k * 256 : k * 256 + 128, k * 256 + 128 : k * 256 + 256]
        off = -mul3(mul3(ta, uab), tb)
        ups.append(
            jnp.concatenate(
                [jnp.concatenate([ta, off], axis=1), jnp.concatenate([zero, tb], axis=1)], axis=0
            )
        )

    rest = jnp.concatenate([own[...]] + [others[k] for k in range(3)], axis=0)
    for k in range(4):
        x = mul(rest[:, :256], split(lows[k]), NT)
        x_ref[:, k * 256 : (k + 1) * 256] = x
        if k < 3:
            later = tri[(k + 1) * 256 :, k * 256 : (k + 1) * 256]
            rest = rest[:, 256:] - mul(x, split(later), NT)

    def put(r, c, value):
        h, l = split(value)
        uh_ref[r * 256 : r * 256 + value.shape[0], c * 256 : c * 256 + value.shape[1]] = h
        ul_ref[r * 256 : r * 256 + value.shape[0], c * 256 : c * 256 + value.shape[1]] = l

    for k in range(2):
        ta, tb = ups[2 * k], ups[2 * k + 1]
        uab = tri[k * 512 : k * 512 + 256, k * 512 + 256 : k * 512 + 512]
        put(2 * k, 2 * k, ta)
        put(2 * k + 1, 2 * k + 1, tb)
        put(2 * k, 2 * k + 1, -mul3(mul3(ta, uab), tb))
        put(2 * k + 1, 2 * k, jnp.zeros((256, 256), F32))
    put(0, 2, tri[0:512, 512:1024])


def update_kernel(place_ref, x_ref, *refs):
    payloads, outs, (coup, sem) = refs[:8], refs[8:12], refs[12:]
    bulk = place_ref[1]
    copies = []
    for dy in range(2):
        for m in range(4):
            src = payloads[4 * dy + m].at[pl.ds(0, COUP)]
            copies.append(
                pltpu.make_async_copy(src, coup.at[:, offset(bulk ^ (2 * m + dy), 128)], sem.at[dy, m])
            )
    for copy in copies:
        copy.start()
    x = x_ref[...]
    for copy in copies:
        copy.wait()
    upd = mul(x, split(coup[...]), NT)
    for k, out in enumerate(outs):
        out[...] = upd[32 * k : 32 * (k + 1)]


def second_kernel(place_ref, x_ref, rest_ref, uh_ref, ul_ref, mine, from_x, from_core, from_both, out_ref):
    x = x_ref[0:32, :]
    out_ref[:, 0:1024] = x
    parts = []
    for k in range(4):
        way = place_ref[0] ^ k
        upd = jnp.where(
            way == 0,
            mine[...],
            jnp.where(way == 2, from_x[...], jnp.where(way == 1, from_core[...], from_both[...])),
        )
        parts.append(rest_ref[:, k * 256 : (k + 1) * 256] - upd)
    ra = jnp.concatenate(parts[:2], axis=1)
    rb = jnp.concatenate(parts[2:], axis=1)

    def u(r, c):
        rows, cols = slice(r * 512, r * 512 + 512), slice(c * 512, c * 512 + 512)
        return uh_ref[rows, cols], ul_ref[rows, cols]

    xa = mul(ra, u(0, 0))
    xb = mul(rb - mul(xa, u(0, 1)), u(1, 1))
    out_ref[:, 1024:1536] = xa
    out_ref[:, 1536:2048] = xb


BOTH = ("bulk", "rep")

PACK, INVERT, ROWS = 1_000_000_000, 3_500_000_000, 1_000_000_000


def swap_z(x, m):
    return lax.ppermute(x, "bulk", [(k, k ^ (2 * m)) for k in range(8)])


def swap_y(x):
    return lax.ppermute(x, "bulk", [(k, k ^ 1) for k in range(8)])


def swap_rep(x, bits):
    return lax.ppermute(x, "rep", [(k, k ^ bits) for k in range(4)])


def cross(x, stage):
    pairs = []
    for rep in range(4):
        for bulk in range(8):
            to = (rep ^ 2, bulk) if (rep & 1) == stage else (rep, bulk ^ 1)
            pairs.append((bulk * 4 + rep, to[1] * 4 + to[0]))
    return lax.ppermute(x, BOTH, pairs)


def after(x, *deps):
    return lax.optimization_barrier((x,) + deps)[0]


ANY = pl.BlockSpec(memory_space=pl.ANY)
VMEM = pl.BlockSpec(memory_space=pltpu.VMEM)
SMEM = pl.BlockSpec(memory_space=pltpu.SMEM)


def call(kernel, out, specs, outs, scratch, flops, size, name):
    return pl.pallas_call(
        kernel,
        out_shape=out,
        in_specs=specs,
        out_specs=outs,
        scratch_shapes=scratch,
        compiler_params=pltpu.CompilerParams(vmem_limit_bytes=size << 20),
        cost_estimate=pl.CostEstimate(flops=flops, bytes_accessed=2 << 20, transcendentals=0),
        name=name,
    )


def shape(*dims, dtype=F32):
    return jax.ShapeDtypeStruct(dims, dtype)


def dmas(*dims):
    return pltpu.SemaphoreType.DMA(dims)


def per_device(orbitals, triangles, coupling, diagonals):
    rep, bulk = lax.axis_index("rep"), lax.axis_index("bulk")
    place = jnp.stack([rep, bulk]).astype(jnp.int32)
    blocks = orbitals.reshape(4, 2, 32, 256)

    out = call(
        pack_kernel, [shape(PAYLOAD, 128)] * 4, [SMEM, ANY, ANY], [VMEM] * 4, [dmas(4, 5)], PACK, 60, "pack"
    )(place, coupling, blocks)
    stay = [out[0]] + [swap_z(out[m], m) for m in range(1, 4)]
    came = [swap_y(out[0])]

    t = call(
        invert_kernel,
        shape(264, 128),
        [SMEM, ANY, ANY],
        VMEM,
        [pltpu.VMEM((2, 128), F32), dmas(2)],
        INVERT,
        60,
        "invert",
    )(place, triangles, diagonals)
    t = after(t, came[0], stay[1])

    tz = [swap_z(t, m) for m in range(1, 4)]
    near = jnp.stack([t, tz[0], tz[1]])
    near_now = after(near, stay[2], stay[3])
    near0 = cross(near_now, 0)
    near1 = cross(near_now, 1)
    near01 = cross(after(near0, tz[2]), 1)
    far = after(tz[2], near0)[None]
    far0 = cross(far, 0)
    far1 = cross(far, 1)
    far01 = cross(far0, 1)
    held = [near, near0, near1, near01, far, far0, far1, far01]
    swaps = [swap_rep(b, 1) for b in held]

    came += [swap_y(p) for p in stay[1:]]
    left, right = call(
        rows_kernel,
        [shape(32, 1024)] * 2,
        [SMEM] + [ANY] * 8,
        [VMEM] * 2,
        [pltpu.VMEM((8, 32, 256), F32), dmas(2, 4, 2)],
        ROWS,
        4,
        "rows",
    )(place, *stay, *came)
    others = [swap_rep(after(left, far0), bits) for bits in (2, 1, 3)]

    x, uh, ul = call(
        first_kernel,
        [shape(128, 1024)] + [shape(1024, 1024, dtype=BF16)] * 2,
        [SMEM, VMEM, VMEM] + [ANY] * 16,
        [VMEM] * 3,
        [pltpu.VMEM((1024, 1024), F32), pltpu.VMEM((2, 8, 8, 128), F32), dmas(2, 8, 3), dmas(8, 3)],
        5_000_000_000,
        32,
        "first_panel",
    )(place, left, jnp.stack(others), *held, *swaps)

    mine, to_x, to_core, to_both = call(
        update_kernel,
        [shape(32, 256)] * 4,
        [SMEM, VMEM] + [ANY] * 8,
        [VMEM] * 4,
        [pltpu.VMEM((256, 1024), F32), dmas(2, 4)],
        2_000_000_000,
        32,
        "update",
    )(place, x, *stay, *came)
    back = [swap_rep(to_x, 2), swap_rep(to_core, 1), swap_rep(to_both, 3)]

    return call(
        second_kernel,
        shape(32, 2048),
        [SMEM] + [VMEM] * 8,
        VMEM,
        [],
        2_500_000_000,
        32,
        "second_panel",
    )(place, x, right, uh, ul, mine, *back)


def solution(mesh):
    special = mesh.shape["bulk"] == 8 and mesh.shape["rep"] == 4

    def run(orbitals, triangles, coupling, diagonals):
        fits = orbitals.shape == (1024, 2048) and triangles.shape == (1024, 1024)
        body = per_device if special and fits else per_device_any
        return jax.shard_map(
            body,
            mesh=mesh,
            in_specs=(P("rep", "bulk"), P("rep", "bulk"), P("rep", "bulk"), P(None, "bulk")),
            out_specs=P(("rep", "bulk"), None),
            check_vma=False,
        )(orbitals, triangles, coupling, diagonals)

    return run
```

```python
import jax
import jax.numpy as jnp
from jax import lax
from jax.experimental import pallas as pl
from jax.experimental.pallas import tpu as pltpu
from jax.sharding import PartitionSpec as P

F32 = jnp.float32
BF16 = jnp.bfloat16
NN = (((1,), (0,)), ((), ()))
NT = (((1,), (1,)), ((), ()))


def unpack(triangles, diagonals):
    first_block = jnp.tril(triangles, -1) + jnp.diag(diagonals[0])
    second_block = jnp.tril(triangles.T, -1) + jnp.diag(diagonals[1])
    return (first_block, second_block)


def per_device_any(orbitals, triangles, coupling, diagonals):
    tri_rows, couple_rows = (
        lax.all_gather(triangles, "rep", axis=0, tiled=True),
        lax.all_gather(coupling, "rep", axis=0, tiled=True),
    )
    tri_whole, couple_whole, diag_whole = (
        lax.all_gather(tri_rows, "bulk", axis=1, tiled=True),
        lax.all_gather(couple_rows, "bulk", axis=1, tiled=True),
        lax.all_gather(diagonals, "bulk", axis=1, tiled=True),
    )
    first_block, second_block = unpack(tri_whole, diag_whole)
    panel = first_block.shape[0]
    groups = lax.axis_size("bulk")
    local_rows = orbitals.shape[0] // groups
    blocks = orbitals.reshape(groups, local_rows, orbitals.shape[1])
    received = lax.all_to_all(blocks, "bulk", split_axis=0, concat_axis=2, tiled=True)
    rows_now = received.reshape(local_rows, received.shape[2])
    left_part = rows_now[:, :panel]
    right_part = rows_now[:, panel:]
    solved_one = jax.scipy.linalg.solve_triangular(first_block, left_part.T, lower=True).T
    update = jnp.dot(
        solved_one,
        couple_whole.T,
        precision=lax.Precision.HIGHEST,
        preferred_element_type=jnp.float32,
    )
    solved_two = jax.scipy.linalg.solve_triangular(
        second_block, (right_part - update).T, lower=True
    ).T
    return jnp.concatenate([solved_one, solved_two], axis=1)


def dot(a, b, dims=NN):
    return lax.dot_general(a, b, dims, preferred_element_type=F32)


def dot_exact(a, b):
    return lax.dot_general(a, b, NN, precision=lax.Precision.HIGHEST, preferred_element_type=F32)


def split(x):
    high = x.astype(BF16)
    return high, (x - high.astype(F32)).astype(BF16)


def mul(x, b, dims=NN):
    xh, xl = split(x)
    bh, bl = b
    m = x.shape[0]
    both = dot(jnp.concatenate([xh, xl], axis=0), bh, dims)
    return (both[:m] + both[m:]) + dot(xh, bl, dims)


def mul3(a, b):
    (ah, al), (bh, bl) = split(a), split(b)
    return dot(ah, bh) + (dot(al, bh) + dot(ah, bl))


def iotas(n):
    return lax.broadcasted_iota(jnp.int32, (n, n), 0), lax.broadcasted_iota(jnp.int32, (n, n), 1)


def invert_kernel(place_ref, tri_hbm, diag_hbm, t_ref, diag_ref, sem):
    rep, bulk = place_ref[0], place_ref[1]
    rows, n = tri_hbm.shape
    copies = [
        pltpu.make_async_copy(tri_hbm, t_ref.at[pl.ds(0, rows)], sem.at[0]),
        pltpu.make_async_copy(diag_hbm, diag_ref, sem.at[1]),
    ]
    for copy in copies:
        copy.start()
    for copy in copies:
        copy.wait()
    inv = 1.0 / diag_ref[...]
    t_ref[rows : rows + 8, :] = jnp.concatenate([inv, jnp.zeros((6, n), F32)], axis=0)

    @pl.when(rep == bulk // 2)
    def _():
        start = pl.multiple_of((bulk % 2) * n, n)
        block = t_ref[pl.ds(start, n), :]
        i, j = iotas(n)
        eye = i == j
        ans = []
        for which in range(2):
            row, col = (i, j) if which == 0 else (j, i)
            along = inv[which : which + 1, :]
            d = jnp.where(eye, along, 0.0)
            down = jnp.sum(d, axis=1, keepdims=True)
            part = (row >> 1 == col >> 1) & (row > col)
            ans.append(d - jnp.where(part, block * along * down, 0.0))
        level = 1
        while (1 << level) < n:
            for which in range(2):
                row, col = (i, j) if which == 0 else (j, i)
                part = (row >> (level + 1) == col >> (level + 1)) & (row >> level > col >> level)
                t = ans[which]
                ans[which] = t - mul3(mul3(t, jnp.where(part, block, 0.0)), t)
            level += 1
        t_ref[pl.ds(start, n), :] = jnp.where(i >= j, ans[0], ans[1])


def spread_kernel(place_ref, orb, b1, b2, b3, sem):
    z = place_ref[1] >> 1
    copies = [
        pltpu.make_async_copy(orb.at[z ^ m], ref, sem.at[m])
        for m, ref in ((1, b1), (2, b2), (3, b3))
    ]
    for copy in copies:
        copy.start()
    for copy in copies:
        copy.wait()


def leave_kernel(place_ref, orb, b1, b2, b3, out, sem):
    z, y = place_ref[1] >> 1, place_ref[1] & 1
    copies = [pltpu.make_async_copy(orb.at[z, 1 - y], out.at[0], sem.at[0])]
    for m, ref in ((1, b1), (2, b2), (3, b3)):
        copies.append(pltpu.make_async_copy(ref.at[1 - y], out.at[m], sem.at[m]))
    for copy in copies:
        copy.start()
    for copy in copies:
        copy.wait()


def rows_kernel(place_ref, orb, b1, b2, b3, came, left, right, res, sem):
    z, y = place_ref[1] >> 1, place_ref[1] & 1
    copies = [pltpu.make_async_copy(orb.at[z, y], res.at[2 * z + y], sem.at[0, 0])]
    for m, ref in ((1, b1), (2, b2), (3, b3)):
        copies.append(pltpu.make_async_copy(ref.at[y], res.at[2 * (z ^ m) + y], sem.at[0, m]))
    for m in range(4):
        copies.append(pltpu.make_async_copy(came.at[m], res.at[2 * (z ^ m) + 1 - y], sem.at[1, m]))
    for copy in copies:
        copy.start()
    for copy in copies:
        copy.wait()
    for k in range(4):
        left[:, k * 256 : (k + 1) * 256] = res[k]
        right[:, k * 256 : (k + 1) * 256] = res[4 + k]


def origin(place_ref, crossed, first, second, m):
    rep, bulk = place_ref[0], place_ref[1]
    core = (rep & 1) ^ crossed
    dx = jnp.where(core == 0, first, second)
    dy = jnp.where(core == 0, second, first)
    return rep ^ (2 * dx + crossed), bulk ^ (2 * m + dy), dx


def pieces(crossed):
    found = []
    for second in range(2):
        for first in range(2):
            for m in range(4):
                found.append((2 * second + first, m, (crossed, first, second, m)))
    return found


def offset(index, size):
    return pl.ds(pl.multiple_of(index * size, size), size)


def first_kernel(place_ref, pair, other_pair, *refs):
    bufs, (x_ref, uh_ref, ul_ref, tri, diag, sem, sem2) = refs[:8], refs[8:]
    copies = []
    for crossed in range(2):
        for buf, entry, args in pieces(crossed):
            rep, bulk, dx = origin(place_ref, *args)
            src = bufs[4 * crossed + buf]
            copies.append(
                pltpu.make_async_copy(
                    src.at[entry, pl.ds(0, 256), :],
                    tri.at[offset(rep, 256), offset(bulk, 128)],
                    sem.at[crossed, buf, entry],
                )
            )
            if not crossed:
                copies.append(
                    pltpu.make_async_copy(src.at[entry, pl.ds(256, 8), :], diag.at[dx, bulk], sem2.at[buf, entry])
                )
    for copy in copies:
        copy.start()
    for copy in copies:
        copy.wait()

    n = 128
    i, j = iotas(n)
    lower, upper, eye = i > j, i < j, i == j

    def low_block(k):
        block = tri[k * n : (k + 1) * n, k * n : (k + 1) * n]
        return jnp.where(lower, block, 0.0) + jnp.where(eye, diag[0, k, 0:1, :], 0.0)

    def up_block(k):
        block = tri[k * n : (k + 1) * n, k * n : (k + 1) * n]
        return jnp.where(upper, block, 0.0) + jnp.where(eye, diag[0, k, 1:2, :], 0.0)

    zero = jnp.zeros((n, n), F32)
    lows = []
    for k in range(4):
        ta, tb = low_block(2 * k), low_block(2 * k + 1)
        lba = tri[k * 256 + 128 : k * 256 + 256, k * 256 : k * 256 + 128]
        off = -mul3(mul3(tb, lba), ta)
        lows.append(
            jnp.concatenate(
                [jnp.concatenate([ta, zero], axis=1), jnp.concatenate([off, tb], axis=1)], axis=0
            )
        )
    ups = []
    for k in range(4):
        ta, tb = up_block(2 * k), up_block(2 * k + 1)
        uab = tri[k * 256 : k * 256 + 128, k * 256 + 128 : k * 256 + 256]
        off = -mul3(mul3(ta, uab), tb)
        ups.append(
            jnp.concatenate(
                [jnp.concatenate([ta, off], axis=1), jnp.concatenate([zero, tb], axis=1)], axis=0
            )
        )

    rest = jnp.concatenate([pair[0], pair[1], other_pair[0], other_pair[1]], axis=0)
    for k in range(4):
        x = mul(rest[:, :256], split(lows[k]), NT)
        x_ref[:, k * 256 : (k + 1) * 256] = x
        if k < 3:
            later = tri[(k + 1) * 256 :, k * 256 : (k + 1) * 256]
            rest = rest[:, 256:] - mul(x, split(later), NT)

    def put(r, c, value):
        h, l = split(value)
        uh_ref[r * 256 : r * 256 + value.shape[0], c * 256 : c * 256 + value.shape[1]] = h
        ul_ref[r * 256 : r * 256 + value.shape[0], c * 256 : c * 256 + value.shape[1]] = l

    for k in range(2):
        ta, tb = ups[2 * k], ups[2 * k + 1]
        uab = tri[k * 512 : k * 512 + 256, k * 512 + 256 : k * 512 + 512]
        put(2 * k, 2 * k, ta)
        put(2 * k + 1, 2 * k + 1, tb)
        put(2 * k, 2 * k + 1, -mul3(mul3(ta, uab), tb))
        put(2 * k + 1, 2 * k, jnp.zeros((256, 256), F32))
    put(0, 2, tri[0:512, 512:1024])


def update_kernel(place_ref, x_ref, *refs):
    held, outs, (coup, sem) = refs[:8], refs[8:12], refs[12:]
    bulk = place_ref[1]
    copies = []
    for dy in range(2):
        for m in range(4):
            dst = coup.at[:, offset(bulk ^ (2 * m + dy), 128)]
            copies.append(pltpu.make_async_copy(held[4 * dy + m], dst, sem.at[dy, m]))
    for copy in copies:
        copy.start()
    x = x_ref[...]
    for copy in copies:
        copy.wait()
    upd = mul(x, split(coup[...]), NT)
    for k, out in enumerate(outs):
        out[...] = upd[32 * k : 32 * (k + 1)]


def second_kernel(place_ref, x_ref, rest_ref, uh_ref, ul_ref, mine, from_x, from_core, from_both, out_ref):
    x = x_ref[0:32, :]
    out_ref[:, 0:1024] = x
    parts = []
    for k in range(4):
        way = place_ref[0] ^ k
        upd = jnp.where(
            way == 0,
            mine[...],
            jnp.where(way == 2, from_x[...], jnp.where(way == 1, from_core[...], from_both[...])),
        )
        parts.append(rest_ref[:, k * 256 : (k + 1) * 256] - upd)
    ra = jnp.concatenate(parts[:2], axis=1)
    rb = jnp.concatenate(parts[2:], axis=1)

    def u(r, c):
        rows, cols = slice(r * 512, r * 512 + 512), slice(c * 512, c * 512 + 512)
        return uh_ref[rows, cols], ul_ref[rows, cols]

    xa = mul(ra, u(0, 0))
    xb = mul(rb - mul(xa, u(0, 1)), u(1, 1))
    out_ref[:, 1024:1536] = xa
    out_ref[:, 1536:2048] = xb


BOTH = ("bulk", "rep")

SPREAD, INVERT, LEAVE, ROWS = 1_000_000_000, 3_500_000_000, 500_000_000, 1_000_000_000


def swap_z(x, m):
    return lax.ppermute(x, "bulk", [(k, k ^ (2 * m)) for k in range(8)])


def swap_y(x):
    return lax.ppermute(x, "bulk", [(k, k ^ 1) for k in range(8)])


def swap_rep(x, bits):
    return lax.ppermute(x, "rep", [(k, k ^ bits) for k in range(4)])


def cross(x, stage):
    pairs = []
    for rep in range(4):
        for bulk in range(8):
            to = (rep ^ 2, bulk) if (rep & 1) == stage else (rep, bulk ^ 1)
            pairs.append((bulk * 4 + rep, to[1] * 4 + to[0]))
    return lax.ppermute(x, BOTH, pairs)


def after(x, *deps):
    return lax.optimization_barrier((x,) + deps)[0]


ANY = pl.BlockSpec(memory_space=pl.ANY)
VMEM = pl.BlockSpec(memory_space=pltpu.VMEM)
SMEM = pl.BlockSpec(memory_space=pltpu.SMEM)


def call(kernel, out, specs, outs, scratch, flops, size, name):
    return pl.pallas_call(
        kernel,
        out_shape=out,
        in_specs=specs,
        out_specs=outs,
        scratch_shapes=scratch,
        compiler_params=pltpu.CompilerParams(vmem_limit_bytes=size << 20),
        cost_estimate=pl.CostEstimate(flops=flops, bytes_accessed=2 << 20, transcendentals=0),
        name=name,
    )


def shape(*dims, dtype=F32):
    return jax.ShapeDtypeStruct(dims, dtype)


def dmas(*dims):
    return pltpu.SemaphoreType.DMA(dims)


def per_device(orbitals, triangles, coupling, diagonals):
    rep, bulk = lax.axis_index("rep"), lax.axis_index("bulk")
    place = jnp.stack([rep, bulk]).astype(jnp.int32)
    blocks = orbitals.reshape(4, 2, 32, 256)

    b_out = call(
        spread_kernel, [shape(2, 32, 256)] * 3, [SMEM, ANY], [VMEM] * 3, [dmas(4)], SPREAD, 60, "spread"
    )(place, blocks)
    b_z = [swap_z(b, m + 1) for m, b in enumerate(b_out)]
    c_stay, c_came = [coupling], [swap_y(coupling)]

    t = call(
        invert_kernel,
        shape(264, 128),
        [SMEM, ANY, ANY],
        VMEM,
        [pltpu.VMEM((2, 128), F32), dmas(2)],
        INVERT,
        60,
        "invert",
    )(place, triangles, diagonals)
    t = after(t, *b_z)

    tz = [swap_z(t, m) for m in range(1, 4)]
    leave = call(
        leave_kernel, shape(4, 32, 256), [SMEM] + [ANY] * 4, VMEM, [dmas(4)], LEAVE, 4, "leave"
    )(place, blocks, *b_z)
    came = swap_y(leave)

    held = jnp.stack([t] + tz)
    c_stay += [swap_z(after(coupling, held), m) for m in range(1, 4)]
    held_now = after(held, came, *c_came)
    got0 = cross(held_now, 0)
    got1 = cross(held_now, 1)
    got01 = cross(after(got0, c_stay[1], c_stay[2]), 1)
    bufs = [held, got0, got1, got01]

    c_came += [swap_y(c) for c in c_stay[1:]]

    left, right = call(
        rows_kernel,
        [shape(32, 1024)] * 2,
        [SMEM] + [ANY] * 5,
        [VMEM] * 2,
        [pltpu.VMEM((8, 32, 256), F32), dmas(2, 4)],
        ROWS,
        4,
        "rows",
    )(place, blocks, *b_z, came)
    left = after(left, *[c_stay[2]])
    pair = jnp.stack([left, swap_rep(left, 2)])
    other_pair = swap_rep(pair, 1)
    swaps = [swap_rep(b, 1) for b in bufs[:3]] + [swap_rep(after(got01, pair, c_came[1], c_stay[3]), 1)]

    x, uh, ul = call(
        first_kernel,
        [shape(128, 1024)] + [shape(1024, 1024, dtype=BF16)] * 2,
        [SMEM, VMEM, VMEM] + [ANY] * 8,
        [VMEM] * 3,
        [pltpu.VMEM((1024, 1024), F32), pltpu.VMEM((2, 8, 8, 128), F32), dmas(2, 4, 4), dmas(4, 4)],
        5_000_000_000,
        32,
        "first_panel",
    )(place, pair, other_pair, *bufs, *swaps)

    mine, to_x, to_core, to_both = call(
        update_kernel,
        [shape(32, 256)] * 4,
        [SMEM, VMEM] + [ANY] * 8,
        [VMEM] * 4,
        [pltpu.VMEM((256, 1024), F32), dmas(2, 4)],
        2_000_000_000,
        32,
        "update",
    )(place, x, *c_stay, *c_came)
    back = [swap_rep(to_x, 2), swap_rep(to_core, 1), swap_rep(to_both, 3)]

    return call(
        second_kernel,
        shape(32, 2048),
        [SMEM] + [VMEM] * 8,
        VMEM,
        [],
        2_500_000_000,
        32,
        "second_panel",
    )(place, x, right, uh, ul, mine, *back)


def solution(mesh):
    special = mesh.shape["bulk"] == 8 and mesh.shape["rep"] == 4

    def run(orbitals, triangles, coupling, diagonals):
        fits = orbitals.shape == (1024, 2048) and triangles.shape == (1024, 1024)
        body = per_device if special and fits else per_device_any
        return jax.shard_map(
            body,
            mesh=mesh,
            in_specs=(P("rep", "bulk"), P("rep", "bulk"), P("rep", "bulk"), P(None, "bulk")),
            out_specs=P(("rep", "bulk"), None),
            check_vma=False,
        )(orbitals, triangles, coupling, diagonals)

    return run
```

```python
import jax
import jax.numpy as jnp
from jax import lax
from jax.experimental import pallas as pl
from jax.experimental.pallas import tpu as pltpu
from jax.sharding import PartitionSpec as P

F32 = jnp.float32
BF16 = jnp.bfloat16
NN = (((1,), (0,)), ((), ()))
NT = (((1,), (1,)), ((), ()))


def unpack(triangles, diagonals):
    first_block = jnp.tril(triangles, -1) + jnp.diag(diagonals[0])
    second_block = jnp.tril(triangles.T, -1) + jnp.diag(diagonals[1])
    return (first_block, second_block)


def per_device_any(orbitals, triangles, coupling, diagonals):
    tri_rows, couple_rows = (
        lax.all_gather(triangles, "rep", axis=0, tiled=True),
        lax.all_gather(coupling, "rep", axis=0, tiled=True),
    )
    tri_whole, couple_whole, diag_whole = (
        lax.all_gather(tri_rows, "bulk", axis=1, tiled=True),
        lax.all_gather(couple_rows, "bulk", axis=1, tiled=True),
        lax.all_gather(diagonals, "bulk", axis=1, tiled=True),
    )
    first_block, second_block = unpack(tri_whole, diag_whole)
    panel = first_block.shape[0]
    groups = lax.axis_size("bulk")
    local_rows = orbitals.shape[0] // groups
    blocks = orbitals.reshape(groups, local_rows, orbitals.shape[1])
    received = lax.all_to_all(blocks, "bulk", split_axis=0, concat_axis=2, tiled=True)
    rows_now = received.reshape(local_rows, received.shape[2])
    left_part = rows_now[:, :panel]
    right_part = rows_now[:, panel:]
    solved_one = jax.scipy.linalg.solve_triangular(first_block, left_part.T, lower=True).T
    update = jnp.dot(
        solved_one,
        couple_whole.T,
        precision=lax.Precision.HIGHEST,
        preferred_element_type=jnp.float32,
    )
    solved_two = jax.scipy.linalg.solve_triangular(
        second_block, (right_part - update).T, lower=True
    ).T
    return jnp.concatenate([solved_one, solved_two], axis=1)


def dot(a, b, dims=NN):
    return lax.dot_general(a, b, dims, preferred_element_type=F32)


def dot_exact(a, b):
    return lax.dot_general(a, b, NN, precision=lax.Precision.HIGHEST, preferred_element_type=F32)


def split(x):
    high = x.astype(BF16)
    return high, (x - high.astype(F32)).astype(BF16)


def mul(x, b, dims=NN):
    xh, xl = split(x)
    bh, bl = b
    m = x.shape[0]
    both = dot(jnp.concatenate([xh, xl], axis=0), bh, dims)
    return (both[:m] + both[m:]) + dot(xh, bl, dims)


def mul3(a, b):
    (ah, al), (bh, bl) = split(a), split(b)
    return dot(ah, bh) + (dot(al, bh) + dot(ah, bl))


def iotas(n):
    return lax.broadcasted_iota(jnp.int32, (n, n), 0), lax.broadcasted_iota(jnp.int32, (n, n), 1)


def invert_kernel(place_ref, tri_ref, diag_ref, t_ref):
    rep, bulk = place_ref[0], place_ref[1]
    rows, n = tri_ref.shape
    inv = 1.0 / diag_ref[...]
    t_ref[0:rows, :] = tri_ref[...]
    t_ref[rows : rows + 8, :] = jnp.concatenate([inv, jnp.zeros((6, n), F32)], axis=0)

    @pl.when(rep == bulk // 2)
    def _():
        start = pl.multiple_of((bulk % 2) * n, n)
        block = tri_ref[pl.ds(start, n), :]
        i, j = iotas(n)
        eye = i == j
        ans = []
        for which in range(2):
            row, col = (i, j) if which == 0 else (j, i)
            along = inv[which : which + 1, :]
            d = jnp.where(eye, along, 0.0)
            down = jnp.sum(d, axis=1, keepdims=True)
            part = (row >> 1 == col >> 1) & (row > col)
            ans.append(d - jnp.where(part, block * along * down, 0.0))
        level = 1
        while (1 << level) < n:
            for which in range(2):
                row, col = (i, j) if which == 0 else (j, i)
                part = (row >> (level + 1) == col >> (level + 1)) & (row >> level > col >> level)
                t = ans[which]
                ans[which] = t - mul3(mul3(t, jnp.where(part, block, 0.0)), t)
            level += 1
        t_ref[pl.ds(start, n), :] = jnp.where(i >= j, ans[0], ans[1])


def spread_kernel(place_ref, orb, b1, b2, b3):
    z = place_ref[1] >> 1
    for m, ref in ((1, b1), (2, b2), (3, b3)):
        ref[...] = orb[z ^ m]


def leave_kernel(place_ref, orb, b1, b2, b3, out):
    z, y = place_ref[1] >> 1, place_ref[1] & 1
    out[0] = orb[z, 1 - y]
    for m, ref in ((1, b1), (2, b2), (3, b3)):
        out[m] = ref[1 - y]


def rows_kernel(place_ref, orb, b1, b2, b3, came, left, both):
    z, y = place_ref[1] >> 1, place_ref[1] & 1

    def put(m, dy, value):
        k = 2 * (z ^ m) + (y ^ dy)
        both[k >> 2, :, pl.ds(pl.multiple_of((k & 3) * 256, 256), 256)] = value

    put(0, 0, orb[z, y])
    for m, ref in ((1, b1), (2, b2), (3, b3)):
        put(m, 0, ref[y])
    for m in range(4):
        put(m, 1, came[m])
    left[...] = both[0]


def origin(place_ref, crossed, first, second, m):
    rep, bulk = place_ref[0], place_ref[1]
    core = (rep & 1) ^ crossed
    dx = jnp.where(core == 0, first, second)
    dy = jnp.where(core == 0, second, first)
    return rep ^ (2 * dx + crossed), bulk ^ (2 * m + dy)


def pieces(bufs):
    found = []
    for crossed in range(2):
        for second in range(2):
            for first in range(2):
                for m in range(4):
                    found.append((bufs[4 * crossed + 2 * second + first].at[m], (crossed, first, second, m)))
    return found


def offset(index, size):
    return pl.ds(pl.multiple_of(index * size, size), size)


def place_pieces(place_ref, bufs, upper, high, low, diag):
    for piece, args in pieces(bufs):
        rep, bulk = origin(place_ref, *args)

        @pl.when((rep <= bulk // 2) if upper else (rep >= bulk // 2))
        def _():
            h, l = split(piece[0:256, :])
            high[offset(rep, 256), offset(bulk, 128)] = h
            low[offset(rep, 256), offset(bulk, 128)] = l

        @pl.when(rep == bulk // 2)
        def _():
            diag[bulk, 0:128, :] = piece[pl.ds(pl.multiple_of((bulk % 2) * 128, 128), 128), :]
            diag[bulk, 128:136, :] = piece[256:264, :]


def mul_pairs(a, b):
    (ah, al), (bh, bl) = a, b
    return dot(ah, bh) + (dot(al, bh) + dot(ah, bl))


def pair_of(high, low, r, c, size):
    rows, cols = slice(r, r + size), slice(c, c + size)
    return high[rows, cols], low[rows, cols]


def join(a, b, c, d):
    return jnp.concatenate([jnp.concatenate([a, b], axis=1), jnp.concatenate([c, d], axis=1)], axis=0)


def first_kernel(place_ref, pair, other_pair, *refs):
    bufs, (x_ref, high, low, diag) = refs[:8], refs[8:]
    place_pieces(place_ref, bufs, False, high, low, diag)
    n = 128
    i, j = iotas(n)

    def block(k):
        return jnp.where(i > j, diag[k, 0:n, :], 0.0) + jnp.where(i == j, diag[k, n : n + 1, :], 0.0)

    zero = jnp.zeros((n, n), F32)
    inverses = []
    for k in range(4):
        ta, tb = block(2 * k), block(2 * k + 1)
        pa, pb = split(ta), split(tb)
        off = -mul_pairs(split(mul_pairs(pb, pair_of(high, low, 256 * k + n, 256 * k, n))), pa)
        inverses.append(split(join(ta, zero, off, tb)))

    rest = jnp.concatenate([pair[0], pair[1], other_pair[0], other_pair[1]], axis=0)
    for k in range(4):
        x = mul(rest[:, :256], inverses[k], NT)
        x_ref[:, k * 256 : (k + 1) * 256] = x
        if k < 3:
            rows, cols = slice((k + 1) * 256, 1024), slice(k * 256, (k + 1) * 256)
            rest = rest[:, 256:] - mul(x, (high[rows, cols], low[rows, cols]), NT)


def update_kernel(place_ref, x_ref, *refs):
    held, outs, (high, low) = refs[:8], refs[8:12], refs[12:]
    bulk = place_ref[1]
    for dy in range(2):
        for m in range(4):
            h, l = split(held[4 * dy + m][...])
            high[:, offset(bulk ^ (2 * m + dy), 128)] = h
            low[:, offset(bulk ^ (2 * m + dy), 128)] = l
    upd = mul(x_ref[...], (high[...], low[...]), NT)
    for k, out in enumerate(outs):
        out[...] = upd[32 * k : 32 * (k + 1)]


def second_factor_kernel(place_ref, *refs):
    bufs, (high, low, diag) = refs[:8], refs[8:]
    place_pieces(place_ref, bufs, True, high, low, diag)
    n = 128
    i, j = iotas(n)

    def block(k):
        return jnp.where(i < j, diag[k, 0:n, :], 0.0) + jnp.where(i == j, diag[k, n + 1 : n + 2, :], 0.0)

    zero = jnp.zeros((n, n), F32)
    inverses = []
    for k in range(4):
        ta, tb = block(2 * k), block(2 * k + 1)
        pa, pb = split(ta), split(tb)
        off = -mul_pairs(split(mul_pairs(pa, pair_of(high, low, 256 * k, 256 * k + n, n))), pb)
        inverses.append(split(join(ta, off, zero, tb)))

    def put(r, c, value):
        high[r : r + 256, c : c + 256], low[r : r + 256, c : c + 256] = value

    for k in range(2):
        at = 512 * k
        pa, pb = inverses[2 * k], inverses[2 * k + 1]
        off = -mul_pairs(split(mul_pairs(pa, pair_of(high, low, at, at + 256, 256))), pb)
        put(at, at, pa)
        put(at + 256, at + 256, pb)
        put(at, at + 256, split(off))
        put(at + 256, at, (jnp.zeros((256, 256), BF16),) * 2)


def second_kernel(place_ref, x_ref, both_ref, uh_ref, ul_ref, mine, from_x, from_core, from_both, out_ref):
    x = x_ref[0:32, :]
    out_ref[:, 0:1024] = x
    parts = []
    for k in range(4):
        way = place_ref[0] ^ k
        upd = jnp.where(
            way == 0,
            mine[...],
            jnp.where(way == 2, from_x[...], jnp.where(way == 1, from_core[...], from_both[...])),
        )
        parts.append(both_ref[1, :, k * 256 : (k + 1) * 256] - upd)
    ra = jnp.concatenate(parts[:2], axis=1)
    rb = jnp.concatenate(parts[2:], axis=1)

    def u(r, c):
        rows, cols = slice(r * 512, r * 512 + 512), slice(c * 512, c * 512 + 512)
        return uh_ref[rows, cols], ul_ref[rows, cols]

    xa = mul(ra, u(0, 0))
    xb = mul(rb - mul(xa, u(0, 1)), u(1, 1))
    out_ref[:, 1024:1536] = xa
    out_ref[:, 1536:2048] = xb


BOTH = ("bulk", "rep")

SPREAD, INVERT, LEAVE, ROWS, FIRST, SECOND = 1_000_000_000, 3_500_000_000, 500_000_000, 1_000_000_000, 4_000_000_000, 3_000_000_000


def swap_z(x, m):
    return lax.ppermute(x, "bulk", [(k, k ^ (2 * m)) for k in range(8)])


def swap_y(x):
    return lax.ppermute(x, "bulk", [(k, k ^ 1) for k in range(8)])


def swap_rep(x, bits):
    return lax.ppermute(x, "rep", [(k, k ^ bits) for k in range(4)])


def cross(x, stage):
    pairs = []
    for rep in range(4):
        for bulk in range(8):
            to = (rep ^ 2, bulk) if (rep & 1) == stage else (rep, bulk ^ 1)
            pairs.append((bulk * 4 + rep, to[1] * 4 + to[0]))
    return lax.ppermute(x, BOTH, pairs)


def after(x, *deps):
    return lax.optimization_barrier((x,) + deps)[0]


ANY = pl.BlockSpec(memory_space=pl.ANY)
VMEM = pl.BlockSpec(memory_space=pltpu.VMEM)
SMEM = pl.BlockSpec(memory_space=pltpu.SMEM)


def call(kernel, out, specs, outs, scratch, flops, size, name):
    return pl.pallas_call(
        kernel,
        out_shape=out,
        in_specs=specs,
        out_specs=outs,
        scratch_shapes=scratch,
        compiler_params=pltpu.CompilerParams(vmem_limit_bytes=size << 20),
        cost_estimate=pl.CostEstimate(flops=flops, bytes_accessed=2 << 20, transcendentals=0),
        name=name,
    )


def shape(*dims, dtype=F32):
    return jax.ShapeDtypeStruct(dims, dtype)


def per_device(orbitals, triangles, coupling, diagonals):
    rep, bulk = lax.axis_index("rep"), lax.axis_index("bulk")
    place = jnp.stack([rep, bulk]).astype(jnp.int32)
    blocks = orbitals.reshape(4, 2, 32, 256)

    b_out = call(spread_kernel, [shape(2, 32, 256)] * 3, [SMEM, VMEM], [VMEM] * 3, [], SPREAD, 4, "spread")(
        place, blocks
    )
    b_z = [swap_z(b, m + 1) for m, b in enumerate(b_out)]
    c_stay, c_came = [coupling, swap_z(coupling, 1)], [swap_y(coupling)]

    t = call(invert_kernel, shape(264, 128), [SMEM, VMEM, VMEM], VMEM, [], INVERT, 4, "invert")(
        place, triangles, diagonals
    )
    t = after(t, c_came[0], c_stay[1], *b_z)

    tz = [swap_z(t, m) for m in range(1, 4)]
    leave = call(leave_kernel, shape(4, 32, 256), [SMEM] + [VMEM] * 4, VMEM, [], LEAVE, 4, "leave")(
        place, blocks, *b_z
    )
    came = swap_y(leave)
    c_came.append(swap_y(c_stay[1]))

    held = jnp.stack([t] + tz)
    c_stay += [swap_z(after(coupling, held), m) for m in range(2, 4)]
    held_now = after(held, came, c_came[1])
    got0 = cross(held_now, 0)
    got1 = cross(held_now, 1)
    got01 = cross(after(got0, c_stay[2]), 1)
    bufs = [held, got0, got1, got01]
    c_came += [swap_y(c) for c in c_stay[2:]]

    left, both = call(
        rows_kernel,
        [shape(32, 1024), shape(2, 32, 1024)],
        [SMEM] + [VMEM] * 5,
        [VMEM] * 2,
        [],
        ROWS,
        4,
        "rows",
    )(place, blocks, *b_z, came)
    left = after(left, c_stay[2])
    pair = jnp.stack([left, swap_rep(left, 2)])
    other_pair = swap_rep(pair, 1)
    bufs += [swap_rep(b, 1) for b in bufs[:3]] + [swap_rep(after(got01, pair, c_stay[3]), 1)]

    scratch = [pltpu.VMEM((8, 136, 128), F32)]
    halves = [shape(1024, 1024, dtype=BF16)] * 2
    x = call(
        first_kernel,
        shape(128, 1024),
        [SMEM] + [VMEM] * 10,
        VMEM,
        [pltpu.VMEM((1024, 1024), BF16)] * 2 + scratch,
        FIRST,
        24,
        "first_panel",
    )(place, pair, other_pair, *bufs)

    mine, to_x, to_core, to_both = call(
        update_kernel,
        [shape(32, 256)] * 4,
        [SMEM] + [VMEM] * 9,
        [VMEM] * 4,
        [pltpu.VMEM((256, 1024), BF16)] * 2,
        2_000_000_000,
        24,
        "update",
    )(place, x, *c_stay, *c_came)
    back = [swap_rep(to_x, 2), swap_rep(to_core, 1), swap_rep(to_both, 3)]

    uh, ul = call(
        second_factor_kernel, halves, [SMEM] + [VMEM] * 8, [VMEM] * 2, scratch, SECOND, 24, "second_factor"
    )(after(place, mine), *bufs)

    return call(second_kernel, shape(32, 2048), [SMEM] + [VMEM] * 8, VMEM, [], 2_500_000_000, 24, "second_panel")(
        place, x, both, uh, ul, mine, *back
    )


def solution(mesh):
    special = mesh.shape["bulk"] == 8 and mesh.shape["rep"] == 4

    def run(orbitals, triangles, coupling, diagonals):
        fits = orbitals.shape == (1024, 2048) and triangles.shape == (1024, 1024)
        body = per_device if special and fits else per_device_any
        return jax.shard_map(
            body,
            mesh=mesh,
            in_specs=(P("rep", "bulk"), P("rep", "bulk"), P("rep", "bulk"), P(None, "bulk")),
            out_specs=P(("rep", "bulk"), None),
            check_vma=False,
        )(orbitals, triangles, coupling, diagonals)

    return run
```

```python
import jax
import jax.numpy as jnp
from jax import lax
from jax.experimental import pallas as pl
from jax.experimental.pallas import tpu as pltpu
from jax.sharding import PartitionSpec as P

F32 = jnp.float32
BF16 = jnp.bfloat16
NN = (((1,), (0,)), ((), ()))
NT = (((1,), (1,)), ((), ()))


def unpack(triangles, diagonals):
    first_block = jnp.tril(triangles, -1) + jnp.diag(diagonals[0])
    second_block = jnp.tril(triangles.T, -1) + jnp.diag(diagonals[1])
    return (first_block, second_block)


def per_device_any(orbitals, triangles, coupling, diagonals):
    tri_rows, couple_rows = (
        lax.all_gather(triangles, "rep", axis=0, tiled=True),
        lax.all_gather(coupling, "rep", axis=0, tiled=True),
    )
    tri_whole, couple_whole, diag_whole = (
        lax.all_gather(tri_rows, "bulk", axis=1, tiled=True),
        lax.all_gather(couple_rows, "bulk", axis=1, tiled=True),
        lax.all_gather(diagonals, "bulk", axis=1, tiled=True),
    )
    first_block, second_block = unpack(tri_whole, diag_whole)
    panel = first_block.shape[0]
    groups = lax.axis_size("bulk")
    local_rows = orbitals.shape[0] // groups
    blocks = orbitals.reshape(groups, local_rows, orbitals.shape[1])
    received = lax.all_to_all(blocks, "bulk", split_axis=0, concat_axis=2, tiled=True)
    rows_now = received.reshape(local_rows, received.shape[2])
    left_part = rows_now[:, :panel]
    right_part = rows_now[:, panel:]
    solved_one = jax.scipy.linalg.solve_triangular(first_block, left_part.T, lower=True).T
    update = jnp.dot(
        solved_one,
        couple_whole.T,
        precision=lax.Precision.HIGHEST,
        preferred_element_type=jnp.float32,
    )
    solved_two = jax.scipy.linalg.solve_triangular(
        second_block, (right_part - update).T, lower=True
    ).T
    return jnp.concatenate([solved_one, solved_two], axis=1)


def dot(a, b, dims=NN):
    return lax.dot_general(a, b, dims, preferred_element_type=F32)


def dot_exact(a, b):
    return lax.dot_general(a, b, NN, precision=lax.Precision.HIGHEST, preferred_element_type=F32)


def split(x):
    high = x.astype(BF16)
    return high, (x - high.astype(F32)).astype(BF16)


def mul(x, b, dims=NN):
    xh, xl = split(x)
    bh, bl = b
    m = x.shape[0]
    both = dot(jnp.concatenate([xh, xl], axis=0), bh, dims)
    return (both[:m] + both[m:]) + dot(xh, bl, dims)


def mul3(a, b):
    (ah, al), (bh, bl) = split(a), split(b)
    return dot(ah, bh) + (dot(al, bh) + dot(ah, bl))


def iotas(n):
    return lax.broadcasted_iota(jnp.int32, (n, n), 0), lax.broadcasted_iota(jnp.int32, (n, n), 1)


def invert_kernel(place_ref, tri_ref, diag_ref, t_ref):
    rep, bulk = place_ref[0], place_ref[1]
    rows, n = tri_ref.shape
    inv = 1.0 / diag_ref[...]
    t_ref[0:rows, :] = tri_ref[...]
    t_ref[rows : rows + 8, :] = jnp.concatenate([inv, jnp.zeros((6, n), F32)], axis=0)

    @pl.when(rep == bulk // 2)
    def _():
        start = pl.multiple_of((bulk % 2) * n, n)
        block = tri_ref[pl.ds(start, n), :]
        i, j = iotas(n)
        eye = i == j
        ans = []
        for which in range(2):
            row, col = (i, j) if which == 0 else (j, i)
            along = inv[which : which + 1, :]
            d = jnp.where(eye, along, 0.0)
            down = jnp.sum(d, axis=1, keepdims=True)
            part = (row >> 1 == col >> 1) & (row > col)
            ans.append(d - jnp.where(part, block * along * down, 0.0))
        level = 1
        while (1 << level) < n:
            for which in range(2):
                row, col = (i, j) if which == 0 else (j, i)
                part = (row >> (level + 1) == col >> (level + 1)) & (row >> level > col >> level)
                t = ans[which]
                ans[which] = t - mul3(mul3(t, jnp.where(part, block, 0.0)), t)
            level += 1
        t_ref[pl.ds(start, n), :] = jnp.where(i >= j, ans[0], ans[1])


def leave_kernel(place_ref, orb, out):
    y = place_ref[1] & 1
    for k in range(4):
        out[k] = orb[k, 1 - y]


def spread_kernel(place_ref, orb, came, b1, b2, b3):
    z, y = place_ref[1] >> 1, place_ref[1] & 1
    for m, ref in ((1, b1), (2, b2), (3, b3)):
        ref[0] = orb[z ^ m, y]
        ref[1] = came[z ^ m]


def rows_kernel(place_ref, orb, came, b1, b2, b3, left, both):
    z, y = place_ref[1] >> 1, place_ref[1] & 1

    def put(m, dy, value):
        k = 2 * (z ^ m) + (y ^ dy)
        both[k >> 2, :, pl.ds(pl.multiple_of((k & 3) * 256, 256), 256)] = value

    put(0, 0, orb[z, y])
    put(0, 1, came[z])
    for m, ref in ((1, b1), (2, b2), (3, b3)):
        put(m, 0, ref[0])
        put(m, 1, ref[1])
    left[...] = both[0]


def origin(place_ref, crossed, first, second, m):
    rep, bulk = place_ref[0], place_ref[1]
    core = (rep & 1) ^ crossed
    dx = jnp.where(core == 0, first, second)
    dy = jnp.where(core == 0, second, first)
    return rep ^ (2 * dx + crossed), bulk ^ (2 * m + dy)


def pieces(bufs):
    found = []
    for crossed in range(2):
        for second in range(2):
            for first in range(2):
                for m in range(4):
                    found.append((bufs[4 * crossed + 2 * second + first].at[m], (crossed, first, second, m)))
    return found


def offset(index, size):
    return pl.ds(pl.multiple_of(index * size, size), size)


def place_pieces(place_ref, bufs, upper, high, low, diag):
    for piece, args in pieces(bufs):
        rep, bulk = origin(place_ref, *args)

        @pl.when((rep <= bulk // 2) if upper else (rep >= bulk // 2))
        def _():
            h, l = split(piece[0:256, :])
            high[offset(rep, 256), offset(bulk, 128)] = h
            low[offset(rep, 256), offset(bulk, 128)] = l

        @pl.when(rep == bulk // 2)
        def _():
            diag[bulk, 0:128, :] = piece[pl.ds(pl.multiple_of((bulk % 2) * 128, 128), 128), :]
            diag[bulk, 128:136, :] = piece[256:264, :]


def mul_pairs(a, b):
    (ah, al), (bh, bl) = a, b
    return dot(ah, bh) + (dot(al, bh) + dot(ah, bl))


def pair_of(high, low, r, c, size):
    rows, cols = slice(r, r + size), slice(c, c + size)
    return high[rows, cols], low[rows, cols]


def join(a, b, c, d):
    return jnp.concatenate([jnp.concatenate([a, b], axis=1), jnp.concatenate([c, d], axis=1)], axis=0)


def first_kernel(place_ref, pair, other_pair, *refs):
    bufs, (x_ref, high, low, diag) = refs[:8], refs[8:]
    place_pieces(place_ref, bufs, False, high, low, diag)
    n = 128
    i, j = iotas(n)

    def block(k):
        return jnp.where(i > j, diag[k, 0:n, :], 0.0) + jnp.where(i == j, diag[k, n : n + 1, :], 0.0)

    zero = jnp.zeros((n, n), F32)
    inverses = []
    for k in range(4):
        ta, tb = block(2 * k), block(2 * k + 1)
        pa, pb = split(ta), split(tb)
        off = -mul_pairs(split(mul_pairs(pb, pair_of(high, low, 256 * k + n, 256 * k, n))), pa)
        inverses.append(split(join(ta, zero, off, tb)))

    rest = jnp.concatenate([pair[0], pair[1], other_pair[0], other_pair[1]], axis=0)
    for k in range(4):
        x = mul(rest[:, :256], inverses[k], NT)
        x_ref[:, k * 256 : (k + 1) * 256] = x
        if k < 3:
            rows, cols = slice((k + 1) * 256, 1024), slice(k * 256, (k + 1) * 256)
            rest = rest[:, 256:] - mul(x, (high[rows, cols], low[rows, cols]), NT)


def update_kernel(place_ref, x_ref, *refs):
    held, outs, (high, low) = refs[:8], refs[8:12], refs[12:]
    bulk = place_ref[1]
    for dy in range(2):
        for m in range(4):
            h, l = split(held[4 * dy + m][...])
            high[:, offset(bulk ^ (2 * m + dy), 128)] = h
            low[:, offset(bulk ^ (2 * m + dy), 128)] = l
    upd = mul(x_ref[...], (high[...], low[...]), NT)
    for k, out in enumerate(outs):
        out[...] = upd[32 * k : 32 * (k + 1)]


def second_factor_kernel(place_ref, *refs):
    bufs, (high, low, diag) = refs[:8], refs[8:]
    place_pieces(place_ref, bufs, True, high, low, diag)
    n = 128
    i, j = iotas(n)

    def block(k):
        return jnp.where(i < j, diag[k, 0:n, :], 0.0) + jnp.where(i == j, diag[k, n + 1 : n + 2, :], 0.0)

    zero = jnp.zeros((n, n), F32)
    inverses = []
    for k in range(4):
        ta, tb = block(2 * k), block(2 * k + 1)
        pa, pb = split(ta), split(tb)
        off = -mul_pairs(split(mul_pairs(pa, pair_of(high, low, 256 * k, 256 * k + n, n))), pb)
        inverses.append(split(join(ta, off, zero, tb)))

    def put(r, c, value):
        high[r : r + 256, c : c + 256], low[r : r + 256, c : c + 256] = value

    for k in range(2):
        at = 512 * k
        pa, pb = inverses[2 * k], inverses[2 * k + 1]
        off = -mul_pairs(split(mul_pairs(pa, pair_of(high, low, at, at + 256, 256))), pb)
        put(at, at, pa)
        put(at + 256, at + 256, pb)
        put(at, at + 256, split(off))
        put(at + 256, at, (jnp.zeros((256, 256), BF16),) * 2)


def second_kernel(place_ref, x_ref, both_ref, uh_ref, ul_ref, mine, from_x, from_core, from_both, out_ref):
    x = x_ref[0:32, :]
    out_ref[:, 0:1024] = x
    parts = []
    for k in range(4):
        way = place_ref[0] ^ k
        upd = jnp.where(
            way == 0,
            mine[...],
            jnp.where(way == 2, from_x[...], jnp.where(way == 1, from_core[...], from_both[...])),
        )
        parts.append(both_ref[1, :, k * 256 : (k + 1) * 256] - upd)
    ra = jnp.concatenate(parts[:2], axis=1)
    rb = jnp.concatenate(parts[2:], axis=1)

    def u(r, c):
        rows, cols = slice(r * 512, r * 512 + 512), slice(c * 512, c * 512 + 512)
        return uh_ref[rows, cols], ul_ref[rows, cols]

    xa = mul(ra, u(0, 0))
    xb = mul(rb - mul(xa, u(0, 1)), u(1, 1))
    out_ref[:, 1024:1536] = xa
    out_ref[:, 1536:2048] = xb


BOTH = ("bulk", "rep")

SPREAD, INVERT, LEAVE, ROWS, FIRST, SECOND = 1_000_000_000, 3_500_000_000, 500_000_000, 1_000_000_000, 4_000_000_000, 3_000_000_000


def swap_z(x, m):
    return lax.ppermute(x, "bulk", [(k, k ^ (2 * m)) for k in range(8)])


def swap_y(x):
    return lax.ppermute(x, "bulk", [(k, k ^ 1) for k in range(8)])


def swap_rep(x, bits):
    return lax.ppermute(x, "rep", [(k, k ^ bits) for k in range(4)])


def cross(x, stage):
    pairs = []
    for rep in range(4):
        for bulk in range(8):
            to = (rep ^ 2, bulk) if (rep & 1) == stage else (rep, bulk ^ 1)
            pairs.append((bulk * 4 + rep, to[1] * 4 + to[0]))
    return lax.ppermute(x, BOTH, pairs)


def after(x, *deps):
    return lax.optimization_barrier((x,) + deps)[0]


ANY = pl.BlockSpec(memory_space=pl.ANY)
VMEM = pl.BlockSpec(memory_space=pltpu.VMEM)
SMEM = pl.BlockSpec(memory_space=pltpu.SMEM)


def call(kernel, out, specs, outs, scratch, flops, size, name):
    return pl.pallas_call(
        kernel,
        out_shape=out,
        in_specs=specs,
        out_specs=outs,
        scratch_shapes=scratch,
        compiler_params=pltpu.CompilerParams(vmem_limit_bytes=size << 20),
        cost_estimate=pl.CostEstimate(flops=flops, bytes_accessed=2 << 20, transcendentals=0),
        name=name,
    )


def shape(*dims, dtype=F32):
    return jax.ShapeDtypeStruct(dims, dtype)


def per_device(orbitals, triangles, coupling, diagonals):
    rep, bulk = lax.axis_index("rep"), lax.axis_index("bulk")
    place = jnp.stack([rep, bulk]).astype(jnp.int32)
    blocks = orbitals.reshape(4, 2, 32, 256)

    c_stay, c_came = [coupling, swap_z(coupling, 1)], [swap_y(coupling)]
    t = call(invert_kernel, shape(264, 128), [SMEM, VMEM, VMEM], VMEM, [], INVERT, 4, "invert")(
        place, triangles, diagonals
    )
    t = after(t, c_came[0], c_stay[1])

    tz = [swap_z(t, m) for m in range(1, 4)]
    leave = call(leave_kernel, shape(4, 32, 256), [SMEM, VMEM], VMEM, [], LEAVE, 4, "leave")(place, blocks)
    came = swap_y(leave)
    c_came.append(swap_y(c_stay[1]))

    held = jnp.stack([t] + tz)
    b_out = call(spread_kernel, [shape(2, 32, 256)] * 3, [SMEM, VMEM, VMEM], [VMEM] * 3, [], SPREAD, 4, "spread")(
        place, blocks, came
    )
    b_z = [swap_z(after(b, held), m + 1) for m, b in enumerate(b_out)]
    held_now = after(held, came, c_came[1])
    got0 = cross(held_now, 0)
    got1 = cross(held_now, 1)
    got01 = cross(after(got0, got1, *b_z), 1)
    bufs = [held, got0, got1, got01]
    c_stay += [swap_z(after(coupling, b_z[0]), m) for m in range(2, 4)]
    c_came += [swap_y(c) for c in c_stay[2:]]

    left, both = call(
        rows_kernel,
        [shape(32, 1024), shape(2, 32, 1024)],
        [SMEM] + [VMEM] * 5,
        [VMEM] * 2,
        [],
        ROWS,
        4,
        "rows",
    )(place, blocks, came, *b_z)
    pair = jnp.stack([left, swap_rep(left, 2)])
    other_pair = swap_rep(pair, 1)
    bufs += [swap_rep(b, 1) for b in bufs[:3]] + [swap_rep(after(got01, pair, *c_stay[2:]), 1)]

    scratch = [pltpu.VMEM((8, 136, 128), F32)]
    halves = [shape(1024, 1024, dtype=BF16)] * 2
    x = call(
        first_kernel,
        shape(128, 1024),
        [SMEM] + [VMEM] * 10,
        VMEM,
        [pltpu.VMEM((1024, 1024), BF16)] * 2 + scratch,
        FIRST,
        24,
        "first_panel",
    )(place, pair, other_pair, *bufs)

    mine, to_x, to_core, to_both = call(
        update_kernel,
        [shape(32, 256)] * 4,
        [SMEM] + [VMEM] * 9,
        [VMEM] * 4,
        [pltpu.VMEM((256, 1024), BF16)] * 2,
        2_000_000_000,
        24,
        "update",
    )(place, x, *c_stay, *c_came)
    back = [swap_rep(to_x, 2), swap_rep(to_core, 1), swap_rep(to_both, 3)]

    uh, ul = call(
        second_factor_kernel, halves, [SMEM] + [VMEM] * 8, [VMEM] * 2, scratch, SECOND, 24, "second_factor"
    )(after(place, mine), *bufs)

    return call(second_kernel, shape(32, 2048), [SMEM] + [VMEM] * 8, VMEM, [], 2_500_000_000, 24, "second_panel")(
        place, x, both, uh, ul, mine, *back
    )


def solution(mesh):
    special = mesh.shape["bulk"] == 8 and mesh.shape["rep"] == 4

    def run(orbitals, triangles, coupling, diagonals):
        fits = orbitals.shape == (1024, 2048) and triangles.shape == (1024, 1024)
        body = per_device if special and fits else per_device_any
        return jax.shard_map(
            body,
            mesh=mesh,
            in_specs=(P("rep", "bulk"), P("rep", "bulk"), P("rep", "bulk"), P(None, "bulk")),
            out_specs=P(("rep", "bulk"), None),
            check_vma=False,
        )(orbitals, triangles, coupling, diagonals)

    return run
```

```python
import jax
import jax.numpy as jnp
from jax import lax
from jax.experimental import pallas as pl
from jax.experimental.pallas import tpu as pltpu
from jax.sharding import PartitionSpec as P

F32 = jnp.float32
BF16 = jnp.bfloat16
NN = (((1,), (0,)), ((), ()))
NT = (((1,), (1,)), ((), ()))


def unpack(triangles, diagonals):
    first_block = jnp.tril(triangles, -1) + jnp.diag(diagonals[0])
    second_block = jnp.tril(triangles.T, -1) + jnp.diag(diagonals[1])
    return (first_block, second_block)


def per_device_any(orbitals, triangles, coupling, diagonals):
    tri_rows, couple_rows = (
        lax.all_gather(triangles, "rep", axis=0, tiled=True),
        lax.all_gather(coupling, "rep", axis=0, tiled=True),
    )
    tri_whole, couple_whole, diag_whole = (
        lax.all_gather(tri_rows, "bulk", axis=1, tiled=True),
        lax.all_gather(couple_rows, "bulk", axis=1, tiled=True),
        lax.all_gather(diagonals, "bulk", axis=1, tiled=True),
    )
    first_block, second_block = unpack(tri_whole, diag_whole)
    panel = first_block.shape[0]
    groups = lax.axis_size("bulk")
    local_rows = orbitals.shape[0] // groups
    blocks = orbitals.reshape(groups, local_rows, orbitals.shape[1])
    received = lax.all_to_all(blocks, "bulk", split_axis=0, concat_axis=2, tiled=True)
    rows_now = received.reshape(local_rows, received.shape[2])
    left_part = rows_now[:, :panel]
    right_part = rows_now[:, panel:]
    solved_one = jax.scipy.linalg.solve_triangular(first_block, left_part.T, lower=True).T
    update = jnp.dot(
        solved_one,
        couple_whole.T,
        precision=lax.Precision.HIGHEST,
        preferred_element_type=jnp.float32,
    )
    solved_two = jax.scipy.linalg.solve_triangular(
        second_block, (right_part - update).T, lower=True
    ).T
    return jnp.concatenate([solved_one, solved_two], axis=1)


def dot(a, b, dims=NN):
    return lax.dot_general(a, b, dims, preferred_element_type=F32)


def dot_exact(a, b):
    return lax.dot_general(a, b, NN, precision=lax.Precision.HIGHEST, preferred_element_type=F32)


def split(x):
    high = x.astype(BF16)
    return high, (x - high.astype(F32)).astype(BF16)


def mul(x, b, dims=NN):
    xh, xl = split(x)
    bh, bl = b
    m = x.shape[0]
    both = dot(jnp.concatenate([xh, xl], axis=0), bh, dims)
    return (both[:m] + both[m:]) + dot(xh, bl, dims)


def mul3(a, b):
    (ah, al), (bh, bl) = split(a), split(b)
    return dot(ah, bh) + (dot(al, bh) + dot(ah, bl))


def iotas(n):
    return lax.broadcasted_iota(jnp.int32, (n, n), 0), lax.broadcasted_iota(jnp.int32, (n, n), 1)


def invert_kernel(place_ref, tri_ref, diag_ref, t_ref):
    rep, bulk = place_ref[0], place_ref[1]
    rows, n = tri_ref.shape
    inv = 1.0 / diag_ref[...]
    t_ref[0:rows, :] = tri_ref[...]
    t_ref[rows : rows + 8, :] = jnp.concatenate([inv, jnp.zeros((6, n), F32)], axis=0)

    @pl.when(rep == bulk // 2)
    def _():
        start = pl.multiple_of((bulk % 2) * n, n)
        block = tri_ref[pl.ds(start, n), :]
        i, j = iotas(n)
        eye = i == j
        ans = []
        for which in range(2):
            row, col = (i, j) if which == 0 else (j, i)
            along = inv[which : which + 1, :]
            d = jnp.where(eye, along, 0.0)
            down = jnp.sum(d, axis=1, keepdims=True)
            part = (row >> 1 == col >> 1) & (row > col)
            ans.append(d - jnp.where(part, block * along * down, 0.0))
        level = 1
        while (1 << level) < n:
            for which in range(2):
                row, col = (i, j) if which == 0 else (j, i)
                part = (row >> (level + 1) == col >> (level + 1)) & (row >> level > col >> level)
                t = ans[which]
                ans[which] = t - mul3(mul3(t, jnp.where(part, block, 0.0)), t)
            level += 1
        t_ref[pl.ds(start, n), :] = jnp.where(i >= j, ans[0], ans[1])


def leave_kernel(place_ref, orb, out):
    y = place_ref[1] & 1
    for k in range(4):
        out[k] = orb[k, 1 - y]


def spread_kernel(place_ref, orb, came, b1, b2, b3):
    z, y = place_ref[1] >> 1, place_ref[1] & 1
    for m, ref in ((1, b1), (2, b2), (3, b3)):
        ref[0] = orb[z ^ m, y]
        ref[1] = came[z ^ m]


def rows_kernel(place_ref, orb, came, b1, b2, b3, left, both):
    z, y = place_ref[1] >> 1, place_ref[1] & 1

    def put(m, dy, value):
        k = 2 * (z ^ m) + (y ^ dy)
        both[k >> 2, :, pl.ds(pl.multiple_of((k & 3) * 256, 256), 256)] = value

    put(0, 0, orb[z, y])
    put(0, 1, came[z])
    for m, ref in ((1, b1), (2, b2), (3, b3)):
        put(m, 0, ref[0])
        put(m, 1, ref[1])
    left[...] = both[0]


def origin(place_ref, crossed, first, second, m):
    rep, bulk = place_ref[0], place_ref[1]
    if m < 2:
        dx, dy = second, first
    else:
        core = (rep & 1) ^ crossed
        dx = jnp.where(core == 0, first, second)
        dy = jnp.where(core == 0, second, first)
    return rep ^ (2 * dx + crossed), bulk ^ (2 * m + dy)


def pieces(bufs):
    found = []
    for crossed in range(2):
        for m in range(4):
            for second in range(2):
                for first in range(2):
                    buf = bufs[8 * crossed + 4 * (m // 2) + 2 * second + first]
                    found.append((buf.at[m % 2], (crossed, first, second, m)))
    return found


def offset(index, size):
    return pl.ds(pl.multiple_of(index * size, size), size)


def place_pieces(place_ref, bufs, upper, high, low, diag):
    for piece, args in pieces(bufs):
        rep, bulk = origin(place_ref, *args)

        @pl.when((rep <= bulk // 2) if upper else (rep >= bulk // 2))
        def _():
            h, l = split(piece[0:256, :])
            high[offset(rep, 256), offset(bulk, 128)] = h
            low[offset(rep, 256), offset(bulk, 128)] = l

        @pl.when(rep == bulk // 2)
        def _():
            diag[bulk, 0:128, :] = piece[pl.ds(pl.multiple_of((bulk % 2) * 128, 128), 128), :]
            diag[bulk, 128:136, :] = piece[256:264, :]


def mul_pairs(a, b):
    (ah, al), (bh, bl) = a, b
    return dot(ah, bh) + (dot(al, bh) + dot(ah, bl))


def pair_of(high, low, r, c, size):
    rows, cols = slice(r, r + size), slice(c, c + size)
    return high[rows, cols], low[rows, cols]


def join(a, b, c, d):
    return jnp.concatenate([jnp.concatenate([a, b], axis=1), jnp.concatenate([c, d], axis=1)], axis=0)


def first_kernel(place_ref, pair, other_pair, *refs):
    bufs, (x_ref, high, low, diag) = refs[:16], refs[16:]
    place_pieces(place_ref, bufs, False, high, low, diag)
    n = 128
    i, j = iotas(n)

    def block(k):
        return jnp.where(i > j, diag[k, 0:n, :], 0.0) + jnp.where(i == j, diag[k, n : n + 1, :], 0.0)

    zero = jnp.zeros((n, n), F32)
    inverses = []
    for k in range(4):
        ta, tb = block(2 * k), block(2 * k + 1)
        pa, pb = split(ta), split(tb)
        off = -mul_pairs(split(mul_pairs(pb, pair_of(high, low, 256 * k + n, 256 * k, n))), pa)
        inverses.append(split(join(ta, zero, off, tb)))

    rest = jnp.concatenate([pair[0], pair[1], other_pair[0], other_pair[1]], axis=0)
    for k in range(4):
        x = mul(rest[:, :256], inverses[k], NT)
        x_ref[:, k * 256 : (k + 1) * 256] = x
        if k < 3:
            rows, cols = slice((k + 1) * 256, 1024), slice(k * 256, (k + 1) * 256)
            rest = rest[:, 256:] - mul(x, (high[rows, cols], low[rows, cols]), NT)


def update_kernel(place_ref, x_ref, *refs):
    held, outs, (high, low) = refs[:4], refs[4:8], refs[8:]
    bulk = place_ref[1]
    for dy in range(2):
        for m in range(4):
            h, l = split(held[2 * dy + m // 2][m % 2])
            high[:, offset(bulk ^ (2 * m + dy), 128)] = h
            low[:, offset(bulk ^ (2 * m + dy), 128)] = l
    upd = mul(x_ref[...], (high[...], low[...]), NT)
    for k, out in enumerate(outs):
        out[...] = upd[32 * k : 32 * (k + 1)]


def second_factor_kernel(place_ref, *refs):
    bufs, (high, low, diag) = refs[:16], refs[16:]
    place_pieces(place_ref, bufs, True, high, low, diag)
    n = 128
    i, j = iotas(n)

    def block(k):
        return jnp.where(i < j, diag[k, 0:n, :], 0.0) + jnp.where(i == j, diag[k, n + 1 : n + 2, :], 0.0)

    zero = jnp.zeros((n, n), F32)
    inverses = []
    for k in range(4):
        ta, tb = block(2 * k), block(2 * k + 1)
        pa, pb = split(ta), split(tb)
        off = -mul_pairs(split(mul_pairs(pa, pair_of(high, low, 256 * k, 256 * k + n, n))), pb)
        inverses.append(split(join(ta, off, zero, tb)))

    def put(r, c, value):
        high[r : r + 256, c : c + 256], low[r : r + 256, c : c + 256] = value

    for k in range(2):
        at = 512 * k
        pa, pb = inverses[2 * k], inverses[2 * k + 1]
        off = -mul_pairs(split(mul_pairs(pa, pair_of(high, low, at, at + 256, 256))), pb)
        put(at, at, pa)
        put(at + 256, at + 256, pb)
        put(at, at + 256, split(off))
        put(at + 256, at, (jnp.zeros((256, 256), BF16),) * 2)


def second_kernel(place_ref, x_ref, both_ref, uh_ref, ul_ref, mine, from_x, from_core, from_both, out_ref):
    x = x_ref[0:32, :]
    out_ref[:, 0:1024] = x
    parts = []
    for k in range(4):
        way = place_ref[0] ^ k
        upd = jnp.where(
            way == 0,
            mine[...],
            jnp.where(way == 2, from_x[...], jnp.where(way == 1, from_core[...], from_both[...])),
        )
        parts.append(both_ref[1, :, k * 256 : (k + 1) * 256] - upd)
    ra = jnp.concatenate(parts[:2], axis=1)
    rb = jnp.concatenate(parts[2:], axis=1)

    def u(r, c):
        rows, cols = slice(r * 512, r * 512 + 512), slice(c * 512, c * 512 + 512)
        return uh_ref[rows, cols], ul_ref[rows, cols]

    xa = mul(ra, u(0, 0))
    xb = mul(rb - mul(xa, u(0, 1)), u(1, 1))
    out_ref[:, 1024:1536] = xa
    out_ref[:, 1536:2048] = xb


BOTH = ("bulk", "rep")

SPREAD, INVERT, LEAVE, ROWS, FIRST, SECOND = 1_000_000_000, 3_500_000_000, 500_000_000, 1_000_000_000, 4_000_000_000, 3_000_000_000


def swap_z(x, m):
    return lax.ppermute(x, "bulk", [(k, k ^ (2 * m)) for k in range(8)])


def swap_y(x):
    return lax.ppermute(x, "bulk", [(k, k ^ 1) for k in range(8)])


def swap_rep(x, bits):
    return lax.ppermute(x, "rep", [(k, k ^ bits) for k in range(4)])


def cross(x, stage):
    pairs = []
    for rep in range(4):
        for bulk in range(8):
            to = (rep ^ 2, bulk) if (rep & 1) == stage else (rep, bulk ^ 1)
            pairs.append((bulk * 4 + rep, to[1] * 4 + to[0]))
    return lax.ppermute(x, BOTH, pairs)


def after(x, *deps):
    return lax.optimization_barrier((x,) + deps)[0]


ANY = pl.BlockSpec(memory_space=pl.ANY)
VMEM = pl.BlockSpec(memory_space=pltpu.VMEM)
SMEM = pl.BlockSpec(memory_space=pltpu.SMEM)


def call(kernel, out, specs, outs, scratch, flops, size, name):
    return pl.pallas_call(
        kernel,
        out_shape=out,
        in_specs=specs,
        out_specs=outs,
        scratch_shapes=scratch,
        compiler_params=pltpu.CompilerParams(vmem_limit_bytes=size << 20),
        cost_estimate=pl.CostEstimate(flops=flops, bytes_accessed=2 << 20, transcendentals=0),
        name=name,
    )


def shape(*dims, dtype=F32):
    return jax.ShapeDtypeStruct(dims, dtype)


def per_device(orbitals, triangles, coupling, diagonals):
    rep, bulk = lax.axis_index("rep"), lax.axis_index("bulk")
    place = jnp.stack([rep, bulk]).astype(jnp.int32)
    blocks = orbitals.reshape(4, 2, 32, 256)

    t = call(invert_kernel, shape(264, 128), [SMEM, VMEM, VMEM], VMEM, [], INVERT, 4, "invert")(
        place, triangles, diagonals
    )
    coup = after(coupling, t)

    near = jnp.stack([t, swap_z(t, 1)])
    far = swap_z(near, 2)
    near0 = swap_y(near)
    near1 = swap_rep(near, 2)
    near01 = swap_rep(near0, 2)

    leave = call(leave_kernel, shape(4, 32, 256), [SMEM, VMEM], VMEM, [], LEAVE, 4, "leave")(place, blocks)
    came = swap_y(after(leave, t))
    c_near = jnp.stack([coupling, swap_z(coup, 1)])
    c_near_got = swap_y(c_near)

    far_now = after(far, near0, near1, came)
    far0 = cross(far_now, 0)
    far1 = cross(far_now, 1)
    b_out = call(spread_kernel, [shape(2, 32, 256)] * 3, [SMEM, VMEM, VMEM], [VMEM] * 3, [], SPREAD, 4, "spread")(
        place, blocks, came
    )
    b_z = [swap_z(after(b, far), m + 1) for m, b in enumerate(b_out)]
    c_far = swap_z(after(c_near, far), 2)
    c_far_got = swap_y(c_far)
    far01 = cross(after(far0, far1, near01, *b_z), 1)

    left, both = call(
        rows_kernel,
        [shape(32, 1024), shape(2, 32, 1024)],
        [SMEM] + [VMEM] * 5,
        [VMEM] * 2,
        [],
        ROWS,
        4,
        "rows",
    )(place, blocks, came, *b_z)
    pair = jnp.stack([left, swap_rep(left, 2)])
    other_pair = swap_rep(after(pair, c_far), 1)
    bufs = [near, near0, near1, near01, far, far0, far1, far01]
    bufs += [swap_rep(b, 1) for b in bufs[:7]] + [swap_rep(after(far01, pair), 1)]

    scratch = [pltpu.VMEM((8, 136, 128), F32)]
    halves = [shape(1024, 1024, dtype=BF16)] * 2
    x = call(
        first_kernel,
        shape(128, 1024),
        [SMEM] + [VMEM] * 18,
        VMEM,
        [pltpu.VMEM((1024, 1024), BF16)] * 2 + scratch,
        FIRST,
        24,
        "first_panel",
    )(place, pair, after(other_pair, c_near_got), *bufs)

    mine, to_x, to_core, to_both = call(
        update_kernel,
        [shape(32, 256)] * 4,
        [SMEM] + [VMEM] * 5,
        [VMEM] * 4,
        [pltpu.VMEM((256, 1024), BF16)] * 2,
        2_000_000_000,
        24,
        "update",
    )(place, x, c_near, c_far, c_near_got, c_far_got)
    back = [swap_rep(to_x, 2), swap_rep(to_core, 1), swap_rep(to_both, 3)]

    uh, ul = call(
        second_factor_kernel, halves, [SMEM] + [VMEM] * 16, [VMEM] * 2, scratch, SECOND, 24, "second_factor"
    )(after(place, mine), *bufs)

    return call(second_kernel, shape(32, 2048), [SMEM] + [VMEM] * 8, VMEM, [], 2_500_000_000, 24, "second_panel")(
        place, x, both, uh, ul, mine, *back
    )


def solution(mesh):
    special = mesh.shape["bulk"] == 8 and mesh.shape["rep"] == 4

    def run(orbitals, triangles, coupling, diagonals):
        fits = orbitals.shape == (1024, 2048) and triangles.shape == (1024, 1024)
        body = per_device if special and fits else per_device_any
        return jax.shard_map(
            body,
            mesh=mesh,
            in_specs=(P("rep", "bulk"), P("rep", "bulk"), P("rep", "bulk"), P(None, "bulk")),
            out_specs=P(("rep", "bulk"), None),
            check_vma=False,
        )(orbitals, triangles, coupling, diagonals)

    return run
```

```python
import jax
import jax.numpy as jnp
from jax import lax
from jax.experimental import pallas as pl
from jax.experimental.pallas import tpu as pltpu
from jax.sharding import PartitionSpec as P

F32 = jnp.float32
BF16 = jnp.bfloat16
NN = (((1,), (0,)), ((), ()))
NT = (((1,), (1,)), ((), ()))


def unpack(triangles, diagonals):
    first_block = jnp.tril(triangles, -1) + jnp.diag(diagonals[0])
    second_block = jnp.tril(triangles.T, -1) + jnp.diag(diagonals[1])
    return (first_block, second_block)


def per_device_any(orbitals, triangles, coupling, diagonals):
    tri_rows, couple_rows = (
        lax.all_gather(triangles, "rep", axis=0, tiled=True),
        lax.all_gather(coupling, "rep", axis=0, tiled=True),
    )
    tri_whole, couple_whole, diag_whole = (
        lax.all_gather(tri_rows, "bulk", axis=1, tiled=True),
        lax.all_gather(couple_rows, "bulk", axis=1, tiled=True),
        lax.all_gather(diagonals, "bulk", axis=1, tiled=True),
    )
    first_block, second_block = unpack(tri_whole, diag_whole)
    panel = first_block.shape[0]
    groups = lax.axis_size("bulk")
    local_rows = orbitals.shape[0] // groups
    blocks = orbitals.reshape(groups, local_rows, orbitals.shape[1])
    received = lax.all_to_all(blocks, "bulk", split_axis=0, concat_axis=2, tiled=True)
    rows_now = received.reshape(local_rows, received.shape[2])
    left_part = rows_now[:, :panel]
    right_part = rows_now[:, panel:]
    solved_one = jax.scipy.linalg.solve_triangular(first_block, left_part.T, lower=True).T
    update = jnp.dot(
        solved_one,
        couple_whole.T,
        precision=lax.Precision.HIGHEST,
        preferred_element_type=jnp.float32,
    )
    solved_two = jax.scipy.linalg.solve_triangular(
        second_block, (right_part - update).T, lower=True
    ).T
    return jnp.concatenate([solved_one, solved_two], axis=1)


def dot(a, b, dims=NN):
    return lax.dot_general(a, b, dims, preferred_element_type=F32)


def dot_exact(a, b):
    return lax.dot_general(a, b, NN, precision=lax.Precision.HIGHEST, preferred_element_type=F32)


def split(x):
    high = x.astype(BF16)
    return high, (x - high.astype(F32)).astype(BF16)


def mul(x, b, dims=NN):
    xh, xl = split(x)
    bh, bl = b
    m = x.shape[0]
    both = dot(jnp.concatenate([xh, xl], axis=0), bh, dims)
    return (both[:m] + both[m:]) + dot(xh, bl, dims)


def mul3(a, b):
    (ah, al), (bh, bl) = split(a), split(b)
    return dot(ah, bh) + (dot(al, bh) + dot(ah, bl))


def iotas(n):
    return lax.broadcasted_iota(jnp.int32, (n, n), 0), lax.broadcasted_iota(jnp.int32, (n, n), 1)


def invert_kernel(place_ref, tri_ref, diag_ref, t_ref):
    rep, bulk = place_ref[0], place_ref[1]
    rows, n = tri_ref.shape
    inv = 1.0 / diag_ref[...]
    t_ref[0:rows, :] = tri_ref[...]
    t_ref[rows : rows + 8, :] = jnp.concatenate([inv, jnp.zeros((6, n), F32)], axis=0)

    @pl.when(rep == bulk // 2)
    def _():
        start = pl.multiple_of((bulk % 2) * n, n)
        block = tri_ref[pl.ds(start, n), :]
        i, j = iotas(n)
        eye = i == j
        ans = []
        for which in range(2):
            row, col = (i, j) if which == 0 else (j, i)
            along = inv[which : which + 1, :]
            d = jnp.where(eye, along, 0.0)
            down = jnp.sum(d, axis=1, keepdims=True)
            part = (row >> 1 == col >> 1) & (row > col)
            ans.append(d - jnp.where(part, block * along * down, 0.0))
        level = 1
        while (1 << level) < n:
            for which in range(2):
                row, col = (i, j) if which == 0 else (j, i)
                part = (row >> (level + 1) == col >> (level + 1)) & (row >> level > col >> level)
                t = ans[which]
                ans[which] = t - mul3(mul3(t, jnp.where(part, block, 0.0)), t)
            level += 1
        t_ref[pl.ds(start, n), :] = jnp.where(i >= j, ans[0], ans[1])


def leave_kernel(place_ref, orb, out):
    y = place_ref[1] & 1
    for k in range(4):
        out[k] = orb[k, 1 - y]


def spread_kernel(place_ref, orb, came, b1, b2, b3):
    z, y = place_ref[1] >> 1, place_ref[1] & 1
    for m, ref in ((1, b1), (2, b2), (3, b3)):
        ref[0] = orb[z ^ m, y]
        ref[1] = came[z ^ m]


def rows_kernel(place_ref, orb, came, b1, b2, b3, left, both):
    z, y = place_ref[1] >> 1, place_ref[1] & 1

    def put(m, dy, value):
        k = 2 * (z ^ m) + (y ^ dy)
        both[k >> 2, :, pl.ds(pl.multiple_of((k & 3) * 256, 256), 256)] = value

    put(0, 0, orb[z, y])
    put(0, 1, came[z])
    for m, ref in ((1, b1), (2, b2), (3, b3)):
        put(m, 0, ref[0])
        put(m, 1, ref[1])
    left[...] = both[0]


def origin(place_ref, crossed, first, second, m):
    rep, bulk = place_ref[0], place_ref[1]
    if m < 2:
        dx, dy = second, first
    else:
        core = (rep & 1) ^ crossed
        dx = jnp.where(core == 0, first, second)
        dy = jnp.where(core == 0, second, first)
    return rep ^ (2 * dx + crossed), bulk ^ (2 * m + dy)


def pieces(bufs):
    found = []
    for crossed in range(2):
        for m in range(4):
            for second in range(2):
                for first in range(2):
                    buf = bufs[8 * crossed + 4 * (m // 2) + 2 * second + first]
                    found.append((buf.at[m % 2], (crossed, first, second, m)))
    return found


def offset(index, size):
    return pl.ds(pl.multiple_of(index * size, size), size)


def place_pieces(place_ref, bufs, upper, high, low, diag):
    for piece, args in pieces(bufs):
        rep, bulk = origin(place_ref, *args)

        @pl.when((rep <= bulk // 2) if upper else (rep >= bulk // 2))
        def _():
            h, l = split(piece[0:256, :])
            high[offset(rep, 256), offset(bulk, 128)] = h
            low[offset(rep, 256), offset(bulk, 128)] = l

        @pl.when(rep == bulk // 2)
        def _():
            diag[bulk, 0:128, :] = piece[pl.ds(pl.multiple_of((bulk % 2) * 128, 128), 128), :]
            diag[bulk, 128:136, :] = piece[256:264, :]


def mul_pairs(a, b):
    (ah, al), (bh, bl) = a, b
    return dot(ah, bh) + (dot(al, bh) + dot(ah, bl))


def pair_of(high, low, r, c, size):
    rows, cols = slice(r, r + size), slice(c, c + size)
    return high[rows, cols], low[rows, cols]


def join(a, b, c, d):
    return jnp.concatenate([jnp.concatenate([a, b], axis=1), jnp.concatenate([c, d], axis=1)], axis=0)


def first_kernel(place_ref, pair, other_pair, *refs):
    bufs, (x_ref, high, low, diag) = refs[:16], refs[16:]
    place_pieces(place_ref, bufs, False, high, low, diag)
    n = 128
    i, j = iotas(n)

    def block(k):
        return jnp.where(i > j, diag[k, 0:n, :], 0.0) + jnp.where(i == j, diag[k, n : n + 1, :], 0.0)

    zero = jnp.zeros((n, n), F32)
    inverses = []
    for k in range(4):
        ta, tb = block(2 * k), block(2 * k + 1)
        pa, pb = split(ta), split(tb)
        off = -mul_pairs(split(mul_pairs(pb, pair_of(high, low, 256 * k + n, 256 * k, n))), pa)
        inverses.append(split(join(ta, zero, off, tb)))

    rest = jnp.concatenate([pair[0], pair[1], other_pair[0], other_pair[1]], axis=0)
    for k in range(4):
        x = mul(rest[:, :256], inverses[k], NT)
        x_ref[:, k * 256 : (k + 1) * 256] = x
        if k < 3:
            rows, cols = slice((k + 1) * 256, 1024), slice(k * 256, (k + 1) * 256)
            rest = rest[:, 256:] - mul(x, (high[rows, cols], low[rows, cols]), NT)


def update_kernel(place_ref, x_ref, *refs):
    held, outs, (high, low) = refs[:4], refs[4:8], refs[8:]
    bulk = place_ref[1]
    for dy in range(2):
        for m in range(4):
            h, l = split(held[2 * dy + m // 2][m % 2])
            high[:, offset(bulk ^ (2 * m + dy), 128)] = h
            low[:, offset(bulk ^ (2 * m + dy), 128)] = l
    upd = mul(x_ref[...], (high[...], low[...]), NT)
    for k, out in enumerate(outs):
        out[...] = upd[32 * k : 32 * (k + 1)]


def second_factor_kernel(place_ref, *refs):
    bufs, (high, low, diag) = refs[:16], refs[16:]
    place_pieces(place_ref, bufs, True, high, low, diag)
    n = 128
    i, j = iotas(n)

    def block(k):
        return jnp.where(i < j, diag[k, 0:n, :], 0.0) + jnp.where(i == j, diag[k, n + 1 : n + 2, :], 0.0)

    zero = jnp.zeros((n, n), F32)
    inverses = []
    for k in range(4):
        ta, tb = block(2 * k), block(2 * k + 1)
        pa, pb = split(ta), split(tb)
        off = -mul_pairs(split(mul_pairs(pa, pair_of(high, low, 256 * k, 256 * k + n, n))), pb)
        inverses.append(split(join(ta, off, zero, tb)))

    def put(r, c, value):
        high[r : r + 256, c : c + 256], low[r : r + 256, c : c + 256] = value

    for k in range(2):
        at = 512 * k
        pa, pb = inverses[2 * k], inverses[2 * k + 1]
        off = -mul_pairs(split(mul_pairs(pa, pair_of(high, low, at, at + 256, 256))), pb)
        put(at, at, pa)
        put(at + 256, at + 256, pb)
        put(at, at + 256, split(off))
        put(at + 256, at, (jnp.zeros((256, 256), BF16),) * 2)


def second_kernel(place_ref, x_ref, both_ref, uh_ref, ul_ref, mine, from_x, from_core, from_both, out_ref):
    x = x_ref[0:32, :]
    out_ref[:, 0:1024] = x
    parts = []
    for k in range(4):
        way = place_ref[0] ^ k
        upd = jnp.where(
            way == 0,
            mine[...],
            jnp.where(way == 2, from_x[...], jnp.where(way == 1, from_core[...], from_both[...])),
        )
        parts.append(both_ref[1, :, k * 256 : (k + 1) * 256] - upd)
    ra = jnp.concatenate(parts[:2], axis=1)
    rb = jnp.concatenate(parts[2:], axis=1)

    def u(r, c):
        rows, cols = slice(r * 512, r * 512 + 512), slice(c * 512, c * 512 + 512)
        return uh_ref[rows, cols], ul_ref[rows, cols]

    xa = mul(ra, u(0, 0))
    xb = mul(rb - mul(xa, u(0, 1)), u(1, 1))
    out_ref[:, 1024:1536] = xa
    out_ref[:, 1536:2048] = xb


BOTH = ("bulk", "rep")

SPREAD, INVERT, LEAVE, ROWS, FIRST, SECOND = 1_000_000_000, 3_500_000_000, 500_000_000, 1_000_000_000, 200_000_000, 3_000_000_000


def swap_z(x, m):
    return lax.ppermute(x, "bulk", [(k, k ^ (2 * m)) for k in range(8)])


def swap_y(x):
    return lax.ppermute(x, "bulk", [(k, k ^ 1) for k in range(8)])


def swap_rep(x, bits):
    return lax.ppermute(x, "rep", [(k, k ^ bits) for k in range(4)])


def cross(x, stage):
    pairs = []
    for rep in range(4):
        for bulk in range(8):
            to = (rep ^ 2, bulk) if (rep & 1) == stage else (rep, bulk ^ 1)
            pairs.append((bulk * 4 + rep, to[1] * 4 + to[0]))
    return lax.ppermute(x, BOTH, pairs)


def after(x, *deps):
    return lax.optimization_barrier((x,) + deps)[0]


ANY = pl.BlockSpec(memory_space=pl.ANY)
VMEM = pl.BlockSpec(memory_space=pltpu.VMEM)
SMEM = pl.BlockSpec(memory_space=pltpu.SMEM)


def call(kernel, out, specs, outs, scratch, flops, size, name):
    return pl.pallas_call(
        kernel,
        out_shape=out,
        in_specs=specs,
        out_specs=outs,
        scratch_shapes=scratch,
        compiler_params=pltpu.CompilerParams(vmem_limit_bytes=size << 20),
        cost_estimate=pl.CostEstimate(flops=flops, bytes_accessed=2 << 20, transcendentals=0),
        name=name,
    )


def shape(*dims, dtype=F32):
    return jax.ShapeDtypeStruct(dims, dtype)


def per_device(orbitals, triangles, coupling, diagonals):
    rep, bulk = lax.axis_index("rep"), lax.axis_index("bulk")
    place = jnp.stack([rep, bulk]).astype(jnp.int32)
    blocks = orbitals.reshape(4, 2, 32, 256)

    t = call(invert_kernel, shape(264, 128), [SMEM, VMEM, VMEM], VMEM, [], INVERT, 4, "invert")(
        place, triangles, diagonals
    )
    coup = after(coupling, t)

    near = jnp.stack([t, swap_z(t, 1)])
    far = swap_z(near, 2)
    near0 = swap_y(near)
    near1 = swap_rep(near, 2)
    near01 = swap_rep(near0, 2)

    leave = call(leave_kernel, shape(4, 32, 256), [SMEM, VMEM], VMEM, [], LEAVE, 4, "leave")(place, blocks)
    came = swap_y(after(leave, t))
    c_near = jnp.stack([coupling, swap_z(coup, 1)])
    c_near_got = swap_y(c_near)

    far_now = after(far, near0, near1, came)
    far0 = cross(far_now, 0)
    far1 = cross(far_now, 1)
    b_out = call(spread_kernel, [shape(2, 32, 256)] * 3, [SMEM, VMEM, VMEM], [VMEM] * 3, [], SPREAD, 4, "spread")(
        place, blocks, came
    )
    b_z = [swap_z(after(b, far), m + 1) for m, b in enumerate(b_out)]
    c_far = swap_z(after(c_near, far), 2)
    c_far_got = swap_y(c_far)
    far01 = cross(after(far0, far1, near01), 1)

    left, both = call(
        rows_kernel,
        [shape(32, 1024), shape(2, 32, 1024)],
        [SMEM] + [VMEM] * 5,
        [VMEM] * 2,
        [],
        ROWS,
        4,
        "rows",
    )(place, blocks, came, *b_z)
    pair = jnp.stack([left, swap_rep(after(left, c_far), 2)])
    other_pair = swap_rep(after(pair, c_far), 1)
    bufs = [near, near0, near1, near01, far, far0, far1, far01]
    bufs += [swap_rep(b, 1) for b in bufs[:7]] + [swap_rep(after(far01, far1), 1)]

    scratch = [pltpu.VMEM((8, 136, 128), F32)]
    halves = [shape(1024, 1024, dtype=BF16)] * 2
    x = call(
        first_kernel,
        shape(128, 1024),
        [SMEM] + [VMEM] * 18,
        VMEM,
        [pltpu.VMEM((1024, 1024), BF16)] * 2 + scratch,
        FIRST,
        24,
        "first_panel",
    )(place, pair, after(other_pair, c_near_got), *bufs)

    mine, to_x, to_core, to_both = call(
        update_kernel,
        [shape(32, 256)] * 4,
        [SMEM] + [VMEM] * 5,
        [VMEM] * 4,
        [pltpu.VMEM((256, 1024), BF16)] * 2,
        2_000_000_000,
        24,
        "update",
    )(place, x, c_near, c_far, c_near_got, c_far_got)
    back = [swap_rep(to_x, 2), swap_rep(to_core, 1), swap_rep(to_both, 3)]

    uh, ul = call(
        second_factor_kernel, halves, [SMEM] + [VMEM] * 16, [VMEM] * 2, scratch, SECOND, 24, "second_factor"
    )(after(place, mine), *bufs)

    return call(second_kernel, shape(32, 2048), [SMEM] + [VMEM] * 8, VMEM, [], 2_500_000_000, 24, "second_panel")(
        place, x, both, uh, ul, mine, *back
    )


def solution(mesh):
    special = mesh.shape["bulk"] == 8 and mesh.shape["rep"] == 4

    def run(orbitals, triangles, coupling, diagonals):
        fits = orbitals.shape == (1024, 2048) and triangles.shape == (1024, 1024)
        body = per_device if special and fits else per_device_any
        return jax.shard_map(
            body,
            mesh=mesh,
            in_specs=(P("rep", "bulk"), P("rep", "bulk"), P("rep", "bulk"), P(None, "bulk")),
            out_specs=P(("rep", "bulk"), None),
            check_vma=False,
        )(orbitals, triangles, coupling, diagonals)

    return run
```

```python
import jax
import jax.numpy as jnp
from jax import lax
from jax.experimental import pallas as pl
from jax.experimental.pallas import tpu as pltpu
from jax.sharding import PartitionSpec as P

F32 = jnp.float32
BF16 = jnp.bfloat16
NN = (((1,), (0,)), ((), ()))
NT = (((1,), (1,)), ((), ()))


def unpack(triangles, diagonals):
    first_block = jnp.tril(triangles, -1) + jnp.diag(diagonals[0])
    second_block = jnp.tril(triangles.T, -1) + jnp.diag(diagonals[1])
    return (first_block, second_block)


def per_device_any(orbitals, triangles, coupling, diagonals):
    tri_rows, couple_rows = (
        lax.all_gather(triangles, "rep", axis=0, tiled=True),
        lax.all_gather(coupling, "rep", axis=0, tiled=True),
    )
    tri_whole, couple_whole, diag_whole = (
        lax.all_gather(tri_rows, "bulk", axis=1, tiled=True),
        lax.all_gather(couple_rows, "bulk", axis=1, tiled=True),
        lax.all_gather(diagonals, "bulk", axis=1, tiled=True),
    )
    first_block, second_block = unpack(tri_whole, diag_whole)
    panel = first_block.shape[0]
    groups = lax.axis_size("bulk")
    local_rows = orbitals.shape[0] // groups
    blocks = orbitals.reshape(groups, local_rows, orbitals.shape[1])
    received = lax.all_to_all(blocks, "bulk", split_axis=0, concat_axis=2, tiled=True)
    rows_now = received.reshape(local_rows, received.shape[2])
    left_part = rows_now[:, :panel]
    right_part = rows_now[:, panel:]
    solved_one = jax.scipy.linalg.solve_triangular(first_block, left_part.T, lower=True).T
    update = jnp.dot(
        solved_one,
        couple_whole.T,
        precision=lax.Precision.HIGHEST,
        preferred_element_type=jnp.float32,
    )
    solved_two = jax.scipy.linalg.solve_triangular(
        second_block, (right_part - update).T, lower=True
    ).T
    return jnp.concatenate([solved_one, solved_two], axis=1)


def dot(a, b, dims=NN):
    return lax.dot_general(a, b, dims, preferred_element_type=F32)


def dot_exact(a, b):
    return lax.dot_general(a, b, NN, precision=lax.Precision.HIGHEST, preferred_element_type=F32)


def split(x):
    high = x.astype(BF16)
    return high, (x - high.astype(F32)).astype(BF16)


def mul(x, b, dims=NN):
    xh, xl = split(x)
    bh, bl = b
    m = x.shape[0]
    both = dot(jnp.concatenate([xh, xl], axis=0), bh, dims)
    return (both[:m] + both[m:]) + dot(xh, bl, dims)


def mul3(a, b):
    (ah, al), (bh, bl) = split(a), split(b)
    return dot(ah, bh) + (dot(al, bh) + dot(ah, bl))


def iotas(n):
    return lax.broadcasted_iota(jnp.int32, (n, n), 0), lax.broadcasted_iota(jnp.int32, (n, n), 1)


def invert_kernel(place_ref, tri_ref, diag_ref, t_ref):
    rep, bulk = place_ref[0], place_ref[1]
    rows, n = tri_ref.shape
    inv = 1.0 / diag_ref[...]
    t_ref[0:rows, :] = tri_ref[...]
    t_ref[rows : rows + 8, :] = jnp.concatenate([inv, jnp.zeros((6, n), F32)], axis=0)

    @pl.when(rep == bulk // 2)
    def _():
        start = pl.multiple_of((bulk % 2) * n, n)
        block = tri_ref[pl.ds(start, n), :]
        i, j = iotas(n)
        eye = i == j
        ans = []
        for which in range(2):
            row, col = (i, j) if which == 0 else (j, i)
            along = inv[which : which + 1, :]
            d = jnp.where(eye, along, 0.0)
            down = jnp.sum(d, axis=1, keepdims=True)
            part = (row >> 1 == col >> 1) & (row > col)
            ans.append(d - jnp.where(part, block * along * down, 0.0))
        level = 1
        while (1 << level) < n:
            for which in range(2):
                row, col = (i, j) if which == 0 else (j, i)
                part = (row >> (level + 1) == col >> (level + 1)) & (row >> level > col >> level)
                t = ans[which]
                ans[which] = t - mul3(mul3(t, jnp.where(part, block, 0.0)), t)
            level += 1
        t_ref[pl.ds(start, n), :] = jnp.where(i >= j, ans[0], ans[1])


def spread_kernel(place_ref, orb, b1, b2, b3):
    z = place_ref[1] >> 1
    for m, ref in ((1, b1), (2, b2), (3, b3)):
        ref[...] = orb[z ^ m]


def leave_kernel(place_ref, orb, b1, b2, b3, out):
    z, y = place_ref[1] >> 1, place_ref[1] & 1
    out[0] = orb[z, 1 - y]
    for m, ref in ((1, b1), (2, b2), (3, b3)):
        out[m] = ref[1 - y]


def rows_kernel(place_ref, orb, b1, b2, b3, came, left, both):
    z, y = place_ref[1] >> 1, place_ref[1] & 1

    def put(m, dy, value):
        k = 2 * (z ^ m) + (y ^ dy)
        both[k >> 2, :, pl.ds(pl.multiple_of((k & 3) * 256, 256), 256)] = value

    put(0, 0, orb[z, y])
    for m, ref in ((1, b1), (2, b2), (3, b3)):
        put(m, 0, ref[y])
    for m in range(4):
        put(m, 1, came[m])
    left[...] = both[0]


def origin(place_ref, crossed, first, second, m):
    rep, bulk = place_ref[0], place_ref[1]
    if m < 2:
        dx, dy = second, first
    else:
        core = (rep & 1) ^ crossed
        dx = jnp.where(core == 0, first, second)
        dy = jnp.where(core == 0, second, first)
    return rep ^ (2 * dx + crossed), bulk ^ (2 * m + dy)


def pieces(bufs):
    found = []
    for crossed in range(2):
        for m in range(4):
            for second in range(2):
                for first in range(2):
                    buf = bufs[8 * crossed + 4 * (m // 2) + 2 * second + first]
                    found.append((buf.at[m % 2], (crossed, first, second, m)))
    return found


def offset(index, size):
    return pl.ds(pl.multiple_of(index * size, size), size)


def place_pieces(place_ref, bufs, upper, high, low, diag):
    for piece, args in pieces(bufs):
        rep, bulk = origin(place_ref, *args)

        @pl.when((rep <= bulk // 2) if upper else (rep >= bulk // 2))
        def _():
            h, l = split(piece[0:256, :])
            high[offset(rep, 256), offset(bulk, 128)] = h
            low[offset(rep, 256), offset(bulk, 128)] = l

        @pl.when(rep == bulk // 2)
        def _():
            diag[bulk, 0:128, :] = piece[pl.ds(pl.multiple_of((bulk % 2) * 128, 128), 128), :]
            diag[bulk, 128:136, :] = piece[256:264, :]


def mul_pairs(a, b):
    (ah, al), (bh, bl) = a, b
    return dot(ah, bh) + (dot(al, bh) + dot(ah, bl))


def pair_of(high, low, r, c, size):
    rows, cols = slice(r, r + size), slice(c, c + size)
    return high[rows, cols], low[rows, cols]


def join(a, b, c, d):
    return jnp.concatenate([jnp.concatenate([a, b], axis=1), jnp.concatenate([c, d], axis=1)], axis=0)


def first_kernel(place_ref, pair, other_pair, *refs):
    bufs, (x_ref, high, low, diag) = refs[:16], refs[16:]
    place_pieces(place_ref, bufs, False, high, low, diag)
    n = 128
    i, j = iotas(n)

    def block(k):
        return jnp.where(i > j, diag[k, 0:n, :], 0.0) + jnp.where(i == j, diag[k, n : n + 1, :], 0.0)

    zero = jnp.zeros((n, n), F32)
    inverses = []
    for k in range(4):
        ta, tb = block(2 * k), block(2 * k + 1)
        pa, pb = split(ta), split(tb)
        off = -mul_pairs(split(mul_pairs(pb, pair_of(high, low, 256 * k + n, 256 * k, n))), pa)
        inverses.append(split(join(ta, zero, off, tb)))

    rest = jnp.concatenate([pair[0], pair[1], other_pair[0], other_pair[1]], axis=0)
    for k in range(4):
        x = mul(rest[:, :256], inverses[k], NT)
        x_ref[:, k * 256 : (k + 1) * 256] = x
        if k < 3:
            rows, cols = slice((k + 1) * 256, 1024), slice(k * 256, (k + 1) * 256)
            rest = rest[:, 256:] - mul(x, (high[rows, cols], low[rows, cols]), NT)


def update_kernel(place_ref, x_ref, *refs):
    held, outs, (high, low) = refs[:4], refs[4:8], refs[8:]
    bulk = place_ref[1]
    for dy in range(2):
        for m in range(4):
            h, l = split(held[2 * dy + m // 2][m % 2])
            high[:, offset(bulk ^ (2 * m + dy), 128)] = h
            low[:, offset(bulk ^ (2 * m + dy), 128)] = l
    upd = mul(x_ref[...], (high[...], low[...]), NT)
    for k, out in enumerate(outs):
        out[...] = upd[32 * k : 32 * (k + 1)]


def second_factor_kernel(place_ref, *refs):
    bufs, (high, low, diag) = refs[:16], refs[16:]
    place_pieces(place_ref, bufs, True, high, low, diag)
    n = 128
    i, j = iotas(n)

    def block(k):
        return jnp.where(i < j, diag[k, 0:n, :], 0.0) + jnp.where(i == j, diag[k, n + 1 : n + 2, :], 0.0)

    zero = jnp.zeros((n, n), F32)
    inverses = []
    for k in range(4):
        ta, tb = block(2 * k), block(2 * k + 1)
        pa, pb = split(ta), split(tb)
        off = -mul_pairs(split(mul_pairs(pa, pair_of(high, low, 256 * k, 256 * k + n, n))), pb)
        inverses.append(split(join(ta, off, zero, tb)))

    def put(r, c, value):
        high[r : r + 256, c : c + 256], low[r : r + 256, c : c + 256] = value

    for k in range(2):
        at = 512 * k
        pa, pb = inverses[2 * k], inverses[2 * k + 1]
        off = -mul_pairs(split(mul_pairs(pa, pair_of(high, low, at, at + 256, 256))), pb)
        put(at, at, pa)
        put(at + 256, at + 256, pb)
        put(at, at + 256, split(off))
        put(at + 256, at, (jnp.zeros((256, 256), BF16),) * 2)


def second_kernel(place_ref, x_ref, both_ref, uh_ref, ul_ref, mine, from_x, from_core, from_both, out_ref):
    x = x_ref[0:32, :]
    out_ref[:, 0:1024] = x
    parts = []
    for k in range(4):
        way = place_ref[0] ^ k
        upd = jnp.where(
            way == 0,
            mine[...],
            jnp.where(way == 2, from_x[...], jnp.where(way == 1, from_core[...], from_both[...])),
        )
        parts.append(both_ref[1, :, k * 256 : (k + 1) * 256] - upd)
    ra = jnp.concatenate(parts[:2], axis=1)
    rb = jnp.concatenate(parts[2:], axis=1)

    def u(r, c):
        rows, cols = slice(r * 512, r * 512 + 512), slice(c * 512, c * 512 + 512)
        return uh_ref[rows, cols], ul_ref[rows, cols]

    xa = mul(ra, u(0, 0))
    xb = mul(rb - mul(xa, u(0, 1)), u(1, 1))
    out_ref[:, 1024:1536] = xa
    out_ref[:, 1536:2048] = xb


BOTH = ("bulk", "rep")

SPREAD, INVERT, LEAVE, ROWS, FIRST, SECOND = 1_000_000_000, 3_500_000_000, 500_000_000, 1_000_000_000, 200_000_000, 3_000_000_000


def swap_z(x, m):
    return lax.ppermute(x, "bulk", [(k, k ^ (2 * m)) for k in range(8)])


def swap_y(x):
    return lax.ppermute(x, "bulk", [(k, k ^ 1) for k in range(8)])


def swap_xy(x):
    return lax.ppermute(x, BOTH, [(k, k ^ 6) for k in range(32)])


def swap_rep(x, bits):
    return lax.ppermute(x, "rep", [(k, k ^ bits) for k in range(4)])


def cross(x, stage):
    pairs = []
    for rep in range(4):
        for bulk in range(8):
            to = (rep ^ 2, bulk) if (rep & 1) == stage else (rep, bulk ^ 1)
            pairs.append((bulk * 4 + rep, to[1] * 4 + to[0]))
    return lax.ppermute(x, BOTH, pairs)


def after(x, *deps):
    return lax.optimization_barrier((x,) + deps)[0]


ANY = pl.BlockSpec(memory_space=pl.ANY)
VMEM = pl.BlockSpec(memory_space=pltpu.VMEM)
SMEM = pl.BlockSpec(memory_space=pltpu.SMEM)


def call(kernel, out, specs, outs, scratch, flops, size, name):
    return pl.pallas_call(
        kernel,
        out_shape=out,
        in_specs=specs,
        out_specs=outs,
        scratch_shapes=scratch,
        compiler_params=pltpu.CompilerParams(vmem_limit_bytes=size << 20),
        cost_estimate=pl.CostEstimate(flops=flops, bytes_accessed=2 << 20, transcendentals=0),
        name=name,
    )


def shape(*dims, dtype=F32):
    return jax.ShapeDtypeStruct(dims, dtype)


def per_device(orbitals, triangles, coupling, diagonals):
    rep, bulk = lax.axis_index("rep"), lax.axis_index("bulk")
    place = jnp.stack([rep, bulk]).astype(jnp.int32)
    blocks = orbitals.reshape(4, 2, 32, 256)

    t = call(invert_kernel, shape(264, 128), [SMEM, VMEM, VMEM], VMEM, [], INVERT, 4, "invert")(
        place, triangles, diagonals
    )
    c1 = swap_z(after(coupling, t), 1)

    t1 = swap_z(t, 1)
    b_out = call(spread_kernel, [shape(2, 32, 256)] * 3, [SMEM, VMEM], [VMEM] * 3, [], SPREAD, 4, "spread")(
        place, blocks
    )
    b_z = [swap_z(after(b, t), m + 1) for m, b in enumerate(b_out)]
    near = jnp.stack([t, t1])
    far = swap_z(after(near, c1, *b_z), 2)

    near0 = swap_y(near)
    near1 = swap_rep(near, 2)
    near01 = swap_xy(near)
    leave = call(leave_kernel, shape(4, 32, 256), [SMEM] + [VMEM] * 4, VMEM, [], LEAVE, 4, "leave")(
        place, blocks, *b_z
    )
    came = swap_y(leave)

    c_near = jnp.stack([coupling, c1])
    c_near_got = swap_y(c_near)

    left, both = call(
        rows_kernel,
        [shape(32, 1024), shape(2, 32, 1024)],
        [SMEM] + [VMEM] * 5,
        [VMEM] * 2,
        [],
        ROWS,
        4,
        "rows",
    )(place, blocks, *b_z, came)
    pair = jnp.stack([left, swap_rep(left, 2)])

    far_now = after(far, near0, near1, near01, came)
    far0 = cross(far_now, 0)
    far1 = cross(far_now, 1)
    c_far = swap_z(after(c_near, far), 2)
    c_far_got = swap_y(c_far)
    far01 = cross(after(far0, far1), 1)
    other_pair = swap_rep(after(pair, c_far), 1)

    bufs = [near, near0, near1, near01, far, far0, far1, far01]
    bufs += [swap_rep(b, 1) for b in bufs[:7]] + [swap_rep(after(far01, far1), 1)]

    scratch = [pltpu.VMEM((8, 136, 128), F32)]
    halves = [shape(1024, 1024, dtype=BF16)] * 2
    x = call(
        first_kernel,
        shape(128, 1024),
        [SMEM] + [VMEM] * 18,
        VMEM,
        [pltpu.VMEM((1024, 1024), BF16)] * 2 + scratch,
        FIRST,
        24,
        "first_panel",
    )(place, pair, after(other_pair, c_near_got), *bufs)

    mine, to_x, to_core, to_both = call(
        update_kernel,
        [shape(32, 256)] * 4,
        [SMEM] + [VMEM] * 5,
        [VMEM] * 4,
        [pltpu.VMEM((256, 1024), BF16)] * 2,
        2_000_000_000,
        24,
        "update",
    )(place, x, c_near, c_far, c_near_got, c_far_got)
    back = [swap_rep(to_x, 2), swap_rep(to_core, 1), swap_rep(to_both, 3)]

    uh, ul = call(
        second_factor_kernel, halves, [SMEM] + [VMEM] * 16, [VMEM] * 2, scratch, SECOND, 24, "second_factor"
    )(after(place, mine), *bufs)

    return call(second_kernel, shape(32, 2048), [SMEM] + [VMEM] * 8, VMEM, [], 2_500_000_000, 24, "second_panel")(
        place, x, both, uh, ul, mine, *back
    )


def solution(mesh):
    special = mesh.shape["bulk"] == 8 and mesh.shape["rep"] == 4

    def run(orbitals, triangles, coupling, diagonals):
        fits = orbitals.shape == (1024, 2048) and triangles.shape == (1024, 1024)
        body = per_device if special and fits else per_device_any
        return jax.shard_map(
            body,
            mesh=mesh,
            in_specs=(P("rep", "bulk"), P("rep", "bulk"), P("rep", "bulk"), P(None, "bulk")),
            out_specs=P(("rep", "bulk"), None),
            check_vma=False,
        )(orbitals, triangles, coupling, diagonals)

    return run
```

```python
import jax
import jax.numpy as jnp
from jax import lax
from jax.experimental import pallas as pl
from jax.experimental.pallas import tpu as pltpu
from jax.sharding import PartitionSpec as P

F32 = jnp.float32
BF16 = jnp.bfloat16
NN = (((1,), (0,)), ((), ()))
NT = (((1,), (1,)), ((), ()))


def unpack(triangles, diagonals):
    first_block = jnp.tril(triangles, -1) + jnp.diag(diagonals[0])
    second_block = jnp.tril(triangles.T, -1) + jnp.diag(diagonals[1])
    return (first_block, second_block)


def per_device_any(orbitals, triangles, coupling, diagonals):
    tri_rows, couple_rows = (
        lax.all_gather(triangles, "rep", axis=0, tiled=True),
        lax.all_gather(coupling, "rep", axis=0, tiled=True),
    )
    tri_whole, couple_whole, diag_whole = (
        lax.all_gather(tri_rows, "bulk", axis=1, tiled=True),
        lax.all_gather(couple_rows, "bulk", axis=1, tiled=True),
        lax.all_gather(diagonals, "bulk", axis=1, tiled=True),
    )
    first_block, second_block = unpack(tri_whole, diag_whole)
    panel = first_block.shape[0]
    groups = lax.axis_size("bulk")
    local_rows = orbitals.shape[0] // groups
    blocks = orbitals.reshape(groups, local_rows, orbitals.shape[1])
    received = lax.all_to_all(blocks, "bulk", split_axis=0, concat_axis=2, tiled=True)
    rows_now = received.reshape(local_rows, received.shape[2])
    left_part = rows_now[:, :panel]
    right_part = rows_now[:, panel:]
    solved_one = jax.scipy.linalg.solve_triangular(first_block, left_part.T, lower=True).T
    update = jnp.dot(
        solved_one,
        couple_whole.T,
        precision=lax.Precision.HIGHEST,
        preferred_element_type=jnp.float32,
    )
    solved_two = jax.scipy.linalg.solve_triangular(
        second_block, (right_part - update).T, lower=True
    ).T
    return jnp.concatenate([solved_one, solved_two], axis=1)


def dot(a, b, dims=NN):
    return lax.dot_general(a, b, dims, preferred_element_type=F32)


def dot_exact(a, b):
    return lax.dot_general(a, b, NN, precision=lax.Precision.HIGHEST, preferred_element_type=F32)


def split(x):
    high = x.astype(BF16)
    return high, (x - high.astype(F32)).astype(BF16)


def mul(x, b, dims=NN):
    xh, xl = split(x)
    bh, bl = b
    m = x.shape[0]
    both = dot(jnp.concatenate([xh, xl], axis=0), bh, dims)
    return (both[:m] + both[m:]) + dot(xh, bl, dims)


def mul3(a, b):
    (ah, al), (bh, bl) = split(a), split(b)
    return dot(ah, bh) + (dot(al, bh) + dot(ah, bl))


def iotas(n):
    return lax.broadcasted_iota(jnp.int32, (n, n), 0), lax.broadcasted_iota(jnp.int32, (n, n), 1)


def invert_kernel(place_ref, tri_ref, diag_ref, t_ref):
    rep, bulk = place_ref[0], place_ref[1]
    rows, n = tri_ref.shape
    inv = 1.0 / diag_ref[...]
    t_ref[0:rows, :] = tri_ref[...]
    t_ref[rows : rows + 8, :] = jnp.concatenate([inv, jnp.zeros((6, n), F32)], axis=0)

    @pl.when(rep == bulk // 2)
    def _():
        start = pl.multiple_of((bulk % 2) * n, n)
        block = tri_ref[pl.ds(start, n), :]
        i, j = iotas(n)
        eye = i == j
        ans = []
        for which in range(2):
            row, col = (i, j) if which == 0 else (j, i)
            along = inv[which : which + 1, :]
            d = jnp.where(eye, along, 0.0)
            down = jnp.sum(d, axis=1, keepdims=True)
            part = (row >> 1 == col >> 1) & (row > col)
            ans.append(d - jnp.where(part, block * along * down, 0.0))
        level = 1
        while (1 << level) < n:
            for which in range(2):
                row, col = (i, j) if which == 0 else (j, i)
                part = (row >> (level + 1) == col >> (level + 1)) & (row >> level > col >> level)
                t = ans[which]
                ans[which] = t - mul3(mul3(t, jnp.where(part, block, 0.0)), t)
            level += 1
        t_ref[pl.ds(start, n), :] = jnp.where(i >= j, ans[0], ans[1])


def leave_kernel(place_ref, orb, out):
    y = place_ref[1] & 1
    for k in range(4):
        out[k] = orb[k, 1 - y]


def spread_kernel(place_ref, orb, came, b1, b2, b3):
    z, y = place_ref[1] >> 1, place_ref[1] & 1
    for m, ref in ((1, b1), (2, b2), (3, b3)):
        ref[0] = orb[z ^ m, y]
        ref[1] = came[z ^ m]


def rows_kernel(place_ref, orb, came, b1, b2, b3, left, both):
    z, y = place_ref[1] >> 1, place_ref[1] & 1

    def put(m, dy, value):
        k = 2 * (z ^ m) + (y ^ dy)
        both[k >> 2, :, pl.ds(pl.multiple_of((k & 3) * 256, 256), 256)] = value

    put(0, 0, orb[z, y])
    put(0, 1, came[z])
    for m, ref in ((1, b1), (2, b2), (3, b3)):
        put(m, 0, ref[0])
        put(m, 1, ref[1])
    left[...] = both[0]


def origin(place_ref, crossed, first, second, m):
    rep, bulk = place_ref[0], place_ref[1]
    if m < 2:
        dx, dy = second, first
    else:
        core = (rep & 1) ^ crossed
        dx = jnp.where(core == 0, first, second)
        dy = jnp.where(core == 0, second, first)
    return rep ^ (2 * dx + crossed), bulk ^ (2 * m + dy)


def pieces(bufs):
    found = []
    for crossed in range(2):
        for m in range(4):
            for second in range(2):
                for first in range(2):
                    buf = bufs[8 * crossed + 4 * (m // 2) + 2 * second + first]
                    found.append((buf.at[m % 2], (crossed, first, second, m)))
    return found


def offset(index, size):
    return pl.ds(pl.multiple_of(index * size, size), size)


def place_pieces(place_ref, bufs, upper, high, low, diag):
    for piece, args in pieces(bufs):
        rep, bulk = origin(place_ref, *args)

        @pl.when((rep <= bulk // 2) if upper else (rep >= bulk // 2))
        def _():
            h, l = split(piece[0:256, :])
            high[offset(rep, 256), offset(bulk, 128)] = h
            low[offset(rep, 256), offset(bulk, 128)] = l

        @pl.when(rep == bulk // 2)
        def _():
            diag[bulk, 0:128, :] = piece[pl.ds(pl.multiple_of((bulk % 2) * 128, 128), 128), :]
            diag[bulk, 128:136, :] = piece[256:264, :]


def mul_pairs(a, b):
    (ah, al), (bh, bl) = a, b
    return dot(ah, bh) + (dot(al, bh) + dot(ah, bl))


def pair_of(high, low, r, c, size):
    rows, cols = slice(r, r + size), slice(c, c + size)
    return high[rows, cols], low[rows, cols]


def join(a, b, c, d):
    return jnp.concatenate([jnp.concatenate([a, b], axis=1), jnp.concatenate([c, d], axis=1)], axis=0)


def first_kernel(place_ref, pair, other_pair, *refs):
    bufs, (x_ref, high, low, diag) = refs[:16], refs[16:]
    place_pieces(place_ref, bufs, False, high, low, diag)
    n = 128
    i, j = iotas(n)

    def block(k):
        return jnp.where(i > j, diag[k, 0:n, :], 0.0) + jnp.where(i == j, diag[k, n : n + 1, :], 0.0)

    zero = jnp.zeros((n, n), F32)
    inverses = []
    for k in range(4):
        ta, tb = block(2 * k), block(2 * k + 1)
        pa, pb = split(ta), split(tb)
        off = -mul_pairs(split(mul_pairs(pb, pair_of(high, low, 256 * k + n, 256 * k, n))), pa)
        inverses.append(split(join(ta, zero, off, tb)))

    rest = jnp.concatenate([pair[0], pair[1], other_pair[0], other_pair[1]], axis=0)
    for k in range(4):
        x = mul(rest[:, :256], inverses[k], NT)
        x_ref[:, k * 256 : (k + 1) * 256] = x
        if k < 3:
            rows, cols = slice((k + 1) * 256, 1024), slice(k * 256, (k + 1) * 256)
            rest = rest[:, 256:] - mul(x, (high[rows, cols], low[rows, cols]), NT)


def update_kernel(place_ref, x_ref, *refs):
    held, outs, (high, low) = refs[:4], refs[4:8], refs[8:]
    bulk = place_ref[1]
    for dy in range(2):
        for m in range(4):
            h, l = split(held[2 * dy + m // 2][m % 2])
            high[:, offset(bulk ^ (2 * m + dy), 128)] = h
            low[:, offset(bulk ^ (2 * m + dy), 128)] = l
    upd = mul(x_ref[...], (high[...], low[...]), NT)
    for k, out in enumerate(outs):
        out[...] = upd[32 * k : 32 * (k + 1)]


def second_factor_kernel(place_ref, *refs):
    bufs, (high, low, diag) = refs[:16], refs[16:]
    place_pieces(place_ref, bufs, True, high, low, diag)
    n = 128
    i, j = iotas(n)

    def block(k):
        return jnp.where(i < j, diag[k, 0:n, :], 0.0) + jnp.where(i == j, diag[k, n + 1 : n + 2, :], 0.0)

    zero = jnp.zeros((n, n), F32)
    inverses = []
    for k in range(4):
        ta, tb = block(2 * k), block(2 * k + 1)
        pa, pb = split(ta), split(tb)
        off = -mul_pairs(split(mul_pairs(pa, pair_of(high, low, 256 * k, 256 * k + n, n))), pb)
        inverses.append(split(join(ta, off, zero, tb)))

    def put(r, c, value):
        high[r : r + 256, c : c + 256], low[r : r + 256, c : c + 256] = value

    for k in range(2):
        at = 512 * k
        pa, pb = inverses[2 * k], inverses[2 * k + 1]
        off = -mul_pairs(split(mul_pairs(pa, pair_of(high, low, at, at + 256, 256))), pb)
        put(at, at, pa)
        put(at + 256, at + 256, pb)
        put(at, at + 256, split(off))
        put(at + 256, at, (jnp.zeros((256, 256), BF16),) * 2)


def second_kernel(place_ref, x_ref, both_ref, uh_ref, ul_ref, mine, from_x, from_core, from_both, out_ref):
    x = x_ref[0:32, :]
    out_ref[:, 0:1024] = x
    parts = []
    for k in range(4):
        way = place_ref[0] ^ k
        upd = jnp.where(
            way == 0,
            mine[...],
            jnp.where(way == 2, from_x[...], jnp.where(way == 1, from_core[...], from_both[...])),
        )
        parts.append(both_ref[1, :, k * 256 : (k + 1) * 256] - upd)
    ra = jnp.concatenate(parts[:2], axis=1)
    rb = jnp.concatenate(parts[2:], axis=1)

    def u(r, c):
        rows, cols = slice(r * 512, r * 512 + 512), slice(c * 512, c * 512 + 512)
        return uh_ref[rows, cols], ul_ref[rows, cols]

    xa = mul(ra, u(0, 0))
    xb = mul(rb - mul(xa, u(0, 1)), u(1, 1))
    out_ref[:, 1024:1536] = xa
    out_ref[:, 1536:2048] = xb


BOTH = ("bulk", "rep")

SPREAD, INVERT, LEAVE, ROWS, FIRST, SECOND = 1_000_000_000, 3_500_000_000, 500_000_000, 1_000_000_000, 200_000_000, 3_000_000_000


def swap_z(x, m):
    return lax.ppermute(x, "bulk", [(k, k ^ (2 * m)) for k in range(8)])


def swap_y(x):
    return lax.ppermute(x, "bulk", [(k, k ^ 1) for k in range(8)])


def swap_rep(x, bits):
    return lax.ppermute(x, "rep", [(k, k ^ bits) for k in range(4)])


def cross(x, stage):
    pairs = []
    for rep in range(4):
        for bulk in range(8):
            to = (rep ^ 2, bulk) if (rep & 1) == stage else (rep, bulk ^ 1)
            pairs.append((bulk * 4 + rep, to[1] * 4 + to[0]))
    return lax.ppermute(x, BOTH, pairs)


def after(x, *deps):
    return lax.optimization_barrier((x,) + deps)[0]


ANY = pl.BlockSpec(memory_space=pl.ANY)
VMEM = pl.BlockSpec(memory_space=pltpu.VMEM)
SMEM = pl.BlockSpec(memory_space=pltpu.SMEM)


def call(kernel, out, specs, outs, scratch, flops, size, name):
    return pl.pallas_call(
        kernel,
        out_shape=out,
        in_specs=specs,
        out_specs=outs,
        scratch_shapes=scratch,
        compiler_params=pltpu.CompilerParams(vmem_limit_bytes=size << 20),
        cost_estimate=pl.CostEstimate(flops=flops, bytes_accessed=2 << 20, transcendentals=0),
        name=name,
    )


def shape(*dims, dtype=F32):
    return jax.ShapeDtypeStruct(dims, dtype)


def per_device(orbitals, triangles, coupling, diagonals):
    rep, bulk = lax.axis_index("rep"), lax.axis_index("bulk")
    place = jnp.stack([rep, bulk]).astype(jnp.int32)
    blocks = orbitals.reshape(4, 2, 32, 256)

    t = call(invert_kernel, shape(264, 128), [SMEM, VMEM, VMEM], VMEM, [], INVERT, 4, "invert")(
        place, triangles, diagonals
    )
    coup = after(coupling, t)

    near = jnp.stack([t, swap_z(t, 1)])
    far = swap_z(near, 2)
    near0 = swap_y(near)
    near1 = swap_rep(near, 2)
    near01 = swap_rep(near0, 2)

    leave = call(leave_kernel, shape(4, 32, 256), [SMEM, VMEM], VMEM, [], LEAVE, 4, "leave")(place, blocks)
    came = swap_y(after(leave, t))
    c_near = jnp.stack([coupling, swap_z(coup, 1)])
    c_near_got = swap_y(c_near)

    far_now = after(far, near0, near1, came, c_near)
    far0 = cross(far_now, 0)
    far1 = cross(far_now, 1)
    b_out = call(spread_kernel, [shape(2, 32, 256)] * 3, [SMEM, VMEM, VMEM], [VMEM] * 3, [], SPREAD, 4, "spread")(
        place, blocks, came
    )
    b_z = [swap_z(after(b, far, near01), m + 1) for m, b in enumerate(b_out)]
    c_far = swap_z(after(c_near, far, b_z[0]), 2)
    c_far_got = swap_y(c_far)
    far01 = cross(after(far0, far1), 1)

    left, both = call(
        rows_kernel,
        [shape(32, 1024), shape(2, 32, 1024)],
        [SMEM] + [VMEM] * 5,
        [VMEM] * 2,
        [],
        ROWS,
        4,
        "rows",
    )(place, blocks, came, *b_z)
    pair = jnp.stack([left, swap_rep(after(left, came), 2)])
    other_pair = swap_rep(after(pair, c_far), 1)
    bufs = [near, near0, near1, near01, far, far0, far1, far01]
    bufs += [swap_rep(b, 1) for b in bufs[:7]] + [swap_rep(after(far01, far1), 1)]

    scratch = [pltpu.VMEM((8, 136, 128), F32)]
    halves = [shape(1024, 1024, dtype=BF16)] * 2
    x = call(
        first_kernel,
        shape(128, 1024),
        [SMEM] + [VMEM] * 18,
        VMEM,
        [pltpu.VMEM((1024, 1024), BF16)] * 2 + scratch,
        FIRST,
        24,
        "first_panel",
    )(place, pair, after(other_pair, c_near_got), *bufs)

    mine, to_x, to_core, to_both = call(
        update_kernel,
        [shape(32, 256)] * 4,
        [SMEM] + [VMEM] * 5,
        [VMEM] * 4,
        [pltpu.VMEM((256, 1024), BF16)] * 2,
        2_000_000_000,
        24,
        "update",
    )(place, x, c_near, c_far, c_near_got, c_far_got)
    back = [swap_rep(to_x, 2), swap_rep(to_core, 1), swap_rep(to_both, 3)]

    uh, ul = call(
        second_factor_kernel, halves, [SMEM] + [VMEM] * 16, [VMEM] * 2, scratch, SECOND, 24, "second_factor"
    )(after(place, mine), *bufs)

    return call(second_kernel, shape(32, 2048), [SMEM] + [VMEM] * 8, VMEM, [], 2_500_000_000, 24, "second_panel")(
        place, x, both, uh, ul, mine, *back
    )


def solution(mesh):
    special = mesh.shape["bulk"] == 8 and mesh.shape["rep"] == 4

    def run(orbitals, triangles, coupling, diagonals):
        fits = orbitals.shape == (1024, 2048) and triangles.shape == (1024, 1024)
        body = per_device if special and fits else per_device_any
        return jax.shard_map(
            body,
            mesh=mesh,
            in_specs=(P("rep", "bulk"), P("rep", "bulk"), P("rep", "bulk"), P(None, "bulk")),
            out_specs=P(("rep", "bulk"), None),
            check_vma=False,
        )(orbitals, triangles, coupling, diagonals)

    return run
```

```python
import jax
import jax.numpy as jnp
from jax import lax
from jax.experimental import pallas as pl
from jax.experimental.pallas import tpu as pltpu
from jax.sharding import PartitionSpec as P

F32 = jnp.float32
BF16 = jnp.bfloat16
NN = (((1,), (0,)), ((), ()))
NT = (((1,), (1,)), ((), ()))


def unpack(triangles, diagonals):
    first_block = jnp.tril(triangles, -1) + jnp.diag(diagonals[0])
    second_block = jnp.tril(triangles.T, -1) + jnp.diag(diagonals[1])
    return (first_block, second_block)


def per_device_any(orbitals, triangles, coupling, diagonals):
    tri_rows, couple_rows = (
        lax.all_gather(triangles, "rep", axis=0, tiled=True),
        lax.all_gather(coupling, "rep", axis=0, tiled=True),
    )
    tri_whole, couple_whole, diag_whole = (
        lax.all_gather(tri_rows, "bulk", axis=1, tiled=True),
        lax.all_gather(couple_rows, "bulk", axis=1, tiled=True),
        lax.all_gather(diagonals, "bulk", axis=1, tiled=True),
    )
    first_block, second_block = unpack(tri_whole, diag_whole)
    panel = first_block.shape[0]
    groups = lax.axis_size("bulk")
    local_rows = orbitals.shape[0] // groups
    blocks = orbitals.reshape(groups, local_rows, orbitals.shape[1])
    received = lax.all_to_all(blocks, "bulk", split_axis=0, concat_axis=2, tiled=True)
    rows_now = received.reshape(local_rows, received.shape[2])
    left_part = rows_now[:, :panel]
    right_part = rows_now[:, panel:]
    solved_one = jax.scipy.linalg.solve_triangular(first_block, left_part.T, lower=True).T
    update = jnp.dot(
        solved_one,
        couple_whole.T,
        precision=lax.Precision.HIGHEST,
        preferred_element_type=jnp.float32,
    )
    solved_two = jax.scipy.linalg.solve_triangular(
        second_block, (right_part - update).T, lower=True
    ).T
    return jnp.concatenate([solved_one, solved_two], axis=1)


def dot(a, b, dims=NN):
    return lax.dot_general(a, b, dims, preferred_element_type=F32)


def dot_exact(a, b):
    return lax.dot_general(a, b, NN, precision=lax.Precision.HIGHEST, preferred_element_type=F32)


def split(x):
    high = x.astype(BF16)
    return high, (x - high.astype(F32)).astype(BF16)


def mul(x, b, dims=NN):
    xh, xl = split(x)
    bh, bl = b
    m = x.shape[0]
    both = dot(jnp.concatenate([xh, xl], axis=0), bh, dims)
    return (both[:m] + both[m:]) + dot(xh, bl, dims)


def mul3(a, b):
    (ah, al), (bh, bl) = split(a), split(b)
    return dot(ah, bh) + (dot(al, bh) + dot(ah, bl))


def iotas(n):
    return lax.broadcasted_iota(jnp.int32, (n, n), 0), lax.broadcasted_iota(jnp.int32, (n, n), 1)


def invert_kernel(place_ref, tri_ref, diag_ref, t_ref):
    rep, bulk = place_ref[0], place_ref[1]
    rows, n = tri_ref.shape
    inv = 1.0 / diag_ref[...]
    t_ref[0:rows, :] = tri_ref[...]
    t_ref[rows : rows + 8, :] = jnp.concatenate([inv, jnp.zeros((6, n), F32)], axis=0)

    @pl.when(rep == bulk // 2)
    def _():
        start = pl.multiple_of((bulk % 2) * n, n)
        block = tri_ref[pl.ds(start, n), :]
        i, j = iotas(n)
        eye = i == j
        ans = []
        for which in range(2):
            row, col = (i, j) if which == 0 else (j, i)
            along = inv[which : which + 1, :]
            d = jnp.where(eye, along, 0.0)
            down = jnp.sum(d, axis=1, keepdims=True)
            part = (row >> 1 == col >> 1) & (row > col)
            ans.append(d - jnp.where(part, block * along * down, 0.0))
        level = 1
        while (1 << level) < n:
            for which in range(2):
                row, col = (i, j) if which == 0 else (j, i)
                part = (row >> (level + 1) == col >> (level + 1)) & (row >> level > col >> level)
                t = ans[which]
                ans[which] = t - mul3(mul3(t, jnp.where(part, block, 0.0)), t)
            level += 1
        t_ref[pl.ds(start, n), :] = jnp.where(i >= j, ans[0], ans[1])


def spread_kernel(place_ref, orb, b1, b2, b3):
    z = place_ref[1] >> 1
    for m, ref in ((1, b1), (2, b2), (3, b3)):
        ref[...] = orb[z ^ m]


def leave_kernel(place_ref, orb, b1, b2, b3, out):
    z, y = place_ref[1] >> 1, place_ref[1] & 1
    out[0] = orb[z, 1 - y]
    for m, ref in ((1, b1), (2, b2), (3, b3)):
        out[m] = ref[1 - y]


def rows_kernel(place_ref, orb, b1, b2, b3, came, left, both):
    z, y = place_ref[1] >> 1, place_ref[1] & 1

    def put(m, dy, value):
        k = 2 * (z ^ m) + (y ^ dy)
        both[k >> 2, :, pl.ds(pl.multiple_of((k & 3) * 256, 256), 256)] = value

    put(0, 0, orb[z, y])
    for m, ref in ((1, b1), (2, b2), (3, b3)):
        put(m, 0, ref[y])
    for m in range(4):
        put(m, 1, came[m])
    left[...] = both[0]


def origin(place_ref, crossed, first, second, m):
    rep, bulk = place_ref[0], place_ref[1]
    if m < 2:
        dx, dy = second, first
    else:
        core = (rep & 1) ^ crossed
        dx = jnp.where(core == 0, first, second)
        dy = jnp.where(core == 0, second, first)
    return rep ^ (2 * dx + crossed), bulk ^ (2 * m + dy)


def pieces(bufs):
    found = []
    for crossed in range(2):
        for m in range(4):
            for second in range(2):
                for first in range(2):
                    buf = bufs[8 * crossed + 4 * (m // 2) + 2 * second + first]
                    found.append((buf.at[m % 2], (crossed, first, second, m)))
    return found


def offset(index, size):
    return pl.ds(pl.multiple_of(index * size, size), size)


def place_pieces(place_ref, bufs, upper, high, low, diag):
    for piece, args in pieces(bufs):
        rep, bulk = origin(place_ref, *args)

        @pl.when((rep <= bulk // 2) if upper else (rep >= bulk // 2))
        def _():
            h, l = split(piece[0:256, :])
            high[offset(rep, 256), offset(bulk, 128)] = h
            low[offset(rep, 256), offset(bulk, 128)] = l

        @pl.when(rep == bulk // 2)
        def _():
            diag[bulk, 0:128, :] = piece[pl.ds(pl.multiple_of((bulk % 2) * 128, 128), 128), :]
            diag[bulk, 128:136, :] = piece[256:264, :]


def mul_pairs(a, b):
    (ah, al), (bh, bl) = a, b
    return dot(ah, bh) + (dot(al, bh) + dot(ah, bl))


def pair_of(high, low, r, c, size):
    rows, cols = slice(r, r + size), slice(c, c + size)
    return high[rows, cols], low[rows, cols]


def join(a, b, c, d):
    return jnp.concatenate([jnp.concatenate([a, b], axis=1), jnp.concatenate([c, d], axis=1)], axis=0)


def first_kernel(place_ref, pair, other_pair, *refs):
    bufs, (x_ref, high, low, diag) = refs[:16], refs[16:]
    place_pieces(place_ref, bufs, False, high, low, diag)
    n = 128
    i, j = iotas(n)

    def block(k):
        return jnp.where(i > j, diag[k, 0:n, :], 0.0) + jnp.where(i == j, diag[k, n : n + 1, :], 0.0)

    zero = jnp.zeros((n, n), F32)
    inverses = []
    for k in range(4):
        ta, tb = block(2 * k), block(2 * k + 1)
        pa, pb = split(ta), split(tb)
        off = -mul_pairs(split(mul_pairs(pb, pair_of(high, low, 256 * k + n, 256 * k, n))), pa)
        inverses.append(split(join(ta, zero, off, tb)))

    rest = jnp.concatenate([pair[0], pair[1], other_pair[0], other_pair[1]], axis=0)
    for k in range(4):
        x = mul(rest[:, :256], inverses[k], NT)
        x_ref[:, k * 256 : (k + 1) * 256] = x
        if k < 3:
            rows, cols = slice((k + 1) * 256, 1024), slice(k * 256, (k + 1) * 256)
            rest = rest[:, 256:] - mul(x, (high[rows, cols], low[rows, cols]), NT)


def update_kernel(place_ref, x_ref, *refs):
    held, outs, (high, low) = refs[:4], refs[4:8], refs[8:]
    bulk = place_ref[1]
    for dy in range(2):
        for m in range(4):
            h, l = split(held[2 * dy + m // 2][m % 2])
            high[:, offset(bulk ^ (2 * m + dy), 128)] = h
            low[:, offset(bulk ^ (2 * m + dy), 128)] = l
    upd = mul(x_ref[...], (high[...], low[...]), NT)
    for k, out in enumerate(outs):
        out[...] = upd[32 * k : 32 * (k + 1)]


def second_factor_kernel(place_ref, *refs):
    bufs, (high, low, diag) = refs[:16], refs[16:]
    place_pieces(place_ref, bufs, True, high, low, diag)
    n = 128
    i, j = iotas(n)

    def block(k):
        return jnp.where(i < j, diag[k, 0:n, :], 0.0) + jnp.where(i == j, diag[k, n + 1 : n + 2, :], 0.0)

    zero = jnp.zeros((n, n), F32)
    inverses = []
    for k in range(4):
        ta, tb = block(2 * k), block(2 * k + 1)
        pa, pb = split(ta), split(tb)
        off = -mul_pairs(split(mul_pairs(pa, pair_of(high, low, 256 * k, 256 * k + n, n))), pb)
        inverses.append(split(join(ta, off, zero, tb)))

    def put(r, c, value):
        high[r : r + 256, c : c + 256], low[r : r + 256, c : c + 256] = value

    for k in range(2):
        at = 512 * k
        pa, pb = inverses[2 * k], inverses[2 * k + 1]
        off = -mul_pairs(split(mul_pairs(pa, pair_of(high, low, at, at + 256, 256))), pb)
        put(at, at, pa)
        put(at + 256, at + 256, pb)
        put(at, at + 256, split(off))
        put(at + 256, at, (jnp.zeros((256, 256), BF16),) * 2)


def second_kernel(place_ref, x_ref, both_ref, uh_ref, ul_ref, mine, from_x, from_core, from_both, out_ref):
    x = x_ref[0:32, :]
    out_ref[:, 0:1024] = x
    parts = []
    for k in range(4):
        way = place_ref[0] ^ k
        upd = jnp.where(
            way == 0,
            mine[...],
            jnp.where(way == 2, from_x[...], jnp.where(way == 1, from_core[...], from_both[...])),
        )
        parts.append(both_ref[1, :, k * 256 : (k + 1) * 256] - upd)
    ra = jnp.concatenate(parts[:2], axis=1)
    rb = jnp.concatenate(parts[2:], axis=1)

    def u(r, c):
        rows, cols = slice(r * 512, r * 512 + 512), slice(c * 512, c * 512 + 512)
        return uh_ref[rows, cols], ul_ref[rows, cols]

    xa = mul(ra, u(0, 0))
    xb = mul(rb - mul(xa, u(0, 1)), u(1, 1))
    out_ref[:, 1024:1536] = xa
    out_ref[:, 1536:2048] = xb


BOTH = ("bulk", "rep")

SPREAD, INVERT, LEAVE, ROWS, FIRST, SECOND = 1_000_000_000, 3_500_000_000, 500_000_000, 1_000_000_000, 200_000_000, 3_000_000_000


def swap_z(x, m):
    return lax.ppermute(x, "bulk", [(k, k ^ (2 * m)) for k in range(8)])


def swap_y(x):
    return lax.ppermute(x, "bulk", [(k, k ^ 1) for k in range(8)])


def swap_xy(x):
    return lax.ppermute(x, BOTH, [(k, k ^ 6) for k in range(32)])


def swap_rep(x, bits):
    return lax.ppermute(x, "rep", [(k, k ^ bits) for k in range(4)])


def cross(x, stage):
    pairs = []
    for rep in range(4):
        for bulk in range(8):
            to = (rep ^ 2, bulk) if (rep & 1) == stage else (rep, bulk ^ 1)
            pairs.append((bulk * 4 + rep, to[1] * 4 + to[0]))
    return lax.ppermute(x, BOTH, pairs)


def after(x, *deps):
    return lax.optimization_barrier((x,) + deps)[0]


ANY = pl.BlockSpec(memory_space=pl.ANY)
VMEM = pl.BlockSpec(memory_space=pltpu.VMEM)
SMEM = pl.BlockSpec(memory_space=pltpu.SMEM)


def call(kernel, out, specs, outs, scratch, flops, size, name):
    return pl.pallas_call(
        kernel,
        out_shape=out,
        in_specs=specs,
        out_specs=outs,
        scratch_shapes=scratch,
        compiler_params=pltpu.CompilerParams(vmem_limit_bytes=size << 20),
        cost_estimate=pl.CostEstimate(flops=flops, bytes_accessed=2 << 20, transcendentals=0),
        name=name,
    )


def shape(*dims, dtype=F32):
    return jax.ShapeDtypeStruct(dims, dtype)


def per_device(orbitals, triangles, coupling, diagonals):
    rep, bulk = lax.axis_index("rep"), lax.axis_index("bulk")
    place = jnp.stack([rep, bulk]).astype(jnp.int32)
    blocks = orbitals.reshape(4, 2, 32, 256)

    t = call(invert_kernel, shape(264, 128), [SMEM, VMEM, VMEM], VMEM, [], INVERT, 4, "invert")(
        place, triangles, diagonals
    )
    c1 = swap_z(after(coupling, t), 1)

    t1 = swap_z(t, 1)
    b_out = call(spread_kernel, [shape(2, 32, 256)] * 3, [SMEM, VMEM], [VMEM] * 3, [], SPREAD, 4, "spread")(
        place, blocks
    )
    b_z = [swap_z(after(b, t), m + 1) for m, b in enumerate(b_out)]
    near = jnp.stack([t, t1])
    near_now = after(near, *b_z)
    far = swap_z(near_now, 2)

    near0 = swap_y(near_now)
    near1 = swap_rep(near_now, 2)
    near01 = swap_rep(near0, 2)
    leave = call(leave_kernel, shape(4, 32, 256), [SMEM] + [VMEM] * 4, VMEM, [], LEAVE, 4, "leave")(
        place, blocks, *b_z
    )
    came = swap_y(leave)

    c_near = jnp.stack([coupling, c1])
    c_near_got = swap_y(c_near)

    left, both = call(
        rows_kernel,
        [shape(32, 1024), shape(2, 32, 1024)],
        [SMEM] + [VMEM] * 5,
        [VMEM] * 2,
        [],
        ROWS,
        4,
        "rows",
    )(place, blocks, *b_z, came)
    pair = jnp.stack([left, swap_rep(left, 2)])

    far_now = after(far, near0, near1, came, c_near)
    far0 = cross(far_now, 0)
    far1 = cross(far_now, 1)
    c_far = swap_z(after(c_near, far, near01, came), 2)
    c_far_got = swap_y(c_far)
    far01 = cross(after(far0, far1), 1)
    other_pair = swap_rep(after(pair, c_far), 1)

    bufs = [near, near0, near1, near01, far, far0, far1, far01]
    bufs += [swap_rep(b, 1) for b in bufs[:7]] + [swap_rep(after(far01, far1), 1)]

    scratch = [pltpu.VMEM((8, 136, 128), F32)]
    halves = [shape(1024, 1024, dtype=BF16)] * 2
    x = call(
        first_kernel,
        shape(128, 1024),
        [SMEM] + [VMEM] * 18,
        VMEM,
        [pltpu.VMEM((1024, 1024), BF16)] * 2 + scratch,
        FIRST,
        24,
        "first_panel",
    )(place, pair, after(other_pair, c_near_got), *bufs)

    mine, to_x, to_core, to_both = call(
        update_kernel,
        [shape(32, 256)] * 4,
        [SMEM] + [VMEM] * 5,
        [VMEM] * 4,
        [pltpu.VMEM((256, 1024), BF16)] * 2,
        2_000_000_000,
        24,
        "update",
    )(place, x, c_near, c_far, c_near_got, c_far_got)
    back = [swap_rep(to_x, 2), swap_rep(to_core, 1), swap_rep(to_both, 3)]

    uh, ul = call(
        second_factor_kernel, halves, [SMEM] + [VMEM] * 16, [VMEM] * 2, scratch, SECOND, 24, "second_factor"
    )(after(place, mine), *bufs)

    return call(second_kernel, shape(32, 2048), [SMEM] + [VMEM] * 8, VMEM, [], 2_500_000_000, 24, "second_panel")(
        place, x, both, uh, ul, mine, *back
    )


def solution(mesh):
    special = mesh.shape["bulk"] == 8 and mesh.shape["rep"] == 4

    def run(orbitals, triangles, coupling, diagonals):
        fits = orbitals.shape == (1024, 2048) and triangles.shape == (1024, 1024)
        body = per_device if special and fits else per_device_any
        return jax.shard_map(
            body,
            mesh=mesh,
            in_specs=(P("rep", "bulk"), P("rep", "bulk"), P("rep", "bulk"), P(None, "bulk")),
            out_specs=P(("rep", "bulk"), None),
            check_vma=False,
        )(orbitals, triangles, coupling, diagonals)

    return run
```

```python
import jax
import jax.numpy as jnp
from jax import lax
from jax.experimental import pallas as pl
from jax.experimental.pallas import tpu as pltpu
from jax.sharding import PartitionSpec as P

F32 = jnp.float32
BF16 = jnp.bfloat16
NN = (((1,), (0,)), ((), ()))
NT = (((1,), (1,)), ((), ()))


def unpack(triangles, diagonals):
    first_block = jnp.tril(triangles, -1) + jnp.diag(diagonals[0])
    second_block = jnp.tril(triangles.T, -1) + jnp.diag(diagonals[1])
    return (first_block, second_block)


def per_device_any(orbitals, triangles, coupling, diagonals):
    tri_rows, couple_rows = (
        lax.all_gather(triangles, "rep", axis=0, tiled=True),
        lax.all_gather(coupling, "rep", axis=0, tiled=True),
    )
    tri_whole, couple_whole, diag_whole = (
        lax.all_gather(tri_rows, "bulk", axis=1, tiled=True),
        lax.all_gather(couple_rows, "bulk", axis=1, tiled=True),
        lax.all_gather(diagonals, "bulk", axis=1, tiled=True),
    )
    first_block, second_block = unpack(tri_whole, diag_whole)
    panel = first_block.shape[0]
    groups = lax.axis_size("bulk")
    local_rows = orbitals.shape[0] // groups
    blocks = orbitals.reshape(groups, local_rows, orbitals.shape[1])
    received = lax.all_to_all(blocks, "bulk", split_axis=0, concat_axis=2, tiled=True)
    rows_now = received.reshape(local_rows, received.shape[2])
    left_part = rows_now[:, :panel]
    right_part = rows_now[:, panel:]
    solved_one = jax.scipy.linalg.solve_triangular(first_block, left_part.T, lower=True).T
    update = jnp.dot(
        solved_one,
        couple_whole.T,
        precision=lax.Precision.HIGHEST,
        preferred_element_type=jnp.float32,
    )
    solved_two = jax.scipy.linalg.solve_triangular(
        second_block, (right_part - update).T, lower=True
    ).T
    return jnp.concatenate([solved_one, solved_two], axis=1)


def dot(a, b, dims=NN):
    return lax.dot_general(a, b, dims, preferred_element_type=F32)


def dot_exact(a, b):
    return lax.dot_general(a, b, NN, precision=lax.Precision.HIGHEST, preferred_element_type=F32)


def split(x):
    high = x.astype(BF16)
    return high, (x - high.astype(F32)).astype(BF16)


def mul(x, b, dims=NN):
    xh, xl = split(x)
    bh, bl = b
    m = x.shape[0]
    both = dot(jnp.concatenate([xh, xl], axis=0), bh, dims)
    return (both[:m] + both[m:]) + dot(xh, bl, dims)


def mul3(a, b):
    (ah, al), (bh, bl) = split(a), split(b)
    return dot(ah, bh) + (dot(al, bh) + dot(ah, bl))


def iotas(n):
    return lax.broadcasted_iota(jnp.int32, (n, n), 0), lax.broadcasted_iota(jnp.int32, (n, n), 1)


def invert_kernel(place_ref, tri_ref, inv_ref, t_ref):
    rep, bulk = place_ref[0], place_ref[1]
    rows, n = tri_ref.shape
    inv = inv_ref[...]
    t_ref[0:rows, :] = tri_ref[...]
    t_ref[rows : rows + 8, :] = jnp.concatenate([inv, jnp.zeros((6, n), F32)], axis=0)

    @pl.when(rep == bulk // 2)
    def _():
        start = pl.multiple_of((bulk % 2) * n, n)
        block = tri_ref[pl.ds(start, n), :]
        i, j = iotas(n)
        eye = i == j
        ans = []
        for which in range(2):
            row, col = (i, j) if which == 0 else (j, i)
            along = inv[which : which + 1, :]
            d = jnp.where(eye, along, 0.0)
            down = jnp.sum(d, axis=1, keepdims=True)
            part = (row >> 1 == col >> 1) & (row > col)
            ans.append(d - jnp.where(part, block * along * down, 0.0))
        level = 1
        while (1 << level) < n:
            for which in range(2):
                row, col = (i, j) if which == 0 else (j, i)
                part = (row >> (level + 1) == col >> (level + 1)) & (row >> level > col >> level)
                t = ans[which]
                ans[which] = t - mul3(mul3(t, jnp.where(part, block, 0.0)), t)
            level += 1
        t_ref[pl.ds(start, n), :] = jnp.where(i >= j, ans[0], ans[1])


def spread_kernel(place_ref, orb, b1, b2, b3):
    z = place_ref[1] >> 1
    for m, ref in ((1, b1), (2, b2), (3, b3)):
        ref[...] = orb[z ^ m]


def leave_kernel(place_ref, orb, b1, b2, b3, out):
    z, y = place_ref[1] >> 1, place_ref[1] & 1
    out[0] = orb[z, 1 - y]
    for m, ref in ((1, b1), (2, b2), (3, b3)):
        out[m] = ref[1 - y]


def rows_kernel(place_ref, orb, b1, b2, b3, came, left, both):
    z, y = place_ref[1] >> 1, place_ref[1] & 1

    def put(m, dy, value):
        k = 2 * (z ^ m) + (y ^ dy)
        both[k >> 2, :, pl.ds(pl.multiple_of((k & 3) * 256, 256), 256)] = value

    put(0, 0, orb[z, y])
    for m, ref in ((1, b1), (2, b2), (3, b3)):
        put(m, 0, ref[y])
    for m in range(4):
        put(m, 1, came[m])
    left[...] = both[0]


def pair_kernel(left, left_x, later, out):
    out[0] = left[...]
    out[1] = left_x[...]


def origin(place_ref, crossed, first, second, m):
    rep, bulk = place_ref[0], place_ref[1]
    if m < 2:
        dx, dy = second, first
    else:
        core = (rep & 1) ^ crossed
        dx = jnp.where(core == 0, first, second)
        dy = jnp.where(core == 0, second, first)
    return rep ^ (2 * dx + crossed), bulk ^ (2 * m + dy)


def pieces(bufs):
    found = []
    for crossed in range(2):
        for m in range(4):
            for second in range(2):
                for first in range(2):
                    buf = bufs[8 * crossed + 4 * (m // 2) + 2 * second + first]
                    found.append((buf.at[m % 2], (crossed, first, second, m)))
    return found


def offset(index, size):
    return pl.ds(pl.multiple_of(index * size, size), size)


def place_pieces(place_ref, bufs, upper, high, low, diag):
    for piece, args in pieces(bufs):
        rep, bulk = origin(place_ref, *args)

        @pl.when((rep <= bulk // 2) if upper else (rep >= bulk // 2))
        def _():
            h, l = split(piece[0:256, :])
            high[offset(rep, 256), offset(bulk, 128)] = h
            low[offset(rep, 256), offset(bulk, 128)] = l

        @pl.when(rep == bulk // 2)
        def _():
            diag[bulk, 0:128, :] = piece[pl.ds(pl.multiple_of((bulk % 2) * 128, 128), 128), :]
            diag[bulk, 128:136, :] = piece[256:264, :]


def mul_pairs(a, b):
    (ah, al), (bh, bl) = a, b
    return dot(ah, bh) + (dot(al, bh) + dot(ah, bl))


def pair_of(high, low, r, c, size):
    rows, cols = slice(r, r + size), slice(c, c + size)
    return high[rows, cols], low[rows, cols]


def join(a, b, c, d):
    return jnp.concatenate([jnp.concatenate([a, b], axis=1), jnp.concatenate([c, d], axis=1)], axis=0)


def first_kernel(place_ref, pair, other_pair, *refs):
    bufs, (x_ref, high, low, diag) = refs[:16], refs[16:]
    place_pieces(place_ref, bufs, False, high, low, diag)
    n = 128
    i, j = iotas(n)

    def block(k):
        return jnp.where(i > j, diag[k, 0:n, :], 0.0) + jnp.where(i == j, diag[k, n : n + 1, :], 0.0)

    zero = jnp.zeros((n, n), F32)
    inverses = []
    for k in range(4):
        ta, tb = block(2 * k), block(2 * k + 1)
        pa, pb = split(ta), split(tb)
        off = -mul_pairs(split(mul_pairs(pb, pair_of(high, low, 256 * k + n, 256 * k, n))), pa)
        inverses.append(split(join(ta, zero, off, tb)))

    rest = jnp.concatenate([pair[0], pair[1], other_pair[0], other_pair[1]], axis=0)
    for k in range(4):
        x = mul(rest[:, :256], inverses[k], NT)
        x_ref[:, k * 256 : (k + 1) * 256] = x
        if k < 3:
            rows, cols = slice((k + 1) * 256, 1024), slice(k * 256, (k + 1) * 256)
            rest = rest[:, 256:] - mul(x, (high[rows, cols], low[rows, cols]), NT)


def update_kernel(place_ref, x_ref, *refs):
    held, outs, (high, low) = refs[:4], refs[4:8], refs[8:]
    bulk = place_ref[1]
    for dy in range(2):
        for m in range(4):
            h, l = split(held[2 * dy + m // 2][m % 2])
            high[:, offset(bulk ^ (2 * m + dy), 128)] = h
            low[:, offset(bulk ^ (2 * m + dy), 128)] = l
    upd = mul(x_ref[...], (high[...], low[...]), NT)
    for k, out in enumerate(outs):
        out[...] = upd[32 * k : 32 * (k + 1)]


def second_factor_kernel(place_ref, *refs):
    bufs, (high, low, diag) = refs[:16], refs[16:]
    place_pieces(place_ref, bufs, True, high, low, diag)
    n = 128
    i, j = iotas(n)

    def block(k):
        return jnp.where(i < j, diag[k, 0:n, :], 0.0) + jnp.where(i == j, diag[k, n + 1 : n + 2, :], 0.0)

    zero = jnp.zeros((n, n), F32)
    inverses = []
    for k in range(4):
        ta, tb = block(2 * k), block(2 * k + 1)
        pa, pb = split(ta), split(tb)
        off = -mul_pairs(split(mul_pairs(pa, pair_of(high, low, 256 * k, 256 * k + n, n))), pb)
        inverses.append(split(join(ta, off, zero, tb)))

    def put(r, c, value):
        high[r : r + 256, c : c + 256], low[r : r + 256, c : c + 256] = value

    for k in range(2):
        at = 512 * k
        pa, pb = inverses[2 * k], inverses[2 * k + 1]
        off = -mul_pairs(split(mul_pairs(pa, pair_of(high, low, at, at + 256, 256))), pb)
        put(at, at, pa)
        put(at + 256, at + 256, pb)
        put(at, at + 256, split(off))
        put(at + 256, at, (jnp.zeros((256, 256), BF16),) * 2)


def second_kernel(place_ref, x_ref, both_ref, uh_ref, ul_ref, mine, from_x, from_core, from_both, out_ref):
    x = x_ref[0:32, :]
    out_ref[:, 0:1024] = x
    parts = []
    for k in range(4):
        way = place_ref[0] ^ k
        upd = jnp.where(
            way == 0,
            mine[...],
            jnp.where(way == 2, from_x[...], jnp.where(way == 1, from_core[...], from_both[...])),
        )
        parts.append(both_ref[1, :, k * 256 : (k + 1) * 256] - upd)
    ra = jnp.concatenate(parts[:2], axis=1)
    rb = jnp.concatenate(parts[2:], axis=1)

    def u(r, c):
        rows, cols = slice(r * 512, r * 512 + 512), slice(c * 512, c * 512 + 512)
        return uh_ref[rows, cols], ul_ref[rows, cols]

    xa = mul(ra, u(0, 0))
    xb = mul(rb - mul(xa, u(0, 1)), u(1, 1))
    out_ref[:, 1024:1536] = xa
    out_ref[:, 1536:2048] = xb


BOTH = ("bulk", "rep")

SPREAD, INVERT, LEAVE, ROWS, FIRST, SECOND, PAIR = 1_000_000_000, 3_500_000_000, 500_000_000, 1_000_000_000, 200_000_000, 3_000_000_000, 4_000_000_000


def swap_z(x, m):
    return lax.ppermute(x, "bulk", [(k, k ^ (2 * m)) for k in range(8)])


def swap_y(x):
    return lax.ppermute(x, "bulk", [(k, k ^ 1) for k in range(8)])


def swap_xy(x):
    return lax.ppermute(x, BOTH, [(k, k ^ 6) for k in range(32)])


def swap_rep(x, bits):
    return lax.ppermute(x, "rep", [(k, k ^ bits) for k in range(4)])


def cross(x, stage):
    pairs = []
    for rep in range(4):
        for bulk in range(8):
            to = (rep ^ 2, bulk) if (rep & 1) == stage else (rep, bulk ^ 1)
            pairs.append((bulk * 4 + rep, to[1] * 4 + to[0]))
    return lax.ppermute(x, BOTH, pairs)


def after(x, *deps):
    return lax.optimization_barrier((x,) + deps)[0]


ANY = pl.BlockSpec(memory_space=pl.ANY)
VMEM = pl.BlockSpec(memory_space=pltpu.VMEM)
SMEM = pl.BlockSpec(memory_space=pltpu.SMEM)


def call(kernel, out, specs, outs, scratch, flops, size, name):
    return pl.pallas_call(
        kernel,
        out_shape=out,
        in_specs=specs,
        out_specs=outs,
        scratch_shapes=scratch,
        compiler_params=pltpu.CompilerParams(vmem_limit_bytes=size << 20),
        cost_estimate=pl.CostEstimate(flops=flops, bytes_accessed=2 << 20, transcendentals=0),
        name=name,
    )


def shape(*dims, dtype=F32):
    return jax.ShapeDtypeStruct(dims, dtype)


def per_device(orbitals, triangles, coupling, diagonals):
    rep, bulk = lax.axis_index("rep"), lax.axis_index("bulk")
    place = jnp.stack([rep, bulk]).astype(jnp.int32)
    blocks = orbitals.reshape(4, 2, 32, 256)

    t = call(invert_kernel, shape(264, 128), [SMEM, VMEM, VMEM], VMEM, [], INVERT, 4, "invert")(
        place, triangles, 1.0 / diagonals
    )
    c1 = swap_z(after(coupling, t), 1)

    t1 = swap_z(t, 1)
    b_out = call(spread_kernel, [shape(2, 32, 256)] * 3, [SMEM, VMEM], [VMEM] * 3, [], SPREAD, 4, "spread")(
        place, blocks
    )
    b_z = [swap_z(after(b, t), m + 1) for m, b in enumerate(b_out)]
    near = jnp.stack([t, t1])
    near_now = after(near, *b_z)
    far = swap_z(near_now, 2)

    near0 = swap_y(near_now)
    near1 = swap_rep(near_now, 2)
    near01 = swap_rep(near0, 2)
    leave = call(leave_kernel, shape(4, 32, 256), [SMEM] + [VMEM] * 4, VMEM, [], LEAVE, 4, "leave")(
        place, blocks, *b_z
    )
    came = swap_y(leave)

    c_near = jnp.stack([coupling, c1])
    c_near_got = swap_y(c_near)

    left, both = call(
        rows_kernel,
        [shape(32, 1024), shape(2, 32, 1024)],
        [SMEM] + [VMEM] * 5,
        [VMEM] * 2,
        [],
        ROWS,
        4,
        "rows",
    )(place, blocks, *b_z, came)
    left_x = swap_rep(left, 2)

    far_now = after(far, came, c_near)
    far0 = cross(far_now, 0)
    far1 = cross(far_now, 1)
    c_far = swap_z(after(c_near, far, near01, near1), 2)
    c_far_got = swap_y(c_far)
    swaps = [swap_rep(b, 1) for b in (near, near0, near1, near01, far)]
    far01 = cross(after(far0, far1, *swaps[:3]), 1)
    pair = call(pair_kernel, shape(2, 32, 1024), [VMEM] * 3, VMEM, [], PAIR, 4, "pair")(left, left_x, c_far)
    other_pair = swap_rep(pair, 1)

    bufs = [near, near0, near1, near01, far, far0, far1, far01]
    bufs += swaps + [swap_rep(b, 1) for b in bufs[5:7]] + [swap_rep(after(far01, far1), 1)]

    scratch = [pltpu.VMEM((8, 136, 128), F32)]
    halves = [shape(1024, 1024, dtype=BF16)] * 2
    x = call(
        first_kernel,
        shape(128, 1024),
        [SMEM] + [VMEM] * 18,
        VMEM,
        [pltpu.VMEM((1024, 1024), BF16)] * 2 + scratch,
        FIRST,
        24,
        "first_panel",
    )(place, pair, after(other_pair, c_near_got), *bufs)

    mine, to_x, to_core, to_both = call(
        update_kernel,
        [shape(32, 256)] * 4,
        [SMEM] + [VMEM] * 5,
        [VMEM] * 4,
        [pltpu.VMEM((256, 1024), BF16)] * 2,
        2_000_000_000,
        24,
        "update",
    )(place, x, c_near, c_far, c_near_got, c_far_got)
    back = [swap_rep(to_x, 2), swap_rep(to_core, 1), swap_rep(to_both, 3)]

    uh, ul = call(
        second_factor_kernel, halves, [SMEM] + [VMEM] * 16, [VMEM] * 2, scratch, SECOND, 24, "second_factor"
    )(after(place, mine), *bufs)

    return call(second_kernel, shape(32, 2048), [SMEM] + [VMEM] * 8, VMEM, [], 2_500_000_000, 24, "second_panel")(
        place, x, both, uh, ul, mine, *back
    )


def solution(mesh):
    special = mesh.shape["bulk"] == 8 and mesh.shape["rep"] == 4

    def run(orbitals, triangles, coupling, diagonals):
        fits = orbitals.shape == (1024, 2048) and triangles.shape == (1024, 1024)
        body = per_device if special and fits else per_device_any
        return jax.shard_map(
            body,
            mesh=mesh,
            in_specs=(P("rep", "bulk"), P("rep", "bulk"), P("rep", "bulk"), P(None, "bulk")),
            out_specs=P(("rep", "bulk"), None),
            check_vma=False,
        )(orbitals, triangles, coupling, diagonals)

    return run
```

```python
import jax
import jax.numpy as jnp
from jax import lax
from jax.experimental import pallas as pl
from jax.experimental.pallas import tpu as pltpu
from jax.sharding import PartitionSpec as P

F32 = jnp.float32
BF16 = jnp.bfloat16
NN = (((1,), (0,)), ((), ()))
NT = (((1,), (1,)), ((), ()))


def unpack(triangles, diagonals):
    first_block = jnp.tril(triangles, -1) + jnp.diag(diagonals[0])
    second_block = jnp.tril(triangles.T, -1) + jnp.diag(diagonals[1])
    return (first_block, second_block)


def per_device_any(orbitals, triangles, coupling, diagonals):
    tri_rows, couple_rows = (
        lax.all_gather(triangles, "rep", axis=0, tiled=True),
        lax.all_gather(coupling, "rep", axis=0, tiled=True),
    )
    tri_whole, couple_whole, diag_whole = (
        lax.all_gather(tri_rows, "bulk", axis=1, tiled=True),
        lax.all_gather(couple_rows, "bulk", axis=1, tiled=True),
        lax.all_gather(diagonals, "bulk", axis=1, tiled=True),
    )
    first_block, second_block = unpack(tri_whole, diag_whole)
    panel = first_block.shape[0]
    groups = lax.axis_size("bulk")
    local_rows = orbitals.shape[0] // groups
    blocks = orbitals.reshape(groups, local_rows, orbitals.shape[1])
    received = lax.all_to_all(blocks, "bulk", split_axis=0, concat_axis=2, tiled=True)
    rows_now = received.reshape(local_rows, received.shape[2])
    left_part = rows_now[:, :panel]
    right_part = rows_now[:, panel:]
    solved_one = jax.scipy.linalg.solve_triangular(first_block, left_part.T, lower=True).T
    update = jnp.dot(
        solved_one,
        couple_whole.T,
        precision=lax.Precision.HIGHEST,
        preferred_element_type=jnp.float32,
    )
    solved_two = jax.scipy.linalg.solve_triangular(
        second_block, (right_part - update).T, lower=True
    ).T
    return jnp.concatenate([solved_one, solved_two], axis=1)


def dot(a, b, dims=NN):
    return lax.dot_general(a, b, dims, preferred_element_type=F32)


def dot_exact(a, b):
    return lax.dot_general(a, b, NN, precision=lax.Precision.HIGHEST, preferred_element_type=F32)


def split(x):
    high = x.astype(BF16)
    return high, (x - high.astype(F32)).astype(BF16)


def mul(x, b, dims=NN):
    xh, xl = split(x)
    bh, bl = b
    m = x.shape[0]
    both = dot(jnp.concatenate([xh, xl], axis=0), bh, dims)
    return (both[:m] + both[m:]) + dot(xh, bl, dims)


def mul3(a, b):
    (ah, al), (bh, bl) = split(a), split(b)
    return dot(ah, bh) + (dot(al, bh) + dot(ah, bl))


def iotas(n):
    return lax.broadcasted_iota(jnp.int32, (n, n), 0), lax.broadcasted_iota(jnp.int32, (n, n), 1)


def invert_kernel(place_ref, tri_ref, inv_ref, t_ref):
    rep, bulk = place_ref[0], place_ref[1]
    rows, n = tri_ref.shape
    inv = inv_ref[...]
    t_ref[0:rows, :] = tri_ref[...]
    t_ref[rows : rows + 8, :] = jnp.concatenate([inv, jnp.zeros((6, n), F32)], axis=0)

    @pl.when(rep == bulk // 2)
    def _():
        start = pl.multiple_of((bulk % 2) * n, n)
        block = tri_ref[pl.ds(start, n), :]
        i, j = iotas(n)
        eye = i == j
        ans = []
        for which in range(2):
            row, col = (i, j) if which == 0 else (j, i)
            along = inv[which : which + 1, :]
            d = jnp.where(eye, along, 0.0)
            down = jnp.sum(d, axis=1, keepdims=True)
            part = (row >> 1 == col >> 1) & (row > col)
            ans.append(d - jnp.where(part, block * along * down, 0.0))
        level = 1
        while (1 << level) < n:
            for which in range(2):
                row, col = (i, j) if which == 0 else (j, i)
                part = (row >> (level + 1) == col >> (level + 1)) & (row >> level > col >> level)
                t = ans[which]
                ans[which] = t - mul3(mul3(t, jnp.where(part, block, 0.0)), t)
            level += 1
        t_ref[pl.ds(start, n), :] = jnp.where(i >= j, ans[0], ans[1])


def spread_kernel(place_ref, orb, b1, b2, b3):
    z = place_ref[1] >> 1
    for m, ref in ((1, b1), (2, b2), (3, b3)):
        ref[...] = orb[z ^ m]


def leave_kernel(place_ref, orb, b1, b2, b3, out):
    z, y = place_ref[1] >> 1, place_ref[1] & 1
    out[0] = orb[z, 1 - y]
    for m, ref in ((1, b1), (2, b2), (3, b3)):
        out[m] = ref[1 - y]


def rows_kernel(place_ref, orb, b1, b2, b3, came, left, both):
    z, y = place_ref[1] >> 1, place_ref[1] & 1

    def put(m, dy, value):
        k = 2 * (z ^ m) + (y ^ dy)
        both[k >> 2, :, pl.ds(pl.multiple_of((k & 3) * 256, 256), 256)] = value

    put(0, 0, orb[z, y])
    for m, ref in ((1, b1), (2, b2), (3, b3)):
        put(m, 0, ref[y])
    for m in range(4):
        put(m, 1, came[m])
    left[...] = both[0]


def pair_kernel(left, left_x, later, out):
    out[0] = left[...]
    out[1] = left_x[...]


def origin(place_ref, crossed, first, second, m):
    rep, bulk = place_ref[0], place_ref[1]
    if m < 2:
        dx, dy = second, first
    else:
        core = (rep & 1) ^ crossed
        dx = jnp.where(core == 0, first, second)
        dy = jnp.where(core == 0, second, first)
    return rep ^ (2 * dx + crossed), bulk ^ (2 * m + dy)


def pieces(bufs):
    found = []
    for crossed in range(2):
        for m in range(4):
            for second in range(2):
                for first in range(2):
                    buf = bufs[8 * crossed + 4 * (m // 2) + 2 * second + first]
                    found.append((buf.at[m % 2], (crossed, first, second, m)))
    return found


def offset(index, size):
    return pl.ds(pl.multiple_of(index * size, size), size)


def place_pieces(place_ref, bufs, upper, high, low, diag):
    for piece, args in pieces(bufs):
        rep, bulk = origin(place_ref, *args)

        @pl.when((rep <= bulk // 2) if upper else (rep >= bulk // 2))
        def _():
            h, l = split(piece[0:256, :])
            high[offset(rep, 256), offset(bulk, 128)] = h
            low[offset(rep, 256), offset(bulk, 128)] = l

        @pl.when(rep == bulk // 2)
        def _():
            diag[bulk, 0:128, :] = piece[pl.ds(pl.multiple_of((bulk % 2) * 128, 128), 128), :]
            diag[bulk, 128:136, :] = piece[256:264, :]


def mul_pairs(a, b):
    (ah, al), (bh, bl) = a, b
    return dot(ah, bh) + (dot(al, bh) + dot(ah, bl))


def pair_of(high, low, r, c, size):
    rows, cols = slice(r, r + size), slice(c, c + size)
    return high[rows, cols], low[rows, cols]


def join(a, b, c, d):
    return jnp.concatenate([jnp.concatenate([a, b], axis=1), jnp.concatenate([c, d], axis=1)], axis=0)


def first_kernel(place_ref, pair, other_pair, *refs):
    bufs, (x_ref, high, low, diag) = refs[:16], refs[16:]
    place_pieces(place_ref, bufs, False, high, low, diag)
    n = 128
    i, j = iotas(n)

    def block(k):
        return jnp.where(i > j, diag[k, 0:n, :], 0.0) + jnp.where(i == j, diag[k, n : n + 1, :], 0.0)

    zero = jnp.zeros((n, n), F32)
    inverses = []
    for k in range(4):
        ta, tb = block(2 * k), block(2 * k + 1)
        pa, pb = split(ta), split(tb)
        off = -mul_pairs(split(mul_pairs(pb, pair_of(high, low, 256 * k + n, 256 * k, n))), pa)
        inverses.append(split(join(ta, zero, off, tb)))

    rest = jnp.concatenate([pair[0], pair[1], other_pair[0], other_pair[1]], axis=0)
    for k in range(4):
        x = mul(rest[:, :256], inverses[k], NT)
        x_ref[:, k * 256 : (k + 1) * 256] = x
        if k < 3:
            rows, cols = slice((k + 1) * 256, 1024), slice(k * 256, (k + 1) * 256)
            rest = rest[:, 256:] - mul(x, (high[rows, cols], low[rows, cols]), NT)


def update_kernel(place_ref, x_ref, *refs):
    held, outs, (high, low) = refs[:4], refs[4:8], refs[8:]
    bulk = place_ref[1]
    for dy in range(2):
        for m in range(4):
            h, l = split(held[2 * dy + m // 2][m % 2])
            high[:, offset(bulk ^ (2 * m + dy), 128)] = h
            low[:, offset(bulk ^ (2 * m + dy), 128)] = l
    upd = mul(x_ref[...], (high[...], low[...]), NT)
    for k, out in enumerate(outs):
        out[...] = upd[32 * k : 32 * (k + 1)]


def second_factor_kernel(place_ref, *refs):
    bufs, (high, low, diag) = refs[:16], refs[16:]
    place_pieces(place_ref, bufs, True, high, low, diag)
    n = 128
    i, j = iotas(n)

    def block(k):
        return jnp.where(i < j, diag[k, 0:n, :], 0.0) + jnp.where(i == j, diag[k, n + 1 : n + 2, :], 0.0)

    zero = jnp.zeros((n, n), F32)
    inverses = []
    for k in range(4):
        ta, tb = block(2 * k), block(2 * k + 1)
        pa, pb = split(ta), split(tb)
        off = -mul_pairs(split(mul_pairs(pa, pair_of(high, low, 256 * k, 256 * k + n, n))), pb)
        inverses.append(split(join(ta, off, zero, tb)))

    def put(r, c, value):
        high[r : r + 256, c : c + 256], low[r : r + 256, c : c + 256] = value

    for k in range(2):
        at = 512 * k
        pa, pb = inverses[2 * k], inverses[2 * k + 1]
        off = -mul_pairs(split(mul_pairs(pa, pair_of(high, low, at, at + 256, 256))), pb)
        put(at, at, pa)
        put(at + 256, at + 256, pb)
        put(at, at + 256, split(off))
        put(at + 256, at, (jnp.zeros((256, 256), BF16),) * 2)


def second_kernel(place_ref, x_ref, both_ref, uh_ref, ul_ref, mine, from_x, from_core, from_both, out_ref):
    x = x_ref[0:32, :]
    out_ref[:, 0:1024] = x
    parts = []
    for k in range(4):
        way = place_ref[0] ^ k
        upd = jnp.where(
            way == 0,
            mine[...],
            jnp.where(way == 2, from_x[...], jnp.where(way == 1, from_core[...], from_both[...])),
        )
        parts.append(both_ref[1, :, k * 256 : (k + 1) * 256] - upd)
    ra = jnp.concatenate(parts[:2], axis=1)
    rb = jnp.concatenate(parts[2:], axis=1)

    def u(r, c):
        rows, cols = slice(r * 512, r * 512 + 512), slice(c * 512, c * 512 + 512)
        return uh_ref[rows, cols], ul_ref[rows, cols]

    xa = mul(ra, u(0, 0))
    xb = mul(rb - mul(xa, u(0, 1)), u(1, 1))
    out_ref[:, 1024:1536] = xa
    out_ref[:, 1536:2048] = xb


BOTH = ("bulk", "rep")

SPREAD, INVERT, LEAVE, ROWS, FIRST, SECOND, PAIR = 1_000_000_000, 3_500_000_000, 500_000_000, 1_000_000_000, 200_000_000, 3_000_000_000, 4_000_000_000


def swap_z(x, m):
    return lax.ppermute(x, "bulk", [(k, k ^ (2 * m)) for k in range(8)])


def swap_y(x):
    return lax.ppermute(x, "bulk", [(k, k ^ 1) for k in range(8)])


def swap_xy(x):
    return lax.ppermute(x, BOTH, [(k, k ^ 6) for k in range(32)])


def swap_rep(x, bits):
    return lax.ppermute(x, "rep", [(k, k ^ bits) for k in range(4)])


def cross(x, stage):
    pairs = []
    for rep in range(4):
        for bulk in range(8):
            to = (rep ^ 2, bulk) if (rep & 1) == stage else (rep, bulk ^ 1)
            pairs.append((bulk * 4 + rep, to[1] * 4 + to[0]))
    return lax.ppermute(x, BOTH, pairs)


def after(x, *deps):
    return lax.optimization_barrier((x,) + deps)[0]


ANY = pl.BlockSpec(memory_space=pl.ANY)
VMEM = pl.BlockSpec(memory_space=pltpu.VMEM)
SMEM = pl.BlockSpec(memory_space=pltpu.SMEM)


def call(kernel, out, specs, outs, scratch, flops, size, name):
    return pl.pallas_call(
        kernel,
        out_shape=out,
        in_specs=specs,
        out_specs=outs,
        scratch_shapes=scratch,
        compiler_params=pltpu.CompilerParams(vmem_limit_bytes=size << 20),
        cost_estimate=pl.CostEstimate(flops=flops, bytes_accessed=2 << 20, transcendentals=0),
        name=name,
    )


def shape(*dims, dtype=F32):
    return jax.ShapeDtypeStruct(dims, dtype)


def per_device(orbitals, triangles, coupling, diagonals):
    rep, bulk = lax.axis_index("rep"), lax.axis_index("bulk")
    place = jnp.stack([rep, bulk]).astype(jnp.int32)
    blocks = orbitals.reshape(4, 2, 32, 256)

    t = call(invert_kernel, shape(264, 128), [SMEM, VMEM, VMEM], VMEM, [], INVERT, 4, "invert")(
        place, triangles, 1.0 / diagonals
    )
    c1 = swap_z(after(coupling, t), 1)

    t1 = swap_z(t, 1)
    b_out = call(spread_kernel, [shape(2, 32, 256)] * 3, [SMEM, VMEM], [VMEM] * 3, [], SPREAD, 4, "spread")(
        place, blocks
    )
    b_z = [swap_z(after(b, t), m + 1) for m, b in enumerate(b_out)]
    near = jnp.stack([t, t1])
    near_now = after(near, *b_z)
    far = swap_z(near_now, 2)

    near0 = swap_y(near_now)
    near1 = swap_rep(near_now, 2)
    near01 = swap_rep(near0, 2)
    leave = call(leave_kernel, shape(4, 32, 256), [SMEM] + [VMEM] * 4, VMEM, [], LEAVE, 4, "leave")(
        place, blocks, *b_z
    )
    came = swap_y(leave)

    c_near = jnp.stack([coupling, c1])
    c_near_got = swap_y(c_near)

    left, both = call(
        rows_kernel,
        [shape(32, 1024), shape(2, 32, 1024)],
        [SMEM] + [VMEM] * 5,
        [VMEM] * 2,
        [],
        ROWS,
        4,
        "rows",
    )(place, blocks, *b_z, came)
    left_x = swap_rep(left, 2)

    far_now = after(far, came)
    far0 = cross(far_now, 0)
    far1 = cross(far_now, 1)
    c_far = swap_z(after(c_near, far, near01, near1), 2)
    c_far_got = swap_y(c_far)
    swaps = [swap_rep(b, 1) for b in (near, near0, near1, near01, far)]
    far01 = cross(after(far0, far1, *swaps[:3]), 1)
    pair = call(pair_kernel, shape(2, 32, 1024), [VMEM] * 3, VMEM, [], PAIR, 4, "pair")(left, left_x, c_far)
    other_pair = swap_rep(pair, 1)

    bufs = [near, near0, near1, near01, far, far0, far1, far01]
    bufs += swaps + [swap_rep(b, 1) for b in bufs[5:7]] + [swap_rep(after(far01, far1), 1)]

    scratch = [pltpu.VMEM((8, 136, 128), F32)]
    halves = [shape(1024, 1024, dtype=BF16)] * 2
    x = call(
        first_kernel,
        shape(128, 1024),
        [SMEM] + [VMEM] * 18,
        VMEM,
        [pltpu.VMEM((1024, 1024), BF16)] * 2 + scratch,
        FIRST,
        24,
        "first_panel",
    )(place, pair, after(other_pair, c_near_got), *bufs)

    mine, to_x, to_core, to_both = call(
        update_kernel,
        [shape(32, 256)] * 4,
        [SMEM] + [VMEM] * 5,
        [VMEM] * 4,
        [pltpu.VMEM((256, 1024), BF16)] * 2,
        2_000_000_000,
        24,
        "update",
    )(place, x, c_near, c_far, c_near_got, c_far_got)
    back = [swap_rep(to_x, 2), swap_rep(to_core, 1), swap_rep(to_both, 3)]

    uh, ul = call(
        second_factor_kernel, halves, [SMEM] + [VMEM] * 16, [VMEM] * 2, scratch, SECOND, 24, "second_factor"
    )(after(place, mine), *bufs)

    return call(second_kernel, shape(32, 2048), [SMEM] + [VMEM] * 8, VMEM, [], 2_500_000_000, 24, "second_panel")(
        place, x, both, uh, ul, mine, *back
    )


def solution(mesh):
    special = mesh.shape["bulk"] == 8 and mesh.shape["rep"] == 4

    def run(orbitals, triangles, coupling, diagonals):
        fits = orbitals.shape == (1024, 2048) and triangles.shape == (1024, 1024)
        body = per_device if special and fits else per_device_any
        return jax.shard_map(
            body,
            mesh=mesh,
            in_specs=(P("rep", "bulk"), P("rep", "bulk"), P("rep", "bulk"), P(None, "bulk")),
            out_specs=P(("rep", "bulk"), None),
            check_vma=False,
        )(orbitals, triangles, coupling, diagonals)

    return run
```

```python
import jax
import jax.numpy as jnp
from jax import lax
from jax.experimental import pallas as pl
from jax.experimental.pallas import tpu as pltpu
from jax.sharding import PartitionSpec as P

F32 = jnp.float32
BF16 = jnp.bfloat16
NN = (((1,), (0,)), ((), ()))
NT = (((1,), (1,)), ((), ()))


def unpack(triangles, diagonals):
    first_block = jnp.tril(triangles, -1) + jnp.diag(diagonals[0])
    second_block = jnp.tril(triangles.T, -1) + jnp.diag(diagonals[1])
    return (first_block, second_block)


def per_device_any(orbitals, triangles, coupling, diagonals):
    tri_rows, couple_rows = (
        lax.all_gather(triangles, "rep", axis=0, tiled=True),
        lax.all_gather(coupling, "rep", axis=0, tiled=True),
    )
    tri_whole, couple_whole, diag_whole = (
        lax.all_gather(tri_rows, "bulk", axis=1, tiled=True),
        lax.all_gather(couple_rows, "bulk", axis=1, tiled=True),
        lax.all_gather(diagonals, "bulk", axis=1, tiled=True),
    )
    first_block, second_block = unpack(tri_whole, diag_whole)
    panel = first_block.shape[0]
    groups = lax.axis_size("bulk")
    local_rows = orbitals.shape[0] // groups
    blocks = orbitals.reshape(groups, local_rows, orbitals.shape[1])
    received = lax.all_to_all(blocks, "bulk", split_axis=0, concat_axis=2, tiled=True)
    rows_now = received.reshape(local_rows, received.shape[2])
    left_part = rows_now[:, :panel]
    right_part = rows_now[:, panel:]
    solved_one = jax.scipy.linalg.solve_triangular(first_block, left_part.T, lower=True).T
    update = jnp.dot(
        solved_one,
        couple_whole.T,
        precision=lax.Precision.HIGHEST,
        preferred_element_type=jnp.float32,
    )
    solved_two = jax.scipy.linalg.solve_triangular(
        second_block, (right_part - update).T, lower=True
    ).T
    return jnp.concatenate([solved_one, solved_two], axis=1)


def dot(a, b, dims=NN):
    return lax.dot_general(a, b, dims, preferred_element_type=F32)


def dot_exact(a, b):
    return lax.dot_general(a, b, NN, precision=lax.Precision.HIGHEST, preferred_element_type=F32)


def split(x):
    high = x.astype(BF16)
    return high, (x - high.astype(F32)).astype(BF16)


def mul(x, b, dims=NN):
    xh, xl = split(x)
    bh, bl = b
    m = x.shape[0]
    both = dot(jnp.concatenate([xh, xl], axis=0), bh, dims)
    return (both[:m] + both[m:]) + dot(xh, bl, dims)


def mul3(a, b):
    (ah, al), (bh, bl) = split(a), split(b)
    return dot(ah, bh) + (dot(al, bh) + dot(ah, bl))


def iotas(n):
    return lax.broadcasted_iota(jnp.int32, (n, n), 0), lax.broadcasted_iota(jnp.int32, (n, n), 1)


def invert_kernel(place_ref, tri_ref, diag_ref, t_ref):
    rep, bulk = place_ref[0], place_ref[1]
    rows, n = tri_ref.shape
    inv = 1.0 / diag_ref[...]
    t_ref[0:rows, :] = tri_ref[...]
    t_ref[rows : rows + 8, :] = jnp.concatenate([inv, jnp.zeros((6, n), F32)], axis=0)

    @pl.when(rep == bulk // 2)
    def _():
        start = pl.multiple_of((bulk % 2) * n, n)
        block = tri_ref[pl.ds(start, n), :]
        i, j = iotas(n)
        eye = i == j
        ans = []
        for which in range(2):
            row, col = (i, j) if which == 0 else (j, i)
            along = inv[which : which + 1, :]
            d = jnp.where(eye, along, 0.0)
            down = jnp.sum(d, axis=1, keepdims=True)
            part = (row >> 1 == col >> 1) & (row > col)
            ans.append(d - jnp.where(part, block * along * down, 0.0))
        level = 1
        while (1 << level) < n:
            for which in range(2):
                row, col = (i, j) if which == 0 else (j, i)
                part = (row >> (level + 1) == col >> (level + 1)) & (row >> level > col >> level)
                t = ans[which]
                ans[which] = t - mul3(mul3(t, jnp.where(part, block, 0.0)), t)
            level += 1
        t_ref[pl.ds(start, n), :] = jnp.where(i >= j, ans[0], ans[1])


def leave_kernel(place_ref, orb, out):
    y = place_ref[1] & 1
    for k in range(4):
        out[k] = orb[k, 1 - y]


def spread_kernel(place_ref, orb, came, b1, b2, b3):
    z, y = place_ref[1] >> 1, place_ref[1] & 1
    for m, ref in ((1, b1), (2, b2), (3, b3)):
        ref[0] = orb[z ^ m, y]
        ref[1] = came[z ^ m]


def rows_kernel(place_ref, orb, came, b1, b2, b3, left, both):
    z, y = place_ref[1] >> 1, place_ref[1] & 1

    def put(m, dy, value):
        k = 2 * (z ^ m) + (y ^ dy)
        both[k >> 2, :, pl.ds(pl.multiple_of((k & 3) * 256, 256), 256)] = value

    put(0, 0, orb[z, y])
    put(0, 1, came[z])
    for m, ref in ((1, b1), (2, b2), (3, b3)):
        put(m, 0, ref[0])
        put(m, 1, ref[1])
    left[...] = both[0]


def origin(place_ref, crossed, first, second, m):
    rep, bulk = place_ref[0], place_ref[1]
    if m % 2 == 0:
        dx, dy = second, first
    else:
        core = (rep & 1) ^ crossed
        dx = jnp.where(core == 0, first, second)
        dy = jnp.where(core == 0, second, first)
    return rep ^ (2 * dx + crossed), bulk ^ (2 * m + dy)


def pieces(bufs):
    found = []
    for crossed in range(2):
        for m in range(4):
            for second in range(2):
                for first in range(2):
                    buf = bufs[8 * crossed + 4 * (m % 2) + 2 * second + first]
                    found.append((buf.at[m // 2], (crossed, first, second, m)))
    return found


def offset(index, size):
    return pl.ds(pl.multiple_of(index * size, size), size)


def place_pieces(place_ref, bufs, upper, high, low, diag):
    for piece, args in pieces(bufs):
        rep, bulk = origin(place_ref, *args)

        @pl.when((rep <= bulk // 2) if upper else (rep >= bulk // 2))
        def _():
            h, l = split(piece[0:256, :])
            high[offset(rep, 256), offset(bulk, 128)] = h
            low[offset(rep, 256), offset(bulk, 128)] = l

        @pl.when(rep == bulk // 2)
        def _():
            diag[bulk, 0:128, :] = piece[pl.ds(pl.multiple_of((bulk % 2) * 128, 128), 128), :]
            diag[bulk, 128:136, :] = piece[256:264, :]


def mul_pairs(a, b):
    (ah, al), (bh, bl) = a, b
    return dot(ah, bh) + (dot(al, bh) + dot(ah, bl))


def pair_of(high, low, r, c, size):
    rows, cols = slice(r, r + size), slice(c, c + size)
    return high[rows, cols], low[rows, cols]


def join(a, b, c, d):
    return jnp.concatenate([jnp.concatenate([a, b], axis=1), jnp.concatenate([c, d], axis=1)], axis=0)


def first_kernel(place_ref, pair, other_pair, *refs):
    bufs, (x_ref, high, low, diag) = refs[:16], refs[16:]
    place_pieces(place_ref, bufs, False, high, low, diag)
    n = 128
    i, j = iotas(n)

    def block(k):
        return jnp.where(i > j, diag[k, 0:n, :], 0.0) + jnp.where(i == j, diag[k, n : n + 1, :], 0.0)

    zero = jnp.zeros((n, n), F32)
    inverses = []
    for k in range(4):
        ta, tb = block(2 * k), block(2 * k + 1)
        pa, pb = split(ta), split(tb)
        off = -mul_pairs(split(mul_pairs(pb, pair_of(high, low, 256 * k + n, 256 * k, n))), pa)
        inverses.append(split(join(ta, zero, off, tb)))

    rest = jnp.concatenate([pair[0], pair[1], other_pair[0], other_pair[1]], axis=0)
    for k in range(4):
        x = mul(rest[:, :256], inverses[k], NT)
        x_ref[:, k * 256 : (k + 1) * 256] = x
        if k < 3:
            rows, cols = slice((k + 1) * 256, 1024), slice(k * 256, (k + 1) * 256)
            rest = rest[:, 256:] - mul(x, (high[rows, cols], low[rows, cols]), NT)


def update_kernel(place_ref, x_ref, *refs):
    held, outs, (high, low) = refs[:4], refs[4:8], refs[8:]
    bulk = place_ref[1]
    for dy in range(2):
        for m in range(4):
            h, l = split(held[2 * dy + m % 2][m // 2])
            high[:, offset(bulk ^ (2 * m + dy), 128)] = h
            low[:, offset(bulk ^ (2 * m + dy), 128)] = l
    upd = mul(x_ref[...], (high[...], low[...]), NT)
    for k, out in enumerate(outs):
        out[...] = upd[32 * k : 32 * (k + 1)]


def second_factor_kernel(place_ref, *refs):
    bufs, (high, low, diag) = refs[:16], refs[16:]
    place_pieces(place_ref, bufs, True, high, low, diag)
    n = 128
    i, j = iotas(n)

    def block(k):
        return jnp.where(i < j, diag[k, 0:n, :], 0.0) + jnp.where(i == j, diag[k, n + 1 : n + 2, :], 0.0)

    zero = jnp.zeros((n, n), F32)
    inverses = []
    for k in range(4):
        ta, tb = block(2 * k), block(2 * k + 1)
        pa, pb = split(ta), split(tb)
        off = -mul_pairs(split(mul_pairs(pa, pair_of(high, low, 256 * k, 256 * k + n, n))), pb)
        inverses.append(split(join(ta, off, zero, tb)))

    def put(r, c, value):
        high[r : r + 256, c : c + 256], low[r : r + 256, c : c + 256] = value

    for k in range(2):
        at = 512 * k
        pa, pb = inverses[2 * k], inverses[2 * k + 1]
        off = -mul_pairs(split(mul_pairs(pa, pair_of(high, low, at, at + 256, 256))), pb)
        put(at, at, pa)
        put(at + 256, at + 256, pb)
        put(at, at + 256, split(off))
        put(at + 256, at, (jnp.zeros((256, 256), BF16),) * 2)


def second_kernel(place_ref, x_ref, both_ref, uh_ref, ul_ref, mine, from_x, from_core, from_both, out_ref):
    x = x_ref[0:32, :]
    out_ref[:, 0:1024] = x
    parts = []
    for k in range(4):
        way = place_ref[0] ^ k
        upd = jnp.where(
            way == 0,
            mine[...],
            jnp.where(way == 2, from_x[...], jnp.where(way == 1, from_core[...], from_both[...])),
        )
        parts.append(both_ref[1, :, k * 256 : (k + 1) * 256] - upd)
    ra = jnp.concatenate(parts[:2], axis=1)
    rb = jnp.concatenate(parts[2:], axis=1)

    def u(r, c):
        rows, cols = slice(r * 512, r * 512 + 512), slice(c * 512, c * 512 + 512)
        return uh_ref[rows, cols], ul_ref[rows, cols]

    xa = mul(ra, u(0, 0))
    xb = mul(rb - mul(xa, u(0, 1)), u(1, 1))
    out_ref[:, 1024:1536] = xa
    out_ref[:, 1536:2048] = xb


BOTH = ("bulk", "rep")

SPREAD, INVERT, LEAVE, ROWS, FIRST, SECOND = 1_000_000_000, 3_500_000_000, 500_000_000, 1_000_000_000, 200_000_000, 3_000_000_000


def swap_z(x, m):
    return lax.ppermute(x, "bulk", [(k, k ^ (2 * m)) for k in range(8)])


def swap_y(x):
    return lax.ppermute(x, "bulk", [(k, k ^ 1) for k in range(8)])


def swap_rep(x, bits):
    return lax.ppermute(x, "rep", [(k, k ^ bits) for k in range(4)])


def cross(x, stage):
    pairs = []
    for rep in range(4):
        for bulk in range(8):
            to = (rep ^ 2, bulk) if (rep & 1) == stage else (rep, bulk ^ 1)
            pairs.append((bulk * 4 + rep, to[1] * 4 + to[0]))
    return lax.ppermute(x, BOTH, pairs)


def after(x, *deps):
    return lax.optimization_barrier((x,) + deps)[0]


ANY = pl.BlockSpec(memory_space=pl.ANY)
VMEM = pl.BlockSpec(memory_space=pltpu.VMEM)
SMEM = pl.BlockSpec(memory_space=pltpu.SMEM)


def call(kernel, out, specs, outs, scratch, flops, size, name):
    return pl.pallas_call(
        kernel,
        out_shape=out,
        in_specs=specs,
        out_specs=outs,
        scratch_shapes=scratch,
        compiler_params=pltpu.CompilerParams(vmem_limit_bytes=size << 20),
        cost_estimate=pl.CostEstimate(flops=flops, bytes_accessed=2 << 20, transcendentals=0),
        name=name,
    )


def shape(*dims, dtype=F32):
    return jax.ShapeDtypeStruct(dims, dtype)


def per_device(orbitals, triangles, coupling, diagonals):
    rep, bulk = lax.axis_index("rep"), lax.axis_index("bulk")
    place = jnp.stack([rep, bulk]).astype(jnp.int32)
    blocks = orbitals.reshape(4, 2, 32, 256)

    t = call(invert_kernel, shape(264, 128), [SMEM, VMEM, VMEM], VMEM, [], INVERT, 4, "invert")(
        place, triangles, diagonals
    )
    coup = after(coupling, t)

    near = jnp.stack([t, swap_z(t, 2)])
    far = swap_z(near, 1)
    near0 = swap_y(near)
    near1 = swap_rep(near, 2)
    near01 = swap_rep(near0, 2)

    leave = call(leave_kernel, shape(4, 32, 256), [SMEM, VMEM], VMEM, [], LEAVE, 4, "leave")(place, blocks)
    came = swap_y(after(leave, t))
    c_near = jnp.stack([coupling, swap_z(after(coup, near), 2)])
    c_near_got = swap_y(c_near)

    far_now = after(far, near0, near1, came, c_near)
    far0 = cross(far_now, 0)
    far1 = cross(far_now, 1)
    b_out = call(spread_kernel, [shape(2, 32, 256)] * 3, [SMEM, VMEM, VMEM], [VMEM] * 3, [], SPREAD, 4, "spread")(
        place, blocks, came
    )
    b_z = [swap_z(after(b, far), m + 1) for m, b in enumerate(b_out)]
    c_far = swap_z(after(c_near, far, b_z[0]), 1)
    c_far_got = swap_y(c_far)
    far01 = cross(after(far0, far1, near01), 1)

    left, both = call(
        rows_kernel,
        [shape(32, 1024), shape(2, 32, 1024)],
        [SMEM] + [VMEM] * 5,
        [VMEM] * 2,
        [],
        ROWS,
        4,
        "rows",
    )(place, blocks, came, *b_z)
    pair = jnp.stack([left, swap_rep(after(left, came), 2)])
    other_pair = swap_rep(after(pair, c_far), 1)
    bufs = [near, near0, near1, near01, far, far0, far1, far01]
    bufs += [swap_rep(b, 1) for b in bufs[:7]] + [swap_rep(after(far01, far1), 1)]

    scratch = [pltpu.VMEM((8, 136, 128), F32)]
    halves = [shape(1024, 1024, dtype=BF16)] * 2
    x = call(
        first_kernel,
        shape(128, 1024),
        [SMEM] + [VMEM] * 18,
        VMEM,
        [pltpu.VMEM((1024, 1024), BF16)] * 2 + scratch,
        FIRST,
        24,
        "first_panel",
    )(place, pair, after(other_pair, c_near_got), *bufs)

    mine, to_x, to_core, to_both = call(
        update_kernel,
        [shape(32, 256)] * 4,
        [SMEM] + [VMEM] * 5,
        [VMEM] * 4,
        [pltpu.VMEM((256, 1024), BF16)] * 2,
        2_000_000_000,
        24,
        "update",
    )(place, x, c_near, c_far, c_near_got, c_far_got)
    back = [swap_rep(to_x, 2), swap_rep(to_core, 1), swap_rep(to_both, 3)]

    uh, ul = call(
        second_factor_kernel, halves, [SMEM] + [VMEM] * 16, [VMEM] * 2, scratch, SECOND, 24, "second_factor"
    )(after(place, mine), *bufs)

    return call(second_kernel, shape(32, 2048), [SMEM] + [VMEM] * 8, VMEM, [], 2_500_000_000, 24, "second_panel")(
        place, x, both, uh, ul, mine, *back
    )


def solution(mesh):
    special = mesh.shape["bulk"] == 8 and mesh.shape["rep"] == 4

    def run(orbitals, triangles, coupling, diagonals):
        fits = orbitals.shape == (1024, 2048) and triangles.shape == (1024, 1024)
        body = per_device if special and fits else per_device_any
        return jax.shard_map(
            body,
            mesh=mesh,
            in_specs=(P("rep", "bulk"), P("rep", "bulk"), P("rep", "bulk"), P(None, "bulk")),
            out_specs=P(("rep", "bulk"), None),
            check_vma=False,
        )(orbitals, triangles, coupling, diagonals)

    return run
```

```python
import jax
import jax.numpy as jnp
from jax import lax
from jax.experimental import pallas as pl
from jax.experimental.pallas import tpu as pltpu
from jax.sharding import PartitionSpec as P

F32 = jnp.float32
BF16 = jnp.bfloat16
NN = (((1,), (0,)), ((), ()))
NT = (((1,), (1,)), ((), ()))


def unpack(triangles, diagonals):
    first_block = jnp.tril(triangles, -1) + jnp.diag(diagonals[0])
    second_block = jnp.tril(triangles.T, -1) + jnp.diag(diagonals[1])
    return (first_block, second_block)


def per_device_any(orbitals, triangles, coupling, diagonals):
    tri_rows, couple_rows = (
        lax.all_gather(triangles, "rep", axis=0, tiled=True),
        lax.all_gather(coupling, "rep", axis=0, tiled=True),
    )
    tri_whole, couple_whole, diag_whole = (
        lax.all_gather(tri_rows, "bulk", axis=1, tiled=True),
        lax.all_gather(couple_rows, "bulk", axis=1, tiled=True),
        lax.all_gather(diagonals, "bulk", axis=1, tiled=True),
    )
    first_block, second_block = unpack(tri_whole, diag_whole)
    panel = first_block.shape[0]
    groups = lax.axis_size("bulk")
    local_rows = orbitals.shape[0] // groups
    blocks = orbitals.reshape(groups, local_rows, orbitals.shape[1])
    received = lax.all_to_all(blocks, "bulk", split_axis=0, concat_axis=2, tiled=True)
    rows_now = received.reshape(local_rows, received.shape[2])
    left_part = rows_now[:, :panel]
    right_part = rows_now[:, panel:]
    solved_one = jax.scipy.linalg.solve_triangular(first_block, left_part.T, lower=True).T
    update = jnp.dot(
        solved_one,
        couple_whole.T,
        precision=lax.Precision.HIGHEST,
        preferred_element_type=jnp.float32,
    )
    solved_two = jax.scipy.linalg.solve_triangular(
        second_block, (right_part - update).T, lower=True
    ).T
    return jnp.concatenate([solved_one, solved_two], axis=1)


def dot(a, b, dims=NN):
    return lax.dot_general(a, b, dims, preferred_element_type=F32)


def dot_exact(a, b):
    return lax.dot_general(a, b, NN, precision=lax.Precision.HIGHEST, preferred_element_type=F32)


def split(x):
    high = x.astype(BF16)
    return high, (x - high.astype(F32)).astype(BF16)


def mul(x, b, dims=NN):
    xh, xl = split(x)
    bh, bl = b
    m = x.shape[0]
    both = dot(jnp.concatenate([xh, xl], axis=0), bh, dims)
    return (both[:m] + both[m:]) + dot(xh, bl, dims)


def mul3(a, b):
    (ah, al), (bh, bl) = split(a), split(b)
    return dot(ah, bh) + (dot(al, bh) + dot(ah, bl))


def iotas(n):
    return lax.broadcasted_iota(jnp.int32, (n, n), 0), lax.broadcasted_iota(jnp.int32, (n, n), 1)


def invert_kernel(place_ref, tri_ref, diag_ref, t_ref):
    rep, bulk = place_ref[0], place_ref[1]
    rows, n = tri_ref.shape
    inv = 1.0 / diag_ref[...]
    t_ref[0:rows, :] = tri_ref[...]
    t_ref[rows : rows + 8, :] = jnp.concatenate([inv, jnp.zeros((6, n), F32)], axis=0)

    @pl.when(rep == bulk // 2)
    def _():
        start = pl.multiple_of((bulk % 2) * n, n)
        block = tri_ref[pl.ds(start, n), :]
        i, j = iotas(n)
        eye = i == j
        ans = []
        for which in range(2):
            row, col = (i, j) if which == 0 else (j, i)
            along = inv[which : which + 1, :]
            d = jnp.where(eye, along, 0.0)
            down = jnp.sum(d, axis=1, keepdims=True)
            part = (row >> 1 == col >> 1) & (row > col)
            ans.append(d - jnp.where(part, block * along * down, 0.0))
        level = 1
        while (1 << level) < n:
            for which in range(2):
                row, col = (i, j) if which == 0 else (j, i)
                part = (row >> (level + 1) == col >> (level + 1)) & (row >> level > col >> level)
                t = ans[which]
                ans[which] = t - mul3(mul3(t, jnp.where(part, block, 0.0)), t)
            level += 1
        t_ref[pl.ds(start, n), :] = jnp.where(i >= j, ans[0], ans[1])


def leave_kernel(place_ref, orb, out):
    y = place_ref[1] & 1
    for k in range(4):
        out[k] = orb[k, 1 - y]


def spread_kernel(place_ref, orb, came, b1, b2, b3):
    z, y = place_ref[1] >> 1, place_ref[1] & 1
    for m, ref in ((1, b1), (2, b2), (3, b3)):
        ref[0] = orb[z ^ m, y]
        ref[1] = came[z ^ m]


def rows_kernel(place_ref, orb, came, b1, b2, b3, left, both):
    z, y = place_ref[1] >> 1, place_ref[1] & 1

    def put(m, dy, value):
        k = 2 * (z ^ m) + (y ^ dy)
        both[k >> 2, :, pl.ds(pl.multiple_of((k & 3) * 256, 256), 256)] = value

    put(0, 0, orb[z, y])
    put(0, 1, came[z])
    for m, ref in ((1, b1), (2, b2), (3, b3)):
        put(m, 0, ref[0])
        put(m, 1, ref[1])
    left[...] = both[0]


def pair_kernel(left, left_x, later, out):
    out[0] = left[...]
    out[1] = left_x[...]


def origin(place_ref, crossed, first, second, m):
    rep, bulk = place_ref[0], place_ref[1]
    if m % 2 == 0:
        dx, dy = second, first
    else:
        core = (rep & 1) ^ crossed
        dx = jnp.where(core == 0, first, second)
        dy = jnp.where(core == 0, second, first)
    return rep ^ (2 * dx + crossed), bulk ^ (2 * m + dy)


def pieces(bufs):
    found = []
    for crossed in range(2):
        near, far, far01 = bufs[3 * crossed : 3 * crossed + 3]
        for m in range(4):
            for second in range(2):
                for first in range(2):
                    entry = 2 * (2 * second + first) + m // 2
                    buf = near if m % 2 == 0 else far
                    if entry > 5 and m % 2 == 1:
                        buf, entry = far01, m // 2
                    found.append((buf.at[entry], (crossed, first, second, m)))
    return found


def offset(index, size):
    return pl.ds(pl.multiple_of(index * size, size), size)


def place_pieces(place_ref, bufs, upper, high, low, diag):
    for piece, args in pieces(bufs):
        rep, bulk = origin(place_ref, *args)

        @pl.when((rep <= bulk // 2) if upper else (rep >= bulk // 2))
        def _():
            h, l = split(piece[0:256, :])
            high[offset(rep, 256), offset(bulk, 128)] = h
            low[offset(rep, 256), offset(bulk, 128)] = l

        @pl.when(rep == bulk // 2)
        def _():
            diag[bulk, 0:128, :] = piece[pl.ds(pl.multiple_of((bulk % 2) * 128, 128), 128), :]
            diag[bulk, 128:136, :] = piece[256:264, :]


def mul_pairs(a, b):
    (ah, al), (bh, bl) = a, b
    return dot(ah, bh) + (dot(al, bh) + dot(ah, bl))


def pair_of(high, low, r, c, size):
    rows, cols = slice(r, r + size), slice(c, c + size)
    return high[rows, cols], low[rows, cols]


def join(a, b, c, d):
    return jnp.concatenate([jnp.concatenate([a, b], axis=1), jnp.concatenate([c, d], axis=1)], axis=0)


def first_kernel(place_ref, pair, other_pair, *refs):
    bufs, (x_ref, high, low, diag) = refs[:6], refs[6:]
    place_pieces(place_ref, bufs, False, high, low, diag)
    n = 128
    i, j = iotas(n)

    def block(k):
        return jnp.where(i > j, diag[k, 0:n, :], 0.0) + jnp.where(i == j, diag[k, n : n + 1, :], 0.0)

    zero = jnp.zeros((n, n), F32)
    inverses = []
    for k in range(4):
        ta, tb = block(2 * k), block(2 * k + 1)
        pa, pb = split(ta), split(tb)
        off = -mul_pairs(split(mul_pairs(pb, pair_of(high, low, 256 * k + n, 256 * k, n))), pa)
        inverses.append(split(join(ta, zero, off, tb)))

    rest = jnp.concatenate([pair[0], pair[1], other_pair[0], other_pair[1]], axis=0)
    for k in range(4):
        x = mul(rest[:, :256], inverses[k], NT)
        x_ref[:, k * 256 : (k + 1) * 256] = x
        if k < 3:
            rows, cols = slice((k + 1) * 256, 1024), slice(k * 256, (k + 1) * 256)
            rest = rest[:, 256:] - mul(x, (high[rows, cols], low[rows, cols]), NT)


def update_kernel(place_ref, x_ref, *refs):
    held, outs, (high, low) = refs[:4], refs[4:8], refs[8:]
    bulk = place_ref[1]
    for dy in range(2):
        for m in range(4):
            h, l = split(held[2 * dy + m % 2][m // 2])
            high[:, offset(bulk ^ (2 * m + dy), 128)] = h
            low[:, offset(bulk ^ (2 * m + dy), 128)] = l
    upd = mul(x_ref[...], (high[...], low[...]), NT)
    for k, out in enumerate(outs):
        out[...] = upd[32 * k : 32 * (k + 1)]


def second_factor_kernel(place_ref, *refs):
    bufs, (high, low, diag) = refs[:6], refs[6:]
    place_pieces(place_ref, bufs, True, high, low, diag)
    n = 128
    i, j = iotas(n)

    def block(k):
        return jnp.where(i < j, diag[k, 0:n, :], 0.0) + jnp.where(i == j, diag[k, n + 1 : n + 2, :], 0.0)

    zero = jnp.zeros((n, n), F32)
    inverses = []
    for k in range(4):
        ta, tb = block(2 * k), block(2 * k + 1)
        pa, pb = split(ta), split(tb)
        off = -mul_pairs(split(mul_pairs(pa, pair_of(high, low, 256 * k, 256 * k + n, n))), pb)
        inverses.append(split(join(ta, off, zero, tb)))

    def put(r, c, value):
        high[r : r + 256, c : c + 256], low[r : r + 256, c : c + 256] = value

    for k in range(2):
        at = 512 * k
        pa, pb = inverses[2 * k], inverses[2 * k + 1]
        off = -mul_pairs(split(mul_pairs(pa, pair_of(high, low, at, at + 256, 256))), pb)
        put(at, at, pa)
        put(at + 256, at + 256, pb)
        put(at, at + 256, split(off))
        put(at + 256, at, (jnp.zeros((256, 256), BF16),) * 2)


def second_kernel(place_ref, x_ref, both_ref, uh_ref, ul_ref, mine, from_x, from_core, from_both, out_ref):
    x = x_ref[0:32, :]
    out_ref[:, 0:1024] = x
    parts = []
    for k in range(4):
        way = place_ref[0] ^ k
        upd = jnp.where(
            way == 0,
            mine[...],
            jnp.where(way == 2, from_x[...], jnp.where(way == 1, from_core[...], from_both[...])),
        )
        parts.append(both_ref[1, :, k * 256 : (k + 1) * 256] - upd)
    ra = jnp.concatenate(parts[:2], axis=1)
    rb = jnp.concatenate(parts[2:], axis=1)

    def u(r, c):
        rows, cols = slice(r * 512, r * 512 + 512), slice(c * 512, c * 512 + 512)
        return uh_ref[rows, cols], ul_ref[rows, cols]

    xa = mul(ra, u(0, 0))
    xb = mul(rb - mul(xa, u(0, 1)), u(1, 1))
    out_ref[:, 1024:1536] = xa
    out_ref[:, 1536:2048] = xb


BOTH = ("bulk", "rep")

SPREAD, INVERT, LEAVE, ROWS, FIRST, SECOND, PAIR = 1_000_000_000, 3_500_000_000, 500_000_000, 1_000_000_000, 200_000_000, 3_000_000_000, 4_000_000_000


def swap_z(x, m):
    return lax.ppermute(x, "bulk", [(k, k ^ (2 * m)) for k in range(8)])


def swap_y(x):
    return lax.ppermute(x, "bulk", [(k, k ^ 1) for k in range(8)])


def swap_rep(x, bits):
    return lax.ppermute(x, "rep", [(k, k ^ bits) for k in range(4)])


def cross(x, stage):
    pairs = []
    for rep in range(4):
        for bulk in range(8):
            to = (rep ^ 2, bulk) if (rep & 1) == stage else (rep, bulk ^ 1)
            pairs.append((bulk * 4 + rep, to[1] * 4 + to[0]))
    return lax.ppermute(x, BOTH, pairs)


def after(x, *deps):
    return lax.optimization_barrier((x,) + deps)[0]


ANY = pl.BlockSpec(memory_space=pl.ANY)
VMEM = pl.BlockSpec(memory_space=pltpu.VMEM)
SMEM = pl.BlockSpec(memory_space=pltpu.SMEM)


def call(kernel, out, specs, outs, scratch, flops, size, name):
    return pl.pallas_call(
        kernel,
        out_shape=out,
        in_specs=specs,
        out_specs=outs,
        scratch_shapes=scratch,
        compiler_params=pltpu.CompilerParams(vmem_limit_bytes=size << 20),
        cost_estimate=pl.CostEstimate(flops=flops, bytes_accessed=2 << 20, transcendentals=0),
        name=name,
    )


def shape(*dims, dtype=F32):
    return jax.ShapeDtypeStruct(dims, dtype)


def per_device(orbitals, triangles, coupling, diagonals):
    rep, bulk = lax.axis_index("rep"), lax.axis_index("bulk")
    place = jnp.stack([rep, bulk]).astype(jnp.int32)
    blocks = orbitals.reshape(4, 2, 32, 256)

    t = call(invert_kernel, shape(264, 128), [SMEM, VMEM, VMEM], VMEM, [], INVERT, 4, "invert")(
        place, triangles, diagonals
    )
    coup = after(coupling, t)

    near = jnp.stack([t, swap_z(t, 2)])
    far = swap_z(near, 1)
    near0 = swap_y(near)
    near1 = swap_rep(near, 2)
    near01 = swap_rep(near0, 2)

    leave = call(leave_kernel, shape(4, 32, 256), [SMEM, VMEM], VMEM, [], LEAVE, 4, "leave")(place, blocks)
    came = swap_y(after(leave, t))
    c_near = jnp.stack([coupling, swap_z(after(coup, near), 2)])
    c_near_got = swap_y(c_near)

    far_now = after(far, near0, near1, came)
    far0 = cross(far_now, 0)
    far1 = cross(far_now, 1)
    b_out = call(spread_kernel, [shape(2, 32, 256)] * 3, [SMEM, VMEM, VMEM], [VMEM] * 3, [], SPREAD, 4, "spread")(
        place, blocks, came
    )
    b_z = [swap_z(after(b, far, c_near, near01), m + 1) for m, b in enumerate(b_out)]
    c_far = swap_z(after(c_near, far, b_z[0]), 1)
    c_far_got = swap_y(c_far)
    far01 = cross(after(far0, far1), 1)

    left, both = call(
        rows_kernel,
        [shape(32, 1024), shape(2, 32, 1024)],
        [SMEM] + [VMEM] * 5,
        [VMEM] * 2,
        [],
        ROWS,
        4,
        "rows",
    )(place, blocks, came, *b_z)
    left_x = swap_rep(left, 2)
    pair = call(pair_kernel, shape(2, 32, 1024), [VMEM] * 3, VMEM, [], PAIR, 4, "pair")(left, left_x, c_far)
    other_pair = swap_rep(pair, 1)
    near_all = jnp.concatenate([near, near0, near1, near01], axis=0)
    far_all = jnp.concatenate([far, far0, far1], axis=0)
    bufs = [near_all, far_all, far01]
    bufs += [swap_rep(after(near_all, *b_z), 1), swap_rep(after(far_all, far1), 1), swap_rep(after(far01, far1), 1)]

    scratch = [pltpu.VMEM((8, 136, 128), F32)]
    halves = [shape(1024, 1024, dtype=BF16)] * 2
    x = call(
        first_kernel,
        shape(128, 1024),
        [SMEM] + [VMEM] * 8,
        VMEM,
        [pltpu.VMEM((1024, 1024), BF16)] * 2 + scratch,
        FIRST,
        24,
        "first_panel",
    )(place, pair, after(other_pair, c_near_got), *bufs)

    mine, to_x, to_core, to_both = call(
        update_kernel,
        [shape(32, 256)] * 4,
        [SMEM] + [VMEM] * 5,
        [VMEM] * 4,
        [pltpu.VMEM((256, 1024), BF16)] * 2,
        2_000_000_000,
        24,
        "update",
    )(place, x, c_near, c_far, c_near_got, c_far_got)
    back = [swap_rep(to_x, 2), swap_rep(to_core, 1), swap_rep(to_both, 3)]

    uh, ul = call(
        second_factor_kernel, halves, [SMEM] + [VMEM] * 6, [VMEM] * 2, scratch, SECOND, 24, "second_factor"
    )(after(place, mine), *bufs)

    return call(second_kernel, shape(32, 2048), [SMEM] + [VMEM] * 8, VMEM, [], 2_500_000_000, 24, "second_panel")(
        place, x, both, uh, ul, mine, *back
    )


def solution(mesh):
    special = mesh.shape["bulk"] == 8 and mesh.shape["rep"] == 4

    def run(orbitals, triangles, coupling, diagonals):
        fits = orbitals.shape == (1024, 2048) and triangles.shape == (1024, 1024)
        body = per_device if special and fits else per_device_any
        return jax.shard_map(
            body,
            mesh=mesh,
            in_specs=(P("rep", "bulk"), P("rep", "bulk"), P("rep", "bulk"), P(None, "bulk")),
            out_specs=P(("rep", "bulk"), None),
            check_vma=False,
        )(orbitals, triangles, coupling, diagonals)

    return run
```

```python
import jax
import jax.numpy as jnp
from jax import lax
from jax.experimental import pallas as pl
from jax.experimental.pallas import tpu as pltpu
from jax.sharding import PartitionSpec as P

F32 = jnp.float32
BF16 = jnp.bfloat16
NN = (((1,), (0,)), ((), ()))
NT = (((1,), (1,)), ((), ()))


def unpack(triangles, diagonals):
    first_block = jnp.tril(triangles, -1) + jnp.diag(diagonals[0])
    second_block = jnp.tril(triangles.T, -1) + jnp.diag(diagonals[1])
    return (first_block, second_block)


def per_device_any(orbitals, triangles, coupling, diagonals):
    tri_rows, couple_rows = (
        lax.all_gather(triangles, "rep", axis=0, tiled=True),
        lax.all_gather(coupling, "rep", axis=0, tiled=True),
    )
    tri_whole, couple_whole, diag_whole = (
        lax.all_gather(tri_rows, "bulk", axis=1, tiled=True),
        lax.all_gather(couple_rows, "bulk", axis=1, tiled=True),
        lax.all_gather(diagonals, "bulk", axis=1, tiled=True),
    )
    first_block, second_block = unpack(tri_whole, diag_whole)
    panel = first_block.shape[0]
    groups = lax.axis_size("bulk")
    local_rows = orbitals.shape[0] // groups
    blocks = orbitals.reshape(groups, local_rows, orbitals.shape[1])
    received = lax.all_to_all(blocks, "bulk", split_axis=0, concat_axis=2, tiled=True)
    rows_now = received.reshape(local_rows, received.shape[2])
    left_part = rows_now[:, :panel]
    right_part = rows_now[:, panel:]
    solved_one = jax.scipy.linalg.solve_triangular(first_block, left_part.T, lower=True).T
    update = jnp.dot(
        solved_one,
        couple_whole.T,
        precision=lax.Precision.HIGHEST,
        preferred_element_type=jnp.float32,
    )
    solved_two = jax.scipy.linalg.solve_triangular(
        second_block, (right_part - update).T, lower=True
    ).T
    return jnp.concatenate([solved_one, solved_two], axis=1)


def dot(a, b, dims=NN):
    return lax.dot_general(a, b, dims, preferred_element_type=F32)


def dot_exact(a, b):
    return lax.dot_general(a, b, NN, precision=lax.Precision.HIGHEST, preferred_element_type=F32)


def split(x):
    high = x.astype(BF16)
    return high, (x - high.astype(F32)).astype(BF16)


def mul(x, b, dims=NN):
    xh, xl = split(x)
    bh, bl = b
    m = x.shape[0]
    both = dot(jnp.concatenate([xh, xl], axis=0), bh, dims)
    return (both[:m] + both[m:]) + dot(xh, bl, dims)


def mul3(a, b):
    (ah, al), (bh, bl) = split(a), split(b)
    return dot(ah, bh) + (dot(al, bh) + dot(ah, bl))


def iotas(n):
    return lax.broadcasted_iota(jnp.int32, (n, n), 0), lax.broadcasted_iota(jnp.int32, (n, n), 1)


def invert_kernel(place_ref, tri_ref, diag_ref, t_ref):
    rep, bulk = place_ref[0], place_ref[1]
    rows, n = tri_ref.shape
    inv = 1.0 / diag_ref[...]
    t_ref[0:rows, :] = tri_ref[...]
    t_ref[rows : rows + 8, :] = jnp.concatenate([inv, jnp.zeros((6, n), F32)], axis=0)

    @pl.when(rep == bulk // 2)
    def _():
        start = pl.multiple_of((bulk % 2) * n, n)
        block = tri_ref[pl.ds(start, n), :]
        i, j = iotas(n)
        eye = i == j
        ans = []
        for which in range(2):
            row, col = (i, j) if which == 0 else (j, i)
            along = inv[which : which + 1, :]
            d = jnp.where(eye, along, 0.0)
            down = jnp.sum(d, axis=1, keepdims=True)
            part = (row >> 1 == col >> 1) & (row > col)
            ans.append(d - jnp.where(part, block * along * down, 0.0))
        level = 1
        while (1 << level) < n:
            for which in range(2):
                row, col = (i, j) if which == 0 else (j, i)
                part = (row >> (level + 1) == col >> (level + 1)) & (row >> level > col >> level)
                t = ans[which]
                ans[which] = t - mul3(mul3(t, jnp.where(part, block, 0.0)), t)
            level += 1
        t_ref[pl.ds(start, n), :] = jnp.where(i >= j, ans[0], ans[1])


def leave_kernel(place_ref, orb, out):
    y = place_ref[1] & 1
    for k in range(4):
        out[k] = orb[k, 1 - y]


def spread_kernel(place_ref, orb, came, b1, b2, b3):
    z, y = place_ref[1] >> 1, place_ref[1] & 1
    for m, ref in ((1, b1), (2, b2), (3, b3)):
        ref[0] = orb[z ^ m, y]
        ref[1] = came[z ^ m]


def rows_kernel(place_ref, orb, came, b1, b2, b3, left, both):
    z, y = place_ref[1] >> 1, place_ref[1] & 1

    def put(m, dy, value):
        k = 2 * (z ^ m) + (y ^ dy)
        both[k >> 2, :, pl.ds(pl.multiple_of((k & 3) * 256, 256), 256)] = value

    put(0, 0, orb[z, y])
    put(0, 1, came[z])
    for m, ref in ((1, b1), (2, b2), (3, b3)):
        put(m, 0, ref[0])
        put(m, 1, ref[1])
    left[...] = both[0]


def origin(place_ref, crossed, first, second, m):
    rep, bulk = place_ref[0], place_ref[1]
    if m % 2 == 0:
        dx, dy = second, first
    else:
        core = (rep & 1) ^ crossed
        dx = jnp.where(core == 0, first, second)
        dy = jnp.where(core == 0, second, first)
    return rep ^ (2 * dx + crossed), bulk ^ (2 * m + dy)


def pieces(bufs):
    found = []
    for crossed in range(2):
        for m in range(4):
            for second in range(2):
                for first in range(2):
                    buf = bufs[8 * crossed + 4 * (m % 2) + 2 * second + first]
                    found.append((buf.at[m // 2], (crossed, first, second, m)))
    return found


def offset(index, size):
    return pl.ds(pl.multiple_of(index * size, size), size)


def place_pieces(place_ref, bufs, upper, high, low, diag):
    for piece, args in pieces(bufs):
        rep, bulk = origin(place_ref, *args)

        @pl.when((rep <= bulk // 2) if upper else (rep >= bulk // 2))
        def _():
            h, l = split(piece[0:256, :])
            high[offset(rep, 256), offset(bulk, 128)] = h
            low[offset(rep, 256), offset(bulk, 128)] = l

        @pl.when(rep == bulk // 2)
        def _():
            diag[bulk, 0:128, :] = piece[pl.ds(pl.multiple_of((bulk % 2) * 128, 128), 128), :]
            diag[bulk, 128:136, :] = piece[256:264, :]


def mul_pairs(a, b):
    (ah, al), (bh, bl) = a, b
    return dot(ah, bh) + (dot(al, bh) + dot(ah, bl))


def pair_of(high, low, r, c, size):
    rows, cols = slice(r, r + size), slice(c, c + size)
    return high[rows, cols], low[rows, cols]


def join(a, b, c, d):
    return jnp.concatenate([jnp.concatenate([a, b], axis=1), jnp.concatenate([c, d], axis=1)], axis=0)


def first_kernel(place_ref, pair, other_pair, *refs):
    bufs, (x_ref, high, low, diag) = refs[:16], refs[16:]
    place_pieces(place_ref, bufs, False, high, low, diag)
    n = 128
    i, j = iotas(n)

    def block(k):
        return jnp.where(i > j, diag[k, 0:n, :], 0.0) + jnp.where(i == j, diag[k, n : n + 1, :], 0.0)

    zero = jnp.zeros((n, n), F32)
    inverses = []
    for k in range(4):
        ta, tb = block(2 * k), block(2 * k + 1)
        pa, pb = split(ta), split(tb)
        off = -mul_pairs(split(mul_pairs(pb, pair_of(high, low, 256 * k + n, 256 * k, n))), pa)
        inverses.append(split(join(ta, zero, off, tb)))

    rest = jnp.concatenate([pair[0], pair[1], other_pair[0], other_pair[1]], axis=0)
    for k in range(4):
        x = mul(rest[:, :256], inverses[k], NT)
        x_ref[:, k * 256 : (k + 1) * 256] = x
        if k < 3:
            rows, cols = slice((k + 1) * 256, 1024), slice(k * 256, (k + 1) * 256)
            rest = rest[:, 256:] - mul(x, (high[rows, cols], low[rows, cols]), NT)


def update_kernel(place_ref, x_ref, *refs):
    held, outs, (high, low) = refs[:4], refs[4:8], refs[8:]
    bulk = place_ref[1]
    for dy in range(2):
        for m in range(4):
            h, l = split(held[2 * dy + m % 2][m // 2])
            high[:, offset(bulk ^ (2 * m + dy), 128)] = h
            low[:, offset(bulk ^ (2 * m + dy), 128)] = l
    upd = mul(x_ref[...], (high[...], low[...]), NT)
    for k, out in enumerate(outs):
        out[...] = upd[32 * k : 32 * (k + 1)]


def second_factor_kernel(place_ref, *refs):
    bufs, (high, low, diag) = refs[:16], refs[16:]
    place_pieces(place_ref, bufs, True, high, low, diag)
    n = 128
    i, j = iotas(n)

    def block(k):
        return jnp.where(i < j, diag[k, 0:n, :], 0.0) + jnp.where(i == j, diag[k, n + 1 : n + 2, :], 0.0)

    zero = jnp.zeros((n, n), F32)
    inverses = []
    for k in range(4):
        ta, tb = block(2 * k), block(2 * k + 1)
        pa, pb = split(ta), split(tb)
        off = -mul_pairs(split(mul_pairs(pa, pair_of(high, low, 256 * k, 256 * k + n, n))), pb)
        inverses.append(split(join(ta, off, zero, tb)))

    def put(r, c, value):
        high[r : r + 256, c : c + 256], low[r : r + 256, c : c + 256] = value

    for k in range(2):
        at = 512 * k
        pa, pb = inverses[2 * k], inverses[2 * k + 1]
        off = -mul_pairs(split(mul_pairs(pa, pair_of(high, low, at, at + 256, 256))), pb)
        put(at, at, pa)
        put(at + 256, at + 256, pb)
        put(at, at + 256, split(off))
        put(at + 256, at, (jnp.zeros((256, 256), BF16),) * 2)


def second_kernel(place_ref, x_ref, both_ref, uh_ref, ul_ref, mine, from_x, from_core, from_both, out_ref):
    x = x_ref[0:32, :]
    out_ref[:, 0:1024] = x
    parts = []
    for k in range(4):
        way = place_ref[0] ^ k
        upd = jnp.where(
            way == 0,
            mine[...],
            jnp.where(way == 2, from_x[...], jnp.where(way == 1, from_core[...], from_both[...])),
        )
        parts.append(both_ref[1, :, k * 256 : (k + 1) * 256] - upd)
    ra = jnp.concatenate(parts[:2], axis=1)
    rb = jnp.concatenate(parts[2:], axis=1)

    def u(r, c):
        rows, cols = slice(r * 512, r * 512 + 512), slice(c * 512, c * 512 + 512)
        return uh_ref[rows, cols], ul_ref[rows, cols]

    xa = mul(ra, u(0, 0))
    xb = mul(rb - mul(xa, u(0, 1)), u(1, 1))
    out_ref[:, 1024:1536] = xa
    out_ref[:, 1536:2048] = xb


BOTH = ("bulk", "rep")

SPREAD, INVERT, LEAVE, ROWS, FIRST, SECOND = 1_000_000_000, 3_500_000_000, 500_000_000, 1_000_000_000, 200_000_000, 3_000_000_000


def swap_z(x, m):
    return lax.ppermute(x, "bulk", [(k, k ^ (2 * m)) for k in range(8)])


def swap_y(x):
    return lax.ppermute(x, "bulk", [(k, k ^ 1) for k in range(8)])


def swap_rep(x, bits):
    return lax.ppermute(x, "rep", [(k, k ^ bits) for k in range(4)])


def cross(x, stage):
    pairs = []
    for rep in range(4):
        for bulk in range(8):
            to = (rep ^ 2, bulk) if (rep & 1) == stage else (rep, bulk ^ 1)
            pairs.append((bulk * 4 + rep, to[1] * 4 + to[0]))
    return lax.ppermute(x, BOTH, pairs)


def after(x, *deps):
    return lax.optimization_barrier((x,) + deps)[0]


ANY = pl.BlockSpec(memory_space=pl.ANY)
VMEM = pl.BlockSpec(memory_space=pltpu.VMEM)
SMEM = pl.BlockSpec(memory_space=pltpu.SMEM)


def call(kernel, out, specs, outs, scratch, flops, size, name):
    return pl.pallas_call(
        kernel,
        out_shape=out,
        in_specs=specs,
        out_specs=outs,
        scratch_shapes=scratch,
        compiler_params=pltpu.CompilerParams(vmem_limit_bytes=size << 20),
        cost_estimate=pl.CostEstimate(flops=flops, bytes_accessed=2 << 20, transcendentals=0),
        name=name,
    )


def shape(*dims, dtype=F32):
    return jax.ShapeDtypeStruct(dims, dtype)


def per_device(orbitals, triangles, coupling, diagonals):
    rep, bulk = lax.axis_index("rep"), lax.axis_index("bulk")
    place = jnp.stack([rep, bulk]).astype(jnp.int32)
    blocks = orbitals.reshape(4, 2, 32, 256)

    t = call(invert_kernel, shape(264, 128), [SMEM, VMEM, VMEM], VMEM, [], INVERT, 4, "invert")(
        place, triangles, diagonals
    )
    coup = after(coupling, t)

    near = jnp.stack([t, swap_z(t, 2)])
    far = swap_z(near, 1)
    near0 = swap_y(near)
    near1 = swap_rep(near, 2)
    near01 = swap_rep(near0, 2)

    leave = call(leave_kernel, shape(4, 32, 256), [SMEM, VMEM], VMEM, [], LEAVE, 4, "leave")(place, blocks)
    came = swap_y(after(leave, t))
    c_near = jnp.stack([coupling, swap_z(after(coup, near), 2)])
    c_near_got = swap_y(c_near)

    far_now = after(far, near0, near1, came, c_near)
    far0 = cross(far_now, 0)
    far1 = cross(far_now, 1)
    b_out = call(spread_kernel, [shape(2, 32, 256)] * 3, [SMEM, VMEM, VMEM], [VMEM] * 3, [], SPREAD, 4, "spread")(
        place, blocks, came
    )
    b_z = [swap_z(after(b, far), m + 1) for m, b in enumerate(b_out)]
    c_far = swap_z(after(c_near, far0), 1)
    c_far_got = swap_y(c_far)
    far01 = cross(after(far0, far1, near01), 1)

    left, both = call(
        rows_kernel,
        [shape(32, 1024), shape(2, 32, 1024)],
        [SMEM] + [VMEM] * 5,
        [VMEM] * 2,
        [],
        ROWS,
        4,
        "rows",
    )(place, blocks, came, *b_z)
    pair = jnp.stack([left, swap_rep(after(left, came), 2)])
    other_pair = swap_rep(after(pair, c_far), 1)
    bufs = [near, near0, near1, near01, far, far0, far1, far01]
    bufs += [swap_rep(after(b, b_z[2], far0), 1) for b in bufs[:7]] + [swap_rep(after(far01, far1), 1)]

    scratch = [pltpu.VMEM((8, 136, 128), F32)]
    halves = [shape(1024, 1024, dtype=BF16)] * 2
    x = call(
        first_kernel,
        shape(128, 1024),
        [SMEM] + [VMEM] * 18,
        VMEM,
        [pltpu.VMEM((1024, 1024), BF16)] * 2 + scratch,
        FIRST,
        24,
        "first_panel",
    )(place, pair, after(other_pair, c_near_got), *bufs)

    mine, to_x, to_core, to_both = call(
        update_kernel,
        [shape(32, 256)] * 4,
        [SMEM] + [VMEM] * 5,
        [VMEM] * 4,
        [pltpu.VMEM((256, 1024), BF16)] * 2,
        2_000_000_000,
        24,
        "update",
    )(place, x, c_near, c_far, c_near_got, c_far_got)
    back = [swap_rep(to_x, 2), swap_rep(to_core, 1), swap_rep(to_both, 3)]

    uh, ul = call(
        second_factor_kernel, halves, [SMEM] + [VMEM] * 16, [VMEM] * 2, scratch, SECOND, 24, "second_factor"
    )(after(place, mine), *bufs)

    return call(second_kernel, shape(32, 2048), [SMEM] + [VMEM] * 8, VMEM, [], 2_500_000_000, 24, "second_panel")(
        place, x, both, uh, ul, mine, *back
    )


def solution(mesh):
    special = mesh.shape["bulk"] == 8 and mesh.shape["rep"] == 4

    def run(orbitals, triangles, coupling, diagonals):
        fits = orbitals.shape == (1024, 2048) and triangles.shape == (1024, 1024)
        body = per_device if special and fits else per_device_any
        return jax.shard_map(
            body,
            mesh=mesh,
            in_specs=(P("rep", "bulk"), P("rep", "bulk"), P("rep", "bulk"), P(None, "bulk")),
            out_specs=P(("rep", "bulk"), None),
            check_vma=False,
        )(orbitals, triangles, coupling, diagonals)

    return run
```

```python
import jax
import jax.numpy as jnp
from jax import lax
from jax.experimental import pallas as pl
from jax.experimental.pallas import tpu as pltpu
from jax.sharding import PartitionSpec as P

F32 = jnp.float32
BF16 = jnp.bfloat16
NN = (((1,), (0,)), ((), ()))
NT = (((1,), (1,)), ((), ()))


def unpack(triangles, diagonals):
    first_block = jnp.tril(triangles, -1) + jnp.diag(diagonals[0])
    second_block = jnp.tril(triangles.T, -1) + jnp.diag(diagonals[1])
    return (first_block, second_block)


def per_device_any(orbitals, triangles, coupling, diagonals):
    tri_rows, couple_rows = (
        lax.all_gather(triangles, "rep", axis=0, tiled=True),
        lax.all_gather(coupling, "rep", axis=0, tiled=True),
    )
    tri_whole, couple_whole, diag_whole = (
        lax.all_gather(tri_rows, "bulk", axis=1, tiled=True),
        lax.all_gather(couple_rows, "bulk", axis=1, tiled=True),
        lax.all_gather(diagonals, "bulk", axis=1, tiled=True),
    )
    first_block, second_block = unpack(tri_whole, diag_whole)
    panel = first_block.shape[0]
    groups = lax.axis_size("bulk")
    local_rows = orbitals.shape[0] // groups
    blocks = orbitals.reshape(groups, local_rows, orbitals.shape[1])
    received = lax.all_to_all(blocks, "bulk", split_axis=0, concat_axis=2, tiled=True)
    rows_now = received.reshape(local_rows, received.shape[2])
    left_part = rows_now[:, :panel]
    right_part = rows_now[:, panel:]
    solved_one = jax.scipy.linalg.solve_triangular(first_block, left_part.T, lower=True).T
    update = jnp.dot(
        solved_one,
        couple_whole.T,
        precision=lax.Precision.HIGHEST,
        preferred_element_type=jnp.float32,
    )
    solved_two = jax.scipy.linalg.solve_triangular(
        second_block, (right_part - update).T, lower=True
    ).T
    return jnp.concatenate([solved_one, solved_two], axis=1)


def dot(a, b, dims=NN):
    return lax.dot_general(a, b, dims, preferred_element_type=F32)


def dot_exact(a, b):
    return lax.dot_general(a, b, NN, precision=lax.Precision.HIGHEST, preferred_element_type=F32)


def split(x):
    high = x.astype(BF16)
    return high, (x - high.astype(F32)).astype(BF16)


def mul(x, b, dims=NN):
    xh, xl = split(x)
    bh, bl = b
    m = x.shape[0]
    both = dot(jnp.concatenate([xh, xl], axis=0), bh, dims)
    return (both[:m] + both[m:]) + dot(xh, bl, dims)


def mul3(a, b):
    (ah, al), (bh, bl) = split(a), split(b)
    return dot(ah, bh) + (dot(al, bh) + dot(ah, bl))


def iotas(n):
    return lax.broadcasted_iota(jnp.int32, (n, n), 0), lax.broadcasted_iota(jnp.int32, (n, n), 1)


def invert_kernel(place_ref, tri_ref, diag_ref, t_ref):
    rep, bulk = place_ref[0], place_ref[1]
    rows, n = tri_ref.shape
    inv = 1.0 / diag_ref[...]
    t_ref[0:rows, :] = tri_ref[...]
    t_ref[rows : rows + 8, :] = jnp.concatenate([inv, jnp.zeros((6, n), F32)], axis=0)

    @pl.when(rep == bulk // 2)
    def _():
        start = pl.multiple_of((bulk % 2) * n, n)
        block = tri_ref[pl.ds(start, n), :]
        i, j = iotas(n)
        eye = i == j
        ans = []
        for which in range(2):
            row, col = (i, j) if which == 0 else (j, i)
            along = inv[which : which + 1, :]
            d = jnp.where(eye, along, 0.0)
            down = jnp.sum(d, axis=1, keepdims=True)
            part = (row >> 1 == col >> 1) & (row > col)
            ans.append(d - jnp.where(part, block * along * down, 0.0))
        level = 1
        while (1 << level) < n:
            for which in range(2):
                row, col = (i, j) if which == 0 else (j, i)
                part = (row >> (level + 1) == col >> (level + 1)) & (row >> level > col >> level)
                t = ans[which]
                ans[which] = t - mul3(mul3(t, jnp.where(part, block, 0.0)), t)
            level += 1
        t_ref[pl.ds(start, n), :] = jnp.where(i >= j, ans[0], ans[1])


def leave_kernel(place_ref, orb, out):
    y = place_ref[1] & 1
    for k in range(4):
        out[k] = orb[k, 1 - y]


def spread_kernel(place_ref, orb, came, b1, b2, b3):
    z, y = place_ref[1] >> 1, place_ref[1] & 1
    for m, ref in ((1, b1), (2, b2), (3, b3)):
        ref[0] = orb[z ^ m, y]
        ref[1] = came[z ^ m]


def rows_kernel(place_ref, orb, came, b1, b2, b3, left, both):
    z, y = place_ref[1] >> 1, place_ref[1] & 1

    def put(m, dy, value):
        k = 2 * (z ^ m) + (y ^ dy)
        both[k >> 2, :, pl.ds(pl.multiple_of((k & 3) * 256, 256), 256)] = value

    put(0, 0, orb[z, y])
    put(0, 1, came[z])
    for m, ref in ((1, b1), (2, b2), (3, b3)):
        put(m, 0, ref[0])
        put(m, 1, ref[1])
    left[...] = both[0]


def origin(place_ref, crossed, first, second, m):
    rep, bulk = place_ref[0], place_ref[1]
    if m % 2 == 0:
        dx, dy = second, first
    else:
        core = (rep & 1) ^ crossed
        dx = jnp.where(core == 0, first, second)
        dy = jnp.where(core == 0, second, first)
    return rep ^ (2 * dx + crossed), bulk ^ (2 * m + dy)


def pieces(bufs):
    found = []
    for crossed in range(2):
        for m in range(4):
            for second in range(2):
                for first in range(2):
                    buf = bufs[5 * crossed + 2 * (m % 2) + second]
                    entry = 2 * first + m // 2
                    if m % 2 == 1 and first + second == 2:
                        buf, entry = bufs[5 * crossed + 4], m // 2
                    found.append((buf.at[entry], (crossed, first, second, m)))
    return found


def offset(index, size):
    return pl.ds(pl.multiple_of(index * size, size), size)


def place_pieces(place_ref, bufs, upper, high, low, diag):
    for piece, args in pieces(bufs):
        rep, bulk = origin(place_ref, *args)

        @pl.when((rep <= bulk // 2) if upper else (rep >= bulk // 2))
        def _():
            h, l = split(piece[0:256, :])
            high[offset(rep, 256), offset(bulk, 128)] = h
            low[offset(rep, 256), offset(bulk, 128)] = l

        @pl.when(rep == bulk // 2)
        def _():
            diag[bulk, 0:128, :] = piece[pl.ds(pl.multiple_of((bulk % 2) * 128, 128), 128), :]
            diag[bulk, 128:136, :] = piece[256:264, :]


def mul_pairs(a, b):
    (ah, al), (bh, bl) = a, b
    return dot(ah, bh) + (dot(al, bh) + dot(ah, bl))


def pair_of(high, low, r, c, size):
    rows, cols = slice(r, r + size), slice(c, c + size)
    return high[rows, cols], low[rows, cols]


def join(a, b, c, d):
    return jnp.concatenate([jnp.concatenate([a, b], axis=1), jnp.concatenate([c, d], axis=1)], axis=0)


def first_kernel(place_ref, pair, other_pair, *refs):
    bufs, (x_ref, high, low, diag) = refs[:10], refs[10:]
    place_pieces(place_ref, bufs, False, high, low, diag)
    n = 128
    i, j = iotas(n)

    def block(k):
        return jnp.where(i > j, diag[k, 0:n, :], 0.0) + jnp.where(i == j, diag[k, n : n + 1, :], 0.0)

    zero = jnp.zeros((n, n), F32)
    inverses = []
    for k in range(4):
        ta, tb = block(2 * k), block(2 * k + 1)
        pa, pb = split(ta), split(tb)
        off = -mul_pairs(split(mul_pairs(pb, pair_of(high, low, 256 * k + n, 256 * k, n))), pa)
        inverses.append(split(join(ta, zero, off, tb)))

    rest = jnp.concatenate([pair[0], pair[1], other_pair[0], other_pair[1]], axis=0)
    for k in range(4):
        x = mul(rest[:, :256], inverses[k], NT)
        x_ref[:, k * 256 : (k + 1) * 256] = x
        if k < 3:
            rows, cols = slice((k + 1) * 256, 1024), slice(k * 256, (k + 1) * 256)
            rest = rest[:, 256:] - mul(x, (high[rows, cols], low[rows, cols]), NT)


def update_kernel(place_ref, x_ref, *refs):
    held, outs, (high, low) = refs[:4], refs[4:8], refs[8:]
    bulk = place_ref[1]
    for dy in range(2):
        for m in range(4):
            h, l = split(held[2 * dy + m % 2][m // 2])
            high[:, offset(bulk ^ (2 * m + dy), 128)] = h
            low[:, offset(bulk ^ (2 * m + dy), 128)] = l
    upd = mul(x_ref[...], (high[...], low[...]), NT)
    for k, out in enumerate(outs):
        out[...] = upd[32 * k : 32 * (k + 1)]


def second_factor_kernel(place_ref, *refs):
    bufs, (high, low, diag) = refs[:10], refs[10:]
    place_pieces(place_ref, bufs, True, high, low, diag)
    n = 128
    i, j = iotas(n)

    def block(k):
        return jnp.where(i < j, diag[k, 0:n, :], 0.0) + jnp.where(i == j, diag[k, n + 1 : n + 2, :], 0.0)

    zero = jnp.zeros((n, n), F32)
    inverses = []
    for k in range(4):
        ta, tb = block(2 * k), block(2 * k + 1)
        pa, pb = split(ta), split(tb)
        off = -mul_pairs(split(mul_pairs(pa, pair_of(high, low, 256 * k, 256 * k + n, n))), pb)
        inverses.append(split(join(ta, off, zero, tb)))

    def put(r, c, value):
        high[r : r + 256, c : c + 256], low[r : r + 256, c : c + 256] = value

    for k in range(2):
        at = 512 * k
        pa, pb = inverses[2 * k], inverses[2 * k + 1]
        off = -mul_pairs(split(mul_pairs(pa, pair_of(high, low, at, at + 256, 256))), pb)
        put(at, at, pa)
        put(at + 256, at + 256, pb)
        put(at, at + 256, split(off))
        put(at + 256, at, (jnp.zeros((256, 256), BF16),) * 2)


def second_kernel(place_ref, x_ref, both_ref, uh_ref, ul_ref, mine, from_x, from_core, from_both, out_ref):
    x = x_ref[0:32, :]
    out_ref[:, 0:1024] = x
    parts = []
    for k in range(4):
        way = place_ref[0] ^ k
        upd = jnp.where(
            way == 0,
            mine[...],
            jnp.where(way == 2, from_x[...], jnp.where(way == 1, from_core[...], from_both[...])),
        )
        parts.append(both_ref[1, :, k * 256 : (k + 1) * 256] - upd)
    ra = jnp.concatenate(parts[:2], axis=1)
    rb = jnp.concatenate(parts[2:], axis=1)

    def u(r, c):
        rows, cols = slice(r * 512, r * 512 + 512), slice(c * 512, c * 512 + 512)
        return uh_ref[rows, cols], ul_ref[rows, cols]

    xa = mul(ra, u(0, 0))
    xb = mul(rb - mul(xa, u(0, 1)), u(1, 1))
    out_ref[:, 1024:1536] = xa
    out_ref[:, 1536:2048] = xb


BOTH = ("bulk", "rep")

SPREAD, INVERT, LEAVE, ROWS, FIRST, SECOND = 1_000_000_000, 3_500_000_000, 500_000_000, 1_000_000_000, 200_000_000, 3_000_000_000


def swap_z(x, m):
    return lax.ppermute(x, "bulk", [(k, k ^ (2 * m)) for k in range(8)])


def swap_y(x):
    return lax.ppermute(x, "bulk", [(k, k ^ 1) for k in range(8)])


def swap_rep(x, bits):
    return lax.ppermute(x, "rep", [(k, k ^ bits) for k in range(4)])


def cross(x, stage):
    pairs = []
    for rep in range(4):
        for bulk in range(8):
            to = (rep ^ 2, bulk) if (rep & 1) == stage else (rep, bulk ^ 1)
            pairs.append((bulk * 4 + rep, to[1] * 4 + to[0]))
    return lax.ppermute(x, BOTH, pairs)


def after(x, *deps):
    return lax.optimization_barrier((x,) + deps)[0]


ANY = pl.BlockSpec(memory_space=pl.ANY)
VMEM = pl.BlockSpec(memory_space=pltpu.VMEM)
SMEM = pl.BlockSpec(memory_space=pltpu.SMEM)


def call(kernel, out, specs, outs, scratch, flops, size, name):
    return pl.pallas_call(
        kernel,
        out_shape=out,
        in_specs=specs,
        out_specs=outs,
        scratch_shapes=scratch,
        compiler_params=pltpu.CompilerParams(vmem_limit_bytes=size << 20),
        cost_estimate=pl.CostEstimate(flops=flops, bytes_accessed=2 << 20, transcendentals=0),
        name=name,
    )


def shape(*dims, dtype=F32):
    return jax.ShapeDtypeStruct(dims, dtype)


def per_device(orbitals, triangles, coupling, diagonals):
    rep, bulk = lax.axis_index("rep"), lax.axis_index("bulk")
    place = jnp.stack([rep, bulk]).astype(jnp.int32)
    blocks = orbitals.reshape(4, 2, 32, 256)

    t = call(invert_kernel, shape(264, 128), [SMEM, VMEM, VMEM], VMEM, [], INVERT, 4, "invert")(
        place, triangles, diagonals
    )
    coup = after(coupling, t)

    near = jnp.stack([t, swap_z(t, 2)])
    far = swap_z(near, 1)
    near0 = swap_y(near)
    near1 = swap_rep(near, 2)
    near01 = swap_rep(near0, 2)

    leave = call(leave_kernel, shape(4, 32, 256), [SMEM, VMEM], VMEM, [], LEAVE, 4, "leave")(place, blocks)
    came = swap_y(after(leave, t))
    c_near = jnp.stack([coupling, swap_z(after(coup, near), 2)])
    c_near_got = swap_y(c_near)

    far_now = after(far, near0, near1, came, c_near)
    far0 = cross(far_now, 0)
    far1 = cross(far_now, 1)
    b_out = call(spread_kernel, [shape(2, 32, 256)] * 3, [SMEM, VMEM, VMEM], [VMEM] * 3, [], SPREAD, 4, "spread")(
        place, blocks, came
    )
    b_z = [swap_z(after(b, far, *((near01,) if m == 2 else ())), m + 1) for m, b in enumerate(b_out)]
    c_far = swap_z(after(c_near, far0), 1)
    c_far_got = swap_y(c_far)
    far01 = cross(after(far0, far1, near01), 1)

    left, both = call(
        rows_kernel,
        [shape(32, 1024), shape(2, 32, 1024)],
        [SMEM] + [VMEM] * 5,
        [VMEM] * 2,
        [],
        ROWS,
        4,
        "rows",
    )(place, blocks, came, *b_z)
    pair = jnp.stack([left, swap_rep(after(left, came), 2)])
    other_pair = swap_rep(after(pair, c_far), 1)
    bufs = [jnp.concatenate([near, near0], axis=0), jnp.concatenate([near1, near01], axis=0)]
    bufs += [jnp.concatenate([far, far0], axis=0), far1, far01]
    bufs += [swap_rep(after(b, b_z[2], far0), 1) for b in bufs[:4]] + [swap_rep(after(far01, far1), 1)]

    scratch = [pltpu.VMEM((8, 136, 128), F32)]
    halves = [shape(1024, 1024, dtype=BF16)] * 2
    x = call(
        first_kernel,
        shape(128, 1024),
        [SMEM] + [VMEM] * 12,
        VMEM,
        [pltpu.VMEM((1024, 1024), BF16)] * 2 + scratch,
        FIRST,
        24,
        "first_panel",
    )(place, pair, after(other_pair, c_near_got), *bufs)

    mine, to_x, to_core, to_both = call(
        update_kernel,
        [shape(32, 256)] * 4,
        [SMEM] + [VMEM] * 5,
        [VMEM] * 4,
        [pltpu.VMEM((256, 1024), BF16)] * 2,
        2_000_000_000,
        24,
        "update",
    )(place, x, c_near, c_far, c_near_got, c_far_got)
    back = [swap_rep(to_x, 2), swap_rep(to_core, 1), swap_rep(to_both, 3)]

    uh, ul = call(
        second_factor_kernel, halves, [SMEM] + [VMEM] * 10, [VMEM] * 2, scratch, SECOND, 24, "second_factor"
    )(after(place, mine), *bufs)

    return call(second_kernel, shape(32, 2048), [SMEM] + [VMEM] * 8, VMEM, [], 2_500_000_000, 24, "second_panel")(
        place, x, both, uh, ul, mine, *back
    )


def solution(mesh):
    special = mesh.shape["bulk"] == 8 and mesh.shape["rep"] == 4

    def run(orbitals, triangles, coupling, diagonals):
        fits = orbitals.shape == (1024, 2048) and triangles.shape == (1024, 1024)
        body = per_device if special and fits else per_device_any
        return jax.shard_map(
            body,
            mesh=mesh,
            in_specs=(P("rep", "bulk"), P("rep", "bulk"), P("rep", "bulk"), P(None, "bulk")),
            out_specs=P(("rep", "bulk"), None),
            check_vma=False,
        )(orbitals, triangles, coupling, diagonals)

    return run
```

```python
import jax
import jax.numpy as jnp
from jax import lax
from jax.experimental import pallas as pl
from jax.experimental.pallas import tpu as pltpu
from jax.sharding import PartitionSpec as P

F32 = jnp.float32
BF16 = jnp.bfloat16
NN = (((1,), (0,)), ((), ()))
NT = (((1,), (1,)), ((), ()))


def unpack(triangles, diagonals):
    first_block = jnp.tril(triangles, -1) + jnp.diag(diagonals[0])
    second_block = jnp.tril(triangles.T, -1) + jnp.diag(diagonals[1])
    return (first_block, second_block)


def per_device_any(orbitals, triangles, coupling, diagonals):
    tri_rows, couple_rows = (
        lax.all_gather(triangles, "rep", axis=0, tiled=True),
        lax.all_gather(coupling, "rep", axis=0, tiled=True),
    )
    tri_whole, couple_whole, diag_whole = (
        lax.all_gather(tri_rows, "bulk", axis=1, tiled=True),
        lax.all_gather(couple_rows, "bulk", axis=1, tiled=True),
        lax.all_gather(diagonals, "bulk", axis=1, tiled=True),
    )
    first_block, second_block = unpack(tri_whole, diag_whole)
    panel = first_block.shape[0]
    groups = lax.axis_size("bulk")
    local_rows = orbitals.shape[0] // groups
    blocks = orbitals.reshape(groups, local_rows, orbitals.shape[1])
    received = lax.all_to_all(blocks, "bulk", split_axis=0, concat_axis=2, tiled=True)
    rows_now = received.reshape(local_rows, received.shape[2])
    left_part = rows_now[:, :panel]
    right_part = rows_now[:, panel:]
    solved_one = jax.scipy.linalg.solve_triangular(first_block, left_part.T, lower=True).T
    update = jnp.dot(
        solved_one,
        couple_whole.T,
        precision=lax.Precision.HIGHEST,
        preferred_element_type=jnp.float32,
    )
    solved_two = jax.scipy.linalg.solve_triangular(
        second_block, (right_part - update).T, lower=True
    ).T
    return jnp.concatenate([solved_one, solved_two], axis=1)


def dot(a, b, dims=NN):
    return lax.dot_general(a, b, dims, preferred_element_type=F32)


def dot_exact(a, b):
    return lax.dot_general(a, b, NN, precision=lax.Precision.HIGHEST, preferred_element_type=F32)


def split(x):
    high = x.astype(BF16)
    return high, (x - high.astype(F32)).astype(BF16)


def mul(x, b, dims=NN):
    xh, xl = split(x)
    bh, bl = b
    m = x.shape[0]
    both = dot(jnp.concatenate([xh, xl], axis=0), bh, dims)
    return (both[:m] + both[m:]) + dot(xh, bl, dims)


def mul3(a, b):
    (ah, al), (bh, bl) = split(a), split(b)
    return dot(ah, bh) + (dot(al, bh) + dot(ah, bl))


def iotas(n):
    return lax.broadcasted_iota(jnp.int32, (n, n), 0), lax.broadcasted_iota(jnp.int32, (n, n), 1)


def invert_kernel(place_ref, tri_ref, diag_ref, t_ref):
    rep, bulk = place_ref[0], place_ref[1]
    rows, n = tri_ref.shape
    inv = 1.0 / diag_ref[...]
    t_ref[0:rows, :] = tri_ref[...]
    t_ref[rows : rows + 8, :] = jnp.concatenate([inv, jnp.zeros((6, n), F32)], axis=0)

    @pl.when(rep == bulk // 2)
    def _():
        start = pl.multiple_of((bulk % 2) * n, n)
        block = tri_ref[pl.ds(start, n), :]
        i, j = iotas(n)
        eye = i == j
        ans = []
        for which in range(2):
            row, col = (i, j) if which == 0 else (j, i)
            along = inv[which : which + 1, :]
            d = jnp.where(eye, along, 0.0)
            down = jnp.sum(d, axis=1, keepdims=True)
            part = (row >> 1 == col >> 1) & (row > col)
            ans.append(d - jnp.where(part, block * along * down, 0.0))
        level = 1
        while (1 << level) < n:
            for which in range(2):
                row, col = (i, j) if which == 0 else (j, i)
                part = (row >> (level + 1) == col >> (level + 1)) & (row >> level > col >> level)
                t = ans[which]
                ans[which] = t - mul3(mul3(t, jnp.where(part, block, 0.0)), t)
            level += 1
        t_ref[pl.ds(start, n), :] = jnp.where(i >= j, ans[0], ans[1])


def leave_kernel(place_ref, orb, out):
    y = place_ref[1] & 1
    for k in range(4):
        out[k] = orb[k, 1 - y]


def spread_kernel(place_ref, orb, came, b1, b2, b3):
    z, y = place_ref[1] >> 1, place_ref[1] & 1
    for m, ref in ((1, b1), (2, b2), (3, b3)):
        ref[0] = orb[z ^ m, y]
        ref[1] = came[z ^ m]


def rows_kernel(place_ref, orb, came, b1, b2, b3, left, both):
    z, y = place_ref[1] >> 1, place_ref[1] & 1

    def put(m, dy, value):
        k = 2 * (z ^ m) + (y ^ dy)
        both[k >> 2, :, pl.ds(pl.multiple_of((k & 3) * 256, 256), 256)] = value

    put(0, 0, orb[z, y])
    put(0, 1, came[z])
    for m, ref in ((1, b1), (2, b2), (3, b3)):
        put(m, 0, ref[0])
        put(m, 1, ref[1])
    left[...] = both[0]


def origin(place_ref, crossed, first, second, m):
    rep, bulk = place_ref[0], place_ref[1]
    if m % 2 == 0:
        dx, dy = second, first
    else:
        core = (rep & 1) ^ crossed
        dx = jnp.where(core == 0, first, second)
        dy = jnp.where(core == 0, second, first)
    return rep ^ (2 * dx + crossed), bulk ^ (2 * m + dy)


def pieces(bufs):
    found = []
    for crossed in range(2):
        for m in range(4):
            for second in range(2):
                for first in range(2):
                    buf = bufs[8 * crossed + 4 * (m % 2) + 2 * second + first]
                    found.append((buf.at[m // 2], (crossed, first, second, m)))
    return found


def offset(index, size):
    return pl.ds(pl.multiple_of(index * size, size), size)


def place_pieces(place_ref, bufs, upper, high, low, diag):
    for piece, args in pieces(bufs):
        rep, bulk = origin(place_ref, *args)

        @pl.when((rep <= bulk // 2) if upper else (rep >= bulk // 2))
        def _():
            h, l = split(piece[0:256, :])
            high[offset(rep, 256), offset(bulk, 128)] = h
            low[offset(rep, 256), offset(bulk, 128)] = l

        @pl.when(rep == bulk // 2)
        def _():
            diag[bulk, 0:128, :] = piece[pl.ds(pl.multiple_of((bulk % 2) * 128, 128), 128), :]
            diag[bulk, 128:136, :] = piece[256:264, :]


def mul_pairs(a, b):
    (ah, al), (bh, bl) = a, b
    return dot(ah, bh) + (dot(al, bh) + dot(ah, bl))


def pair_of(high, low, r, c, size):
    rows, cols = slice(r, r + size), slice(c, c + size)
    return high[rows, cols], low[rows, cols]


def join(a, b, c, d):
    return jnp.concatenate([jnp.concatenate([a, b], axis=1), jnp.concatenate([c, d], axis=1)], axis=0)


def first_kernel(place_ref, pair, other_pair, *refs):
    bufs, (x_ref, high, low, diag) = refs[:16], refs[16:]
    place_pieces(place_ref, bufs, False, high, low, diag)
    n = 128
    i, j = iotas(n)

    def block(k):
        return jnp.where(i > j, diag[k, 0:n, :], 0.0) + jnp.where(i == j, diag[k, n : n + 1, :], 0.0)

    zero = jnp.zeros((n, n), F32)
    inverses = []
    for k in range(4):
        ta, tb = block(2 * k), block(2 * k + 1)
        pa, pb = split(ta), split(tb)
        off = -mul_pairs(split(mul_pairs(pb, pair_of(high, low, 256 * k + n, 256 * k, n))), pa)
        inverses.append(split(join(ta, zero, off, tb)))

    rest = jnp.concatenate([pair[0], pair[1], other_pair[0], other_pair[1]], axis=0)
    for k in range(4):
        x = mul(rest[:, :256], inverses[k], NT)
        x_ref[:, k * 256 : (k + 1) * 256] = x
        if k < 3:
            rows, cols = slice((k + 1) * 256, 1024), slice(k * 256, (k + 1) * 256)
            rest = rest[:, 256:] - mul(x, (high[rows, cols], low[rows, cols]), NT)


def update_kernel(place_ref, x_ref, *refs):
    held, outs, (high, low) = refs[:4], refs[4:8], refs[8:]
    bulk = place_ref[1]
    for dy in range(2):
        for m in range(4):
            h, l = split(held[2 * dy + m % 2][m // 2])
            high[:, offset(bulk ^ (2 * m + dy), 128)] = h
            low[:, offset(bulk ^ (2 * m + dy), 128)] = l
    upd = mul(x_ref[...], (high[...], low[...]), NT)
    for k, out in enumerate(outs):
        out[...] = upd[32 * k : 32 * (k + 1)]


def second_factor_kernel(place_ref, *refs):
    bufs, (high, low, diag) = refs[:16], refs[16:]
    place_pieces(place_ref, bufs, True, high, low, diag)
    n = 128
    i, j = iotas(n)

    def block(k):
        return jnp.where(i < j, diag[k, 0:n, :], 0.0) + jnp.where(i == j, diag[k, n + 1 : n + 2, :], 0.0)

    zero = jnp.zeros((n, n), F32)
    inverses = []
    for k in range(4):
        ta, tb = block(2 * k), block(2 * k + 1)
        pa, pb = split(ta), split(tb)
        off = -mul_pairs(split(mul_pairs(pa, pair_of(high, low, 256 * k, 256 * k + n, n))), pb)
        inverses.append(split(join(ta, off, zero, tb)))

    def put(r, c, value):
        high[r : r + 256, c : c + 256], low[r : r + 256, c : c + 256] = value

    for k in range(2):
        at = 512 * k
        pa, pb = inverses[2 * k], inverses[2 * k + 1]
        off = -mul_pairs(split(mul_pairs(pa, pair_of(high, low, at, at + 256, 256))), pb)
        put(at, at, pa)
        put(at + 256, at + 256, pb)
        put(at, at + 256, split(off))
        put(at + 256, at, (jnp.zeros((256, 256), BF16),) * 2)


def second_kernel(place_ref, x_ref, both_ref, uh_ref, ul_ref, mine, from_x, from_core, from_both, out_ref):
    x = x_ref[0:32, :]
    out_ref[:, 0:1024] = x
    parts = []
    for k in range(4):
        way = place_ref[0] ^ k
        upd = jnp.where(
            way == 0,
            mine[...],
            jnp.where(way == 2, from_x[...], jnp.where(way == 1, from_core[...], from_both[...])),
        )
        parts.append(both_ref[1, :, k * 256 : (k + 1) * 256] - upd)
    ra = jnp.concatenate(parts[:2], axis=1)
    rb = jnp.concatenate(parts[2:], axis=1)

    def u(r, c):
        rows, cols = slice(r * 512, r * 512 + 512), slice(c * 512, c * 512 + 512)
        return uh_ref[rows, cols], ul_ref[rows, cols]

    xa = mul(ra, u(0, 0))
    xb = mul(rb - mul(xa, u(0, 1)), u(1, 1))
    out_ref[:, 1024:1536] = xa
    out_ref[:, 1536:2048] = xb


BOTH = ("bulk", "rep")

SPREAD, INVERT, LEAVE, ROWS, FIRST, SECOND = 1_000_000_000, 3_500_000_000, 500_000_000, 1_000_000_000, 200_000_000, 3_000_000_000


def swap_z(x, m):
    return lax.ppermute(x, "bulk", [(k, k ^ (2 * m)) for k in range(8)])


def swap_y(x):
    return lax.ppermute(x, "bulk", [(k, k ^ 1) for k in range(8)])


def swap_rep(x, bits):
    return lax.ppermute(x, "rep", [(k, k ^ bits) for k in range(4)])


def cross(x, stage):
    pairs = []
    for rep in range(4):
        for bulk in range(8):
            to = (rep ^ 2, bulk) if (rep & 1) == stage else (rep, bulk ^ 1)
            pairs.append((bulk * 4 + rep, to[1] * 4 + to[0]))
    return lax.ppermute(x, BOTH, pairs)


def after(x, *deps):
    return lax.optimization_barrier((x,) + deps)[0]


ANY = pl.BlockSpec(memory_space=pl.ANY)
VMEM = pl.BlockSpec(memory_space=pltpu.VMEM)
SMEM = pl.BlockSpec(memory_space=pltpu.SMEM)


def call(kernel, out, specs, outs, scratch, flops, size, name):
    return pl.pallas_call(
        kernel,
        out_shape=out,
        in_specs=specs,
        out_specs=outs,
        scratch_shapes=scratch,
        compiler_params=pltpu.CompilerParams(vmem_limit_bytes=size << 20),
        cost_estimate=pl.CostEstimate(flops=flops, bytes_accessed=2 << 20, transcendentals=0),
        name=name,
    )


def shape(*dims, dtype=F32):
    return jax.ShapeDtypeStruct(dims, dtype)


def per_device(orbitals, triangles, coupling, diagonals):
    rep, bulk = lax.axis_index("rep"), lax.axis_index("bulk")
    place = jnp.stack([rep, bulk]).astype(jnp.int32)
    blocks = orbitals.reshape(4, 2, 32, 256)

    t = call(invert_kernel, shape(264, 128), [SMEM, VMEM, VMEM], VMEM, [], INVERT, 4, "invert")(
        place, triangles, diagonals
    )
    coup = after(coupling, t)

    near = jnp.stack([t, swap_z(t, 2)])
    far = swap_z(near, 1)
    near0 = swap_y(near)
    near1 = swap_rep(near, 2)
    near01 = swap_rep(near0, 2)

    leave = call(leave_kernel, shape(4, 32, 256), [SMEM, VMEM], VMEM, [], LEAVE, 4, "leave")(place, blocks)
    came = swap_y(after(leave, t))
    c_near = jnp.stack([coupling, swap_z(after(coup, near), 2)])
    c_near_got = swap_y(c_near)

    far_now = after(far, near0, near1, came, c_near)
    far0 = cross(far_now, 0)
    far1 = cross(far_now, 1)
    b_out = call(spread_kernel, [shape(2, 32, 256)] * 3, [SMEM, VMEM, VMEM], [VMEM] * 3, [], SPREAD, 4, "spread")(
        place, blocks, came
    )
    b_z = [swap_z(after(b, far), m + 1) for m, b in enumerate(b_out)]
    c_far = swap_z(after(c_near, far0), 1)
    c_far_got = swap_y(c_far)
    far01 = cross(after(far0, far1, near01), 1)

    left, both = call(
        rows_kernel,
        [shape(32, 1024), shape(2, 32, 1024)],
        [SMEM] + [VMEM] * 5,
        [VMEM] * 2,
        [],
        ROWS,
        4,
        "rows",
    )(place, blocks, came, *b_z)
    pair = jnp.stack([left, swap_rep(after(left, came), 2)])
    other_pair = swap_rep(after(pair, c_far), 1)
    bufs = [near, near0, near1, near01, far, far0, far1, far01]
    bufs += [swap_rep(after(b, b_z[2], far0), 1) for b in bufs[:7]] + [swap_rep(after(far01, far1), 1)]

    scratch = [pltpu.VMEM((8, 136, 128), F32)]
    halves = [shape(1024, 1024, dtype=BF16)] * 2
    x = call(
        first_kernel,
        shape(128, 1024),
        [SMEM] + [VMEM] * 18,
        VMEM,
        [pltpu.VMEM((1024, 1024), BF16)] * 2 + scratch,
        FIRST,
        24,
        "first_panel",
    )(place, pair, after(other_pair, c_near_got), *bufs)

    uh, ul = call(
        second_factor_kernel, halves, [SMEM] + [VMEM] * 16, [VMEM] * 2, scratch, SECOND, 24, "second_factor"
    )(after(place, x), *bufs)

    mine, to_x, to_core, to_both = call(
        update_kernel,
        [shape(32, 256)] * 4,
        [SMEM] + [VMEM] * 5,
        [VMEM] * 4,
        [pltpu.VMEM((256, 1024), BF16)] * 2,
        2_000_000_000,
        24,
        "update",
    )(place, after(x, uh), c_near, c_far, c_near_got, c_far_got)
    back = [swap_rep(to_x, 2), swap_rep(to_core, 1), swap_rep(to_both, 3)]

    return call(second_kernel, shape(32, 2048), [SMEM] + [VMEM] * 8, VMEM, [], 2_500_000_000, 24, "second_panel")(
        place, x, both, uh, ul, mine, *back
    )


def solution(mesh):
    special = mesh.shape["bulk"] == 8 and mesh.shape["rep"] == 4

    def run(orbitals, triangles, coupling, diagonals):
        fits = orbitals.shape == (1024, 2048) and triangles.shape == (1024, 1024)
        body = per_device if special and fits else per_device_any
        return jax.shard_map(
            body,
            mesh=mesh,
            in_specs=(P("rep", "bulk"), P("rep", "bulk"), P("rep", "bulk"), P(None, "bulk")),
            out_specs=P(("rep", "bulk"), None),
            check_vma=False,
        )(orbitals, triangles, coupling, diagonals)

    return run
```

```python
import jax
import jax.numpy as jnp
from jax import lax
from jax.experimental import pallas as pl
from jax.experimental.pallas import tpu as pltpu
from jax.sharding import PartitionSpec as P

F32 = jnp.float32
BF16 = jnp.bfloat16
NN = (((1,), (0,)), ((), ()))
NT = (((1,), (1,)), ((), ()))


def unpack(triangles, diagonals):
    first_block = jnp.tril(triangles, -1) + jnp.diag(diagonals[0])
    second_block = jnp.tril(triangles.T, -1) + jnp.diag(diagonals[1])
    return (first_block, second_block)


def per_device_any(orbitals, triangles, coupling, diagonals):
    tri_rows, couple_rows = (
        lax.all_gather(triangles, "rep", axis=0, tiled=True),
        lax.all_gather(coupling, "rep", axis=0, tiled=True),
    )
    tri_whole, couple_whole, diag_whole = (
        lax.all_gather(tri_rows, "bulk", axis=1, tiled=True),
        lax.all_gather(couple_rows, "bulk", axis=1, tiled=True),
        lax.all_gather(diagonals, "bulk", axis=1, tiled=True),
    )
    first_block, second_block = unpack(tri_whole, diag_whole)
    panel = first_block.shape[0]
    groups = lax.axis_size("bulk")
    local_rows = orbitals.shape[0] // groups
    blocks = orbitals.reshape(groups, local_rows, orbitals.shape[1])
    received = lax.all_to_all(blocks, "bulk", split_axis=0, concat_axis=2, tiled=True)
    rows_now = received.reshape(local_rows, received.shape[2])
    left_part = rows_now[:, :panel]
    right_part = rows_now[:, panel:]
    solved_one = jax.scipy.linalg.solve_triangular(first_block, left_part.T, lower=True).T
    update = jnp.dot(
        solved_one,
        couple_whole.T,
        precision=lax.Precision.HIGHEST,
        preferred_element_type=jnp.float32,
    )
    solved_two = jax.scipy.linalg.solve_triangular(
        second_block, (right_part - update).T, lower=True
    ).T
    return jnp.concatenate([solved_one, solved_two], axis=1)


def dot(a, b, dims=NN):
    return lax.dot_general(a, b, dims, preferred_element_type=F32)


def dot_exact(a, b):
    return lax.dot_general(a, b, NN, precision=lax.Precision.HIGHEST, preferred_element_type=F32)


def split(x):
    high = x.astype(BF16)
    return high, (x - high.astype(F32)).astype(BF16)


def mul(x, b, dims=NN):
    xh, xl = split(x)
    bh, bl = b
    m = x.shape[0]
    both = dot(jnp.concatenate([xh, xl], axis=0), bh, dims)
    return (both[:m] + both[m:]) + dot(xh, bl, dims)


def mul3(a, b):
    (ah, al), (bh, bl) = split(a), split(b)
    return dot(ah, bh) + (dot(al, bh) + dot(ah, bl))


def iotas(n):
    return lax.broadcasted_iota(jnp.int32, (n, n), 0), lax.broadcasted_iota(jnp.int32, (n, n), 1)


def invert_kernel(place_ref, tri_ref, diag_ref, t_ref):
    rep, bulk = place_ref[0], place_ref[1]
    rows, n = tri_ref.shape
    inv = 1.0 / diag_ref[...]
    t_ref[0:rows, :] = tri_ref[...]
    t_ref[rows : rows + 8, :] = jnp.concatenate([inv, jnp.zeros((6, n), F32)], axis=0)

    @pl.when(rep == bulk // 2)
    def _():
        start = pl.multiple_of((bulk % 2) * n, n)
        block = tri_ref[pl.ds(start, n), :]
        i, j = iotas(n)
        eye = i == j
        ans = []
        for which in range(2):
            row, col = (i, j) if which == 0 else (j, i)
            along = inv[which : which + 1, :]
            d = jnp.where(eye, along, 0.0)
            down = jnp.sum(d, axis=1, keepdims=True)
            part = (row >> 1 == col >> 1) & (row > col)
            ans.append(d - jnp.where(part, block * along * down, 0.0))
        level = 1
        while (1 << level) < n:
            for which in range(2):
                row, col = (i, j) if which == 0 else (j, i)
                part = (row >> (level + 1) == col >> (level + 1)) & (row >> level > col >> level)
                t = ans[which]
                ans[which] = t - mul3(mul3(t, jnp.where(part, block, 0.0)), t)
            level += 1
        t_ref[pl.ds(start, n), :] = jnp.where(i >= j, ans[0], ans[1])


def leave_kernel(place_ref, orb, out):
    y = place_ref[1] & 1
    for k in range(4):
        out[k] = orb[k, 1 - y]


def spread_kernel(place_ref, orb, came, b1, b2, b3):
    z, y = place_ref[1] >> 1, place_ref[1] & 1
    for m, ref in ((1, b1), (2, b2), (3, b3)):
        ref[0] = orb[z ^ m, y]
        ref[1] = came[z ^ m]


def rows_kernel(place_ref, orb, came, b1, b2, b3, left, both):
    z, y = place_ref[1] >> 1, place_ref[1] & 1

    def put(m, dy, value):
        k = 2 * (z ^ m) + (y ^ dy)
        both[k >> 2, :, pl.ds(pl.multiple_of((k & 3) * 256, 256), 256)] = value

    put(0, 0, orb[z, y])
    put(0, 1, came[z])
    for m, ref in ((1, b1), (2, b2), (3, b3)):
        put(m, 0, ref[0])
        put(m, 1, ref[1])
    left[...] = both[0]


def origin(place_ref, crossed, first, second, m):
    rep, bulk = place_ref[0], place_ref[1]
    if m % 2 == 0:
        dx, dy = second, first
    else:
        core = (rep & 1) ^ crossed
        dx = jnp.where(core == 0, first, second)
        dy = jnp.where(core == 0, second, first)
    return rep ^ (2 * dx + crossed), bulk ^ (2 * m + dy)


def pieces(bufs):
    found = []
    for crossed in range(2):
        for m in range(4):
            for second in range(2):
                for first in range(2):
                    buf = bufs[8 * crossed + 4 * (m % 2) + 2 * second + first]
                    found.append((buf.at[m // 2], (crossed, first, second, m)))
    return found


def offset(index, size):
    return pl.ds(pl.multiple_of(index * size, size), size)


def place_pieces(place_ref, bufs, upper, high, low, diag):
    for piece, args in pieces(bufs):
        rep, bulk = origin(place_ref, *args)

        @pl.when((rep <= bulk // 2) if upper else (rep >= bulk // 2))
        def _():
            h, l = split(piece[0:256, :])
            high[offset(rep, 256), offset(bulk, 128)] = h
            low[offset(rep, 256), offset(bulk, 128)] = l

        @pl.when(rep == bulk // 2)
        def _():
            diag[bulk, 0:128, :] = piece[pl.ds(pl.multiple_of((bulk % 2) * 128, 128), 128), :]
            diag[bulk, 128:136, :] = piece[256:264, :]


def mul_pairs(a, b):
    (ah, al), (bh, bl) = a, b
    return dot(ah, bh) + (dot(al, bh) + dot(ah, bl))


def pair_of(high, low, r, c, size):
    rows, cols = slice(r, r + size), slice(c, c + size)
    return high[rows, cols], low[rows, cols]


def join(a, b, c, d):
    return jnp.concatenate([jnp.concatenate([a, b], axis=1), jnp.concatenate([c, d], axis=1)], axis=0)


def first_kernel(place_ref, pair, other_pair, *refs):
    bufs, (x_ref, high, low, diag) = refs[:16], refs[16:]
    place_pieces(place_ref, bufs, False, high, low, diag)
    n = 128
    i, j = iotas(n)

    def block(k):
        return jnp.where(i > j, diag[k, 0:n, :], 0.0) + jnp.where(i == j, diag[k, n : n + 1, :], 0.0)

    zero = jnp.zeros((n, n), F32)
    inverses = []
    for k in range(4):
        ta, tb = block(2 * k), block(2 * k + 1)
        pa, pb = split(ta), split(tb)
        off = -mul_pairs(split(mul_pairs(pb, pair_of(high, low, 256 * k + n, 256 * k, n))), pa)
        inverses.append(split(join(ta, zero, off, tb)))

    rest = jnp.concatenate([pair[0], pair[1], other_pair[0], other_pair[1]], axis=0)
    for k in range(4):
        x = mul(rest[:, :256], inverses[k], NT)
        x_ref[:, k * 256 : (k + 1) * 256] = x
        if k < 3:
            rows, cols = slice((k + 1) * 256, 1024), slice(k * 256, (k + 1) * 256)
            rest = rest[:, 256:] - mul(x, (high[rows, cols], low[rows, cols]), NT)


def update_kernel(place_ref, x_ref, *refs):
    held, outs, (high, low) = refs[:4], refs[4:8], refs[8:]
    bulk = place_ref[1]
    for dy in range(2):
        for m in range(4):
            h, l = split(held[2 * dy + m % 2][m // 2])
            high[:, offset(bulk ^ (2 * m + dy), 128)] = h
            low[:, offset(bulk ^ (2 * m + dy), 128)] = l
    upd = mul(x_ref[...], (high[...], low[...]), NT)
    for k, out in enumerate(outs):
        out[...] = upd[32 * k : 32 * (k + 1)]


def second_factor_kernel(place_ref, *refs):
    bufs, (high, low, diag) = refs[:16], refs[16:]
    place_pieces(place_ref, bufs, True, high, low, diag)
    n = 128
    i, j = iotas(n)

    def block(k):
        return jnp.where(i < j, diag[k, 0:n, :], 0.0) + jnp.where(i == j, diag[k, n + 1 : n + 2, :], 0.0)

    zero = jnp.zeros((n, n), F32)
    inverses = []
    for k in range(4):
        ta, tb = block(2 * k), block(2 * k + 1)
        pa, pb = split(ta), split(tb)
        off = -mul_pairs(split(mul_pairs(pa, pair_of(high, low, 256 * k, 256 * k + n, n))), pb)
        inverses.append(split(join(ta, off, zero, tb)))

    def put(r, c, value):
        high[r : r + 256, c : c + 256], low[r : r + 256, c : c + 256] = value

    for k in range(2):
        at = 512 * k
        pa, pb = inverses[2 * k], inverses[2 * k + 1]
        off = -mul_pairs(split(mul_pairs(pa, pair_of(high, low, at, at + 256, 256))), pb)
        put(at, at, pa)
        put(at + 256, at + 256, pb)
        put(at, at + 256, split(off))
        put(at + 256, at, (jnp.zeros((256, 256), BF16),) * 2)


def second_kernel(place_ref, x_ref, both_ref, uh_ref, ul_ref, mine, from_x, from_core, from_both, out_ref):
    x = x_ref[0:32, :]
    out_ref[:, 0:1024] = x
    parts = []
    for k in range(4):
        way = place_ref[0] ^ k
        upd = jnp.where(
            way == 0,
            mine[...],
            jnp.where(way == 2, from_x[...], jnp.where(way == 1, from_core[...], from_both[...])),
        )
        parts.append(both_ref[1, :, k * 256 : (k + 1) * 256] - upd)
    ra = jnp.concatenate(parts[:2], axis=1)
    rb = jnp.concatenate(parts[2:], axis=1)

    def u(r, c):
        rows, cols = slice(r * 512, r * 512 + 512), slice(c * 512, c * 512 + 512)
        return uh_ref[rows, cols], ul_ref[rows, cols]

    xa = mul(ra, u(0, 0))
    xb = mul(rb - mul(xa, u(0, 1)), u(1, 1))
    out_ref[:, 1024:1536] = xa
    out_ref[:, 1536:2048] = xb


BOTH = ("bulk", "rep")

SPREAD, INVERT, LEAVE, ROWS, FIRST, SECOND = 1_000_000_000, 3_500_000_000, 500_000_000, 1_000_000_000, 200_000_000, 3_000_000_000


def swap_z(x, m):
    return lax.ppermute(x, "bulk", [(k, k ^ (2 * m)) for k in range(8)])


def swap_y(x):
    return lax.ppermute(x, "bulk", [(k, k ^ 1) for k in range(8)])


def swap_rep(x, bits):
    return lax.ppermute(x, "rep", [(k, k ^ bits) for k in range(4)])


def cross(x, stage):
    pairs = []
    for rep in range(4):
        for bulk in range(8):
            to = (rep ^ 2, bulk) if (rep & 1) == stage else (rep, bulk ^ 1)
            pairs.append((bulk * 4 + rep, to[1] * 4 + to[0]))
    return lax.ppermute(x, BOTH, pairs)


def after(x, *deps):
    return lax.optimization_barrier((x,) + deps)[0]


ANY = pl.BlockSpec(memory_space=pl.ANY)
VMEM = pl.BlockSpec(memory_space=pltpu.VMEM)
SMEM = pl.BlockSpec(memory_space=pltpu.SMEM)


def call(kernel, out, specs, outs, scratch, flops, size, name):
    return pl.pallas_call(
        kernel,
        out_shape=out,
        in_specs=specs,
        out_specs=outs,
        scratch_shapes=scratch,
        compiler_params=pltpu.CompilerParams(vmem_limit_bytes=size << 20),
        cost_estimate=pl.CostEstimate(flops=flops, bytes_accessed=2 << 20, transcendentals=0),
        name=name,
    )


def shape(*dims, dtype=F32):
    return jax.ShapeDtypeStruct(dims, dtype)


def per_device(orbitals, triangles, coupling, diagonals):
    rep, bulk = lax.axis_index("rep"), lax.axis_index("bulk")
    place = jnp.stack([rep, bulk]).astype(jnp.int32)
    blocks = orbitals.reshape(4, 2, 32, 256)

    t = call(invert_kernel, shape(264, 128), [SMEM, VMEM, VMEM], VMEM, [], INVERT, 4, "invert")(
        place, triangles, diagonals
    )
    coup = after(coupling, t)

    near = jnp.stack([t, swap_z(t, 2)])
    far = swap_z(near, 1)
    near0 = swap_y(near)
    near1 = swap_rep(near, 2)
    near01 = swap_rep(near0, 2)

    leave = call(leave_kernel, shape(4, 32, 256), [SMEM, VMEM], VMEM, [], LEAVE, 4, "leave")(place, blocks)
    came = swap_y(after(leave, t))
    c_near = jnp.stack([coupling, swap_z(after(coup, near), 2)])
    c_near_got = swap_y(c_near)

    far_now = after(far, near0, near1, came)
    far0 = cross(far_now, 0)
    far1 = cross(far_now, 1)
    b_out = call(spread_kernel, [shape(2, 32, 256)] * 3, [SMEM, VMEM, VMEM], [VMEM] * 3, [], SPREAD, 4, "spread")(
        place, blocks, came
    )
    b_z = [swap_z(after(b, far, *((near01, c_near) if m == 2 else ())), m + 1) for m, b in enumerate(b_out)]
    c_far = swap_z(after(c_near, far0), 1)
    c_far_got = swap_y(c_far)
    far01 = cross(after(far0, far1, near01), 1)

    left, both = call(
        rows_kernel,
        [shape(32, 1024), shape(2, 32, 1024)],
        [SMEM] + [VMEM] * 5,
        [VMEM] * 2,
        [],
        ROWS,
        4,
        "rows",
    )(place, blocks, came, *b_z)
    pair = jnp.stack([left, swap_rep(after(left, came), 2)])
    other_pair = swap_rep(after(pair, c_far), 1)
    bufs = [near, near0, near1, near01, far, far0, far1, far01]
    bufs += [swap_rep(after(b, b_z[2], far0), 1) for b in bufs[:7]] + [swap_rep(after(far01, far1), 1)]

    scratch = [pltpu.VMEM((8, 136, 128), F32)]
    halves = [shape(1024, 1024, dtype=BF16)] * 2
    x = call(
        first_kernel,
        shape(128, 1024),
        [SMEM] + [VMEM] * 18,
        VMEM,
        [pltpu.VMEM((1024, 1024), BF16)] * 2 + scratch,
        FIRST,
        24,
        "first_panel",
    )(place, pair, after(other_pair, c_near_got), *bufs)

    mine, to_x, to_core, to_both = call(
        update_kernel,
        [shape(32, 256)] * 4,
        [SMEM] + [VMEM] * 5,
        [VMEM] * 4,
        [pltpu.VMEM((256, 1024), BF16)] * 2,
        2_000_000_000,
        24,
        "update",
    )(place, x, c_near, c_far, c_near_got, c_far_got)
    back = [swap_rep(to_x, 2), swap_rep(to_core, 1), swap_rep(to_both, 3)]

    uh, ul = call(
        second_factor_kernel, halves, [SMEM] + [VMEM] * 16, [VMEM] * 2, scratch, SECOND, 24, "second_factor"
    )(after(place, mine), *bufs)

    return call(second_kernel, shape(32, 2048), [SMEM] + [VMEM] * 8, VMEM, [], 2_500_000_000, 24, "second_panel")(
        place, x, both, uh, ul, mine, *back
    )


def solution(mesh):
    special = mesh.shape["bulk"] == 8 and mesh.shape["rep"] == 4

    def run(orbitals, triangles, coupling, diagonals):
        fits = orbitals.shape == (1024, 2048) and triangles.shape == (1024, 1024)
        body = per_device if special and fits else per_device_any
        return jax.shard_map(
            body,
            mesh=mesh,
            in_specs=(P("rep", "bulk"), P("rep", "bulk"), P("rep", "bulk"), P(None, "bulk")),
            out_specs=P(("rep", "bulk"), None),
            check_vma=False,
        )(orbitals, triangles, coupling, diagonals)

    return run
```

```python
import jax
import jax.numpy as jnp
from jax import lax
from jax.experimental import pallas as pl
from jax.experimental.pallas import tpu as pltpu
from jax.sharding import PartitionSpec as P

F32 = jnp.float32
BF16 = jnp.bfloat16
NN = (((1,), (0,)), ((), ()))
NT = (((1,), (1,)), ((), ()))


def unpack(triangles, diagonals):
    first_block = jnp.tril(triangles, -1) + jnp.diag(diagonals[0])
    second_block = jnp.tril(triangles.T, -1) + jnp.diag(diagonals[1])
    return (first_block, second_block)


def per_device_any(orbitals, triangles, coupling, diagonals):
    tri_rows, couple_rows = (
        lax.all_gather(triangles, "rep", axis=0, tiled=True),
        lax.all_gather(coupling, "rep", axis=0, tiled=True),
    )
    tri_whole, couple_whole, diag_whole = (
        lax.all_gather(tri_rows, "bulk", axis=1, tiled=True),
        lax.all_gather(couple_rows, "bulk", axis=1, tiled=True),
        lax.all_gather(diagonals, "bulk", axis=1, tiled=True),
    )
    first_block, second_block = unpack(tri_whole, diag_whole)
    panel = first_block.shape[0]
    groups = lax.axis_size("bulk")
    local_rows = orbitals.shape[0] // groups
    blocks = orbitals.reshape(groups, local_rows, orbitals.shape[1])
    received = lax.all_to_all(blocks, "bulk", split_axis=0, concat_axis=2, tiled=True)
    rows_now = received.reshape(local_rows, received.shape[2])
    left_part = rows_now[:, :panel]
    right_part = rows_now[:, panel:]
    solved_one = jax.scipy.linalg.solve_triangular(first_block, left_part.T, lower=True).T
    update = jnp.dot(
        solved_one,
        couple_whole.T,
        precision=lax.Precision.HIGHEST,
        preferred_element_type=jnp.float32,
    )
    solved_two = jax.scipy.linalg.solve_triangular(
        second_block, (right_part - update).T, lower=True
    ).T
    return jnp.concatenate([solved_one, solved_two], axis=1)


def dot(a, b, dims=NN):
    return lax.dot_general(a, b, dims, preferred_element_type=F32)


def dot_exact(a, b):
    return lax.dot_general(a, b, NN, precision=lax.Precision.HIGHEST, preferred_element_type=F32)


def split(x):
    high = x.astype(BF16)
    return high, (x - high.astype(F32)).astype(BF16)


def mul(x, b, dims=NN):
    xh, xl = split(x)
    bh, bl = b
    m = x.shape[0]
    both = dot(jnp.concatenate([xh, xl], axis=0), bh, dims)
    return (both[:m] + both[m:]) + dot(xh, bl, dims)


def mul3(a, b):
    (ah, al), (bh, bl) = split(a), split(b)
    return dot(ah, bh) + (dot(al, bh) + dot(ah, bl))


def iotas(n):
    return lax.broadcasted_iota(jnp.int32, (n, n), 0), lax.broadcasted_iota(jnp.int32, (n, n), 1)


def invert_kernel(place_ref, tri_ref, diag_ref, t_ref):
    rep, bulk = place_ref[0], place_ref[1]
    rows, n = tri_ref.shape
    inv = 1.0 / diag_ref[...]
    t_ref[0:rows, :] = tri_ref[...]
    t_ref[rows : rows + 8, :] = jnp.concatenate([inv, jnp.zeros((6, n), F32)], axis=0)

    @pl.when(rep == bulk // 2)
    def _():
        start = pl.multiple_of((bulk % 2) * n, n)
        block = tri_ref[pl.ds(start, n), :]
        i, j = iotas(n)
        eye = i == j
        ans = []
        for which in range(2):
            row, col = (i, j) if which == 0 else (j, i)
            along = inv[which : which + 1, :]
            d = jnp.where(eye, along, 0.0)
            down = jnp.sum(d, axis=1, keepdims=True)
            part = (row >> 1 == col >> 1) & (row > col)
            ans.append(d - jnp.where(part, block * along * down, 0.0))
        level = 1
        while (1 << level) < n:
            for which in range(2):
                row, col = (i, j) if which == 0 else (j, i)
                part = (row >> (level + 1) == col >> (level + 1)) & (row >> level > col >> level)
                t = ans[which]
                ans[which] = t - mul3(mul3(t, jnp.where(part, block, 0.0)), t)
            level += 1
        t_ref[pl.ds(start, n), :] = jnp.where(i >= j, ans[0], ans[1])


def leave_kernel(place_ref, orb, out):
    y = place_ref[1] & 1
    for k in range(4):
        out[k] = orb[k, 1 - y]


def spread_kernel(place_ref, orb, came, b1, b2, b3):
    z, y = place_ref[1] >> 1, place_ref[1] & 1
    for m, ref in ((1, b1), (2, b2), (3, b3)):
        ref[0] = orb[z ^ m, y]
        ref[1] = came[z ^ m]


def rows_kernel(place_ref, orb, came, b1, b2, b3, left, both):
    z, y = place_ref[1] >> 1, place_ref[1] & 1

    def put(m, dy, value):
        k = 2 * (z ^ m) + (y ^ dy)
        both[k >> 2, :, pl.ds(pl.multiple_of((k & 3) * 256, 256), 256)] = value

    put(0, 0, orb[z, y])
    put(0, 1, came[z])
    for m, ref in ((1, b1), (2, b2), (3, b3)):
        put(m, 0, ref[0])
        put(m, 1, ref[1])
    left[...] = both[0]


def origin(place_ref, crossed, first, second, m):
    rep, bulk = place_ref[0], place_ref[1]
    return rep ^ (2 * second + crossed), bulk ^ (2 * m + first)


def pieces(bufs):
    found = []
    for crossed in range(2):
        for m in range(4):
            for second in range(2):
                for first in range(2):
                    buf = bufs[8 * crossed + 4 * (m % 2) + 2 * second + first]
                    found.append((buf.at[m // 2], (crossed, first, second, m)))
    return found


def offset(index, size):
    return pl.ds(pl.multiple_of(index * size, size), size)


def place_pieces(place_ref, bufs, upper, high, low, diag):
    for piece, args in pieces(bufs):
        rep, bulk = origin(place_ref, *args)

        @pl.when((rep <= bulk // 2) if upper else (rep >= bulk // 2))
        def _():
            h, l = split(piece[0:256, :])
            high[offset(rep, 256), offset(bulk, 128)] = h
            low[offset(rep, 256), offset(bulk, 128)] = l

        @pl.when(rep == bulk // 2)
        def _():
            diag[bulk, 0:128, :] = piece[pl.ds(pl.multiple_of((bulk % 2) * 128, 128), 128), :]
            diag[bulk, 128:136, :] = piece[256:264, :]


def mul_pairs(a, b):
    (ah, al), (bh, bl) = a, b
    return dot(ah, bh) + (dot(al, bh) + dot(ah, bl))


def pair_of(high, low, r, c, size):
    rows, cols = slice(r, r + size), slice(c, c + size)
    return high[rows, cols], low[rows, cols]


def join(a, b, c, d):
    return jnp.concatenate([jnp.concatenate([a, b], axis=1), jnp.concatenate([c, d], axis=1)], axis=0)


def first_kernel(place_ref, pair, other_pair, *refs):
    bufs, (x_ref, high, low, diag) = refs[:16], refs[16:]
    place_pieces(place_ref, bufs, False, high, low, diag)
    n = 128
    i, j = iotas(n)

    def block(k):
        return jnp.where(i > j, diag[k, 0:n, :], 0.0) + jnp.where(i == j, diag[k, n : n + 1, :], 0.0)

    zero = jnp.zeros((n, n), F32)
    inverses = []
    for k in range(4):
        ta, tb = block(2 * k), block(2 * k + 1)
        pa, pb = split(ta), split(tb)
        off = -mul_pairs(split(mul_pairs(pb, pair_of(high, low, 256 * k + n, 256 * k, n))), pa)
        inverses.append(split(join(ta, zero, off, tb)))

    rest = jnp.concatenate([pair[0], pair[1], other_pair[0], other_pair[1]], axis=0)
    for k in range(4):
        x = mul(rest[:, :256], inverses[k], NT)
        x_ref[:, k * 256 : (k + 1) * 256] = x
        if k < 3:
            rows, cols = slice((k + 1) * 256, 1024), slice(k * 256, (k + 1) * 256)
            rest = rest[:, 256:] - mul(x, (high[rows, cols], low[rows, cols]), NT)


def update_kernel(place_ref, x_ref, *refs):
    held, outs, (high, low) = refs[:4], refs[4:8], refs[8:]
    bulk = place_ref[1]
    for dy in range(2):
        for m in range(4):
            h, l = split(held[2 * dy + m % 2][m // 2])
            high[:, offset(bulk ^ (2 * m + dy), 128)] = h
            low[:, offset(bulk ^ (2 * m + dy), 128)] = l
    upd = mul(x_ref[...], (high[...], low[...]), NT)
    for k, out in enumerate(outs):
        out[...] = upd[32 * k : 32 * (k + 1)]


def second_factor_kernel(place_ref, *refs):
    bufs, (high, low, diag) = refs[:16], refs[16:]
    place_pieces(place_ref, bufs, True, high, low, diag)
    n = 128
    i, j = iotas(n)

    def block(k):
        return jnp.where(i < j, diag[k, 0:n, :], 0.0) + jnp.where(i == j, diag[k, n + 1 : n + 2, :], 0.0)

    zero = jnp.zeros((n, n), F32)
    inverses = []
    for k in range(4):
        ta, tb = block(2 * k), block(2 * k + 1)
        pa, pb = split(ta), split(tb)
        off = -mul_pairs(split(mul_pairs(pa, pair_of(high, low, 256 * k, 256 * k + n, n))), pb)
        inverses.append(split(join(ta, off, zero, tb)))

    def put(r, c, value):
        high[r : r + 256, c : c + 256], low[r : r + 256, c : c + 256] = value

    for k in range(2):
        at = 512 * k
        pa, pb = inverses[2 * k], inverses[2 * k + 1]
        off = -mul_pairs(split(mul_pairs(pa, pair_of(high, low, at, at + 256, 256))), pb)
        put(at, at, pa)
        put(at + 256, at + 256, pb)
        put(at, at + 256, split(off))
        put(at + 256, at, (jnp.zeros((256, 256), BF16),) * 2)


def second_kernel(place_ref, x_ref, both_ref, uh_ref, ul_ref, mine, from_x, from_core, from_both, out_ref):
    x = x_ref[0:32, :]
    out_ref[:, 0:1024] = x
    parts = []
    for k in range(4):
        way = place_ref[0] ^ k
        upd = jnp.where(
            way == 0,
            mine[...],
            jnp.where(way == 2, from_x[...], jnp.where(way == 1, from_core[...], from_both[...])),
        )
        parts.append(both_ref[1, :, k * 256 : (k + 1) * 256] - upd)
    ra = jnp.concatenate(parts[:2], axis=1)
    rb = jnp.concatenate(parts[2:], axis=1)

    def u(r, c):
        rows, cols = slice(r * 512, r * 512 + 512), slice(c * 512, c * 512 + 512)
        return uh_ref[rows, cols], ul_ref[rows, cols]

    xa = mul(ra, u(0, 0))
    xb = mul(rb - mul(xa, u(0, 1)), u(1, 1))
    out_ref[:, 1024:1536] = xa
    out_ref[:, 1536:2048] = xb


SPREAD, INVERT, LEAVE, ROWS, FIRST, SECOND = 1_000_000_000, 3_500_000_000, 500_000_000, 1_000_000_000, 200_000_000, 3_000_000_000


def swap_z(x, m):
    return lax.ppermute(x, "bulk", [(k, k ^ (2 * m)) for k in range(8)])


def swap_y(x):
    return lax.ppermute(x, "bulk", [(k, k ^ 1) for k in range(8)])


def swap_rep(x, bits):
    return lax.ppermute(x, "rep", [(k, k ^ bits) for k in range(4)])


def after(x, *deps):
    return lax.optimization_barrier((x,) + deps)[0]


ANY = pl.BlockSpec(memory_space=pl.ANY)
VMEM = pl.BlockSpec(memory_space=pltpu.VMEM)
SMEM = pl.BlockSpec(memory_space=pltpu.SMEM)


def call(kernel, out, specs, outs, scratch, flops, size, name):
    return pl.pallas_call(
        kernel,
        out_shape=out,
        in_specs=specs,
        out_specs=outs,
        scratch_shapes=scratch,
        compiler_params=pltpu.CompilerParams(vmem_limit_bytes=size << 20),
        cost_estimate=pl.CostEstimate(flops=flops, bytes_accessed=2 << 20, transcendentals=0),
        name=name,
    )


def shape(*dims, dtype=F32):
    return jax.ShapeDtypeStruct(dims, dtype)


def per_device(orbitals, triangles, coupling, diagonals):
    rep, bulk = lax.axis_index("rep"), lax.axis_index("bulk")
    place = jnp.stack([rep, bulk]).astype(jnp.int32)
    blocks = orbitals.reshape(4, 2, 32, 256)

    t = call(invert_kernel, shape(264, 128), [SMEM, VMEM, VMEM], VMEM, [], INVERT, 4, "invert")(
        place, triangles, diagonals
    )
    coup = after(coupling, t)

    near = jnp.stack([t, swap_z(t, 2)])
    far = swap_z(near, 1)
    near0 = swap_y(near)
    near1 = swap_rep(near, 2)
    near01 = swap_rep(near0, 2)

    leave = call(leave_kernel, shape(4, 32, 256), [SMEM, VMEM], VMEM, [], LEAVE, 4, "leave")(place, blocks)
    came = swap_y(after(leave, t))
    c_near = jnp.stack([coupling, swap_z(after(coup, near), 2)])
    c_near_got = swap_y(c_near)

    far_now = after(far, near0, near1, came, c_near)
    far0 = swap_y(far_now)
    far1 = swap_rep(far_now, 2)
    b_out = call(spread_kernel, [shape(2, 32, 256)] * 3, [SMEM, VMEM, VMEM], [VMEM] * 3, [], SPREAD, 4, "spread")(
        place, blocks, came
    )
    b_z = [swap_z(after(b, far), m + 1) for m, b in enumerate(b_out)]
    c_far = swap_z(after(c_near, far0), 1)
    c_far_got = swap_y(c_far)
    far01 = swap_rep(after(far0, far1, near01), 2)

    left, both = call(
        rows_kernel,
        [shape(32, 1024), shape(2, 32, 1024)],
        [SMEM] + [VMEM] * 5,
        [VMEM] * 2,
        [],
        ROWS,
        4,
        "rows",
    )(place, blocks, came, *b_z)
    pair = jnp.stack([left, swap_rep(after(left, came), 2)])
    other_pair = swap_rep(after(pair, c_far), 1)
    bufs = [near, near0, near1, near01, far, far0, far1, far01]
    bufs += [swap_rep(after(b, b_z[2], far0), 1) for b in bufs[:7]] + [swap_rep(after(far01, far1), 1)]

    scratch = [pltpu.VMEM((8, 136, 128), F32)]
    halves = [shape(1024, 1024, dtype=BF16)] * 2
    x = call(
        first_kernel,
        shape(128, 1024),
        [SMEM] + [VMEM] * 18,
        VMEM,
        [pltpu.VMEM((1024, 1024), BF16)] * 2 + scratch,
        FIRST,
        24,
        "first_panel",
    )(place, pair, after(other_pair, c_near_got), *bufs)

    mine, to_x, to_core, to_both = call(
        update_kernel,
        [shape(32, 256)] * 4,
        [SMEM] + [VMEM] * 5,
        [VMEM] * 4,
        [pltpu.VMEM((256, 1024), BF16)] * 2,
        2_000_000_000,
        24,
        "update",
    )(place, x, c_near, c_far, c_near_got, c_far_got)
    back = [swap_rep(to_x, 2), swap_rep(to_core, 1), swap_rep(to_both, 3)]

    uh, ul = call(
        second_factor_kernel, halves, [SMEM] + [VMEM] * 16, [VMEM] * 2, scratch, SECOND, 24, "second_factor"
    )(after(place, mine), *bufs)

    return call(second_kernel, shape(32, 2048), [SMEM] + [VMEM] * 8, VMEM, [], 2_500_000_000, 24, "second_panel")(
        place, x, both, uh, ul, mine, *back
    )


def solution(mesh):
    special = mesh.shape["bulk"] == 8 and mesh.shape["rep"] == 4

    def run(orbitals, triangles, coupling, diagonals):
        fits = orbitals.shape == (1024, 2048) and triangles.shape == (1024, 1024)
        body = per_device if special and fits else per_device_any
        return jax.shard_map(
            body,
            mesh=mesh,
            in_specs=(P("rep", "bulk"), P("rep", "bulk"), P("rep", "bulk"), P(None, "bulk")),
            out_specs=P(("rep", "bulk"), None),
            check_vma=False,
        )(orbitals, triangles, coupling, diagonals)

    return run
```

```python
import jax
import jax.numpy as jnp
from jax import lax
from jax.experimental import pallas as pl
from jax.experimental.pallas import tpu as pltpu
from jax.sharding import PartitionSpec as P

F32 = jnp.float32
BF16 = jnp.bfloat16
NN = (((1,), (0,)), ((), ()))
NT = (((1,), (1,)), ((), ()))


def unpack(triangles, diagonals):
    first_block = jnp.tril(triangles, -1) + jnp.diag(diagonals[0])
    second_block = jnp.tril(triangles.T, -1) + jnp.diag(diagonals[1])
    return (first_block, second_block)


def per_device_any(orbitals, triangles, coupling, diagonals):
    tri_rows, couple_rows = (
        lax.all_gather(triangles, "rep", axis=0, tiled=True),
        lax.all_gather(coupling, "rep", axis=0, tiled=True),
    )
    tri_whole, couple_whole, diag_whole = (
        lax.all_gather(tri_rows, "bulk", axis=1, tiled=True),
        lax.all_gather(couple_rows, "bulk", axis=1, tiled=True),
        lax.all_gather(diagonals, "bulk", axis=1, tiled=True),
    )
    first_block, second_block = unpack(tri_whole, diag_whole)
    panel = first_block.shape[0]
    groups = lax.axis_size("bulk")
    local_rows = orbitals.shape[0] // groups
    blocks = orbitals.reshape(groups, local_rows, orbitals.shape[1])
    received = lax.all_to_all(blocks, "bulk", split_axis=0, concat_axis=2, tiled=True)
    rows_now = received.reshape(local_rows, received.shape[2])
    left_part = rows_now[:, :panel]
    right_part = rows_now[:, panel:]
    solved_one = jax.scipy.linalg.solve_triangular(first_block, left_part.T, lower=True).T
    update = jnp.dot(
        solved_one,
        couple_whole.T,
        precision=lax.Precision.HIGHEST,
        preferred_element_type=jnp.float32,
    )
    solved_two = jax.scipy.linalg.solve_triangular(
        second_block, (right_part - update).T, lower=True
    ).T
    return jnp.concatenate([solved_one, solved_two], axis=1)


def dot(a, b, dims=NN):
    return lax.dot_general(a, b, dims, preferred_element_type=F32)


def dot_exact(a, b):
    return lax.dot_general(a, b, NN, precision=lax.Precision.HIGHEST, preferred_element_type=F32)


def split(x):
    high = x.astype(BF16)
    return high, (x - high.astype(F32)).astype(BF16)


def mul(x, b, dims=NN):
    xh, xl = split(x)
    bh, bl = b
    m = x.shape[0]
    both = dot(jnp.concatenate([xh, xl], axis=0), bh, dims)
    return (both[:m] + both[m:]) + dot(xh, bl, dims)


def mul3(a, b):
    (ah, al), (bh, bl) = split(a), split(b)
    return dot(ah, bh) + (dot(al, bh) + dot(ah, bl))


def iotas(n):
    return lax.broadcasted_iota(jnp.int32, (n, n), 0), lax.broadcasted_iota(jnp.int32, (n, n), 1)


def invert_kernel(place_ref, tri_ref, diag_ref, t_ref):
    rep, bulk = place_ref[0], place_ref[1]
    rows, n = tri_ref.shape
    inv = 1.0 / diag_ref[...]
    t_ref[0:rows, :] = tri_ref[...]
    t_ref[rows : rows + 8, :] = jnp.concatenate([inv, jnp.zeros((6, n), F32)], axis=0)

    @pl.when(rep == bulk // 2)
    def _():
        start = pl.multiple_of((bulk % 2) * n, n)
        block = tri_ref[pl.ds(start, n), :]
        i, j = iotas(n)
        eye = i == j
        ans = []
        for which in range(2):
            row, col = (i, j) if which == 0 else (j, i)
            along = inv[which : which + 1, :]
            d = jnp.where(eye, along, 0.0)
            down = jnp.sum(d, axis=1, keepdims=True)
            part = (row >> 1 == col >> 1) & (row > col)
            ans.append(d - jnp.where(part, block * along * down, 0.0))
        level = 1
        while (1 << level) < n:
            for which in range(2):
                row, col = (i, j) if which == 0 else (j, i)
                part = (row >> (level + 1) == col >> (level + 1)) & (row >> level > col >> level)
                t = ans[which]
                ans[which] = t - mul3(mul3(t, jnp.where(part, block, 0.0)), t)
            level += 1
        t_ref[pl.ds(start, n), :] = jnp.where(i >= j, ans[0], ans[1])


def leave_kernel(place_ref, orb, out):
    y = place_ref[1] & 1
    for k in range(4):
        out[k] = orb[k, 1 - y]


def spread_kernel(place_ref, orb, came, b1, b2, b3):
    z, y = place_ref[1] >> 1, place_ref[1] & 1
    for m, ref in ((1, b1), (2, b2), (3, b3)):
        ref[0] = orb[z ^ m, y]
        ref[1] = came[z ^ m]


def rows_kernel(place_ref, orb, came, b1, b2, b3, left, both):
    z, y = place_ref[1] >> 1, place_ref[1] & 1

    def put(m, dy, value):
        k = 2 * (z ^ m) + (y ^ dy)
        both[k >> 2, :, pl.ds(pl.multiple_of((k & 3) * 256, 256), 256)] = value

    put(0, 0, orb[z, y])
    put(0, 1, came[z])
    for m, ref in ((1, b1), (2, b2), (3, b3)):
        put(m, 0, ref[0])
        put(m, 1, ref[1])
    left[...] = both[0]


def origin(place_ref, crossed, first, second, m):
    rep, bulk = place_ref[0], place_ref[1]
    if m % 2 == 0:
        dx, dy = second, first
    else:
        core = (rep & 1) ^ crossed
        dx = jnp.where(core == 0, first, second)
        dy = jnp.where(core == 0, second, first)
    return rep ^ (2 * dx + crossed), bulk ^ (2 * m + dy)


def pieces(bufs):
    found = []
    for crossed in range(2):
        for m in range(4):
            for second in range(2):
                for first in range(2):
                    buf = bufs[8 * crossed + 4 * (m % 2) + 2 * second + first]
                    found.append((buf.at[m // 2], (crossed, first, second, m)))
    return found


def offset(index, size):
    return pl.ds(pl.multiple_of(index * size, size), size)


def place_pieces(place_ref, bufs, upper, high, low, diag):
    for piece, args in pieces(bufs):
        rep, bulk = origin(place_ref, *args)

        @pl.when((rep <= bulk // 2) if upper else (rep >= bulk // 2))
        def _():
            h, l = split(piece[0:256, :])
            high[offset(rep, 256), offset(bulk, 128)] = h
            low[offset(rep, 256), offset(bulk, 128)] = l

        @pl.when(rep == bulk // 2)
        def _():
            diag[bulk, 0:128, :] = piece[pl.ds(pl.multiple_of((bulk % 2) * 128, 128), 128), :]
            diag[bulk, 128:136, :] = piece[256:264, :]


def mul_pairs(a, b):
    (ah, al), (bh, bl) = a, b
    return dot(ah, bh) + (dot(al, bh) + dot(ah, bl))


def pair_of(high, low, r, c, size):
    rows, cols = slice(r, r + size), slice(c, c + size)
    return high[rows, cols], low[rows, cols]


def join(a, b, c, d):
    return jnp.concatenate([jnp.concatenate([a, b], axis=1), jnp.concatenate([c, d], axis=1)], axis=0)


def first_kernel(place_ref, pair, other_pair, *refs):
    bufs, (x_ref, high, low, diag) = refs[:16], refs[16:]
    place_pieces(place_ref, bufs, False, high, low, diag)
    n = 128
    i, j = iotas(n)

    def block(k):
        return jnp.where(i > j, diag[k, 0:n, :], 0.0) + jnp.where(i == j, diag[k, n : n + 1, :], 0.0)

    zero = jnp.zeros((n, n), F32)
    inverses = []
    for k in range(4):
        ta, tb = block(2 * k), block(2 * k + 1)
        pa, pb = split(ta), split(tb)
        off = -mul_pairs(split(mul_pairs(pb, pair_of(high, low, 256 * k + n, 256 * k, n))), pa)
        inverses.append(split(join(ta, zero, off, tb)))

    rest = jnp.concatenate([pair[0], pair[1], other_pair[0], other_pair[1]], axis=0)
    for k in range(4):
        x = mul(rest[:, :256], inverses[k], NT)
        x_ref[:, k * 256 : (k + 1) * 256] = x
        if k < 3:
            rows, cols = slice((k + 1) * 256, 1024), slice(k * 256, (k + 1) * 256)
            rest = rest[:, 256:] - mul(x, (high[rows, cols], low[rows, cols]), NT)


def half_update(x, held, got):
    pairs = [split(piece) for piece in (held[0], held[1], got[0], got[1])]
    high = jnp.concatenate([p[0] for p in pairs], axis=1)
    low = jnp.concatenate([p[1] for p in pairs], axis=1)
    return mul(jnp.concatenate(x, axis=1), (high, low), NT)


def columns(place_ref, x_ref, far):
    bulk = place_ref[1]
    return [x_ref[:, offset(bulk ^ (2 * m + dy), 128)] for dy in range(2) for m in (far, 2 + far)]


def near_kernel(place_ref, x_ref, held, got, out):
    out[...] = half_update(columns(place_ref, x_ref, 0), held, got)


def update_kernel(place_ref, x_ref, near, held, got, *outs):
    upd = near[...] + half_update(columns(place_ref, x_ref, 1), held, got)
    for k, out in enumerate(outs):
        out[...] = upd[32 * k : 32 * (k + 1)]


def second_factor_kernel(place_ref, *refs):
    bufs, (high, low, diag) = refs[:16], refs[16:]
    place_pieces(place_ref, bufs, True, high, low, diag)
    n = 128
    i, j = iotas(n)

    def block(k):
        return jnp.where(i < j, diag[k, 0:n, :], 0.0) + jnp.where(i == j, diag[k, n + 1 : n + 2, :], 0.0)

    zero = jnp.zeros((n, n), F32)
    inverses = []
    for k in range(4):
        ta, tb = block(2 * k), block(2 * k + 1)
        pa, pb = split(ta), split(tb)
        off = -mul_pairs(split(mul_pairs(pa, pair_of(high, low, 256 * k, 256 * k + n, n))), pb)
        inverses.append(split(join(ta, off, zero, tb)))

    def put(r, c, value):
        high[r : r + 256, c : c + 256], low[r : r + 256, c : c + 256] = value

    for k in range(2):
        at = 512 * k
        pa, pb = inverses[2 * k], inverses[2 * k + 1]
        off = -mul_pairs(split(mul_pairs(pa, pair_of(high, low, at, at + 256, 256))), pb)
        put(at, at, pa)
        put(at + 256, at + 256, pb)
        put(at, at + 256, split(off))
        put(at + 256, at, (jnp.zeros((256, 256), BF16),) * 2)


def second_kernel(place_ref, x_ref, both_ref, uh_ref, ul_ref, mine, from_x, from_core, from_both, out_ref):
    x = x_ref[0:32, :]
    out_ref[:, 0:1024] = x
    parts = []
    for k in range(4):
        way = place_ref[0] ^ k
        upd = jnp.where(
            way == 0,
            mine[...],
            jnp.where(way == 2, from_x[...], jnp.where(way == 1, from_core[...], from_both[...])),
        )
        parts.append(both_ref[1, :, k * 256 : (k + 1) * 256] - upd)
    ra = jnp.concatenate(parts[:2], axis=1)
    rb = jnp.concatenate(parts[2:], axis=1)

    def u(r, c):
        rows, cols = slice(r * 512, r * 512 + 512), slice(c * 512, c * 512 + 512)
        return uh_ref[rows, cols], ul_ref[rows, cols]

    xa = mul(ra, u(0, 0))
    xb = mul(rb - mul(xa, u(0, 1)), u(1, 1))
    out_ref[:, 1024:1536] = xa
    out_ref[:, 1536:2048] = xb


BOTH = ("bulk", "rep")

SPREAD, INVERT, LEAVE, ROWS, FIRST, SECOND = 1_000_000_000, 3_500_000_000, 500_000_000, 1_000_000_000, 200_000_000, 3_000_000_000


def swap_z(x, m):
    return lax.ppermute(x, "bulk", [(k, k ^ (2 * m)) for k in range(8)])


def swap_y(x):
    return lax.ppermute(x, "bulk", [(k, k ^ 1) for k in range(8)])


def swap_rep(x, bits):
    return lax.ppermute(x, "rep", [(k, k ^ bits) for k in range(4)])


def cross(x, stage):
    pairs = []
    for rep in range(4):
        for bulk in range(8):
            to = (rep ^ 2, bulk) if (rep & 1) == stage else (rep, bulk ^ 1)
            pairs.append((bulk * 4 + rep, to[1] * 4 + to[0]))
    return lax.ppermute(x, BOTH, pairs)


def after(x, *deps):
    return lax.optimization_barrier((x,) + deps)[0]


ANY = pl.BlockSpec(memory_space=pl.ANY)
VMEM = pl.BlockSpec(memory_space=pltpu.VMEM)
SMEM = pl.BlockSpec(memory_space=pltpu.SMEM)


def call(kernel, out, specs, outs, scratch, flops, size, name):
    return pl.pallas_call(
        kernel,
        out_shape=out,
        in_specs=specs,
        out_specs=outs,
        scratch_shapes=scratch,
        compiler_params=pltpu.CompilerParams(vmem_limit_bytes=size << 20),
        cost_estimate=pl.CostEstimate(flops=flops, bytes_accessed=2 << 20, transcendentals=0),
        name=name,
    )


def shape(*dims, dtype=F32):
    return jax.ShapeDtypeStruct(dims, dtype)


def per_device(orbitals, triangles, coupling, diagonals):
    rep, bulk = lax.axis_index("rep"), lax.axis_index("bulk")
    place = jnp.stack([rep, bulk]).astype(jnp.int32)
    blocks = orbitals.reshape(4, 2, 32, 256)

    t = call(invert_kernel, shape(264, 128), [SMEM, VMEM, VMEM], VMEM, [], INVERT, 4, "invert")(
        place, triangles, diagonals
    )
    coup = after(coupling, t)

    near = jnp.stack([t, swap_z(t, 2)])
    far = swap_z(near, 1)
    near0 = swap_y(near)
    near1 = swap_rep(near, 2)
    near01 = swap_rep(near0, 2)

    leave = call(leave_kernel, shape(4, 32, 256), [SMEM, VMEM], VMEM, [], LEAVE, 4, "leave")(place, blocks)
    came = swap_y(after(leave, t))
    c_near = jnp.stack([coupling, swap_z(after(coup, near), 2)])
    c_near_got = swap_y(c_near)

    far_now = after(far, near0, near1, came, c_near)
    far0 = cross(far_now, 0)
    far1 = cross(far_now, 1)
    b_out = call(spread_kernel, [shape(2, 32, 256)] * 3, [SMEM, VMEM, VMEM], [VMEM] * 3, [], SPREAD, 4, "spread")(
        place, blocks, came
    )
    b_z = [swap_z(after(b, far), m + 1) for m, b in enumerate(b_out)]
    c_far = swap_z(after(c_near, far0), 1)
    c_far_got = swap_y(c_far)
    far01 = cross(after(far0, far1, near01), 1)

    left, both = call(
        rows_kernel,
        [shape(32, 1024), shape(2, 32, 1024)],
        [SMEM] + [VMEM] * 5,
        [VMEM] * 2,
        [],
        ROWS,
        4,
        "rows",
    )(place, blocks, came, *b_z)
    pair = jnp.stack([left, swap_rep(after(left, came), 2)])
    other_pair = swap_rep(after(pair, c_far), 1)
    bufs = [near, near0, near1, near01, far, far0, far1, far01]
    bufs += [swap_rep(after(b, b_z[2], far0), 1) for b in bufs[:7]] + [swap_rep(after(far01, far1), 1)]

    scratch = [pltpu.VMEM((8, 136, 128), F32)]
    halves = [shape(1024, 1024, dtype=BF16)] * 2
    x = call(
        first_kernel,
        shape(128, 1024),
        [SMEM] + [VMEM] * 18,
        VMEM,
        [pltpu.VMEM((1024, 1024), BF16)] * 2 + scratch,
        FIRST,
        24,
        "first_panel",
    )(place, pair, after(other_pair, c_near_got), *bufs)

    near_upd = call(near_kernel, shape(128, 256), [SMEM] + [VMEM] * 3, VMEM, [], 10_000_000, 24, "near_update")(
        place, x, c_near, c_near_got
    )
    mine, to_x, to_core, to_both = call(
        update_kernel,
        [shape(32, 256)] * 4,
        [SMEM] + [VMEM] * 4,
        [VMEM] * 4,
        [],
        2_000_000_000,
        24,
        "update",
    )(place, x, near_upd, c_far, c_far_got)
    back = [swap_rep(to_x, 2), swap_rep(to_core, 1), swap_rep(to_both, 3)]

    uh, ul = call(
        second_factor_kernel, halves, [SMEM] + [VMEM] * 16, [VMEM] * 2, scratch, SECOND, 24, "second_factor"
    )(after(place, mine), *bufs)

    return call(second_kernel, shape(32, 2048), [SMEM] + [VMEM] * 8, VMEM, [], 2_500_000_000, 24, "second_panel")(
        place, x, both, uh, ul, mine, *back
    )


def solution(mesh):
    special = mesh.shape["bulk"] == 8 and mesh.shape["rep"] == 4

    def run(orbitals, triangles, coupling, diagonals):
        fits = orbitals.shape == (1024, 2048) and triangles.shape == (1024, 1024)
        body = per_device if special and fits else per_device_any
        return jax.shard_map(
            body,
            mesh=mesh,
            in_specs=(P("rep", "bulk"), P("rep", "bulk"), P("rep", "bulk"), P(None, "bulk")),
            out_specs=P(("rep", "bulk"), None),
            check_vma=False,
        )(orbitals, triangles, coupling, diagonals)

    return run
```

```python
import jax
import jax.numpy as jnp
from jax import lax
from jax.experimental import pallas as pl
from jax.experimental.pallas import tpu as pltpu
from jax.sharding import PartitionSpec as P

F32 = jnp.float32
BF16 = jnp.bfloat16
NN = (((1,), (0,)), ((), ()))
NT = (((1,), (1,)), ((), ()))


def unpack(triangles, diagonals):
    first_block = jnp.tril(triangles, -1) + jnp.diag(diagonals[0])
    second_block = jnp.tril(triangles.T, -1) + jnp.diag(diagonals[1])
    return (first_block, second_block)


def per_device_any(orbitals, triangles, coupling, diagonals):
    tri_rows, couple_rows = (
        lax.all_gather(triangles, "rep", axis=0, tiled=True),
        lax.all_gather(coupling, "rep", axis=0, tiled=True),
    )
    tri_whole, couple_whole, diag_whole = (
        lax.all_gather(tri_rows, "bulk", axis=1, tiled=True),
        lax.all_gather(couple_rows, "bulk", axis=1, tiled=True),
        lax.all_gather(diagonals, "bulk", axis=1, tiled=True),
    )
    first_block, second_block = unpack(tri_whole, diag_whole)
    panel = first_block.shape[0]
    groups = lax.axis_size("bulk")
    local_rows = orbitals.shape[0] // groups
    blocks = orbitals.reshape(groups, local_rows, orbitals.shape[1])
    received = lax.all_to_all(blocks, "bulk", split_axis=0, concat_axis=2, tiled=True)
    rows_now = received.reshape(local_rows, received.shape[2])
    left_part = rows_now[:, :panel]
    right_part = rows_now[:, panel:]
    solved_one = jax.scipy.linalg.solve_triangular(first_block, left_part.T, lower=True).T
    update = jnp.dot(
        solved_one,
        couple_whole.T,
        precision=lax.Precision.HIGHEST,
        preferred_element_type=jnp.float32,
    )
    solved_two = jax.scipy.linalg.solve_triangular(
        second_block, (right_part - update).T, lower=True
    ).T
    return jnp.concatenate([solved_one, solved_two], axis=1)


def dot(a, b, dims=NN):
    return lax.dot_general(a, b, dims, preferred_element_type=F32)


def dot_exact(a, b):
    return lax.dot_general(a, b, NN, precision=lax.Precision.HIGHEST, preferred_element_type=F32)


def split(x):
    high = x.astype(BF16)
    return high, (x - high.astype(F32)).astype(BF16)


def mul(x, b, dims=NN):
    xh, xl = split(x)
    bh, bl = b
    m = x.shape[0]
    both = dot(jnp.concatenate([xh, xl], axis=0), bh, dims)
    return (both[:m] + both[m:]) + dot(xh, bl, dims)


def mul3(a, b):
    (ah, al), (bh, bl) = split(a), split(b)
    return dot(ah, bh) + (dot(al, bh) + dot(ah, bl))


def iotas(n):
    return lax.broadcasted_iota(jnp.int32, (n, n), 0), lax.broadcasted_iota(jnp.int32, (n, n), 1)


def invert_kernel(place_ref, tri_ref, diag_ref, t_ref):
    rep, bulk = place_ref[0], place_ref[1]
    rows, n = tri_ref.shape
    inv = 1.0 / diag_ref[...]
    t_ref[0:rows, :] = tri_ref[...]
    t_ref[rows : rows + 8, :] = jnp.concatenate([inv, jnp.zeros((6, n), F32)], axis=0)

    @pl.when(rep == bulk // 2)
    def _():
        start = pl.multiple_of((bulk % 2) * n, n)
        block = tri_ref[pl.ds(start, n), :]
        i, j = iotas(n)
        eye = i == j
        ans = []
        for which in range(2):
            row, col = (i, j) if which == 0 else (j, i)
            along = inv[which : which + 1, :]
            d = jnp.where(eye, along, 0.0)
            down = jnp.sum(d, axis=1, keepdims=True)
            part = (row >> 1 == col >> 1) & (row > col)
            ans.append(d - jnp.where(part, block * along * down, 0.0))
        level = 1
        while (1 << level) < n:
            for which in range(2):
                row, col = (i, j) if which == 0 else (j, i)
                part = (row >> (level + 1) == col >> (level + 1)) & (row >> level > col >> level)
                t = ans[which]
                ans[which] = t - mul3(mul3(t, jnp.where(part, block, 0.0)), t)
            level += 1
        t_ref[pl.ds(start, n), :] = jnp.where(i >= j, ans[0], ans[1])


def leave_kernel(place_ref, orb, out):
    y = place_ref[1] & 1
    for k in range(4):
        out[k] = orb[k, 1 - y]


def spread_kernel(place_ref, orb, came, b1, b2, b3):
    z, y = place_ref[1] >> 1, place_ref[1] & 1
    for m, ref in ((1, b1), (2, b2), (3, b3)):
        ref[0] = orb[z ^ m, y]
        ref[1] = came[z ^ m]


def rows_kernel(place_ref, orb, came, b1, b2, b3, left, both):
    z, y = place_ref[1] >> 1, place_ref[1] & 1

    def put(m, dy, value):
        k = 2 * (z ^ m) + (y ^ dy)
        both[k >> 2, :, pl.ds(pl.multiple_of((k & 3) * 256, 256), 256)] = value

    put(0, 0, orb[z, y])
    put(0, 1, came[z])
    for m, ref in ((1, b1), (2, b2), (3, b3)):
        put(m, 0, ref[0])
        put(m, 1, ref[1])
    left[...] = both[0]


def origin(place_ref, crossed, first, second, m):
    rep, bulk = place_ref[0], place_ref[1]
    if m % 2 == 0:
        dx, dy = second, first
    else:
        core = (rep & 1) ^ crossed
        dx = jnp.where(core == 0, first, second)
        dy = jnp.where(core == 0, second, first)
    return rep ^ (2 * dx + crossed), bulk ^ (2 * m + dy)


def pieces(bufs):
    found = []
    for crossed in range(2):
        for m in range(4):
            for second in range(2):
                for first in range(2):
                    buf = bufs[8 * crossed + 4 * (m % 2) + 2 * second + first]
                    found.append((buf.at[m // 2], (crossed, first, second, m)))
    return found


def offset(index, size):
    return pl.ds(pl.multiple_of(index * size, size), size)


def place_pieces(place_ref, bufs, upper, high, low, diag):
    for piece, args in pieces(bufs):
        rep, bulk = origin(place_ref, *args)

        @pl.when((rep <= bulk // 2) if upper else (rep >= bulk // 2))
        def _():
            h, l = split(piece[0:256, :])
            high[offset(rep, 256), offset(bulk, 128)] = h
            low[offset(rep, 256), offset(bulk, 128)] = l

        @pl.when(rep == bulk // 2)
        def _():
            diag[bulk, 0:128, :] = piece[pl.ds(pl.multiple_of((bulk % 2) * 128, 128), 128), :]
            diag[bulk, 128:136, :] = piece[256:264, :]


def mul_pairs(a, b):
    (ah, al), (bh, bl) = a, b
    return dot(ah, bh) + (dot(al, bh) + dot(ah, bl))


def pair_of(high, low, r, c, size):
    rows, cols = slice(r, r + size), slice(c, c + size)
    return high[rows, cols], low[rows, cols]


def join(a, b, c, d):
    return jnp.concatenate([jnp.concatenate([a, b], axis=1), jnp.concatenate([c, d], axis=1)], axis=0)


def first_kernel(place_ref, pair, other_pair, *refs):
    bufs, (x_ref, high, low, diag) = refs[:16], refs[16:]
    place_pieces(place_ref, bufs, False, high, low, diag)
    n = 128
    i, j = iotas(n)

    def block(k):
        return jnp.where(i > j, diag[k, 0:n, :], 0.0) + jnp.where(i == j, diag[k, n : n + 1, :], 0.0)

    zero = jnp.zeros((n, n), F32)
    inverses = []
    for k in range(4):
        ta, tb = block(2 * k), block(2 * k + 1)
        pa, pb = split(ta), split(tb)
        off = -mul_pairs(split(mul_pairs(pb, pair_of(high, low, 256 * k + n, 256 * k, n))), pa)
        inverses.append(split(join(ta, zero, off, tb)))

    rest = jnp.concatenate([pair[0], pair[1], other_pair[0], other_pair[1]], axis=0)
    for k in range(4):
        x = mul(rest[:, :256], inverses[k], NT)
        x_ref[:, k * 256 : (k + 1) * 256] = x
        if k < 3:
            rows, cols = slice((k + 1) * 256, 1024), slice(k * 256, (k + 1) * 256)
            rest = rest[:, 256:] - mul(x, (high[rows, cols], low[rows, cols]), NT)


def half_update(x, held, got):
    pairs = [split(piece) for piece in (held[0], held[1], got[0], got[1])]
    high = jnp.concatenate([p[0] for p in pairs], axis=1)
    low = jnp.concatenate([p[1] for p in pairs], axis=1)
    return mul(jnp.concatenate(x, axis=1), (high, low), NT)


def columns(place_ref, x_ref, far):
    bulk = place_ref[1]
    return [x_ref[:, offset(bulk ^ (2 * m + dy), 128)] for dy in range(2) for m in (far, 2 + far)]


def near_kernel(place_ref, x_ref, held, got, out):
    out[...] = half_update(columns(place_ref, x_ref, 0), held, got)


def update_kernel(place_ref, x_ref, near, held, got, *outs):
    upd = near[...] + half_update(columns(place_ref, x_ref, 1), held, got)
    for k, out in enumerate(outs):
        out[...] = upd[32 * k : 32 * (k + 1)]


def second_factor_kernel(place_ref, *refs):
    bufs, (high, low, diag) = refs[:16], refs[16:]
    place_pieces(place_ref, bufs, True, high, low, diag)
    n = 128
    i, j = iotas(n)

    def block(k):
        return jnp.where(i < j, diag[k, 0:n, :], 0.0) + jnp.where(i == j, diag[k, n + 1 : n + 2, :], 0.0)

    zero = jnp.zeros((n, n), F32)
    inverses = []
    for k in range(4):
        ta, tb = block(2 * k), block(2 * k + 1)
        pa, pb = split(ta), split(tb)
        off = -mul_pairs(split(mul_pairs(pa, pair_of(high, low, 256 * k, 256 * k + n, n))), pb)
        inverses.append(split(join(ta, off, zero, tb)))

    def put(r, c, value):
        high[r : r + 256, c : c + 256], low[r : r + 256, c : c + 256] = value

    for k in range(2):
        at = 512 * k
        pa, pb = inverses[2 * k], inverses[2 * k + 1]
        off = -mul_pairs(split(mul_pairs(pa, pair_of(high, low, at, at + 256, 256))), pb)
        put(at, at, pa)
        put(at + 256, at + 256, pb)
        put(at, at + 256, split(off))
        put(at + 256, at, (jnp.zeros((256, 256), BF16),) * 2)


def second_kernel(place_ref, x_ref, both_ref, uh_ref, ul_ref, mine, from_x, from_core, from_both, out_ref, buf, sem):
    first = pltpu.make_async_copy(x_ref.at[pl.ds(0, 32)], out_ref.at[:, pl.ds(0, 1024)], sem.at[0])
    first.start()
    halves = [
        pltpu.make_async_copy(buf.at[k], out_ref.at[:, pl.ds(1024 + 512 * k, 512)], sem.at[1 + k]) for k in range(2)
    ]
    parts = []
    for k in range(4):
        way = place_ref[0] ^ k
        upd = jnp.where(
            way == 0,
            mine[...],
            jnp.where(way == 2, from_x[...], jnp.where(way == 1, from_core[...], from_both[...])),
        )
        parts.append(both_ref[1, :, k * 256 : (k + 1) * 256] - upd)
    ra = jnp.concatenate(parts[:2], axis=1)
    rb = jnp.concatenate(parts[2:], axis=1)

    def u(r, c):
        rows, cols = slice(r * 512, r * 512 + 512), slice(c * 512, c * 512 + 512)
        return uh_ref[rows, cols], ul_ref[rows, cols]

    xa = mul(ra, u(0, 0))
    buf[0] = xa
    halves[0].start()
    xb = mul(rb - mul(xa, u(0, 1)), u(1, 1))
    buf[1] = xb
    halves[1].start()
    for copy in [first] + halves:
        copy.wait()


BOTH = ("bulk", "rep")

SPREAD, INVERT, LEAVE, ROWS, FIRST, SECOND = 1_000_000_000, 3_500_000_000, 500_000_000, 1_000_000_000, 200_000_000, 3_000_000_000


def swap_z(x, m):
    return lax.ppermute(x, "bulk", [(k, k ^ (2 * m)) for k in range(8)])


def swap_y(x):
    return lax.ppermute(x, "bulk", [(k, k ^ 1) for k in range(8)])


def swap_rep(x, bits):
    return lax.ppermute(x, "rep", [(k, k ^ bits) for k in range(4)])


def cross(x, stage):
    pairs = []
    for rep in range(4):
        for bulk in range(8):
            to = (rep ^ 2, bulk) if (rep & 1) == stage else (rep, bulk ^ 1)
            pairs.append((bulk * 4 + rep, to[1] * 4 + to[0]))
    return lax.ppermute(x, BOTH, pairs)


def after(x, *deps):
    return lax.optimization_barrier((x,) + deps)[0]


ANY = pl.BlockSpec(memory_space=pl.ANY)
VMEM = pl.BlockSpec(memory_space=pltpu.VMEM)
SMEM = pl.BlockSpec(memory_space=pltpu.SMEM)


def call(kernel, out, specs, outs, scratch, flops, size, name):
    return pl.pallas_call(
        kernel,
        out_shape=out,
        in_specs=specs,
        out_specs=outs,
        scratch_shapes=scratch,
        compiler_params=pltpu.CompilerParams(vmem_limit_bytes=size << 20),
        cost_estimate=pl.CostEstimate(flops=flops, bytes_accessed=2 << 20, transcendentals=0),
        name=name,
    )


OUT_SCRATCH = [pltpu.VMEM((2, 32, 512), F32), pltpu.SemaphoreType.DMA((3,))]


def shape(*dims, dtype=F32):
    return jax.ShapeDtypeStruct(dims, dtype)


def per_device(orbitals, triangles, coupling, diagonals):
    rep, bulk = lax.axis_index("rep"), lax.axis_index("bulk")
    place = jnp.stack([rep, bulk]).astype(jnp.int32)
    blocks = orbitals.reshape(4, 2, 32, 256)

    t = call(invert_kernel, shape(264, 128), [SMEM, VMEM, VMEM], VMEM, [], INVERT, 4, "invert")(
        place, triangles, diagonals
    )
    coup = after(coupling, t)

    near = jnp.stack([t, swap_z(t, 2)])
    far = swap_z(near, 1)
    near0 = swap_y(near)
    near1 = swap_rep(near, 2)
    near01 = swap_rep(near0, 2)

    leave = call(leave_kernel, shape(4, 32, 256), [SMEM, VMEM], VMEM, [], LEAVE, 4, "leave")(place, blocks)
    came = swap_y(after(leave, t))
    c_near = jnp.stack([coupling, swap_z(after(coup, near), 2)])
    c_near_got = swap_y(c_near)

    far_now = after(far, near0, near1, came, c_near)
    far0 = cross(far_now, 0)
    far1 = cross(far_now, 1)
    b_out = call(spread_kernel, [shape(2, 32, 256)] * 3, [SMEM, VMEM, VMEM], [VMEM] * 3, [], SPREAD, 4, "spread")(
        place, blocks, came
    )
    b_z = [swap_z(after(b, far), m + 1) for m, b in enumerate(b_out)]
    c_far = swap_z(after(c_near, far0), 1)
    c_far_got = swap_y(c_far)
    far01 = cross(after(far0, far1, near01), 1)

    left, both = call(
        rows_kernel,
        [shape(32, 1024), shape(2, 32, 1024)],
        [SMEM] + [VMEM] * 5,
        [VMEM] * 2,
        [],
        ROWS,
        4,
        "rows",
    )(place, blocks, came, *b_z)
    pair = jnp.stack([left, swap_rep(after(left, came), 2)])
    other_pair = swap_rep(after(pair, c_far), 1)
    bufs = [near, near0, near1, near01, far, far0, far1, far01]
    bufs += [swap_rep(after(b, b_z[2], far0), 1) for b in bufs[:7]] + [swap_rep(after(far01, far1), 1)]

    scratch = [pltpu.VMEM((8, 136, 128), F32)]
    halves = [shape(1024, 1024, dtype=BF16)] * 2
    x = call(
        first_kernel,
        shape(128, 1024),
        [SMEM] + [VMEM] * 18,
        VMEM,
        [pltpu.VMEM((1024, 1024), BF16)] * 2 + scratch,
        FIRST,
        24,
        "first_panel",
    )(place, pair, after(other_pair, c_near_got), *bufs)

    near_upd = call(near_kernel, shape(128, 256), [SMEM] + [VMEM] * 3, VMEM, [], 10_000_000, 24, "near_update")(
        place, x, c_near, c_near_got
    )
    mine, to_x, to_core, to_both = call(
        update_kernel,
        [shape(32, 256)] * 4,
        [SMEM] + [VMEM] * 4,
        [VMEM] * 4,
        [],
        2_000_000_000,
        24,
        "update",
    )(place, x, near_upd, c_far, c_far_got)
    back = [swap_rep(to_x, 2), swap_rep(to_core, 1), swap_rep(to_both, 3)]

    uh, ul = call(
        second_factor_kernel, halves, [SMEM] + [VMEM] * 16, [VMEM] * 2, scratch, SECOND, 24, "second_factor"
    )(after(place, mine), *bufs)

    return call(second_kernel, shape(32, 2048), [SMEM] + [VMEM] * 8, ANY, OUT_SCRATCH, 2_500_000_000, 24, "second_panel")(
        place, x, both, uh, ul, mine, *back
    )


def solution(mesh):
    special = mesh.shape["bulk"] == 8 and mesh.shape["rep"] == 4

    def run(orbitals, triangles, coupling, diagonals):
        fits = orbitals.shape == (1024, 2048) and triangles.shape == (1024, 1024)
        body = per_device if special and fits else per_device_any
        return jax.shard_map(
            body,
            mesh=mesh,
            in_specs=(P("rep", "bulk"), P("rep", "bulk"), P("rep", "bulk"), P(None, "bulk")),
            out_specs=P(("rep", "bulk"), None),
            check_vma=False,
        )(orbitals, triangles, coupling, diagonals)

    return run
```
